32 devices in a mesh: blk: 16 (over z, y, core), across: 2 (over x).
Axes of the slice: x: 2, y: 2, z: 4, core: 2. Of those that a mesh axis runs over, the one named last changes fastest.
Arguments:
- positions: float32 [3, 262144], P(None, ('blk', 'across')), may hold values from -4 to 4
- strengths: float32 [3, 262144], P(None, ('blk', 'across')), may hold values from -2.4 to 2.4
- radius: float32 [262144], P(('blk', 'across')), may hold values from 0.3 to 0.6
- block_count: int32 [2048], P(('blk', 'across')), may hold values from 64 to 128, as said below
- pair_target: int32 [32, 256], P(('blk', 'across')), may hold values from 0 to 127, as said below
- pair_slot: int32 [32, 256], P(('blk', 'across')), may hold values from 0 to 319, as said below
- pair_count: int32 [32], P(('blk', 'across')), may hold values from 64 to 256, as said below
Outputs:
- velocity: float32 [3, 262144], P(None, ('blk', 'across'))
- stretching: float32 [3, 262144], P(None, ('blk', 'across'))
- section_positions: float32 [3, 262144], P(None, ('blk', 'across'))
- section_strengths: float32 [3, 262144], P(None, ('blk', 'across'))
The draws below stay inside these ranges and needn't reach their ends.
Inputs may be any that keep to these rules, and one draw needn't show every extreme that they name: `block_count`: each block's live particles are its first slots; some block is full in every draw. Within one device's list the pairs (pair_target, pair_slot) are all different. `pair_slot`: the window's slots come in five runs of 64: slots k * 64 to (k + 1) * 64 - 1, for k = 0 to 4, are the blocks of the shard k - 2 away (two below, one below, the own shard, one above, two above, on a closed cycle of shards), each at the device's own place within its shard. `pair_count`: some shards use the whole list on every device in every draw; the others use a quarter to a half of it.
All inputs are finite; a program needn't handle non-finite values.
Results may differ from the reference program's by a relative error of at most 0.0001.
Values sent between devices are 32-bit elements; how exact they have to be, the bound alone decides.
No kernel may reach another device: no remote copies, remote signals or barrier semaphores. Data moves between devices by JAX's collectives and lax.ppermute only.
A program may use at most 64 MiB of HBM per device.

```python
import math
import jax
import jax.numpy as jnp
from jax import lax

BLOCK = 128
BLOCKS_DEV = 64
PAIR_GROUP = 16
BLOCKS_SHARD = 128
WINDOW_BLOCKS = 320
PAIRS_MOST = 256
ALL_BLOCKS = 2048
PARTICLES = 262144
N_BLK = 16
N_ACROSS = 2
DEVICES = 32


def draw_lists(key):

    def one_device(device_key):
        shuffled = jax.random.permutation(device_key, BLOCKS_SHARD * WINDOW_BLOCKS)[:PAIRS_MOST].astype(jnp.int32)
        return (shuffled // WINDOW_BLOCKS, shuffled % WINDOW_BLOCKS)
    device_keys = jax.random.split(key, DEVICES)
    return jax.vmap(one_device)(device_keys)


def draw_pair_target(key, part):
    target_rows, slot_rows = draw_lists(key)
    return target_rows.astype(jnp.int32)


def draw_pair_slot(key, part):
    target_rows, slot_rows = draw_lists(key)
    return slot_rows.astype(jnp.int32)


def draw_pair_count(key, part):
    key = jax.random.fold_in(key, 11)
    base_key, tip_key = jax.random.split(key)
    base_count = jax.random.randint(base_key, (DEVICES,), PAIRS_MOST // 4, PAIRS_MOST // 2 + 1, dtype=jnp.int32)
    tip_offset = jax.random.randint(tip_key, (), 0, N_BLK // 4, dtype=jnp.int32)
    shard_index = jnp.arange(DEVICES, dtype=jnp.int32) // N_ACROSS
    at_tip = (shard_index + tip_offset) % (N_BLK // 4) == 0
    return jnp.where(at_tip, PAIRS_MOST, base_count).astype(jnp.int32)


def draw_block_count(key, part):
    key = jax.random.fold_in(key, 5)
    count_key, full_key = jax.random.split(key)
    counts = jax.random.randint(count_key, (ALL_BLOCKS,), BLOCK // 2, BLOCK + 1, dtype=jnp.int32)
    full_block = jax.random.randint(full_key, (), 0, ALL_BLOCKS, dtype=jnp.int32)
    return jnp.where(jnp.arange(ALL_BLOCKS, dtype=jnp.int32) == full_block, BLOCK, counts).astype(jnp.int32)


def steps_of(stream_key, shape, pieces, least, top_value):
    def one(axis_at, blocks):
        draws = jax.random.uniform(jax.random.fold_in(jax.random.fold_in(stream_key, 6), axis_at), (blocks,), jnp.float32, least / len(pieces), top_value / len(pieces))
        return jnp.repeat(jnp.exp(draws), shape[axis_at] // blocks).reshape((-1,) + (1,) * (len(shape) - axis_at - 1))

    level = one(*pieces[0])
    for cut in pieces[1:]:
        level = level * one(*cut)
    return level


def centred(key, shape, deviation, limit, shards=(), kind=jnp.bfloat16):
    values = jax.random.normal(key, shape, jnp.float32) * deviation
    if len(shards) > 0:
        values = steps_of(key, shape, shards, -0.22, 0.18) * values
    return jnp.clip(values, min=-limit, max=limit).astype(kind)


def setup_inputs(seed: int = 0) -> dict:
    arg_keys = jax.random.split(jax.random.key(seed), 8)
    positions = centred(arg_keys[0], (3, PARTICLES), 1.0, 4.0, ((1, 32),), jnp.float32)
    strengths = centred(arg_keys[1], (3, PARTICLES), 0.4, 2.4, ((1, 32),), jnp.float32)
    radius = jnp.clip(jnp.exp(math.log(0.6) - 0.6931472 * jax.random.uniform(arg_keys[2], (PARTICLES,), jnp.float32) ** steps_of(arg_keys[2], (PARTICLES,), ((0, 32),), -0.2, 0.2)), 0.3, 0.6)
    block_count = draw_block_count(jax.random.fold_in(arg_keys[7], 71), 0)
    pair_target = draw_pair_target(jax.random.fold_in(arg_keys[7], 71), 0)
    pair_slot = draw_pair_slot(jax.random.fold_in(arg_keys[7], 71), 0)
    pair_count = draw_pair_count(jax.random.fold_in(arg_keys[7], 71), 0)
    return dict(positions=positions, strengths=strengths, radius=radius, block_count=block_count, pair_target=pair_target, pair_slot=pair_slot, pair_count=pair_count)


biot_factor = 0.07957747154594767
section_step = 0.05

def cross_product(left, right):
    first = left[:, 1] * right[:, 2] - left[:, 2] * right[:, 1]
    second = left[:, 2] * right[:, 0] - left[:, 0] * right[:, 2]
    third = left[:, 0] * right[:, 1] - left[:, 1] * right[:, 0]
    return jnp.stack([first, second, third], axis=1)

def pair_terms(target, source):
    target_pos = target[:, 0:3, :, None]
    target_str = target[:, 3:6, :, None]
    source_pos = source[:, 0:3, None, :]
    source_str = source[:, 3:6, None, :]
    inv_core = 1.0 / source[:, 6, None, :]
    offset_vec = target_pos - source_pos
    scaled = lax.optimization_barrier(jnp.sum(offset_vec * offset_vec, axis=1)) * inv_core * inv_core
    reciprocal = 1.0 / (scaled + 1.0)
    falloff = reciprocal * reciprocal * jnp.sqrt(reciprocal)
    core_cube = inv_core * inv_core * inv_core
    kernel_value = (scaled + 2.5) * falloff * core_cube
    kernel_slope = -(3.0 * scaled + 10.5) * falloff * reciprocal * core_cube * inv_core * inv_core
    swirling = cross_product(offset_vec, source_str)
    tilting = cross_product(target_str, source_str)
    projection = lax.optimization_barrier(jnp.sum(offset_vec * target_str, axis=1))
    velocity = lax.optimization_barrier(jnp.sum(kernel_value[:, None] * swirling, axis=3))
    stretch = lax.optimization_barrier(jnp.sum(kernel_value[:, None] * tilting + (kernel_slope * projection)[:, None] * swirling, axis=3))
    return -biot_factor * jnp.concatenate([velocity, stretch], axis=1)

def accumulate(partial_sum, pair_number, targets, sources, target_rows, source_rows):
    list_length = target_rows.shape[0]
    turns = (pair_number + PAIR_GROUP - 1) // PAIR_GROUP
    offsets = jnp.arange(PAIR_GROUP, dtype=jnp.int32)

    def one_turn(turn_index, partial_sum):
        entry_index = (turn_index * PAIR_GROUP + offsets).astype(jnp.int32)
        usable = (entry_index < pair_number).astype(jnp.float32)
        entry_index = jnp.minimum(entry_index, list_length - 1)
        target_index = target_rows[entry_index]
        source_index = source_rows[entry_index]
        pair_values = pair_terms(targets[target_index], sources[source_index]) * usable[:, None, None]
        return partial_sum.at[target_index].add(pair_values)
    return lax.fori_loop(jnp.int32(0), turns.astype(jnp.int32), one_turn, partial_sum)

def reference(positions, strengths, radius, block_count, pair_target, pair_slot, pair_count):
    slot_index = jnp.arange(BLOCK, dtype=jnp.int32)
    alive_mask = (slot_index[None, :] < block_count[:, None]).astype(jnp.float32)
    position_blocks = positions.reshape(3, ALL_BLOCKS, BLOCK).transpose(1, 0, 2)
    strength_blocks = strengths.reshape(3, ALL_BLOCKS, BLOCK).transpose(1, 0, 2) * alive_mask[:, None, :]
    radius_blocks = radius.reshape(ALL_BLOCKS, 1, BLOCK)
    sources = jnp.concatenate([position_blocks, strength_blocks, radius_blocks], axis=1)
    targets = sources[:, 0:6]
    shard_blocks = BLOCKS_DEV * N_ACROSS

    def per_device(device, partial_sum):
        device = device.astype(jnp.int32)
        shard = device // N_ACROSS
        member = device % N_ACROSS
        slots = pair_slot[device]
        neighbour = (shard + slots // BLOCKS_DEV - 2) % N_BLK
        source_rows = (neighbour * shard_blocks + member * BLOCKS_DEV + slots % BLOCKS_DEV).astype(jnp.int32)
        target_rows = (shard * shard_blocks + pair_target[device]).astype(jnp.int32)
        return accumulate(partial_sum, pair_count[device], targets, sources, target_rows, source_rows)
    start = jnp.zeros((ALL_BLOCKS, 6, BLOCK), jnp.float32)
    partial_sum = lax.fori_loop(jnp.int32(0), jnp.int32(DEVICES), per_device, start)
    result = partial_sum.transpose(1, 0, 2).reshape(6, PARTICLES)
    live_strengths = strength_blocks.transpose(1, 0, 2).reshape(3, PARTICLES)
    velocity = result[0:3]
    stretching = result[3:6]
    return (velocity, stretching, positions + section_step * velocity, live_strengths + section_step * stretching)
```

```python
import functools

import jax
import jax.numpy as jnp
from jax import lax
from jax.experimental import pallas as pl
from jax.experimental.pallas import tpu as pltpu
from jax.sharding import PartitionSpec as P

BLOCK = 128
ROWS = 8
REACH = 2
UNROLL = 4

biot_factor = 0.07957747154594767
section_step = 0.05


def passed_along(value, axis, steps):
    count = lax.axis_size(axis)
    pairs = [(source, (source + steps) % count) for source in range(count)]
    return lax.ppermute(value, axis, pairs)


def rounded(value):
    return value.astype(jnp.bfloat16).astype(jnp.float32)


def split_three(value):
    first = rounded(value)
    rest = value - first
    second = rounded(rest)
    return first, second, rest - second


def row_number(shape):
    return lax.broadcasted_iota(jnp.int32, shape, 0)


def sum_rows(value):
    return value[0:1] + value[1:2] + value[2:3]


def cross(left, right):
    return [
        left[1] * right[2] - left[2] * right[1],
        left[2] * right[0] - left[0] * right[2],
        left[0] * right[1] - left[1] * right[0],
    ]


def rows_of(block, start):
    return [block[start + k : start + k + 1] for k in range(3)]


def lane_slice(index):
    return pl.ds(pl.multiple_of(index * BLOCK, BLOCK), BLOCK)


def target_features(block):
    row = row_number((ROWS, BLOCK))
    centre = jnp.where(row < 3, jnp.mean(block, axis=1, keepdims=True), 0.0)
    moved = block - centre
    pos = rows_of(moved, 0)
    strength = rows_of(moved, 5)
    norm = pos[0] * pos[0] + pos[1] * pos[1] + pos[2] * pos[2]
    own = pos[0] * strength[0] + pos[1] * strength[1] + pos[2] * strength[2]
    one = jnp.ones_like(norm)
    nil = jnp.zeros_like(norm)
    near = jnp.concatenate(pos + [norm, one, nil, nil, nil], axis=0)
    half = [0.5 * s for s in strength]
    tilt = jnp.concatenate(half + [own, nil, nil, nil, nil], axis=0)
    zero = jnp.zeros((ROWS, BLOCK), jnp.float32)
    parts = []
    for value in (near, tilt):
        first, second, third = split_three(value)
        parts += [first, second, third, first, second, first, zero, zero]
    return centre, jnp.concatenate(parts, axis=0).astype(jnp.bfloat16)


def source_features(block, centre, weight):
    row = row_number((ROWS, BLOCK))
    moved = block - centre
    inv_core = moved[4:5]
    inv_square = inv_core * inv_core
    pos = rows_of(moved, 0)
    strength = rows_of(moved, 5)
    norm = pos[0] * pos[0] + pos[1] * pos[1] + pos[2] * pos[2]
    scale = jnp.where(row < 3, -2.0, jnp.where(row == 3, 1.0, 0.0))
    shape = moved * inv_square * scale
    shape = jnp.where(row == 4, norm * inv_square + 1.0, shape)
    first, second, third = split_three(shape)
    zero = jnp.zeros((ROWS, BLOCK), jnp.float32)
    left = jnp.concatenate([first, first, first, second, second, third, zero, zero], axis=0)
    left = left.astype(jnp.bfloat16)
    blank = jnp.zeros_like(left)
    shape = jnp.concatenate(
        [jnp.concatenate([left, blank], axis=1), jnp.concatenate([blank, left], axis=1)], axis=0
    )
    turned = cross(pos, strength)
    nil = jnp.zeros_like(norm)
    charge = jnp.concatenate(strength + turned + [nil, nil], axis=0)
    charge = charge * (inv_square * inv_core * weight)
    high = rounded(charge)
    return shape, jnp.concatenate([high, charge - high], axis=0).astype(jnp.bfloat16)


NT = (((1,), (1,)), ((), ()))


def pair_kernel(
    shards, number, target_list, slot_list, *refs
):
    count = 2 * REACH + 1
    windows, (targets_in, eye_ref) = refs[:count], refs[count : count + 2]
    out_ref, window, targets, features, centres, total, sems = refs[count + 2 :]
    blocks = windows[0].shape[1] // BLOCK
    target_blocks = targets_in.shape[1] // BLOCK
    list_length = target_list.shape[1]
    copies = [pltpu.make_async_copy(targets_in, targets, sems.at[count])]
    for k in range(count):
        copies.append(
            pltpu.make_async_copy(
                windows[k], window.at[:, pl.ds(k * blocks * BLOCK, blocks * BLOCK)], sems.at[k]
            )
        )
    for copy in copies:
        copy.start()
    copies[0].wait()

    def prepare(step, carry):
        for u in range(4):
            b = step * 4 + u
            centre, matrix = target_features(targets[:, lane_slice(b)])
            centres[b] = centre
            turned = lax.dot_general(
                eye_ref[...], matrix, NT, preferred_element_type=jnp.float32
            )
            features[b] = turned.astype(jnp.bfloat16)
            total[b] = jnp.zeros((2 * ROWS, BLOCK), jnp.float32)
        return carry

    lax.fori_loop(0, target_blocks // 4, prepare, 0)
    for copy in copies[1:]:
        copy.wait()
    listed = number[0]

    def turn(step, carry):
        for u in range(UNROLL):
            entry = step * UNROLL + u
            weight = jnp.where(entry < listed, 1.0, 0.0).astype(jnp.float32)
            entry = jnp.minimum(entry, list_length - 1)
            t = target_list[0, entry]
            s = slot_list[0, entry]
            shape, charge = source_features(window[:, lane_slice(s)], centres[t], weight)
            both = jnp.dot(features[t], shape, preferred_element_type=jnp.float32)
            near, tilt = both[:, :BLOCK], both[:, BLOCK:]
            q = lax.rsqrt(near)
            q2 = q * q
            q3 = q2 * q
            f = q3 * (q2 + (2.0 / 3.0))
            h = (q3 * q2) * (q2 + 0.4) * tilt
            fh = f.astype(jnp.bfloat16)
            fl = (f - fh.astype(jnp.float32)).astype(jnp.bfloat16)
            hh = h.astype(jnp.bfloat16)
            hl = (h - hh.astype(jnp.float32)).astype(jnp.bfloat16)
            stacked = jnp.concatenate([fh, fl, hh, hl], axis=0)
            sums = lax.dot_general(charge, stacked, NT, preferred_element_type=jnp.float32)
            fsum = sums[0:8, 0:128] + sums[8:16, 0:128] + sums[0:8, 128:256]
            hsum = sums[0:8, 256:384] + sums[8:16, 256:384] + sums[0:8, 384:512]
            total[t] += jnp.concatenate([fsum, hsum], axis=0)
        return carry

    lax.fori_loop(0, (listed + UNROLL - 1) // UNROLL, turn, 0)

    def finish(step, carry):
        for u in range(4):
            b = step * 4 + u
            block = targets[:, lane_slice(b)] - centres[b]
            sums = total[b]
            pos = rows_of(block, 0)
            strength = rows_of(block, 5)
            fa = rows_of(sums, 0)
            fb = rows_of(sums, 3)
            ha = rows_of(sums, 8)
            hb = rows_of(sums, 11)
            swirl = cross(pos, fa)
            velocity = [(-1.5 * biot_factor) * (swirl[k] - fb[k]) for k in range(3)]
            lean = cross(strength, fa)
            bend = cross(pos, ha)
            stretch = [
                (-1.5 * biot_factor) * lean[k] + (7.5 * biot_factor) * (bend[k] - hb[k])
                for k in range(3)
            ]
            nil = jnp.zeros_like(fa[0])
            out_ref[:, lane_slice(b)] = jnp.concatenate(velocity + stretch + [nil, nil], axis=0)
        return carry

    lax.fori_loop(0, target_blocks // 4, finish, 0)


def pair_sums(number, target_list, slot_list, windows, targets):
    count = len(windows)
    lanes = windows[0].shape[1]
    target_blocks = targets.shape[1] // BLOCK
    eye = jnp.eye(BLOCK, dtype=jnp.bfloat16)
    smem = pl.BlockSpec(memory_space=pltpu.SMEM)
    anyspace = pl.BlockSpec(memory_space=pl.ANY)
    vmem = pl.BlockSpec(memory_space=pltpu.VMEM)
    return pl.pallas_call(
        functools.partial(pair_kernel, count),
        out_shape=jax.ShapeDtypeStruct((ROWS, target_blocks * BLOCK), jnp.float32),
        in_specs=[smem] * 3 + [anyspace] * (count + 1) + [vmem],
        out_specs=vmem,
        scratch_shapes=[
            pltpu.VMEM((ROWS, count * lanes), jnp.float32),
            pltpu.VMEM((ROWS, target_blocks * BLOCK), jnp.float32),
            pltpu.VMEM((target_blocks, BLOCK, BLOCK), jnp.bfloat16),
            pltpu.VMEM((target_blocks, ROWS, BLOCK), jnp.float32),
            pltpu.VMEM((target_blocks, 2 * ROWS, BLOCK), jnp.float32),
            pltpu.SemaphoreType.DMA((count + 1,)),
        ],
        compiler_params=pltpu.CompilerParams(vmem_limit_bytes=48 * 1024 * 1024),
        name="pair_sums",
    )(number, target_list, slot_list, *windows, targets, eye)


def shards(positions, strengths, radius, block_count, pair_target, pair_slot, pair_count):
    blocks = block_count.shape[0]
    lanes = blocks * BLOCK
    slot_index = jnp.arange(BLOCK, dtype=jnp.int32)
    alive = (slot_index[None, :] < block_count[:, None]).astype(jnp.float32)
    live_strengths = strengths * alive.reshape(1, lanes)
    resident = jnp.concatenate(
        [positions, jnp.ones((1, lanes), jnp.float32), 1.0 / radius[None, :], live_strengths], axis=0
    )
    windows = [
        resident if away == 0 else passed_along(resident, "blk", -away)
        for away in range(-REACH, REACH + 1)
    ]
    members = lax.axis_size("across")
    me = lax.axis_index("across")
    if members == 2:
        other = passed_along(resident, "across", 1)
        first = jnp.where(me == 0, resident, other)
        second = jnp.where(me == 0, other, resident)
        targets = jnp.concatenate([first, second], axis=1)
    else:
        targets = lax.all_gather(resident, "across", axis=1, tiled=True)
    sums = pair_sums(pair_count, pair_target, pair_slot, windows, targets)
    if members == 2:
        first, second = sums[:, :lanes], sums[:, lanes:]
        mine = jnp.where(me == 0, first, second)
        away = jnp.where(me == 0, second, first)
        result = mine + passed_along(away, "across", 1)
    else:
        result = lax.psum_scatter(sums, "across", scatter_dimension=1, tiled=True)
    velocity = result[0:3]
    stretching = result[3:6]
    return (
        velocity,
        stretching,
        positions + section_step * velocity,
        live_strengths + section_step * stretching,
    )


def solution(mesh):
    whole = P(None, ("blk", "across"))
    line = P(("blk", "across"))
    return jax.shard_map(
        shards,
        mesh=mesh,
        in_specs=(whole, whole, line, line, P(("blk", "across"), None), P(("blk", "across"), None), line),
        out_specs=(whole, whole, whole, whole),
        check_vma=False,
    )
```

```python
import jax
import jax.numpy as jnp
from jax import lax
from jax.experimental import pallas as pl
from jax.experimental.pallas import tpu as pltpu
from jax.sharding import PartitionSpec as P

BLOCK = 128
ROWS = 8
REACH = 2
GROUP = 8
FEATURES = 64

biot_factor = 0.07957747154594767
section_step = 0.05


def passed_along(value, axis, steps):
    count = lax.axis_size(axis)
    pairs = [(source, (source + steps) % count) for source in range(count)]
    return lax.ppermute(value, axis, pairs)


def rounded(value):
    return value.astype(jnp.bfloat16).astype(jnp.float32)


def split_three(value):
    first = rounded(value)
    rest = value - first
    second = rounded(rest)
    return first, second, rest - second


def cross(left, right):
    return [
        left[1] * right[2] - left[2] * right[1],
        left[2] * right[0] - left[0] * right[2],
        left[0] * right[1] - left[1] * right[0],
    ]


def tile_rows(index, rows):
    return pl.ds(pl.multiple_of(index * rows, rows), rows)


def component(ref, base, number, stride):
    return ref[pl.ds(base + number, GROUP, stride=stride), :]


def store_component(ref, base, number, stride, value):
    ref[pl.ds(base + number, GROUP, stride=stride), :] = value


def target_features(targets, step, centres, rows):
    base = pl.multiple_of(step * (GROUP * ROWS), GROUP * ROWS)
    pos = [component(targets, base, k, ROWS) for k in range(3)]
    strength = [component(targets, base, 5 + k, ROWS) for k in range(3)]
    for k in range(3):
        centre = jnp.broadcast_to(jnp.mean(pos[k], axis=1, keepdims=True), (GROUP, BLOCK))
        store_component(centres, base, k, ROWS, centre)
        pos[k] = pos[k] - centre
    norm = pos[0] * pos[0] + pos[1] * pos[1] + pos[2] * pos[2]
    own = pos[0] * strength[0] + pos[1] * strength[1] + pos[2] * strength[2]
    near = pos + [norm, jnp.ones_like(norm)]
    tilt = [0.5 * s for s in strength] + [own]
    for start, values in ((0, near), (32, tilt)):
        for k, value in enumerate(values):
            parts = split_three(value)
            for slot, part in enumerate((0, 1, 2, 0, 1, 0)):
                store_component(rows, 0, start + 5 * slot + k, FEATURES, parts[part])


def source_features(gathered, weight, left, charge):
    pos = [component(gathered, 0, k, ROWS) for k in range(3)]
    inv_core = component(gathered, 0, 4, ROWS)
    strength = [component(gathered, 0, 5 + k, ROWS) for k in range(3)]
    inv_square = inv_core * inv_core
    norm = pos[0] * pos[0] + pos[1] * pos[1] + pos[2] * pos[2]
    twice = -2.0 * inv_square
    shape = [p * twice for p in pos] + [inv_square, norm * inv_square + 1.0]
    for k, value in enumerate(shape):
        parts = split_three(value)
        for slot, part in enumerate((0, 0, 0, 1, 1, 2)):
            store_component(left, 0, 5 * slot + k, 32, parts[part])
    scale = inv_square * inv_core * weight
    for k, value in enumerate(strength + cross(pos, strength)):
        value = value * scale
        high = rounded(value)
        store_component(charge, 0, k, 2 * ROWS, high)
        store_component(charge, 0, ROWS + k, 2 * ROWS, value - high)


NT = (((1,), (1,)), ((), ()))


def pair_kernel(number, target_list, slot_list, *refs):
    count = 2 * REACH + 1
    windows, (targets_in, eye_ref) = refs[:count], refs[count : count + 2]
    (
        out_ref,
        window,
        targets,
        features,
        centres,
        total,
        feature_rows,
        gathered,
        left,
        charge,
        sems,
    ) = refs[count + 2 :]
    shard_rows = windows[0].shape[0]
    target_blocks = targets_in.shape[0] // ROWS
    list_length = target_list.shape[1]
    copies = [pltpu.make_async_copy(targets_in, targets, sems.at[count])]
    for k in range(count):
        copies.append(
            pltpu.make_async_copy(
                windows[k], window.at[pl.ds(k * shard_rows, shard_rows), :], sems.at[k]
            )
        )
    for copy in copies:
        copy.start()
    centres[...] = jnp.zeros_like(centres)
    feature_rows[...] = jnp.zeros_like(feature_rows)
    left[...] = jnp.zeros_like(left)
    charge[...] = jnp.zeros_like(charge)
    copies[0].wait()

    def prepare(step, carry):
        target_features(targets, step, centres, feature_rows)
        for u in range(GROUP):
            b = step * GROUP + u
            rows = feature_rows[u * FEATURES : (u + 1) * FEATURES, :].astype(jnp.bfloat16)
            turned = lax.dot_general(eye_ref[...], rows, NT, preferred_element_type=jnp.float32)
            features[b] = turned.astype(jnp.bfloat16)
            total[tile_rows(b, 2 * ROWS), :] = jnp.zeros((2 * ROWS, BLOCK), jnp.float32)
        return carry

    lax.fori_loop(0, target_blocks // GROUP, prepare, 0)
    for copy in copies[1:]:
        copy.wait()
    listed = number[0]

    def entry_at(step, u):
        return jnp.minimum(step * GROUP + u, list_length - 1)

    def prepare_sources(step):
        for u in range(GROUP):
            entry = entry_at(step, u)
            t = target_list[0, entry]
            s = slot_list[0, entry]
            gathered[u * ROWS : (u + 1) * ROWS, :] = (
                window[tile_rows(s, ROWS), :] - centres[tile_rows(t, ROWS), :]
            )
        order = lax.broadcasted_iota(jnp.int32, (GROUP, BLOCK), 0) + step * GROUP
        weight = jnp.where(order < listed, 1.0, 0.0).astype(jnp.float32)
        source_features(gathered, weight, left, charge)

    def matrices(step, u):
        t = target_list[0, entry_at(step, u)]
        shape = left[u * 32 : (u + 1) * 32, :].astype(jnp.bfloat16)
        blank = jnp.zeros_like(shape)
        shape = jnp.concatenate(
            [jnp.concatenate([shape, blank], axis=1), jnp.concatenate([blank, shape], axis=1)],
            axis=0,
        )
        return jnp.dot(features[t], shape, preferred_element_type=jnp.float32)

    def weights(both):
        near, tilt = both[:, :BLOCK], both[:, BLOCK:]
        q = lax.rsqrt(near)
        q2 = q * q
        q3 = q2 * q
        f = q3 * (q2 + (2.0 / 3.0))
        h = (q3 * q2) * (q2 + 0.4) * tilt
        fh = f.astype(jnp.bfloat16)
        fl = (f - fh.astype(jnp.float32)).astype(jnp.bfloat16)
        hh = h.astype(jnp.bfloat16)
        hl = (h - hh.astype(jnp.float32)).astype(jnp.bfloat16)
        return jnp.concatenate([fh, fl, hh, hl], axis=0)

    def add_up(step, u, stacked):
        t = target_list[0, entry_at(step, u)]
        pair = charge[u * 2 * ROWS : (u + 1) * 2 * ROWS, :].astype(jnp.bfloat16)
        sums = lax.dot_general(pair, stacked, NT, preferred_element_type=jnp.float32)
        fsum = sums[0:8, 0:128] + sums[8:16, 0:128] + sums[0:8, 128:256]
        hsum = sums[0:8, 256:384] + sums[8:16, 256:384] + sums[0:8, 384:512]
        total[tile_rows(t, 2 * ROWS), :] += jnp.concatenate([fsum, hsum], axis=0)

    steps = (listed + GROUP - 1) // GROUP
    prepare_sources(0)

    def turn(step, carry):
        both = [matrices(step, 0), matrices(step, 1)]
        stacked = []
        for u in range(GROUP):
            stacked.append(weights(both[u]))
            if u + 2 < GROUP:
                both.append(matrices(step, u + 2))
            if u >= 1:
                add_up(step, u - 1, stacked[u - 1])
        add_up(step, GROUP - 1, stacked[GROUP - 1])
        prepare_sources(step + 1)
        return carry

    lax.fori_loop(0, steps, turn, 0)

    def finish(step, carry):
        base = pl.multiple_of(step * (GROUP * ROWS), GROUP * ROWS)
        wide = pl.multiple_of(step * (GROUP * 2 * ROWS), GROUP * 2 * ROWS)
        pos = [
            component(targets, base, k, ROWS) - component(centres, base, k, ROWS) for k in range(3)
        ]
        strength = [component(targets, base, 5 + k, ROWS) for k in range(3)]
        fa, fb, ha, hb = [
            [component(total, wide, start + k, 2 * ROWS) for k in range(3)] for start in (0, 3, 8, 11)
        ]
        swirl = cross(pos, fa)
        lean = cross(strength, fa)
        bend = cross(pos, ha)
        for k in range(3):
            velocity = (-1.5 * biot_factor) * (swirl[k] - fb[k])
            stretch = (-1.5 * biot_factor) * lean[k] + (7.5 * biot_factor) * (bend[k] - hb[k])
            store_component(out_ref, base, k, ROWS, velocity)
            store_component(out_ref, base, 3 + k, ROWS, stretch)
        for k in (6, 7):
            store_component(out_ref, base, k, ROWS, jnp.zeros_like(pos[0]))
        return carry

    lax.fori_loop(0, target_blocks // GROUP, finish, 0)


def pair_sums(number, target_list, slot_list, windows, targets):
    count = len(windows)
    shard_rows = windows[0].shape[0]
    target_rows = targets.shape[0]
    target_blocks = target_rows // ROWS
    eye = jnp.eye(BLOCK, dtype=jnp.bfloat16)
    smem = pl.BlockSpec(memory_space=pltpu.SMEM)
    anyspace = pl.BlockSpec(memory_space=pl.ANY)
    vmem = pl.BlockSpec(memory_space=pltpu.VMEM)
    return pl.pallas_call(
        pair_kernel,
        out_shape=jax.ShapeDtypeStruct((target_rows, BLOCK), jnp.float32),
        in_specs=[smem] * 3 + [anyspace] * (count + 1) + [vmem],
        out_specs=vmem,
        scratch_shapes=[
            pltpu.VMEM((count * shard_rows, BLOCK), jnp.float32),
            pltpu.VMEM((target_rows, BLOCK), jnp.float32),
            pltpu.VMEM((target_blocks, BLOCK, FEATURES), jnp.bfloat16),
            pltpu.VMEM((target_rows, BLOCK), jnp.float32),
            pltpu.VMEM((2 * target_rows, BLOCK), jnp.float32),
            pltpu.VMEM((GROUP * FEATURES, BLOCK), jnp.float32),
            pltpu.VMEM((GROUP * ROWS, BLOCK), jnp.float32),
            pltpu.VMEM((GROUP * 32, BLOCK), jnp.float32),
            pltpu.VMEM((GROUP * 2 * ROWS, BLOCK), jnp.float32),
            pltpu.SemaphoreType.DMA((count + 1,)),
        ],
        compiler_params=pltpu.CompilerParams(vmem_limit_bytes=48 * 1024 * 1024),
        name="pair_sums",
    )(number, target_list, slot_list, *windows, targets, eye)


def tiles(value, blocks):
    rows = value.shape[0]
    return value.reshape(rows, blocks, BLOCK).transpose(1, 0, 2).reshape(blocks * rows, BLOCK)


def rows_again(value, blocks):
    rows = value.shape[0] // blocks
    return value.reshape(blocks, rows, BLOCK).transpose(1, 0, 2).reshape(rows, blocks * BLOCK)


def shards(positions, strengths, radius, block_count, pair_target, pair_slot, pair_count):
    blocks = block_count.shape[0]
    lanes = blocks * BLOCK
    slot_index = jnp.arange(BLOCK, dtype=jnp.int32)
    alive = (slot_index[None, :] < block_count[:, None]).astype(jnp.float32)
    live_strengths = strengths * alive.reshape(1, lanes)
    resident = jnp.concatenate(
        [positions, jnp.ones((1, lanes), jnp.float32), 1.0 / radius[None, :], live_strengths], axis=0
    )
    resident = tiles(resident, blocks)
    windows = [
        resident if away == 0 else passed_along(resident, "blk", -away)
        for away in range(-REACH, REACH + 1)
    ]
    members = lax.axis_size("across")
    me = lax.axis_index("across")
    if members == 2:
        other = passed_along(resident, "across", 1)
        first = jnp.where(me == 0, resident, other)
        second = jnp.where(me == 0, other, resident)
        targets = jnp.concatenate([first, second], axis=0)
    else:
        targets = lax.all_gather(resident, "across", axis=0, tiled=True)
    sums = pair_sums(pair_count, pair_target, pair_slot, windows, targets)
    if members == 2:
        first, second = sums[: blocks * ROWS], sums[blocks * ROWS :]
        mine = jnp.where(me == 0, first, second)
        away = jnp.where(me == 0, second, first)
        result = mine + passed_along(away, "across", 1)
    else:
        result = lax.psum_scatter(sums, "across", scatter_dimension=0, tiled=True)
    result = rows_again(result, blocks)
    velocity = result[0:3]
    stretching = result[3:6]
    return (
        velocity,
        stretching,
        positions + section_step * velocity,
        live_strengths + section_step * stretching,
    )


def solution(mesh):
    whole = P(None, ("blk", "across"))
    line = P(("blk", "across"))
    return jax.shard_map(
        shards,
        mesh=mesh,
        in_specs=(whole, whole, line, line, P(("blk", "across"), None), P(("blk", "across"), None), line),
        out_specs=(whole, whole, whole, whole),
        check_vma=False,
    )
```

```python
import jax
import jax.numpy as jnp
from jax import lax
from jax.experimental import pallas as pl
from jax.experimental.pallas import tpu as pltpu
from jax.sharding import PartitionSpec as P

BLOCK = 128
ROWS = 8
SENT = 7
REACH = 2
GROUP = 8
FEATURES = 64
CLASSES = 4

biot_factor = 0.07957747154594767
section_step = 0.05


def moved(value, axis, target_of):
    pairs = [(source, target_of(source)) for source in range(lax.axis_size(axis))]
    return lax.ppermute(value, axis, pairs)


def to_other_core(source):
    return source ^ 1


def to_paired_chip(source):
    return source ^ 2


def along_chips(count):
    return lambda source: (source + (4 if source & 2 == 0 else -4)) % count


HOME_FLOPS = 10**10
NEAR_FLOPS = 10**10
FAR_FLOPS = 10**10


def rounded(value):
    return value.astype(jnp.bfloat16).astype(jnp.float32)


def split_three(value):
    first = rounded(value)
    rest = value - first
    second = rounded(rest)
    return first, second, rest - second


def cross(left, right):
    return [
        left[1] * right[2] - left[2] * right[1],
        left[2] * right[0] - left[0] * right[2],
        left[0] * right[1] - left[1] * right[0],
    ]


def tile_rows(index, rows):
    return pl.ds(pl.multiple_of(index * rows, rows), rows)


def component(ref, base, number, stride):
    return ref[pl.ds(base + number, GROUP, stride=stride), :]


def store_component(ref, base, number, stride, value):
    ref[pl.ds(base + number, GROUP, stride=stride), :] = value


def target_features(targets, step, centres, rows):
    base = pl.multiple_of(step * (GROUP * ROWS), GROUP * ROWS)
    pos = [component(targets, base, k, ROWS) for k in range(3)]
    strength = [component(targets, base, 3 + k, ROWS) for k in range(3)]
    for k in range(3):
        centre = jnp.broadcast_to(jnp.mean(pos[k], axis=1, keepdims=True), (GROUP, BLOCK))
        store_component(centres, base, k, ROWS, centre)
        pos[k] = pos[k] - centre
    for k in range(3, ROWS):
        store_component(centres, base, k, ROWS, jnp.zeros_like(pos[0]))
    norm = pos[0] * pos[0] + pos[1] * pos[1] + pos[2] * pos[2]
    own = pos[0] * strength[0] + pos[1] * strength[1] + pos[2] * strength[2]
    near = pos + [norm, jnp.ones_like(norm)]
    tilt = [0.5 * s for s in strength] + [own]
    for start, values in ((0, near), (32, tilt)):
        for k, value in enumerate(values):
            parts = split_three(value)
            for slot, part in enumerate((0, 1, 2, 0, 1, 0)):
                store_component(rows, 0, start + 5 * slot + k, FEATURES, parts[part])


def source_features(gathered, weight, left, charge):
    pos = [component(gathered, 0, k, ROWS) for k in range(3)]
    strength = [component(gathered, 0, 3 + k, ROWS) for k in range(3)]
    inv_core = component(gathered, 0, 6, ROWS)
    inv_square = inv_core * inv_core
    norm = pos[0] * pos[0] + pos[1] * pos[1] + pos[2] * pos[2]
    twice = -2.0 * inv_square
    shape = [p * twice for p in pos] + [inv_square, norm * inv_square + 1.0]
    for k, value in enumerate(shape):
        parts = split_three(value)
        for slot, part in enumerate((0, 0, 0, 1, 1, 2)):
            store_component(left, 0, 5 * slot + k, 32, parts[part])
    scale = inv_square * inv_core * weight
    for k, value in enumerate(strength + cross(pos, strength)):
        value = value * scale
        high = rounded(value)
        store_component(charge, 0, k, 2 * ROWS, high)
        store_component(charge, 0, ROWS + k, 2 * ROWS, value - high)


NT = (((1,), (1,)), ((), ()))


def unpack(sent, tile_ref, first):
    blocks = sent.shape[0] // SENT
    for j in range(blocks // GROUP):
        base = pl.multiple_of((first + j * GROUP) * ROWS, GROUP * ROWS)
        for k in range(SENT):
            rows = sent[k * blocks + j * GROUP : k * blocks + (j + 1) * GROUP, :]
            store_component(tile_ref, base, k, ROWS, rows)


def prepare_targets(first, last, state, eye, feature_rows):
    targets, features, centres, total = state

    def prepare(step, carry):
        target_features(targets, step, centres, feature_rows)
        for u in range(GROUP):
            b = step * GROUP + u
            rows = feature_rows[u * FEATURES : (u + 1) * FEATURES, :].astype(jnp.bfloat16)
            turned = lax.dot_general(eye, rows, NT, preferred_element_type=jnp.float32)
            features[b] = turned.astype(jnp.bfloat16)
            total[tile_rows(b, 2 * ROWS), :] = jnp.zeros((2 * ROWS, BLOCK), jnp.float32)
        return carry

    lax.fori_loop(first // GROUP, last // GROUP, prepare, 0)


def unit_matrix():
    row = lax.broadcasted_iota(jnp.int32, (BLOCK, BLOCK), 0)
    column = lax.broadcasted_iota(jnp.int32, (BLOCK, BLOCK), 1)
    return jnp.where(row == column, 1.0, 0.0).astype(jnp.bfloat16)


def run_class(kind, lists, window, state, scratch):
    target_list, slot_list, counts = lists
    _, features, centres, total = state
    gathered, left, charge = scratch
    length = target_list.shape[0] // (CLASSES + 1)
    listed = counts[kind]

    def entry_at(step, u):
        return kind * length + jnp.minimum(step * GROUP + u, listed - 1)

    def prepare_sources(step):
        for u in range(GROUP):
            entry = entry_at(step, u)
            gathered[u * ROWS : (u + 1) * ROWS, :] = (
                window[tile_rows(slot_list[entry], ROWS), :]
                - centres[tile_rows(target_list[entry], ROWS), :]
            )
        order = lax.broadcasted_iota(jnp.int32, (GROUP, BLOCK), 0) + step * GROUP
        weight = jnp.where(order < listed, 1.0, 0.0).astype(jnp.float32)
        source_features(gathered, weight, left, charge)

    def matrices(step, u):
        shape = left[u * 32 : (u + 1) * 32, :].astype(jnp.bfloat16)
        blank = jnp.zeros_like(shape)
        shape = jnp.concatenate(
            [jnp.concatenate([shape, blank], axis=1), jnp.concatenate([blank, shape], axis=1)],
            axis=0,
        )
        t = target_list[entry_at(step, u)]
        return jnp.dot(features[t], shape, preferred_element_type=jnp.float32)

    def weights(both):
        near, tilt = both[:, :BLOCK], both[:, BLOCK:]
        q = lax.rsqrt(near)
        q2 = q * q
        q3 = q2 * q
        f = q3 * (q2 + (2.0 / 3.0))
        h = (q3 * q2) * (q2 + 0.4) * tilt
        fh = f.astype(jnp.bfloat16)
        fl = (f - fh.astype(jnp.float32)).astype(jnp.bfloat16)
        hh = h.astype(jnp.bfloat16)
        hl = (h - hh.astype(jnp.float32)).astype(jnp.bfloat16)
        return jnp.concatenate([fh, fl, hh, hl], axis=0)

    def add_up(step, u, stacked):
        t = target_list[entry_at(step, u)]
        pair = charge[u * 2 * ROWS : (u + 1) * 2 * ROWS, :].astype(jnp.bfloat16)
        sums = lax.dot_general(pair, stacked, NT, preferred_element_type=jnp.float32)
        fsum = sums[0:8, 0:128] + sums[8:16, 0:128] + sums[0:8, 128:256]
        hsum = sums[0:8, 256:384] + sums[8:16, 256:384] + sums[0:8, 384:512]
        total[tile_rows(t, 2 * ROWS), :] += jnp.concatenate([fsum, hsum], axis=0)

    def turn(step, carry):
        both = [matrices(step, 0), matrices(step, 1)]
        stacked = []
        for u in range(GROUP):
            stacked.append(weights(both[u]))
            if u + 2 < GROUP:
                both.append(matrices(step, u + 2))
            if u >= 1:
                add_up(step, u - 1, stacked[u - 1])
        add_up(step, GROUP - 1, stacked[GROUP - 1])
        prepare_sources(step + 1)
        return carry

    @pl.when(listed > 0)
    def _():
        left[...] = jnp.zeros_like(left)
        charge[...] = jnp.zeros_like(charge)
        prepare_sources(0)
        lax.fori_loop(0, (listed + GROUP - 1) // GROUP, turn, 0)


def finish(first, last, state, out_ref):
    targets, _, centres, total = state
    blocks = out_ref.shape[1] // 6

    def one(step, carry):
        base = pl.multiple_of((first + step * GROUP) * ROWS, GROUP * ROWS)
        wide = pl.multiple_of((first + step * GROUP) * 2 * ROWS, GROUP * 2 * ROWS)
        pos = [
            component(targets, base, k, ROWS) - component(centres, base, k, ROWS) for k in range(3)
        ]
        strength = [component(targets, base, 3 + k, ROWS) for k in range(3)]
        fa, fb, ha, hb = [
            [component(total, wide, start + k, 2 * ROWS) for k in range(3)] for start in (0, 3, 8, 11)
        ]
        swirl = cross(pos, fa)
        lean = cross(strength, fa)
        bend = cross(pos, ha)
        member = step * GROUP // blocks
        inside = lax.rem(step * GROUP, blocks)
        for k in range(3):
            velocity = (-1.5 * biot_factor) * (swirl[k] - fb[k])
            stretch = (-1.5 * biot_factor) * lean[k] + (7.5 * biot_factor) * (bend[k] - hb[k])
            out_ref[member, pl.ds(pl.multiple_of(k * blocks + inside, GROUP), GROUP), :] = velocity
            out_ref[member, pl.ds(pl.multiple_of((3 + k) * blocks + inside, GROUP), GROUP), :] = stretch
        return carry

    lax.fori_loop(0, (last - first) // GROUP, one, 0)


def pack_kernel(block_count, positions, strengths, radius, sent):
    blocks = block_count.shape[0]
    lane = lax.broadcasted_iota(jnp.int32, (3, BLOCK), 1)
    for b in range(blocks):
        lanes = slice(b * BLOCK, (b + 1) * BLOCK)
        sent[pl.ds(b, 3, stride=blocks), :] = positions[:, lanes]
        live = jnp.where(lane < block_count[b], strengths[:, lanes], 0.0)
        sent[pl.ds(3 * blocks + b, 3, stride=blocks), :] = live
    sent[6 * blocks :, :] = 1.0 / radius[...]


def sort_list(number, pair_target, pair_slot, lists, blocks, members):
    target_list, slot_list, counts = lists
    length = pair_target.shape[1]
    listed = number[0]
    me = lax.axis_index("across")
    partner = jnp.where(lax.axis_index("blk") % 2 == 0, REACH + 1, REACH - 1)

    def one(step, carry):
        for u in range(GROUP):
            entry = jnp.minimum(step * GROUP + u, length - 1)
            t = pair_target[0, entry]
            s = pair_slot[0, entry]
            t = t - me * blocks
            t = jnp.where(t < 0, t + members * blocks, t)
            run = s // blocks
            mine = t < blocks
            home = run == REACH
            near = home | (run == partner)
            kind = jnp.where(near, jnp.where(home & mine, 0, 1), jnp.where(mine, 3, 2))
            kind = jnp.where(step * GROUP + u < listed, kind, CLASSES)
            at = kind * length
            for c in range(CLASSES):
                at = at + jnp.where(kind == c, carry[c], 0)
            target_list[at] = t
            slot_list[at] = s
            carry = tuple(carry[c] + jnp.where(kind == c, 1, 0) for c in range(CLASSES))
        return carry

    zero = jnp.int32(0)
    found = lax.fori_loop(0, (listed + GROUP - 1) // GROUP, one, (zero,) * CLASSES)
    for c in range(CLASSES):
        counts[c] = found[c]


def home_kernel(number, pair_target, pair_slot, own, *refs):
    target_list, slot_list, counts, targets, features, centres, total = refs[:7]
    feature_rows, gathered, left, charge = refs[7:]
    lists, state = refs[:3], refs[3:7]
    blocks = own.shape[0] // SENT
    unpack(own, targets, 0)
    feature_rows[...] = jnp.zeros_like(feature_rows)
    prepare_targets(0, blocks, state, unit_matrix(), feature_rows)
    sort_list(number, pair_target, pair_slot, lists, blocks, targets.shape[0] // ROWS // blocks)
    run_class(0, lists, targets_as_window(targets, blocks), state, (gathered, left, charge))


class targets_as_window:
    def __init__(self, targets, blocks):
        self.targets, self.start = targets, REACH * blocks * ROWS

    def __getitem__(self, index):
        rows, lanes = index
        return self.targets[pl.ds(pl.multiple_of(rows.start - self.start, ROWS), rows.size), lanes]


def near_kernel(*refs, members):
    target_list, slot_list, counts, own, partner = refs[:5]
    others = refs[5 : 5 + members - 1]
    given = refs[5 + members - 1 :][4:]
    targets, features, centres, total = state = given[:4]
    window, feature_rows, gathered, left, charge = given[4:]
    lists = refs[:3]
    blocks = own.shape[0] // SENT
    for r, other in enumerate(others):
        unpack(other, targets, (r + 1) * blocks)
    feature_rows[...] = jnp.zeros_like(feature_rows)
    prepare_targets(blocks, members * blocks, state, unit_matrix(), feature_rows)
    unpack(own, window, REACH * blocks)
    side = jnp.where(lax.axis_index("blk") % 2 == 0, REACH + 1, REACH - 1)
    unpack(partner, window, side * blocks)
    run_class(1, lists, window, state, (gathered, left, charge))


def far_kernel(target_list, slot_list, counts, paired, passed, crossed, *refs):
    given = refs[4:]
    targets, features, centres, total = state = given[:4]
    window, out_ref = given[4:6]
    gathered, left, charge = given[6:]
    lists = (target_list, slot_list, counts)
    blocks = paired.shape[0] // SENT
    shard = lax.axis_index("blk")
    even = shard // 2 % 2 == 0
    unpack(paired, window, jnp.where(even, 2 * REACH, 0) * blocks)
    unpack(passed, window, jnp.where(even, 0, 2 * REACH) * blocks)
    unpack(crossed, window, jnp.where(shard % 2 == 0, REACH - 1, REACH + 1) * blocks)
    run_class(2, lists, window, state, (gathered, left, charge))
    finish(blocks, targets.shape[0] // ROWS, state, out_ref)


def last_kernel(target_list, slot_list, counts, window, *refs):
    given = refs[4:]
    targets, features, centres, total = state = given[:4]
    out_ref, gathered, left, charge = given[4:]
    lists = (target_list, slot_list, counts)
    run_class(3, lists, window, state, (gathered, left, charge))
    finish(0, window.shape[0] // ROWS // (2 * REACH + 1), state, out_ref)


def section_kernel(sent, sums, *refs):
    returned, (velocity, stretching, section_positions, section_strengths) = refs[:-4], refs[-4:]
    blocks = sent.shape[0] // SENT

    for b in range(blocks):
        lanes = slice(b * BLOCK, (b + 1) * BLOCK)

        def rows(ref, start):
            return ref[pl.ds(start * blocks + b, 3, stride=blocks), :]

        for start, result, stepped in ((0, velocity, section_positions), (3, stretching, section_strengths)):
            value = rows(sums, start)
            for other in returned:
                value = value + rows(other, start)
            result[:, lanes] = value
            stepped[:, lanes] = rows(sent, start) + section_step * value


def call(kernel, name, inputs, outputs, scratch, aliases=None, flops=0):
    smem = pl.BlockSpec(memory_space=pltpu.SMEM)
    vmem = pl.BlockSpec(memory_space=pltpu.VMEM)

    def spec(value):
        return smem if len(value.shape) == 1 or value.dtype == jnp.int32 else vmem

    return pl.pallas_call(
        kernel,
        out_shape=outputs,
        in_specs=[spec(value) for value in inputs],
        out_specs=[spec(value) for value in outputs],
        scratch_shapes=scratch,
        input_output_aliases=aliases or {},
        compiler_params=pltpu.CompilerParams(vmem_limit_bytes=40 * 1024 * 1024),
        cost_estimate=pl.CostEstimate(flops=flops, bytes_accessed=0, transcendentals=0),
        name=name,
    )(*inputs)


def shards(positions, strengths, radius, block_count, pair_target, pair_slot, pair_count):
    blocks = block_count.shape[0]
    length = pair_target.shape[1]
    members = lax.axis_size("across")
    shard = lax.axis_index("blk")
    count = lax.axis_size("blk")

    def f32(*shape):
        return jax.ShapeDtypeStruct(shape, jnp.float32)

    def i32(*shape):
        return jax.ShapeDtypeStruct(shape, jnp.int32)

    (own,) = call(
        pack_kernel,
        "pack",
        (block_count, positions, strengths, radius.reshape(blocks, BLOCK)),
        [f32(SENT * blocks, BLOCK)],
        [],
    )
    paired = moved(own, "blk", to_paired_chip)
    others = [
        moved(own, "across", lambda source: (source - away) % members) for away in range(1, members)
    ]
    partner = moved(own, "blk", to_other_core)
    passed = moved(paired, "blk", along_chips(count))
    core = shard % 2
    chip = shard // 2 % 2
    crossed = moved(jnp.where(core == chip, paired, passed), "blk", to_other_core)

    state_shapes = [
        f32(members * blocks * ROWS, BLOCK),
        jax.ShapeDtypeStruct((members * blocks, BLOCK, FEATURES), jnp.bfloat16),
        f32(members * blocks * ROWS, BLOCK),
        f32(members * blocks * 2 * ROWS, BLOCK),
    ]
    window_shape = f32((2 * REACH + 1) * blocks * ROWS, BLOCK)
    list_shapes = [i32((CLASSES + 1) * length), i32((CLASSES + 1) * length), i32(CLASSES)]
    feature_rows = pltpu.VMEM((GROUP * FEATURES, BLOCK), jnp.float32)
    scratch = [
        pltpu.VMEM((GROUP * ROWS, BLOCK), jnp.float32),
        pltpu.VMEM((GROUP * 32, BLOCK), jnp.float32),
        pltpu.VMEM((GROUP * 2 * ROWS, BLOCK), jnp.float32),
    ]
    window_scratch = pltpu.VMEM(window_shape.shape, jnp.float32)

    def in_place(start, values=4):
        return {start + k: k for k in range(values)}

    results = call(
        home_kernel,
        "home_pairs",
        (pair_count, pair_target, pair_slot, own),
        list_shapes + state_shapes,
        [feature_rows] + scratch,
        flops=HOME_FLOPS,
    )
    lists, state = results[:3], results[3:]
    state = call(
        lambda *refs: near_kernel(*refs, members=members),
        "near_pairs",
        (*lists, own, partner, *others, *state),
        state_shapes,
        [window_scratch, feature_rows] + scratch,
        in_place(4 + members),
        flops=NEAR_FLOPS,
    )
    *state, window, away_sums = call(
        far_kernel,
        "far_pairs",
        (*lists, paired, passed, crossed, *state),
        state_shapes + [window_shape, f32(members - 1, 6 * blocks, BLOCK)],
        scratch,
        in_place(6),
        flops=FAR_FLOPS,
    )
    returned = [
        moved(away_sums[away - 1], "across", lambda source: (source + away) % members)
        for away in range(1, members)
    ]
    *state, sums = call(
        last_kernel,
        "last_pairs",
        (*lists, window, *state),
        state_shapes + [f32(1, 6 * blocks, BLOCK)],
        scratch,
        in_place(4),
        flops=FAR_FLOPS,
    )
    wide = f32(3, blocks * BLOCK)
    return tuple(
        call(section_kernel, "section", (own, sums[0], *returned), [wide] * 4, [])
    )


def solution(mesh):
    whole = P(None, ("blk", "across"))
    line = P(("blk", "across"))
    return jax.shard_map(
        shards,
        mesh=mesh,
        in_specs=(whole, whole, line, line, P(("blk", "across"), None), P(("blk", "across"), None), line),
        out_specs=(whole, whole, whole, whole),
        check_vma=False,
    )
```

```python
import jax
import jax.numpy as jnp
from jax import lax
from jax.experimental import pallas as pl
from jax.experimental.pallas import tpu as pltpu
from jax.sharding import PartitionSpec as P

BLOCK = 128
ROWS = 8
REACH = 2
GROUP = 8
HALF = 4
FEATURES = 64
CLASSES = 8

biot_factor = 0.07957747154594767
section_step = 0.05


def moved(value, axis, target_of):
    pairs = [(source, target_of(source)) for source in range(lax.axis_size(axis))]
    return lax.ppermute(value, axis, pairs)


def to_other_core(source):
    return source ^ 1


def to_paired_chip(source):
    return source ^ 2


def along_chips(count):
    return lambda source: (source + (4 if source & 2 == 0 else -4)) % count


HOME_FLOPS = 10**10
NEAR_FLOPS = 10**10
FAR_FLOPS = 10**10


def rounded(value):
    return value.astype(jnp.bfloat16).astype(jnp.float32)


def split_three(value):
    first = rounded(value)
    rest = value - first
    second = rounded(rest)
    return first, second, rest - second


def cross(left, right):
    return [
        left[1] * right[2] - left[2] * right[1],
        left[2] * right[0] - left[0] * right[2],
        left[0] * right[1] - left[1] * right[0],
    ]


def tile_rows(index, rows):
    return pl.ds(pl.multiple_of(index * rows, rows), rows)


def component(ref, base, number, stride):
    return ref[pl.ds(base + number, GROUP, stride=stride), :]


def store_component(ref, base, number, stride, value):
    ref[pl.ds(base + number, GROUP, stride=stride), :] = value


def target_features(targets, step, centres, rows):
    base = pl.multiple_of(step * (GROUP * ROWS), GROUP * ROWS)
    pos = [component(targets, base, k, ROWS) for k in range(3)]
    strength = [component(targets, base, 3 + k, ROWS) for k in range(3)]
    for k in range(3):
        centre = jnp.broadcast_to(jnp.mean(pos[k], axis=1, keepdims=True), (GROUP, BLOCK))
        store_component(centres, base, k, ROWS, centre)
        pos[k] = pos[k] - centre
    for k in range(3, ROWS):
        store_component(centres, base, k, ROWS, jnp.zeros_like(pos[0]))
    norm = pos[0] * pos[0] + pos[1] * pos[1] + pos[2] * pos[2]
    own = pos[0] * strength[0] + pos[1] * strength[1] + pos[2] * strength[2]
    near = pos + [norm, jnp.ones_like(norm)]
    tilt = [0.5 * s for s in strength] + [own]
    for start, values in ((0, near), (32, tilt)):
        for k, value in enumerate(values):
            parts = split_three(value)
            for slot, part in enumerate((0, 1, 2, 0, 1, 0)):
                store_component(rows, 0, start + 5 * slot + k, BLOCK, parts[part])


def source_features(gathered, weight, left, charge):
    pos = [component(gathered, 0, k, ROWS) for k in range(3)]
    strength = [component(gathered, 0, 3 + k, ROWS) for k in range(3)]
    inv_core = 1.0 / component(gathered, 0, 6, ROWS)
    inv_square = inv_core * inv_core
    norm = pos[0] * pos[0] + pos[1] * pos[1] + pos[2] * pos[2]
    twice = -2.0 * inv_square
    shape = [p * twice for p in pos] + [inv_square, norm * inv_square + 1.0]
    for k, value in enumerate(shape):
        parts = split_three(value)
        for slot, part in enumerate((0, 0, 0, 1, 1, 2)):
            store_component(left, 0, 5 * slot + k, 32, parts[part])
    scale = inv_square * inv_core * weight
    for k, value in enumerate(strength + cross(pos, strength)):
        value = value * scale
        high = rounded(value)
        store_component(charge, 0, k, 2 * ROWS, high)
        store_component(charge, 0, ROWS + k, 2 * ROWS, value - high)


NT = (((1,), (1,)), ((), ()))


def put_tiles(window, first, tiles):
    window[pl.ds(pl.multiple_of(first * ROWS, ROWS), tiles.shape[0]), :] = tiles[...]


def prepare_targets(state, eye, feature_rows):
    targets, features, centres, total = state
    feature_rows[...] = jnp.zeros_like(feature_rows)

    def prepare(step, carry):
        target_features(targets, step, centres, feature_rows)
        for first in range(0, GROUP, 4):
            rows = feature_rows[first * BLOCK : (first + 4) * BLOCK, :].astype(jnp.bfloat16)
            turned = lax.dot_general(eye, rows, NT, preferred_element_type=jnp.float32)
            for u in range(4):
                part = turned[:, u * BLOCK : u * BLOCK + FEATURES]
                features[step * GROUP + first + u] = part.astype(jnp.bfloat16)
        wide = pl.ds(pl.multiple_of(step * GROUP * 2 * ROWS, GROUP * 2 * ROWS), GROUP * 2 * ROWS)
        total[wide, :] = jnp.zeros((GROUP * 2 * ROWS, BLOCK), jnp.float32)
        return carry

    lax.fori_loop(0, features.shape[0] // GROUP, prepare, 0)


def unit_matrix():
    row = lax.broadcasted_iota(jnp.int32, (BLOCK, BLOCK), 0)
    column = lax.broadcasted_iota(jnp.int32, (BLOCK, BLOCK), 1)
    return jnp.where(row == column, 1.0, 0.0).astype(jnp.bfloat16)


def run_class(kind, lists, window, state, scratch):
    _, features, centres, total = state
    gathered, left, charge_next, charge, first_half, second_half = scratch
    listed = lists[2 * ROWS + kind, 0]

    def entry_at(step, u):
        entry = jnp.minimum(step * GROUP + u, listed - 1)
        return entry // BLOCK * (3 * ROWS) + kind, lax.rem(entry, BLOCK)

    def target_of(step, u):
        row, column = entry_at(step, u)
        return lists[row, column]

    def prepare_sources(step):
        for u in range(GROUP):
            row, column = entry_at(step, u)
            gathered[u * ROWS : (u + 1) * ROWS, :] = (
                window[tile_rows(lists[row + ROWS, column], ROWS), :]
                - centres[tile_rows(lists[row, column], ROWS), :]
            )
        order = lax.broadcasted_iota(jnp.int32, (GROUP, BLOCK), 0) + step * GROUP
        weight = jnp.where(order < listed, 1.0, 0.0).astype(jnp.float32)
        source_features(gathered, weight, left, charge_next)

    def products(step, u, held):
        shape = left[u * 32 : (u + 1) * 32, :].astype(jnp.bfloat16)
        blank = jnp.zeros_like(shape)
        shape = jnp.concatenate(
            [jnp.concatenate([shape, blank], axis=1), jnp.concatenate([blank, shape], axis=1)],
            axis=0,
        )
        held[u % HALF] = jnp.dot(
            features[target_of(step, u)], shape, preferred_element_type=jnp.float32
        )

    def weights(u, held):
        near = held[u % HALF, :, :BLOCK]
        tilt = held[u % HALF, :, BLOCK:]
        q = lax.rsqrt(near)
        q2 = q * q
        q3 = q2 * q
        f = q3 * (q2 + (2.0 / 3.0))
        h = (q3 * q2) * (q2 + 0.4) * tilt
        fh = f.astype(jnp.bfloat16)
        fl = (f - fh.astype(jnp.float32)).astype(jnp.bfloat16)
        hh = h.astype(jnp.bfloat16)
        hl = (h - hh.astype(jnp.float32)).astype(jnp.bfloat16)
        return jnp.concatenate([fh, fl, hh, hl], axis=0)

    def add_up(step, u, stacked):
        pair = charge[u * 2 * ROWS : (u + 1) * 2 * ROWS, :]
        sums = lax.dot_general(pair, stacked, NT, preferred_element_type=jnp.float32)
        fsum = sums[0:8, 0:128] + sums[8:16, 0:128] + sums[0:8, 128:256]
        hsum = sums[0:8, 256:384] + sums[8:16, 256:384] + sums[0:8, 384:512]
        total[tile_rows(target_of(step, u), 2 * ROWS), :] += jnp.concatenate([fsum, hsum], axis=0)

    def turn(step, carry):
        stacked = {}
        for u in range(HALF):
            stacked[u] = weights(u, first_half)
            products(step, HALF + u, second_half)
            add_up(step, u, stacked[u])
        prepare_sources(step + 1)
        for u in range(HALF, GROUP):
            stacked[u] = weights(u, second_half)
            products(step + 1, u - HALF, first_half)
            add_up(step, u, stacked[u])
        charge[...] = charge_next[...].astype(jnp.bfloat16)
        return carry

    @pl.when(listed > 0)
    def _():
        left[...] = jnp.zeros_like(left)
        charge_next[...] = jnp.zeros_like(charge_next)
        prepare_sources(0)
        for u in range(HALF):
            products(0, u, first_half)
        charge[...] = charge_next[...].astype(jnp.bfloat16)
        lax.fori_loop(0, (listed + GROUP - 1) // GROUP, turn, 0)


def finish(state, out_ref):
    targets, _, centres, total = state
    blocks = out_ref.shape[1] // 6

    def one(step, carry):
        base = pl.multiple_of(step * GROUP * ROWS, GROUP * ROWS)
        wide = pl.multiple_of(step * GROUP * 2 * ROWS, GROUP * 2 * ROWS)
        pos = [
            component(targets, base, k, ROWS) - component(centres, base, k, ROWS) for k in range(3)
        ]
        strength = [component(targets, base, 3 + k, ROWS) for k in range(3)]
        fa, fb, ha, hb = [
            [component(total, wide, start + k, 2 * ROWS) for k in range(3)] for start in (0, 3, 8, 11)
        ]
        swirl = cross(pos, fa)
        lean = cross(strength, fa)
        bend = cross(pos, ha)
        member = step * GROUP // blocks
        inside = lax.rem(step * GROUP, blocks)
        for k in range(3):
            velocity = (-1.5 * biot_factor) * (swirl[k] - fb[k])
            stretch = (-1.5 * biot_factor) * lean[k] + (7.5 * biot_factor) * (bend[k] - hb[k])
            out_ref[member, pl.ds(pl.multiple_of(k * blocks + inside, GROUP), GROUP), :] = velocity
            out_ref[member, pl.ds(pl.multiple_of((3 + k) * blocks + inside, GROUP), GROUP), :] = stretch
        return carry

    lax.fori_loop(0, targets.shape[0] // ROWS // GROUP, one, 0)


def fetched(copies):
    for copy in copies:
        copy.start()
    for copy in copies:
        copy.wait()


def sort_list(listed, pair_target, pair_slot, sorted_list, blocks, members):
    length = pair_target.shape[1]
    t = pair_target[...]
    s = pair_slot[...]
    t = t - lax.axis_index("across") * blocks
    t = jnp.where(t < 0, t + members * blocks, t)
    partner = jnp.where(lax.axis_index("blk") % 2 == 0, REACH + 1, REACH - 1)
    run = s // blocks
    mine = t < blocks
    t = jnp.where(mine, t, t - blocks)
    home = run == REACH
    near = home | (run == partner)
    kind = jnp.where(
        near, jnp.where(mine, jnp.where(home, 0, 1), 2), jnp.where(mine, 4, 3)
    )
    entry = lax.broadcasted_iota(jnp.int32, (1, length), 1)
    kind = jnp.where(entry < listed, kind, CLASSES - 1)
    member = jnp.where(lax.broadcasted_iota(jnp.int32, (CLASSES, length), 0) == kind, 1.0, 0.0)
    row = lax.broadcasted_iota(jnp.int32, (length, length), 0)
    column = lax.broadcasted_iota(jnp.int32, (length, length), 1)
    before = jnp.where(row < column, 1.0, 0.0).astype(jnp.bfloat16)
    earlier = jnp.dot(member.astype(jnp.bfloat16), before, preferred_element_type=jnp.float32)
    rank = jnp.sum(member * earlier, axis=0, keepdims=True).astype(jnp.int32)
    place = jnp.where(row == rank, 1.0, 0.0).astype(jnp.bfloat16)
    values = [t // BLOCK, t % BLOCK, s // BLOCK, s % BLOCK]
    values = [member * value.astype(jnp.float32) for value in values]
    values = jnp.concatenate(values, axis=0).astype(jnp.bfloat16)
    found = lax.dot_general(values, place, NT, preferred_element_type=jnp.float32)
    number = jnp.broadcast_to(jnp.sum(member, axis=1, keepdims=True), (CLASSES, BLOCK))
    for j in range(length // BLOCK):
        part = found[:, j * BLOCK : (j + 1) * BLOCK]
        high, low = part[0:8], part[8:16]
        slot_high, slot_low = part[16:24], part[24:32]
        rows = [high * BLOCK + low, slot_high * BLOCK + slot_low, number]
        sorted_list[j * 24 : (j + 1) * 24, :] = jnp.concatenate(rows, axis=0).astype(jnp.int32)


class shifted_window:
    def __init__(self, ref, start):
        self.ref, self.start = ref, start * ROWS

    def __getitem__(self, index):
        rows, lanes = index
        return self.ref[pl.ds(pl.multiple_of(rows.start - self.start, ROWS), rows.size), lanes]


def home_kernel(number, pair_target, pair_slot, own, *refs, members):
    sorted_list, features, centres, total = refs[:4]
    feature_rows, list_in, slot_in, count_in, lists, sems = refs[4:10]
    scratch = refs[10:]
    state = (own, features, centres, total)
    blocks = own.shape[0] // ROWS
    pairs = ((number, count_in), (pair_target, list_in), (pair_slot, slot_in))
    fetched([pltpu.make_async_copy(a, b, sems.at[k]) for k, (a, b) in enumerate(pairs)])
    sort_list(count_in[0], list_in, slot_in, sorted_list, blocks, members)
    to_scalars = pltpu.make_async_copy(sorted_list, lists, sems.at[3])
    to_scalars.start()
    prepare_targets(state, unit_matrix(), feature_rows)
    to_scalars.wait()
    run_class(0, lists, shifted_window(own, REACH * blocks), state, scratch)


def side_of_partner():
    return jnp.where(lax.axis_index("blk") % 2 == 0, REACH + 1, REACH - 1)


def near_kernel(sorted_list, own, partner, *refs, members):
    others, refs = refs[: members - 1], refs[members - 1 :]
    targets, features, centres, total = state = refs[:4]
    window, feature_rows, lists, sems = refs[4:8]
    scratch = refs[8:]
    to_scalars = pltpu.make_async_copy(sorted_list, lists, sems.at[0])
    to_scalars.start()
    blocks = own.shape[0] // ROWS
    put_tiles(window, REACH * blocks, own)
    put_tiles(window, side_of_partner() * blocks, partner)
    for r, other in enumerate(others):
        put_tiles(targets, r * blocks, other)
    prepare_targets(state, unit_matrix(), feature_rows)
    to_scalars.wait()
    run_class(2, lists, window, state, scratch)


def partner_kernel(sorted_list, partner, own, features, centres, _, total, lists, sems, *scratch):
    fetched([pltpu.make_async_copy(sorted_list, lists, sems.at[0])])
    window = shifted_window(partner, side_of_partner() * (partner.shape[0] // ROWS))
    run_class(1, lists, window, (own, features, centres, total), scratch)


def far_kernel(sorted_list, paired, passed, crossed, *refs):
    targets, features, centres, _ = refs[:4]
    total, window, out_ref = refs[4:7]
    lists, sems = refs[7:9]
    scratch = refs[9:]
    state = (targets, features, centres, total)
    to_scalars = pltpu.make_async_copy(sorted_list, lists, sems.at[0])
    to_scalars.start()
    blocks = paired.shape[0] // ROWS
    shard = lax.axis_index("blk")
    even = shard // 2 % 2 == 0
    put_tiles(window, jnp.where(even, 2 * REACH, 0) * blocks, paired)
    put_tiles(window, jnp.where(even, 0, 2 * REACH) * blocks, passed)
    put_tiles(window, jnp.where(shard % 2 == 0, REACH - 1, REACH + 1) * blocks, crossed)
    to_scalars.wait()
    run_class(3, lists, window, state, scratch)
    finish(state, out_ref)


def last_kernel(sorted_list, window, own, features, centres, _, total, out_ref, lists, sems, *scratch):
    state = (own, features, centres, total)
    fetched([pltpu.make_async_copy(sorted_list, lists, sems.at[0])])
    run_class(4, lists, window, state, scratch)
    finish(state, out_ref)


def section_kernel(own, sums, *refs):
    returned, (velocity, stretching, section_positions, section_strengths) = refs[:-4], refs[-4:]
    blocks = own.shape[0] // ROWS
    for b in range(blocks):
        lanes = slice(b * BLOCK, (b + 1) * BLOCK)
        for start, result, stepped in ((0, velocity, section_positions), (3, stretching, section_strengths)):
            chosen = pl.ds(start * blocks + b, 3, stride=blocks)
            value = sums[chosen, :]
            for other in returned:
                value = value + other[chosen, :]
            result[:, lanes] = value
            first = b * ROWS + start
            stepped[:, lanes] = own[first : first + 3, :] + section_step * value


def call(kernel, name, inputs, outputs, scratch, aliases=None, far=0, flops=0):
    vmem = pl.BlockSpec(memory_space=pltpu.VMEM)
    hbm = pl.BlockSpec(memory_space=pltpu.HBM)
    held = sum(value.size * value.dtype.itemsize for value in (*inputs, *outputs))
    return pl.pallas_call(
        kernel,
        out_shape=outputs,
        in_specs=[hbm if k < far else vmem for k in range(len(inputs))],
        out_specs=[vmem for value in outputs],
        scratch_shapes=scratch,
        input_output_aliases=aliases or {},
        compiler_params=pltpu.CompilerParams(vmem_limit_bytes=10 * 1024 * 1024 + 2 * held),
        cost_estimate=pl.CostEstimate(flops=flops, bytes_accessed=0, transcendentals=0),
        name=name,
    )(*inputs)


def shards(positions, strengths, radius, block_count, pair_target, pair_slot, pair_count):
    blocks = block_count.shape[0]
    lanes = blocks * BLOCK
    length = pair_target.shape[1]
    members = lax.axis_size("across")
    shard = lax.axis_index("blk")
    count = lax.axis_size("blk")

    def f32(*shape):
        return jax.ShapeDtypeStruct(shape, jnp.float32)

    slot_index = lax.broadcasted_iota(jnp.int32, (blocks, 3, BLOCK), 2)
    live = jnp.where(
        slot_index < block_count[:, None, None],
        strengths.reshape(3, blocks, BLOCK).transpose(1, 0, 2),
        0.0,
    )
    cores = radius.reshape(blocks, 1, BLOCK)
    own = jnp.concatenate(
        [positions.reshape(3, blocks, BLOCK).transpose(1, 0, 2), live, cores, cores], axis=1
    ).reshape(blocks * ROWS, BLOCK)
    paired = moved(own, "blk", to_paired_chip)
    others = [
        moved(own, "across", lambda source: (source - away) % members) for away in range(1, members)
    ]
    partner = moved(own, "blk", to_other_core)

    def state_shapes(number):
        return [
            f32(number * blocks * ROWS, BLOCK),
            jax.ShapeDtypeStruct((number * blocks, BLOCK, FEATURES), jnp.bfloat16),
            f32(number * blocks * ROWS, BLOCK),
            f32(number * blocks * 2 * ROWS, BLOCK),
        ]

    own_shapes, other_shapes = state_shapes(1), state_shapes(members - 1)
    window_shape = f32((2 * REACH + 1) * blocks * ROWS, BLOCK)
    list_shape = jax.ShapeDtypeStruct((3 * ROWS * length // BLOCK, BLOCK), jnp.int32)
    feature_rows = pltpu.VMEM((GROUP * BLOCK, BLOCK), jnp.float32)
    list_scratch = [pltpu.SMEM(list_shape.shape, jnp.int32), pltpu.SemaphoreType.DMA((4,))]
    scratch = [
        pltpu.VMEM((GROUP * ROWS, BLOCK), jnp.float32),
        pltpu.VMEM((GROUP * 32, BLOCK), jnp.float32),
        pltpu.VMEM((GROUP * 2 * ROWS, BLOCK), jnp.float32),
        pltpu.VMEM((GROUP * 2 * ROWS, BLOCK), jnp.bfloat16),
        pltpu.VMEM((HALF, BLOCK, 2 * BLOCK), jnp.float32),
        pltpu.VMEM((HALF, BLOCK, 2 * BLOCK), jnp.float32),
    ]
    window_scratch = pltpu.VMEM(window_shape.shape, jnp.float32)

    lists, *own_state = call(
        lambda *refs: home_kernel(*refs, members=members),
        "home_pairs",
        (pair_count, pair_target, pair_slot, own),
        [list_shape] + own_shapes[1:],
        [
            feature_rows,
            pltpu.VMEM((1, length), jnp.int32),
            pltpu.VMEM((1, length), jnp.int32),
            pltpu.SMEM((1,), jnp.int32),
        ]
        + list_scratch
        + scratch,
        far=3,
        flops=HOME_FLOPS,
    )
    paired, lists = lax.optimization_barrier((paired, lists))
    passed = moved(paired, "blk", along_chips(count))
    other_state = list(call(
        lambda *refs: near_kernel(*refs, members=members),
        "near_pairs",
        (lists, own, partner, *others),
        other_shapes,
        [window_scratch, feature_rows] + list_scratch + scratch,
        flops=NEAR_FLOPS,
    ))
    passed, other_state[3] = lax.optimization_barrier((passed, other_state[3]))
    core = shard % 2
    chip = shard // 2 % 2
    crossed = moved(jnp.where(core == chip, paired, passed), "blk", to_other_core)
    (own_state[2],) = call(
        partner_kernel,
        "partner_pairs",
        (lists, partner, own, *own_state),
        [own_shapes[3]],
        list_scratch + scratch,
        {5: 0},
        flops=HOME_FLOPS,
    )
    crossed, own_state[2] = lax.optimization_barrier((crossed, own_state[2]))
    _, window, away_sums = call(
        far_kernel,
        "far_pairs",
        (lists, paired, passed, crossed, *other_state),
        [other_shapes[3], window_shape, f32(members - 1, 6 * blocks, BLOCK)],
        list_scratch + scratch,
        {7: 0},
        flops=FAR_FLOPS,
    )
    returned = [
        moved(away_sums[away - 1], "across", lambda source: (source + away) % members)
        for away in range(1, members)
    ]
    _, sums = call(
        last_kernel,
        "last_pairs",
        (lists, window, own, *own_state),
        [own_shapes[3], f32(1, 6 * blocks, BLOCK)],
        list_scratch + scratch,
        {5: 0},
        flops=FAR_FLOPS,
    )
    wide = f32(3, lanes)
    return tuple(
        call(section_kernel, "section", (own, sums[0], *returned), [wide] * 4, [])
    )


def solution(mesh):
    whole = P(None, ("blk", "across"))
    line = P(("blk", "across"))
    return jax.shard_map(
        shards,
        mesh=mesh,
        in_specs=(whole, whole, line, line, P(("blk", "across"), None), P(("blk", "across"), None), line),
        out_specs=(whole, whole, whole, whole),
        check_vma=False,
    )
```

```python
import jax
import jax.numpy as jnp
from jax import lax
from jax.experimental import pallas as pl
from jax.experimental.pallas import tpu as pltpu
from jax.sharding import PartitionSpec as P

BLOCK = 128
ROWS = 8
REACH = 2
GROUP = 8
HALF = 4
SLOTS = 1024
FEATURES = 32
CLASSES = 8

biot_factor = 0.07957747154594767
section_step = 0.05


def moved(value, axis, target_of):
    pairs = [(source, target_of(source)) for source in range(lax.axis_size(axis))]
    return lax.ppermute(value, axis, pairs)


def to_other_core(source):
    return source ^ 1


def to_paired_chip(source):
    return source ^ 2


def along_chips(count):
    return lambda source: (source + (4 if source & 2 == 0 else -4)) % count


HOME_FLOPS = 10**10
NEAR_FLOPS = 10**10
FAR_FLOPS = 10**10


def rounded(value):
    return value.astype(jnp.bfloat16).astype(jnp.float32)


def split_three(value):
    first = rounded(value)
    rest = value - first
    second = rounded(rest)
    return first, second, rest - second


def cross(left, right):
    return [
        left[1] * right[2] - left[2] * right[1],
        left[2] * right[0] - left[0] * right[2],
        left[0] * right[1] - left[1] * right[0],
    ]


def tile_rows(index, rows):
    return pl.ds(pl.multiple_of(index * rows, rows), rows)


def component(ref, base, number, stride):
    return ref[pl.ds(base + number, GROUP, stride=stride), :]


def store_component(ref, base, number, stride, value):
    ref[pl.ds(base + number, GROUP, stride=stride), :] = value


def target_features(targets, step, centres, near_rows, tilt_rows):
    base = pl.multiple_of(step * (GROUP * ROWS), GROUP * ROWS)
    pos = [component(targets, base, k, ROWS) for k in range(3)]
    strength = [component(targets, base, 3 + k, ROWS) for k in range(3)]
    for k in range(3):
        centre = jnp.broadcast_to(jnp.mean(pos[k], axis=1, keepdims=True), (GROUP, BLOCK))
        store_component(centres, base, k, ROWS, centre)
        pos[k] = pos[k] - centre
    for k in range(3, ROWS):
        store_component(centres, base, k, ROWS, jnp.zeros_like(pos[0]))
    norm = pos[0] * pos[0] + pos[1] * pos[1] + pos[2] * pos[2]
    own = pos[0] * strength[0] + pos[1] * strength[1] + pos[2] * strength[2]
    near = pos + [norm, jnp.ones_like(norm)]
    tilt = [0.5 * s for s in strength] + [own]
    for rows, values in ((near_rows, near), (tilt_rows, tilt)):
        for k, value in enumerate(values):
            parts = split_three(value)
            for slot, part in enumerate((0, 1, 2, 0, 1, 0)):
                store_component(rows, 0, 5 * slot + k, FEATURES, parts[part])


def source_features(gathered, weight, left, charge):
    pos = [component(gathered, 0, k, ROWS) for k in range(3)]
    strength = [component(gathered, 0, 3 + k, ROWS) for k in range(3)]
    inv_core = 1.0 / component(gathered, 0, 6, ROWS)
    inv_square = inv_core * inv_core
    norm = pos[0] * pos[0] + pos[1] * pos[1] + pos[2] * pos[2]
    twice = -2.0 * inv_square
    shape = [p * twice for p in pos] + [inv_square, norm * inv_square + 1.0]
    for k, value in enumerate(shape):
        parts = split_three(value)
        for slot, part in enumerate((0, 0, 0, 1, 1, 2)):
            store_component(left, 0, 5 * slot + k, FEATURES, parts[part])
    scale = inv_square * inv_core * weight
    for k, value in enumerate(strength + cross(pos, strength)):
        value = value * scale
        high = rounded(value)
        store_component(charge, 0, k, 2 * ROWS, high)
        store_component(charge, 0, ROWS + k, 2 * ROWS, value - high)


NT = (((1,), (1,)), ((), ()))
TN = (((0,), (0,)), ((), ()))


def put_tiles(window, first, tiles):
    window[pl.ds(pl.multiple_of(first * ROWS, ROWS), tiles.shape[0]), :] = tiles[...]


def prepare_targets(state, near_rows, tilt_rows):
    targets, features, centres, total = state
    near_rows[...] = jnp.zeros_like(near_rows)
    tilt_rows[...] = jnp.zeros_like(tilt_rows)
    total[...] = jnp.zeros_like(total)

    def prepare(step, carry):
        target_features(targets, step, centres, near_rows, tilt_rows)
        for u in range(GROUP):
            rows = slice(u * FEATURES, (u + 1) * FEATURES)
            features[step * GROUP + u, :, :BLOCK] = near_rows[rows, :].astype(jnp.bfloat16)
            features[step * GROUP + u, :, BLOCK:] = tilt_rows[rows, :].astype(jnp.bfloat16)
        return carry

    lax.fori_loop(0, features.shape[0] // GROUP, prepare, 0)


def run_class(kind, lists, window, state, scratch):
    _, features, centres, total = state
    gathered, left, charge_next, charge, first_half, second_half = scratch
    listed = lists[2 * ROWS + kind, 0]

    def entry_at(step, u):
        entry = jnp.minimum(step * GROUP + u, listed - 1)
        return entry // BLOCK * (3 * ROWS) + kind, lax.rem(entry, BLOCK)

    def target_of(step, u):
        row, column = entry_at(step, u)
        return lists[row, column]

    def prepare_sources(step):
        for u in range(GROUP):
            row, column = entry_at(step, u)
            gathered[u * ROWS : (u + 1) * ROWS, :] = (
                window[tile_rows(lists[row + ROWS, column], ROWS), :]
                - centres[tile_rows(lists[row, column], ROWS), :]
            )
        order = lax.broadcasted_iota(jnp.int32, (GROUP, BLOCK), 0) + step * GROUP
        weight = jnp.where(order < listed, 1.0, 0.0).astype(jnp.float32)
        source_features(gathered, weight, left, charge_next)

    def products(step, u, held):
        shape = left[u * FEATURES : (u + 1) * FEATURES, :].astype(jnp.bfloat16)
        held[u % HALF] = lax.dot_general(
            shape, features[target_of(step, u)], TN, preferred_element_type=jnp.float32
        )

    def weights(u, held):
        near = held[u % HALF, :, :BLOCK]
        tilt = held[u % HALF, :, BLOCK:]
        q = lax.rsqrt(near)
        q2 = q * q
        q3 = q2 * q
        f = q3 * (q2 + (2.0 / 3.0))
        h = (q3 * q2) * (q2 + 0.4) * tilt
        fh = f.astype(jnp.bfloat16)
        fl = (f - fh.astype(jnp.float32)).astype(jnp.bfloat16)
        hh = h.astype(jnp.bfloat16)
        hl = (h - hh.astype(jnp.float32)).astype(jnp.bfloat16)
        return jnp.concatenate([fh, fl, hh, hl], axis=1)

    def add_up(step, u, stacked):
        pair = charge[u * 2 * ROWS : (u + 1) * 2 * ROWS, :]
        sums = jnp.dot(pair, stacked, preferred_element_type=jnp.float32)
        fsum = sums[0:8, 0:128] + sums[8:16, 0:128] + sums[0:8, 128:256]
        hsum = sums[0:8, 256:384] + sums[8:16, 256:384] + sums[0:8, 384:512]
        total[tile_rows(target_of(step, u), 2 * ROWS), :] += jnp.concatenate([fsum, hsum], axis=0)

    def turn(step, carry):
        stacked = {}
        for u in range(HALF):
            stacked[u] = weights(u, first_half)
            products(step, HALF + u, second_half)
            add_up(step, u, stacked[u])
        prepare_sources(step + 1)
        for u in range(HALF, GROUP):
            stacked[u] = weights(u, second_half)
            products(step + 1, u - HALF, first_half)
            add_up(step, u, stacked[u])
        charge[...] = charge_next[...].astype(jnp.bfloat16)
        return carry

    @pl.when(listed > 0)
    def _():
        left[...] = jnp.zeros_like(left)
        charge_next[...] = jnp.zeros_like(charge_next)
        prepare_sources(0)
        for u in range(HALF):
            products(0, u, first_half)
        charge[...] = charge_next[...].astype(jnp.bfloat16)
        lax.fori_loop(0, (listed + GROUP - 1) // GROUP, turn, 0)


def finish(targets, centres, totals, out_ref):
    blocks = out_ref.shape[1] // 6

    def one(step, carry):
        base = pl.multiple_of(step * GROUP * ROWS, GROUP * ROWS)
        wide = pl.multiple_of(step * GROUP * 2 * ROWS, GROUP * 2 * ROWS)
        pos = [
            component(targets, base, k, ROWS) - component(centres, base, k, ROWS) for k in range(3)
        ]
        strength = [component(targets, base, 3 + k, ROWS) for k in range(3)]
        fa, fb, ha, hb = [
            [
                sum(component(total, wide, start + k, 2 * ROWS) for total in totals)
                for k in range(3)
            ]
            for start in (0, 3, 8, 11)
        ]
        swirl = cross(pos, fa)
        lean = cross(strength, fa)
        bend = cross(pos, ha)
        member = step * GROUP // blocks
        inside = lax.rem(step * GROUP, blocks)
        for k in range(3):
            velocity = (-1.5 * biot_factor) * (swirl[k] - fb[k])
            stretch = (-1.5 * biot_factor) * lean[k] + (7.5 * biot_factor) * (bend[k] - hb[k])
            out_ref[member, pl.ds(pl.multiple_of(k * blocks + inside, GROUP), GROUP), :] = velocity
            out_ref[member, pl.ds(pl.multiple_of((3 + k) * blocks + inside, GROUP), GROUP), :] = stretch
        return carry

    lax.fori_loop(0, targets.shape[0] // ROWS // GROUP, one, 0)


def sort_list(coded, sorted_list, blocks, members):
    length = coded.shape[1]
    t = coded[...] // SLOTS
    s = coded[...] % SLOTS
    t = t - lax.axis_index("across") * blocks
    t = jnp.where(t < 0, t + members * blocks, t)
    partner = jnp.where(lax.axis_index("blk") % 2 == 0, REACH + 1, REACH - 1)
    run = s // blocks
    mine = t < blocks
    t = jnp.where(mine, t, t - blocks)
    home = run == REACH
    near = home | (run == partner)
    kind = jnp.where(
        near, jnp.where(mine, jnp.where(home, 0, 1), 2), jnp.where(mine, 4, 3)
    )
    kind = jnp.where(coded[...] < 0, CLASSES - 1, kind)
    member = jnp.where(lax.broadcasted_iota(jnp.int32, (CLASSES, length), 0) == kind, 1.0, 0.0)
    row = lax.broadcasted_iota(jnp.int32, (length, length), 0)
    column = lax.broadcasted_iota(jnp.int32, (length, length), 1)
    before = jnp.where(row < column, 1.0, 0.0).astype(jnp.bfloat16)
    earlier = jnp.dot(member.astype(jnp.bfloat16), before, preferred_element_type=jnp.float32)
    rank = jnp.sum(member * earlier, axis=0, keepdims=True).astype(jnp.int32)
    place = jnp.where(row == rank, 1.0, 0.0).astype(jnp.bfloat16)
    values = [t // BLOCK, t % BLOCK, s // BLOCK, s % BLOCK]
    values = [member * value.astype(jnp.float32) for value in values]
    values = jnp.concatenate(values, axis=0).astype(jnp.bfloat16)
    found = lax.dot_general(values, place, NT, preferred_element_type=jnp.float32)
    number = jnp.broadcast_to(jnp.sum(member, axis=1, keepdims=True), (CLASSES, BLOCK))
    for j in range(length // BLOCK):
        part = found[:, j * BLOCK : (j + 1) * BLOCK]
        high, low = part[0:8], part[8:16]
        slot_high, slot_low = part[16:24], part[24:32]
        rows = [high * BLOCK + low, slot_high * BLOCK + slot_low, number]
        sorted_list[j * 24 : (j + 1) * 24, :] = jnp.concatenate(rows, axis=0).astype(jnp.int32)


class shifted_window:
    def __init__(self, ref, start):
        self.ref, self.start = ref, start * ROWS

    def __getitem__(self, index):
        rows, lanes = index
        return self.ref[pl.ds(pl.multiple_of(rows.start - self.start, ROWS), rows.size), lanes]


def home_kernel(coded, own, *refs, members):
    sorted_list, features, centres, total = refs[:4]
    near_rows, tilt_rows, lists, sems = refs[4:8]
    scratch = refs[8:]
    state = (own, features, centres, total)
    blocks = own.shape[0] // ROWS
    sort_list(coded, sorted_list, blocks, members)
    to_scalars = pltpu.make_async_copy(sorted_list, lists, sems.at[0])
    to_scalars.start()
    prepare_targets(state, near_rows, tilt_rows)
    to_scalars.wait()
    run_class(0, lists, shifted_window(own, REACH * blocks), state, scratch)


def side_of_partner():
    return jnp.where(lax.axis_index("blk") % 2 == 0, REACH + 1, REACH - 1)


def near_kernel(sorted_list, own, partner, *refs, members):
    others, refs = refs[: members - 1], refs[members - 1 :]
    targets, features, centres, total = state = refs[:4]
    window, near_rows, tilt_rows, lists, sems = refs[4:9]
    scratch = refs[9:]
    to_scalars = pltpu.make_async_copy(sorted_list, lists, sems.at[0])
    to_scalars.start()
    blocks = own.shape[0] // ROWS
    put_tiles(window, REACH * blocks, own)
    put_tiles(window, side_of_partner() * blocks, partner)
    for r, other in enumerate(others):
        put_tiles(targets, r * blocks, other)
    prepare_targets(state, near_rows, tilt_rows)
    to_scalars.wait()
    run_class(2, lists, window, state, scratch)


def partner_kernel(sorted_list, partner, own, features, centres, total, lists, sems, *scratch):
    to_scalars = pltpu.make_async_copy(sorted_list, lists, sems.at[0])
    to_scalars.start()
    total[...] = jnp.zeros_like(total)
    to_scalars.wait()
    window = shifted_window(partner, side_of_partner() * (partner.shape[0] // ROWS))
    run_class(1, lists, window, (own, features, centres, total), scratch)


def far_kernel(sorted_list, paired, passed, crossed, *refs):
    targets, features, centres, near_total = refs[:4]
    window, out_ref, total, lists, sems = refs[4:9]
    scratch = refs[9:]
    state = (targets, features, centres, total)
    to_scalars = pltpu.make_async_copy(sorted_list, lists, sems.at[0])
    to_scalars.start()
    blocks = paired.shape[0] // ROWS
    shard = lax.axis_index("blk")
    even = shard // 2 % 2 == 0
    put_tiles(window, jnp.where(even, 2 * REACH, 0) * blocks, paired)
    put_tiles(window, jnp.where(even, 0, 2 * REACH) * blocks, passed)
    put_tiles(window, jnp.where(shard % 2 == 0, REACH - 1, REACH + 1) * blocks, crossed)
    total[...] = jnp.zeros_like(total)
    to_scalars.wait()
    run_class(3, lists, window, state, scratch)
    finish(targets, centres, (near_total, total), out_ref)


def last_kernel(sorted_list, window, own, features, centres, *refs):
    home_total, partner_total, out_ref, total, lists, sems = refs[:6]
    to_scalars = pltpu.make_async_copy(sorted_list, lists, sems.at[0])
    to_scalars.start()
    total[...] = jnp.zeros_like(total)
    to_scalars.wait()
    run_class(4, lists, window, (own, features, centres, total), refs[6:])
    finish(own, centres, (home_total, partner_total, total), out_ref)


def section_kernel(own, sums, *refs):
    returned, (velocity, stretching, section_positions, section_strengths) = refs[:-4], refs[-4:]
    blocks = own.shape[0] // ROWS
    for b in range(blocks):
        lanes = slice(b * BLOCK, (b + 1) * BLOCK)
        for start, result, stepped in ((0, velocity, section_positions), (3, stretching, section_strengths)):
            chosen = pl.ds(start * blocks + b, 3, stride=blocks)
            value = sums[chosen, :]
            for other in returned:
                value = value + other[chosen, :]
            result[:, lanes] = value
            first = b * ROWS + start
            stepped[:, lanes] = own[first : first + 3, :] + section_step * value


def call(kernel, name, inputs, outputs, scratch, flops=0):
    vmem = pl.BlockSpec(memory_space=pltpu.VMEM)
    held = sum(value.size * value.dtype.itemsize for value in (*inputs, *outputs))
    return pl.pallas_call(
        kernel,
        out_shape=outputs,
        in_specs=[vmem for value in inputs],
        out_specs=[vmem for value in outputs],
        scratch_shapes=scratch,
        compiler_params=pltpu.CompilerParams(vmem_limit_bytes=10 * 1024 * 1024 + 2 * held),
        cost_estimate=pl.CostEstimate(flops=flops, bytes_accessed=0, transcendentals=0),
        name=name,
    )(*inputs)


def shards(positions, strengths, radius, block_count, pair_target, pair_slot, pair_count):
    blocks = block_count.shape[0]
    lanes = blocks * BLOCK
    length = pair_target.shape[1]
    members = lax.axis_size("across")
    shard = lax.axis_index("blk")
    count = lax.axis_size("blk")

    def f32(*shape):
        return jax.ShapeDtypeStruct(shape, jnp.float32)

    row = lax.broadcasted_iota(jnp.int32, (blocks, ROWS, BLOCK), 1)
    lane = lax.broadcasted_iota(jnp.int32, (blocks, ROWS, BLOCK), 2)
    cores = radius.reshape(blocks, 1, BLOCK)
    parts = [value.reshape(3, blocks, BLOCK).transpose(1, 0, 2) for value in (positions, strengths)]
    dead = (row >= 3) & (row < 6) & (lane >= block_count[:, None, None])
    own = jnp.where(dead, 0.0, jnp.concatenate(parts + [cores, cores], axis=1))
    own = own.reshape(blocks * ROWS, BLOCK)
    entry = lax.broadcasted_iota(jnp.int32, (1, length), 1)
    coded = jnp.where(entry < pair_count[0], pair_target * SLOTS + pair_slot, -1)
    paired = moved(own, "blk", to_paired_chip)
    others = [
        moved(own, "across", lambda source: (source - away) % members) for away in range(1, members)
    ]
    partner = moved(own, "blk", to_other_core)

    def state_shapes(number):
        return [
            f32(number * blocks * ROWS, BLOCK),
            jax.ShapeDtypeStruct((number * blocks, FEATURES, 2 * BLOCK), jnp.bfloat16),
            f32(number * blocks * ROWS, BLOCK),
            f32(number * blocks * 2 * ROWS, BLOCK),
        ]

    own_shapes, other_shapes = state_shapes(1), state_shapes(members - 1)
    window_shape = f32((2 * REACH + 1) * blocks * ROWS, BLOCK)
    list_shape = jax.ShapeDtypeStruct((3 * ROWS * length // BLOCK, BLOCK), jnp.int32)
    feature_rows = [pltpu.VMEM((GROUP * FEATURES, BLOCK), jnp.float32)] * 2
    list_scratch = [pltpu.SMEM(list_shape.shape, jnp.int32), pltpu.SemaphoreType.DMA((4,))]
    scratch = [
        pltpu.VMEM((GROUP * ROWS, BLOCK), jnp.float32),
        pltpu.VMEM((GROUP * FEATURES, BLOCK), jnp.float32),
        pltpu.VMEM((GROUP * 2 * ROWS, BLOCK), jnp.float32),
        pltpu.VMEM((GROUP * 2 * ROWS, BLOCK), jnp.bfloat16),
        pltpu.VMEM((HALF, BLOCK, 2 * BLOCK), jnp.float32),
        pltpu.VMEM((HALF, BLOCK, 2 * BLOCK), jnp.float32),
    ]
    window_scratch = pltpu.VMEM(window_shape.shape, jnp.float32)

    lists, *own_state = call(
        lambda *refs: home_kernel(*refs, members=members),
        "home_pairs",
        (coded, own),
        [list_shape] + own_shapes[1:],
        feature_rows + list_scratch + scratch,
        flops=HOME_FLOPS,
    )
    paired, lists = lax.optimization_barrier((paired, lists))
    passed = moved(paired, "blk", along_chips(count))
    other_state = list(call(
        lambda *refs: near_kernel(*refs, members=members),
        "near_pairs",
        (lists, own, partner, *others),
        other_shapes,
        [window_scratch] + feature_rows + list_scratch + scratch,
        flops=NEAR_FLOPS,
    ))
    passed, other_state[3] = lax.optimization_barrier((passed, other_state[3]))
    core = shard % 2
    chip = shard // 2 % 2
    crossed = moved(jnp.where(core == chip, paired, passed), "blk", to_other_core)
    (partner_total,) = call(
        partner_kernel,
        "partner_pairs",
        (lists, partner, own, *own_state[:2]),
        [own_shapes[3]],
        list_scratch + scratch,
        flops=HOME_FLOPS,
    )
    crossed, partner_total = lax.optimization_barrier((crossed, partner_total))
    window, away_sums = call(
        far_kernel,
        "far_pairs",
        (lists, paired, passed, crossed, *other_state),
        [window_shape, f32(members - 1, 6 * blocks, BLOCK)],
        [pltpu.VMEM(other_shapes[3].shape, jnp.float32)] + list_scratch + scratch,
        flops=FAR_FLOPS,
    )
    returned = [
        moved(away_sums[away - 1], "across", lambda source: (source + away) % members)
        for away in range(1, members)
    ]
    (sums,) = call(
        last_kernel,
        "last_pairs",
        (lists, window, own, *own_state, partner_total),
        [f32(1, 6 * blocks, BLOCK)],
        [pltpu.VMEM(own_shapes[3].shape, jnp.float32)] + list_scratch + scratch,
        flops=FAR_FLOPS,
    )
    wide = f32(3, lanes)
    return tuple(
        call(section_kernel, "section", (own, sums[0], *returned), [wide] * 4, [])
    )


def solution(mesh):
    whole = P(None, ("blk", "across"))
    line = P(("blk", "across"))
    return jax.shard_map(
        shards,
        mesh=mesh,
        in_specs=(whole, whole, line, line, P(("blk", "across"), None), P(("blk", "across"), None), line),
        out_specs=(whole, whole, whole, whole),
        check_vma=False,
    )
```

```python
import jax
import jax.numpy as jnp
from jax import lax
from jax.experimental import pallas as pl
from jax.experimental.pallas import tpu as pltpu
from jax.sharding import PartitionSpec as P

BLOCK = 128
ROWS = 8
REACH = 2
GROUP = 8
HALF = 4
SLOTS = 1024
FEATURES = 32
CLASSES = 8

biot_factor = 0.07957747154594767
section_step = 0.05


def moved(value, axis, target_of):
    pairs = [(source, target_of(source)) for source in range(lax.axis_size(axis))]
    return lax.ppermute(value, axis, pairs)


def to_other_core(source):
    return source ^ 1


def to_paired_chip(source):
    return source ^ 2


def along_chips(count):
    return lambda source: (source + (4 if source & 2 == 0 else -4)) % count


HOME_FLOPS = 10**10
NEAR_FLOPS = 10**10
FAR_FLOPS = 10**10


def rounded(value):
    return value.astype(jnp.bfloat16).astype(jnp.float32)


def split_three(value):
    first = rounded(value)
    rest = value - first
    second = rounded(rest)
    return first, second, rest - second


def cross(left, right):
    return [
        left[1] * right[2] - left[2] * right[1],
        left[2] * right[0] - left[0] * right[2],
        left[0] * right[1] - left[1] * right[0],
    ]


def tile_rows(index, rows):
    return pl.ds(pl.multiple_of(index * rows, rows), rows)


def component(ref, base, number, stride):
    return ref[pl.ds(base + number, GROUP, stride=stride), :]


def store_component(ref, base, number, stride, value):
    ref[pl.ds(base + number, GROUP, stride=stride), :] = value


def target_features(targets, step, centres, near_rows, tilt_rows):
    base = pl.multiple_of(step * (GROUP * ROWS), GROUP * ROWS)
    pos = [component(targets, base, k, ROWS) for k in range(3)]
    strength = [component(targets, base, 3 + k, ROWS) for k in range(3)]
    for k in range(3):
        centre = jnp.broadcast_to(jnp.mean(pos[k], axis=1, keepdims=True), (GROUP, BLOCK))
        store_component(centres, base, k, ROWS, centre)
        pos[k] = pos[k] - centre
    for k in range(3, ROWS):
        store_component(centres, base, k, ROWS, jnp.zeros_like(pos[0]))
    norm = pos[0] * pos[0] + pos[1] * pos[1] + pos[2] * pos[2]
    own = pos[0] * strength[0] + pos[1] * strength[1] + pos[2] * strength[2]
    near = pos + [norm, jnp.ones_like(norm)]
    tilt = [0.5 * s for s in strength] + [own]
    for rows, values in ((near_rows, near), (tilt_rows, tilt)):
        for k, value in enumerate(values):
            parts = split_three(value)
            for slot, part in enumerate((0, 1, 2, 0, 1, 0)):
                store_component(rows, 0, 5 * slot + k, FEATURES, parts[part])


def source_features(gathered, weight, left, charge):
    pos = [component(gathered, 0, k, ROWS) for k in range(3)]
    strength = [component(gathered, 0, 3 + k, ROWS) for k in range(3)]
    inv_core = 1.0 / component(gathered, 0, 6, ROWS)
    inv_square = inv_core * inv_core
    norm = pos[0] * pos[0] + pos[1] * pos[1] + pos[2] * pos[2]
    twice = -2.0 * inv_square
    shape = [p * twice for p in pos] + [inv_square, norm * inv_square + 1.0]
    for k, value in enumerate(shape):
        parts = split_three(value)
        for slot, part in enumerate((0, 0, 0, 1, 1, 2)):
            store_component(left, 0, 5 * slot + k, FEATURES, parts[part])
    scale = inv_square * inv_core * weight
    for k, value in enumerate(strength + cross(pos, strength)):
        value = value * scale
        high = rounded(value)
        store_component(charge, 0, k, 2 * ROWS, high)
        store_component(charge, 0, ROWS + k, 2 * ROWS, value - high)


NT = (((1,), (1,)), ((), ()))
TN = (((0,), (0,)), ((), ()))


def put_tiles(window, first, tiles):
    window[pl.ds(pl.multiple_of(first * ROWS, ROWS), tiles.shape[0]), :] = tiles[...]


def prepare_targets(state, near_rows, tilt_rows):
    targets, features, centres, total = state
    near_rows[...] = jnp.zeros_like(near_rows)
    tilt_rows[...] = jnp.zeros_like(tilt_rows)
    total[...] = jnp.zeros_like(total)

    def prepare(step, carry):
        target_features(targets, step, centres, near_rows, tilt_rows)
        for u in range(GROUP):
            rows = slice(u * FEATURES, (u + 1) * FEATURES)
            features[step * GROUP + u, :, :BLOCK] = near_rows[rows, :].astype(jnp.bfloat16)
            features[step * GROUP + u, :, BLOCK:] = tilt_rows[rows, :].astype(jnp.bfloat16)
        return carry

    lax.fori_loop(0, features.shape[0] // GROUP, prepare, 0)


def run_class(kind, lists, window, state, scratch):
    _, features, centres, total = state
    gathered, left, charge_next, charge, first_half, second_half = scratch
    listed = lists[2 * ROWS + kind, 0]

    def entry_at(step, u):
        entry = jnp.minimum(step * GROUP + u, listed - 1)
        return entry // BLOCK * (3 * ROWS) + kind, lax.rem(entry, BLOCK)

    def target_of(step, u):
        row, column = entry_at(step, u)
        return lists[row, column]

    def prepare_sources(step):
        for u in range(GROUP):
            row, column = entry_at(step, u)
            gathered[u * ROWS : (u + 1) * ROWS, :] = (
                window[tile_rows(lists[row + ROWS, column], ROWS), :]
                - centres[tile_rows(lists[row, column], ROWS), :]
            )
        order = lax.broadcasted_iota(jnp.int32, (GROUP, BLOCK), 0) + step * GROUP
        weight = jnp.where(order < listed, 1.0, 0.0).astype(jnp.float32)
        source_features(gathered, weight, left, charge_next)

    def products(step, u, held):
        shape = left[u * FEATURES : (u + 1) * FEATURES, :].astype(jnp.bfloat16)
        held[u % HALF] = lax.dot_general(
            shape, features[target_of(step, u)], TN, preferred_element_type=jnp.float32
        )

    def weights(u, held):
        near = held[u % HALF, :, :BLOCK]
        tilt = held[u % HALF, :, BLOCK:]
        q = lax.rsqrt(near)
        q2 = q * q
        q3 = q2 * q
        f = q3 * (q2 + (2.0 / 3.0))
        h = (q3 * q2) * (q2 + 0.4) * tilt
        fh = f.astype(jnp.bfloat16)
        fl = (f - fh.astype(jnp.float32)).astype(jnp.bfloat16)
        hh = h.astype(jnp.bfloat16)
        hl = (h - hh.astype(jnp.float32)).astype(jnp.bfloat16)
        return jnp.concatenate(
            [jnp.concatenate([fh, fl], axis=1), jnp.concatenate([hh, hl], axis=1)], axis=0
        )

    def add_up(step, u, stacked):
        pair = charge[u * 2 * ROWS : (u + 1) * 2 * ROWS, :]
        blank = jnp.zeros_like(pair)
        pair = jnp.concatenate(
            [jnp.concatenate([pair, blank], axis=1), jnp.concatenate([blank, pair], axis=1)], axis=0
        )
        sums = jnp.dot(pair, stacked, preferred_element_type=jnp.float32)
        fsum = sums[0:8, :BLOCK] + sums[8:16, :BLOCK] + sums[0:8, BLOCK:]
        hsum = sums[16:24, :BLOCK] + sums[24:32, :BLOCK] + sums[16:24, BLOCK:]
        total[tile_rows(target_of(step, u), 2 * ROWS), :] += jnp.concatenate([fsum, hsum], axis=0)

    def turn(step, carry):
        stacked = {}
        for u in range(HALF):
            stacked[u] = weights(u, first_half)
            products(step, HALF + u, second_half)
            add_up(step, u, stacked[u])
        prepare_sources(step + 1)
        for u in range(HALF, GROUP):
            stacked[u] = weights(u, second_half)
            products(step + 1, u - HALF, first_half)
            add_up(step, u, stacked[u])
        charge[...] = charge_next[...].astype(jnp.bfloat16)
        return carry

    @pl.when(listed > 0)
    def _():
        left[...] = jnp.zeros_like(left)
        charge_next[...] = jnp.zeros_like(charge_next)
        prepare_sources(0)
        for u in range(HALF):
            products(0, u, first_half)
        charge[...] = charge_next[...].astype(jnp.bfloat16)
        lax.fori_loop(0, (listed + GROUP - 1) // GROUP, turn, 0)


def finish(targets, centres, totals, out_ref):
    blocks = out_ref.shape[1] // 6

    def one(step, carry):
        base = pl.multiple_of(step * GROUP * ROWS, GROUP * ROWS)
        wide = pl.multiple_of(step * GROUP * 2 * ROWS, GROUP * 2 * ROWS)
        pos = [
            component(targets, base, k, ROWS) - component(centres, base, k, ROWS) for k in range(3)
        ]
        strength = [component(targets, base, 3 + k, ROWS) for k in range(3)]
        fa, fb, ha, hb = [
            [
                sum(component(total, wide, start + k, 2 * ROWS) for total in totals)
                for k in range(3)
            ]
            for start in (0, 3, 8, 11)
        ]
        swirl = cross(pos, fa)
        lean = cross(strength, fa)
        bend = cross(pos, ha)
        member = step * GROUP // blocks
        inside = lax.rem(step * GROUP, blocks)
        for k in range(3):
            velocity = (-1.5 * biot_factor) * (swirl[k] - fb[k])
            stretch = (-1.5 * biot_factor) * lean[k] + (7.5 * biot_factor) * (bend[k] - hb[k])
            out_ref[member, pl.ds(pl.multiple_of(k * blocks + inside, GROUP), GROUP), :] = velocity
            out_ref[member, pl.ds(pl.multiple_of((3 + k) * blocks + inside, GROUP), GROUP), :] = stretch
        return carry

    lax.fori_loop(0, targets.shape[0] // ROWS // GROUP, one, 0)


def sort_list(coded, sorted_list, blocks, members):
    length = coded.shape[1]
    t = coded[...] // SLOTS
    s = coded[...] % SLOTS
    t = t - lax.axis_index("across") * blocks
    t = jnp.where(t < 0, t + members * blocks, t)
    partner = jnp.where(lax.axis_index("blk") % 2 == 0, REACH + 1, REACH - 1)
    run = s // blocks
    mine = t < blocks
    t = jnp.where(mine, t, t - blocks)
    home = run == REACH
    near = home | (run == partner)
    kind = jnp.where(
        near, jnp.where(mine, jnp.where(home, 0, 1), 2), jnp.where(mine, 4, 3)
    )
    kind = jnp.where(coded[...] < 0, CLASSES - 1, kind)
    member = jnp.where(lax.broadcasted_iota(jnp.int32, (CLASSES, length), 0) == kind, 1.0, 0.0)
    row = lax.broadcasted_iota(jnp.int32, (length, length), 0)
    column = lax.broadcasted_iota(jnp.int32, (length, length), 1)
    before = jnp.where(row < column, 1.0, 0.0).astype(jnp.bfloat16)
    earlier = jnp.dot(member.astype(jnp.bfloat16), before, preferred_element_type=jnp.float32)
    rank = jnp.sum(member * earlier, axis=0, keepdims=True).astype(jnp.int32)
    place = jnp.where(row == rank, 1.0, 0.0).astype(jnp.bfloat16)
    values = [t // BLOCK, t % BLOCK, s // BLOCK, s % BLOCK]
    values = [member * value.astype(jnp.float32) for value in values]
    values = jnp.concatenate(values, axis=0).astype(jnp.bfloat16)
    found = lax.dot_general(values, place, NT, preferred_element_type=jnp.float32)
    number = jnp.broadcast_to(jnp.sum(member, axis=1, keepdims=True), (CLASSES, BLOCK))
    for j in range(length // BLOCK):
        part = found[:, j * BLOCK : (j + 1) * BLOCK]
        high, low = part[0:8], part[8:16]
        slot_high, slot_low = part[16:24], part[24:32]
        rows = [high * BLOCK + low, slot_high * BLOCK + slot_low, number]
        sorted_list[j * 24 : (j + 1) * 24, :] = jnp.concatenate(rows, axis=0).astype(jnp.int32)


class shifted_window:
    def __init__(self, ref, start):
        self.ref, self.start = ref, start * ROWS

    def __getitem__(self, index):
        rows, lanes = index
        return self.ref[pl.ds(pl.multiple_of(rows.start - self.start, ROWS), rows.size), lanes]


def home_kernel(coded, own, *refs, members):
    sorted_list, features, centres, total = refs[:4]
    near_rows, tilt_rows, lists, sems = refs[4:8]
    scratch = refs[8:]
    state = (own, features, centres, total)
    blocks = own.shape[0] // ROWS
    sort_list(coded, sorted_list, blocks, members)
    to_scalars = pltpu.make_async_copy(sorted_list, lists, sems.at[0])
    to_scalars.start()
    prepare_targets(state, near_rows, tilt_rows)
    to_scalars.wait()
    run_class(0, lists, shifted_window(own, REACH * blocks), state, scratch)


def side_of_partner():
    return jnp.where(lax.axis_index("blk") % 2 == 0, REACH + 1, REACH - 1)


def near_kernel(sorted_list, own, partner, *refs, members):
    others, refs = refs[: members - 1], refs[members - 1 :]
    targets, features, centres, total = state = refs[:4]
    window, near_rows, tilt_rows, lists, sems = refs[4:9]
    scratch = refs[9:]
    to_scalars = pltpu.make_async_copy(sorted_list, lists, sems.at[0])
    to_scalars.start()
    blocks = own.shape[0] // ROWS
    put_tiles(window, REACH * blocks, own)
    put_tiles(window, side_of_partner() * blocks, partner)
    for r, other in enumerate(others):
        put_tiles(targets, r * blocks, other)
    prepare_targets(state, near_rows, tilt_rows)
    to_scalars.wait()
    run_class(2, lists, window, state, scratch)


def partner_kernel(sorted_list, partner, own, features, centres, total, lists, sems, *scratch):
    to_scalars = pltpu.make_async_copy(sorted_list, lists, sems.at[0])
    to_scalars.start()
    total[...] = jnp.zeros_like(total)
    to_scalars.wait()
    window = shifted_window(partner, side_of_partner() * (partner.shape[0] // ROWS))
    run_class(1, lists, window, (own, features, centres, total), scratch)


def far_kernel(sorted_list, paired, passed, crossed, *refs):
    targets, features, centres, near_total = refs[:4]
    window, out_ref, total, lists, sems = refs[4:9]
    scratch = refs[9:]
    state = (targets, features, centres, total)
    to_scalars = pltpu.make_async_copy(sorted_list, lists, sems.at[0])
    to_scalars.start()
    blocks = paired.shape[0] // ROWS
    shard = lax.axis_index("blk")
    even = shard // 2 % 2 == 0
    put_tiles(window, jnp.where(even, 2 * REACH, 0) * blocks, paired)
    put_tiles(window, jnp.where(even, 0, 2 * REACH) * blocks, passed)
    put_tiles(window, jnp.where(shard % 2 == 0, REACH - 1, REACH + 1) * blocks, crossed)
    total[...] = jnp.zeros_like(total)
    to_scalars.wait()
    run_class(3, lists, window, state, scratch)
    finish(targets, centres, (near_total, total), out_ref)


def last_kernel(sorted_list, window, own, features, centres, *refs):
    home_total, partner_total, out_ref, total, lists, sems = refs[:6]
    to_scalars = pltpu.make_async_copy(sorted_list, lists, sems.at[0])
    to_scalars.start()
    total[...] = jnp.zeros_like(total)
    to_scalars.wait()
    run_class(4, lists, window, (own, features, centres, total), refs[6:])
    finish(own, centres, (home_total, partner_total, total), out_ref)


def section_kernel(own, sums, *refs):
    returned, (velocity, stretching, section_positions, section_strengths) = refs[:-4], refs[-4:]
    blocks = own.shape[0] // ROWS
    for b in range(blocks):
        lanes = slice(b * BLOCK, (b + 1) * BLOCK)
        for start, result, stepped in ((0, velocity, section_positions), (3, stretching, section_strengths)):
            chosen = pl.ds(start * blocks + b, 3, stride=blocks)
            value = sums[chosen, :]
            for other in returned:
                value = value + other[chosen, :]
            result[:, lanes] = value
            first = b * ROWS + start
            stepped[:, lanes] = own[first : first + 3, :] + section_step * value


def call(kernel, name, inputs, outputs, scratch, flops=0):
    vmem = pl.BlockSpec(memory_space=pltpu.VMEM)
    held = sum(value.size * value.dtype.itemsize for value in (*inputs, *outputs))
    return pl.pallas_call(
        kernel,
        out_shape=outputs,
        in_specs=[vmem for value in inputs],
        out_specs=[vmem for value in outputs],
        scratch_shapes=scratch,
        compiler_params=pltpu.CompilerParams(vmem_limit_bytes=10 * 1024 * 1024 + 2 * held),
        cost_estimate=pl.CostEstimate(flops=flops, bytes_accessed=0, transcendentals=0),
        name=name,
    )(*inputs)


def shards(positions, strengths, radius, block_count, pair_target, pair_slot, pair_count):
    blocks = block_count.shape[0]
    lanes = blocks * BLOCK
    length = pair_target.shape[1]
    members = lax.axis_size("across")
    shard = lax.axis_index("blk")
    count = lax.axis_size("blk")

    def f32(*shape):
        return jax.ShapeDtypeStruct(shape, jnp.float32)

    row = lax.broadcasted_iota(jnp.int32, (blocks, ROWS, BLOCK), 1)
    lane = lax.broadcasted_iota(jnp.int32, (blocks, ROWS, BLOCK), 2)
    cores = radius.reshape(blocks, 1, BLOCK)
    parts = [value.reshape(3, blocks, BLOCK).transpose(1, 0, 2) for value in (positions, strengths)]
    dead = (row >= 3) & (row < 6) & (lane >= block_count[:, None, None])
    own = jnp.where(dead, 0.0, jnp.concatenate(parts + [cores, cores], axis=1))
    own = own.reshape(blocks * ROWS, BLOCK)
    entry = lax.broadcasted_iota(jnp.int32, (1, length), 1)
    coded = jnp.where(entry < pair_count[0], pair_target * SLOTS + pair_slot, -1)
    paired = moved(own, "blk", to_paired_chip)
    others = [
        moved(own, "across", lambda source: (source - away) % members) for away in range(1, members)
    ]
    partner = moved(own, "blk", to_other_core)

    def state_shapes(number):
        return [
            f32(number * blocks * ROWS, BLOCK),
            jax.ShapeDtypeStruct((number * blocks, FEATURES, 2 * BLOCK), jnp.bfloat16),
            f32(number * blocks * ROWS, BLOCK),
            f32(number * blocks * 2 * ROWS, BLOCK),
        ]

    own_shapes, other_shapes = state_shapes(1), state_shapes(members - 1)
    window_shape = f32((2 * REACH + 1) * blocks * ROWS, BLOCK)
    list_shape = jax.ShapeDtypeStruct((3 * ROWS * length // BLOCK, BLOCK), jnp.int32)
    feature_rows = [pltpu.VMEM((GROUP * FEATURES, BLOCK), jnp.float32)] * 2
    list_scratch = [pltpu.SMEM(list_shape.shape, jnp.int32), pltpu.SemaphoreType.DMA((4,))]
    scratch = [
        pltpu.VMEM((GROUP * ROWS, BLOCK), jnp.float32),
        pltpu.VMEM((GROUP * FEATURES, BLOCK), jnp.float32),
        pltpu.VMEM((GROUP * 2 * ROWS, BLOCK), jnp.float32),
        pltpu.VMEM((GROUP * 2 * ROWS, BLOCK), jnp.bfloat16),
        pltpu.VMEM((HALF, BLOCK, 2 * BLOCK), jnp.float32),
        pltpu.VMEM((HALF, BLOCK, 2 * BLOCK), jnp.float32),
    ]
    window_scratch = pltpu.VMEM(window_shape.shape, jnp.float32)

    lists, *own_state = call(
        lambda *refs: home_kernel(*refs, members=members),
        "home_pairs",
        (coded, own),
        [list_shape] + own_shapes[1:],
        feature_rows + list_scratch + scratch,
        flops=HOME_FLOPS,
    )
    paired, lists = lax.optimization_barrier((paired, lists))
    passed = moved(paired, "blk", along_chips(count))
    other_state = list(call(
        lambda *refs: near_kernel(*refs, members=members),
        "near_pairs",
        (lists, own, partner, *others),
        other_shapes,
        [window_scratch] + feature_rows + list_scratch + scratch,
        flops=NEAR_FLOPS,
    ))
    passed, other_state[3] = lax.optimization_barrier((passed, other_state[3]))
    core = shard % 2
    chip = shard // 2 % 2
    crossed = moved(jnp.where(core == chip, paired, passed), "blk", to_other_core)
    (partner_total,) = call(
        partner_kernel,
        "partner_pairs",
        (lists, partner, own, *own_state[:2]),
        [own_shapes[3]],
        list_scratch + scratch,
        flops=HOME_FLOPS,
    )
    crossed, partner_total = lax.optimization_barrier((crossed, partner_total))
    window, away_sums = call(
        far_kernel,
        "far_pairs",
        (lists, paired, passed, crossed, *other_state),
        [window_shape, f32(members - 1, 6 * blocks, BLOCK)],
        [pltpu.VMEM(other_shapes[3].shape, jnp.float32)] + list_scratch + scratch,
        flops=FAR_FLOPS,
    )
    returned = [
        moved(away_sums[away - 1], "across", lambda source: (source + away) % members)
        for away in range(1, members)
    ]
    (sums,) = call(
        last_kernel,
        "last_pairs",
        (lists, window, own, *own_state, partner_total),
        [f32(1, 6 * blocks, BLOCK)],
        [pltpu.VMEM(own_shapes[3].shape, jnp.float32)] + list_scratch + scratch,
        flops=FAR_FLOPS,
    )
    wide = f32(3, lanes)
    return tuple(
        call(section_kernel, "section", (own, sums[0], *returned), [wide] * 4, [])
    )


def solution(mesh):
    whole = P(None, ("blk", "across"))
    line = P(("blk", "across"))
    return jax.shard_map(
        shards,
        mesh=mesh,
        in_specs=(whole, whole, line, line, P(("blk", "across"), None), P(("blk", "across"), None), line),
        out_specs=(whole, whole, whole, whole),
        check_vma=False,
    )
```

```python
import jax
import jax.numpy as jnp
from jax import lax
from jax.experimental import pallas as pl
from jax.experimental.pallas import tpu as pltpu
from jax.sharding import PartitionSpec as P

BLOCK = 128
ROWS = 8
REACH = 2
GROUP = 8
HALF = 4
SLOTS = 1024
STRIP = 16
FEATURES = 32
CLASSES = 8

biot_factor = 0.07957747154594767
section_step = 0.05


def moved(value, axis, target_of):
    pairs = [(source, target_of(source)) for source in range(lax.axis_size(axis))]
    return lax.ppermute(value, axis, pairs)


def to_other_core(source):
    return source ^ 1


def to_paired_chip(source):
    return source ^ 2


def along_chips(count):
    return lambda source: (source + (4 if source & 2 == 0 else -4)) % count


HOME_FLOPS = 10**10
NEAR_FLOPS = 10**10
FAR_FLOPS = 10**10


def rounded(value):
    return value.astype(jnp.bfloat16).astype(jnp.float32)


def split_three(value):
    first = rounded(value)
    rest = value - first
    second = rounded(rest)
    return first, second, rest - second


def cross(left, right):
    return [
        left[1] * right[2] - left[2] * right[1],
        left[2] * right[0] - left[0] * right[2],
        left[0] * right[1] - left[1] * right[0],
    ]


def tile_rows(index, rows):
    return pl.ds(pl.multiple_of(index * rows, rows), rows)


def component(ref, base, number, stride):
    return ref[pl.ds(base + number, GROUP, stride=stride), :]


def store_component(ref, base, number, stride, value):
    ref[pl.ds(base + number, GROUP, stride=stride), :] = value


def target_features(targets, step, centres, near_rows, tilt_rows):
    base = pl.multiple_of(step * (GROUP * ROWS), GROUP * ROWS)
    pos = [component(targets, base, k, ROWS) for k in range(3)]
    strength = [component(targets, base, 3 + k, ROWS) for k in range(3)]
    for k in range(3):
        centre = jnp.broadcast_to(jnp.mean(pos[k], axis=1, keepdims=True), (GROUP, BLOCK))
        store_component(centres, base, k, ROWS, centre)
        pos[k] = pos[k] - centre
    for k in range(3, ROWS):
        store_component(centres, base, k, ROWS, jnp.zeros_like(pos[0]))
    norm = pos[0] * pos[0] + pos[1] * pos[1] + pos[2] * pos[2]
    own = pos[0] * strength[0] + pos[1] * strength[1] + pos[2] * strength[2]
    near = pos + [norm, jnp.ones_like(norm)]
    tilt = [0.5 * s for s in strength] + [own]
    for rows, values in ((near_rows, near), (tilt_rows, tilt)):
        for k, value in enumerate(values):
            parts = split_three(value)
            for slot, part in enumerate((0, 1, 2, 0, 1, 0)):
                store_component(rows, 0, 5 * slot + k, FEATURES, parts[part])


def source_features(gathered, weight, left, charge):
    pos = [component(gathered, 0, k, ROWS) for k in range(3)]
    strength = [component(gathered, 0, 3 + k, ROWS) for k in range(3)]
    inv_core = 1.0 / component(gathered, 0, 6, ROWS)
    inv_square = inv_core * inv_core
    norm = pos[0] * pos[0] + pos[1] * pos[1] + pos[2] * pos[2]
    twice = -2.0 * inv_square
    shape = [p * twice for p in pos] + [inv_square, norm * inv_square + 1.0]
    for k, value in enumerate(shape):
        parts = split_three(value)
        for slot, part in enumerate((0, 0, 0, 1, 1, 2)):
            store_component(left, 0, 5 * slot + k, FEATURES, parts[part])
    scale = inv_square * inv_core * weight
    for k, value in enumerate(strength + cross(pos, strength)):
        value = value * scale
        high = rounded(value)
        store_component(charge, 0, k, 2 * ROWS, high)
        store_component(charge, 0, ROWS + k, 2 * ROWS, value - high)


NT = (((1,), (1,)), ((), ()))
TN = (((0,), (0,)), ((), ()))


def put_tiles(window, first, tiles):
    window[pl.ds(pl.multiple_of(first * ROWS, ROWS), tiles.shape[0]), :] = tiles[...]


def prepare_targets(state, near_rows, tilt_rows):
    targets, features, centres, total = state
    near_rows[...] = jnp.zeros_like(near_rows)
    tilt_rows[...] = jnp.zeros_like(tilt_rows)
    total[...] = jnp.zeros_like(total)

    def prepare(step, carry):
        target_features(targets, step, centres, near_rows, tilt_rows)
        for u in range(GROUP):
            rows = slice(u * FEATURES, (u + 1) * FEATURES)
            features[step * GROUP + u, :, :BLOCK] = near_rows[rows, :].astype(jnp.bfloat16)
            features[step * GROUP + u, :, BLOCK:] = tilt_rows[rows, :].astype(jnp.bfloat16)
        return carry

    lax.fori_loop(0, features.shape[0] // GROUP, prepare, 0)


def run_class(kind, lists, window, state, scratch):
    _, features, centres, total = state
    gathered, left, charge_next, charge, first_half, second_half = scratch
    listed = lists[2 * ROWS + kind, 0]

    def entry_at(step, u):
        entry = jnp.minimum(step * GROUP + u, listed - 1)
        return entry // BLOCK * (3 * ROWS) + kind, lax.rem(entry, BLOCK)

    def target_of(step, u):
        row, column = entry_at(step, u)
        return lists[row, column]

    def prepare_sources(step):
        for u in range(GROUP):
            row, column = entry_at(step, u)
            gathered[u * ROWS : (u + 1) * ROWS, :] = (
                window[tile_rows(lists[row + ROWS, column], ROWS), :]
                - centres[tile_rows(lists[row, column], ROWS), :]
            )
        order = lax.broadcasted_iota(jnp.int32, (GROUP, BLOCK), 0) + step * GROUP
        weight = jnp.where(order < listed, 1.0, 0.0).astype(jnp.float32)
        source_features(gathered, weight, left, charge_next)

    def products(step, u, held):
        shape = left[u * FEATURES : (u + 1) * FEATURES, :].astype(jnp.bfloat16)
        held[u % HALF] = lax.dot_general(
            shape, features[target_of(step, u)], TN, preferred_element_type=jnp.float32
        )

    def weights(u, held):
        parts = []
        for first in range(0, BLOCK, STRIP):
            rows = slice(first, first + STRIP)
            near = held[u % HALF, rows, :BLOCK]
            tilt = held[u % HALF, rows, BLOCK:]
            q = lax.rsqrt(near)
            q2 = q * q
            q3 = q2 * q
            f = q3 * (q2 + (2.0 / 3.0))
            h = (q3 * q2) * (q2 + 0.4) * tilt
            fh = f.astype(jnp.bfloat16)
            fl = (f - fh.astype(jnp.float32)).astype(jnp.bfloat16)
            hh = h.astype(jnp.bfloat16)
            hl = (h - hh.astype(jnp.float32)).astype(jnp.bfloat16)
            parts.append((fh, fl, hh, hl))
        fh, fl, hh, hl = [jnp.concatenate(part, axis=0) for part in zip(*parts)]
        return jnp.concatenate(
            [jnp.concatenate([fh, fl], axis=1), jnp.concatenate([hh, hl], axis=1)], axis=0
        )

    def add_up(step, u, stacked):
        pair = charge[u * 2 * ROWS : (u + 1) * 2 * ROWS, :]
        blank = jnp.zeros_like(pair)
        pair = jnp.concatenate(
            [jnp.concatenate([pair, blank], axis=1), jnp.concatenate([blank, pair], axis=1)], axis=0
        )
        sums = jnp.dot(pair, stacked, preferred_element_type=jnp.float32)
        fsum = sums[0:8, :BLOCK] + sums[8:16, :BLOCK] + sums[0:8, BLOCK:]
        hsum = sums[16:24, :BLOCK] + sums[24:32, :BLOCK] + sums[16:24, BLOCK:]
        total[tile_rows(target_of(step, u), 2 * ROWS), :] += jnp.concatenate([fsum, hsum], axis=0)

    def turn(step, carry):
        stacked = {}
        for u in range(HALF):
            stacked[u] = weights(u, first_half)
            products(step, HALF + u, second_half)
            add_up(step, u, stacked[u])
        prepare_sources(step + 1)
        for u in range(HALF, GROUP):
            stacked[u] = weights(u, second_half)
            products(step + 1, u - HALF, first_half)
            add_up(step, u, stacked[u])
        charge[...] = charge_next[...].astype(jnp.bfloat16)
        return carry

    @pl.when(listed > 0)
    def _():
        left[...] = jnp.zeros_like(left)
        charge_next[...] = jnp.zeros_like(charge_next)
        prepare_sources(0)
        for u in range(HALF):
            products(0, u, first_half)
        charge[...] = charge_next[...].astype(jnp.bfloat16)
        lax.fori_loop(0, (listed + GROUP - 1) // GROUP, turn, 0)


def finish(targets, centres, totals, out_ref):
    blocks = out_ref.shape[1] // 6

    def one(step, carry):
        base = pl.multiple_of(step * GROUP * ROWS, GROUP * ROWS)
        wide = pl.multiple_of(step * GROUP * 2 * ROWS, GROUP * 2 * ROWS)
        pos = [
            component(targets, base, k, ROWS) - component(centres, base, k, ROWS) for k in range(3)
        ]
        strength = [component(targets, base, 3 + k, ROWS) for k in range(3)]
        fa, fb, ha, hb = [
            [
                sum(component(total, wide, start + k, 2 * ROWS) for total in totals)
                for k in range(3)
            ]
            for start in (0, 3, 8, 11)
        ]
        swirl = cross(pos, fa)
        lean = cross(strength, fa)
        bend = cross(pos, ha)
        member = step * GROUP // blocks
        inside = lax.rem(step * GROUP, blocks)
        for k in range(3):
            velocity = (-1.5 * biot_factor) * (swirl[k] - fb[k])
            stretch = (-1.5 * biot_factor) * lean[k] + (7.5 * biot_factor) * (bend[k] - hb[k])
            out_ref[member, pl.ds(pl.multiple_of(k * blocks + inside, GROUP), GROUP), :] = velocity
            out_ref[member, pl.ds(pl.multiple_of((3 + k) * blocks + inside, GROUP), GROUP), :] = stretch
        return carry

    lax.fori_loop(0, targets.shape[0] // ROWS // GROUP, one, 0)


def sort_list(coded, sorted_list, blocks, members):
    length = coded.shape[1]
    t = coded[...] // SLOTS
    s = coded[...] % SLOTS
    t = t - lax.axis_index("across") * blocks
    t = jnp.where(t < 0, t + members * blocks, t)
    partner = jnp.where(lax.axis_index("blk") % 2 == 0, REACH + 1, REACH - 1)
    run = s // blocks
    mine = t < blocks
    t = jnp.where(mine, t, t - blocks)
    home = run == REACH
    near = home | (run == partner)
    kind = jnp.where(
        near, jnp.where(mine, jnp.where(home, 0, 1), 2), jnp.where(mine, 4, 3)
    )
    kind = jnp.where(coded[...] < 0, CLASSES - 1, kind)
    member = jnp.where(lax.broadcasted_iota(jnp.int32, (CLASSES, length), 0) == kind, 1.0, 0.0)
    row = lax.broadcasted_iota(jnp.int32, (length, length), 0)
    column = lax.broadcasted_iota(jnp.int32, (length, length), 1)
    before = jnp.where(row < column, 1.0, 0.0).astype(jnp.bfloat16)
    earlier = jnp.dot(member.astype(jnp.bfloat16), before, preferred_element_type=jnp.float32)
    rank = jnp.sum(member * earlier, axis=0, keepdims=True).astype(jnp.int32)
    place = jnp.where(row == rank, 1.0, 0.0).astype(jnp.bfloat16)
    values = [t // BLOCK, t % BLOCK, s // BLOCK, s % BLOCK]
    values = [member * value.astype(jnp.float32) for value in values]
    values = jnp.concatenate(values, axis=0).astype(jnp.bfloat16)
    found = lax.dot_general(values, place, NT, preferred_element_type=jnp.float32)
    number = jnp.broadcast_to(jnp.sum(member, axis=1, keepdims=True), (CLASSES, BLOCK))
    for j in range(length // BLOCK):
        part = found[:, j * BLOCK : (j + 1) * BLOCK]
        high, low = part[0:8], part[8:16]
        slot_high, slot_low = part[16:24], part[24:32]
        rows = [high * BLOCK + low, slot_high * BLOCK + slot_low, number]
        sorted_list[j * 24 : (j + 1) * 24, :] = jnp.concatenate(rows, axis=0).astype(jnp.int32)


class shifted_window:
    def __init__(self, ref, start):
        self.ref, self.start = ref, start * ROWS

    def __getitem__(self, index):
        rows, lanes = index
        return self.ref[pl.ds(pl.multiple_of(rows.start - self.start, ROWS), rows.size), lanes]


def home_kernel(coded, own, *refs, members):
    sorted_list, features, centres, total = refs[:4]
    near_rows, tilt_rows, lists, sems = refs[4:8]
    scratch = refs[8:]
    state = (own, features, centres, total)
    blocks = own.shape[0] // ROWS
    sort_list(coded, sorted_list, blocks, members)
    to_scalars = pltpu.make_async_copy(sorted_list, lists, sems.at[0])
    to_scalars.start()
    prepare_targets(state, near_rows, tilt_rows)
    to_scalars.wait()
    run_class(0, lists, shifted_window(own, REACH * blocks), state, scratch)


def side_of_partner():
    return jnp.where(lax.axis_index("blk") % 2 == 0, REACH + 1, REACH - 1)


def near_kernel(sorted_list, own, partner, *refs, members):
    others, refs = refs[: members - 1], refs[members - 1 :]
    targets, features, centres, total = state = refs[:4]
    window, near_rows, tilt_rows, lists, sems = refs[4:9]
    scratch = refs[9:]
    to_scalars = pltpu.make_async_copy(sorted_list, lists, sems.at[0])
    to_scalars.start()
    blocks = own.shape[0] // ROWS
    put_tiles(window, REACH * blocks, own)
    put_tiles(window, side_of_partner() * blocks, partner)
    for r, other in enumerate(others):
        put_tiles(targets, r * blocks, other)
    prepare_targets(state, near_rows, tilt_rows)
    to_scalars.wait()
    run_class(2, lists, window, state, scratch)


def partner_kernel(sorted_list, partner, own, features, centres, total, lists, sems, *scratch):
    to_scalars = pltpu.make_async_copy(sorted_list, lists, sems.at[0])
    to_scalars.start()
    total[...] = jnp.zeros_like(total)
    to_scalars.wait()
    window = shifted_window(partner, side_of_partner() * (partner.shape[0] // ROWS))
    run_class(1, lists, window, (own, features, centres, total), scratch)


def far_kernel(sorted_list, paired, passed, crossed, *refs):
    targets, features, centres, near_total = refs[:4]
    window, out_ref, total, lists, sems = refs[4:9]
    scratch = refs[9:]
    state = (targets, features, centres, total)
    to_scalars = pltpu.make_async_copy(sorted_list, lists, sems.at[0])
    to_scalars.start()
    blocks = paired.shape[0] // ROWS
    shard = lax.axis_index("blk")
    even = shard // 2 % 2 == 0
    put_tiles(window, jnp.where(even, 2 * REACH, 0) * blocks, paired)
    put_tiles(window, jnp.where(even, 0, 2 * REACH) * blocks, passed)
    put_tiles(window, jnp.where(shard % 2 == 0, REACH - 1, REACH + 1) * blocks, crossed)
    total[...] = jnp.zeros_like(total)
    to_scalars.wait()
    run_class(3, lists, window, state, scratch)
    finish(targets, centres, (near_total, total), out_ref)


def last_kernel(sorted_list, window, own, features, centres, *refs):
    home_total, partner_total, out_ref, total, lists, sems = refs[:6]
    to_scalars = pltpu.make_async_copy(sorted_list, lists, sems.at[0])
    to_scalars.start()
    total[...] = jnp.zeros_like(total)
    to_scalars.wait()
    run_class(4, lists, window, (own, features, centres, total), refs[6:])
    finish(own, centres, (home_total, partner_total, total), out_ref)


def section_kernel(own, sums, *refs):
    returned, (velocity, stretching, section_positions, section_strengths) = refs[:-4], refs[-4:]
    blocks = own.shape[0] // ROWS
    for b in range(blocks):
        lanes = slice(b * BLOCK, (b + 1) * BLOCK)
        for start, result, stepped in ((0, velocity, section_positions), (3, stretching, section_strengths)):
            chosen = pl.ds(start * blocks + b, 3, stride=blocks)
            value = sums[chosen, :]
            for other in returned:
                value = value + other[chosen, :]
            result[:, lanes] = value
            first = b * ROWS + start
            stepped[:, lanes] = own[first : first + 3, :] + section_step * value


def call(kernel, name, inputs, outputs, scratch, flops=0):
    vmem = pl.BlockSpec(memory_space=pltpu.VMEM)
    held = sum(value.size * value.dtype.itemsize for value in (*inputs, *outputs))
    return pl.pallas_call(
        kernel,
        out_shape=outputs,
        in_specs=[vmem for value in inputs],
        out_specs=[vmem for value in outputs],
        scratch_shapes=scratch,
        compiler_params=pltpu.CompilerParams(vmem_limit_bytes=10 * 1024 * 1024 + 2 * held),
        cost_estimate=pl.CostEstimate(flops=flops, bytes_accessed=0, transcendentals=0),
        name=name,
    )(*inputs)


def shards(positions, strengths, radius, block_count, pair_target, pair_slot, pair_count):
    blocks = block_count.shape[0]
    lanes = blocks * BLOCK
    length = pair_target.shape[1]
    members = lax.axis_size("across")
    shard = lax.axis_index("blk")
    count = lax.axis_size("blk")

    def f32(*shape):
        return jax.ShapeDtypeStruct(shape, jnp.float32)

    row = lax.broadcasted_iota(jnp.int32, (blocks, ROWS, BLOCK), 1)
    lane = lax.broadcasted_iota(jnp.int32, (blocks, ROWS, BLOCK), 2)
    cores = radius.reshape(blocks, 1, BLOCK)
    parts = [value.reshape(3, blocks, BLOCK).transpose(1, 0, 2) for value in (positions, strengths)]
    dead = (row >= 3) & (row < 6) & (lane >= block_count[:, None, None])
    own = jnp.where(dead, 0.0, jnp.concatenate(parts + [cores, cores], axis=1))
    own = own.reshape(blocks * ROWS, BLOCK)
    entry = lax.broadcasted_iota(jnp.int32, (1, length), 1)
    coded = jnp.where(entry < pair_count[0], pair_target * SLOTS + pair_slot, -1)
    paired = moved(own, "blk", to_paired_chip)
    others = [
        moved(own, "across", lambda source: (source - away) % members) for away in range(1, members)
    ]
    partner = moved(own, "blk", to_other_core)

    def state_shapes(number):
        return [
            f32(number * blocks * ROWS, BLOCK),
            jax.ShapeDtypeStruct((number * blocks, FEATURES, 2 * BLOCK), jnp.bfloat16),
            f32(number * blocks * ROWS, BLOCK),
            f32(number * blocks * 2 * ROWS, BLOCK),
        ]

    own_shapes, other_shapes = state_shapes(1), state_shapes(members - 1)
    window_shape = f32((2 * REACH + 1) * blocks * ROWS, BLOCK)
    list_shape = jax.ShapeDtypeStruct((3 * ROWS * length // BLOCK, BLOCK), jnp.int32)
    feature_rows = [pltpu.VMEM((GROUP * FEATURES, BLOCK), jnp.float32)] * 2
    list_scratch = [pltpu.SMEM(list_shape.shape, jnp.int32), pltpu.SemaphoreType.DMA((4,))]
    scratch = [
        pltpu.VMEM((GROUP * ROWS, BLOCK), jnp.float32),
        pltpu.VMEM((GROUP * FEATURES, BLOCK), jnp.float32),
        pltpu.VMEM((GROUP * 2 * ROWS, BLOCK), jnp.float32),
        pltpu.VMEM((GROUP * 2 * ROWS, BLOCK), jnp.bfloat16),
        pltpu.VMEM((HALF, BLOCK, 2 * BLOCK), jnp.float32),
        pltpu.VMEM((HALF, BLOCK, 2 * BLOCK), jnp.float32),
    ]
    window_scratch = pltpu.VMEM(window_shape.shape, jnp.float32)

    lists, *own_state = call(
        lambda *refs: home_kernel(*refs, members=members),
        "home_pairs",
        (coded, own),
        [list_shape] + own_shapes[1:],
        feature_rows + list_scratch + scratch,
        flops=HOME_FLOPS,
    )
    paired, lists = lax.optimization_barrier((paired, lists))
    passed = moved(paired, "blk", along_chips(count))
    other_state = list(call(
        lambda *refs: near_kernel(*refs, members=members),
        "near_pairs",
        (lists, own, partner, *others),
        other_shapes,
        [window_scratch] + feature_rows + list_scratch + scratch,
        flops=NEAR_FLOPS,
    ))
    passed, other_state[3] = lax.optimization_barrier((passed, other_state[3]))
    core = shard % 2
    chip = shard // 2 % 2
    crossed = moved(jnp.where(core == chip, paired, passed), "blk", to_other_core)
    (partner_total,) = call(
        partner_kernel,
        "partner_pairs",
        (lists, partner, own, *own_state[:2]),
        [own_shapes[3]],
        list_scratch + scratch,
        flops=HOME_FLOPS,
    )
    crossed, partner_total = lax.optimization_barrier((crossed, partner_total))
    window, away_sums = call(
        far_kernel,
        "far_pairs",
        (lists, paired, passed, crossed, *other_state),
        [window_shape, f32(members - 1, 6 * blocks, BLOCK)],
        [pltpu.VMEM(other_shapes[3].shape, jnp.float32)] + list_scratch + scratch,
        flops=FAR_FLOPS,
    )
    returned = [
        moved(away_sums[away - 1], "across", lambda source: (source + away) % members)
        for away in range(1, members)
    ]
    (sums,) = call(
        last_kernel,
        "last_pairs",
        (lists, window, own, *own_state, partner_total),
        [f32(1, 6 * blocks, BLOCK)],
        [pltpu.VMEM(own_shapes[3].shape, jnp.float32)] + list_scratch + scratch,
        flops=FAR_FLOPS,
    )
    wide = f32(3, lanes)
    return tuple(
        call(section_kernel, "section", (own, sums[0], *returned), [wide] * 4, [])
    )


def solution(mesh):
    whole = P(None, ("blk", "across"))
    line = P(("blk", "across"))
    return jax.shard_map(
        shards,
        mesh=mesh,
        in_specs=(whole, whole, line, line, P(("blk", "across"), None), P(("blk", "across"), None), line),
        out_specs=(whole, whole, whole, whole),
        check_vma=False,
    )
```

```python
import jax
import jax.numpy as jnp
from jax import lax
from jax.experimental import pallas as pl
from jax.experimental.pallas import tpu as pltpu
from jax.sharding import PartitionSpec as P

BLOCK = 128
ROWS = 8
REACH = 2
GROUP = 8
HALF = 4
SLOTS = 1024
FEATURES = 48
CLASSES = 8

biot_factor = 0.07957747154594767
section_step = 0.05


def moved(value, axis, target_of):
    pairs = [(source, target_of(source)) for source in range(lax.axis_size(axis))]
    return lax.ppermute(value, axis, pairs)


def to_other_core(source):
    return source ^ 1


def to_paired_chip(source):
    return source ^ 2


def along_chips(count):
    return lambda source: (source + (4 if source & 2 == 0 else -4)) % count


HOME_FLOPS = 10**10
NEAR_FLOPS = 10**10
FAR_FLOPS = 10**10


def rounded(value):
    return value.astype(jnp.bfloat16).astype(jnp.float32)


def split_three(value):
    first = rounded(value)
    rest = value - first
    second = rounded(rest)
    return first, second, rest - second


def six_slots(tile, order):
    parts = split_three(tile)
    return jnp.concatenate([parts[part] for part in order], axis=0).astype(jnp.bfloat16)


def cross(left, right):
    return [
        left[1] * right[2] - left[2] * right[1],
        left[2] * right[0] - left[0] * right[2],
        left[0] * right[1] - left[1] * right[0],
    ]


def tile_rows(index, rows):
    return pl.ds(pl.multiple_of(index * rows, rows), rows)


def component(ref, base, number, stride):
    return ref[pl.ds(base + number, GROUP, stride=stride), :]


def store_component(ref, base, number, stride, value):
    ref[pl.ds(base + number, GROUP, stride=stride), :] = value


def target_features(targets, step, centres, near_rows, tilt_rows):
    base = pl.multiple_of(step * (GROUP * ROWS), GROUP * ROWS)
    pos = [component(targets, base, k, ROWS) for k in range(3)]
    strength = [component(targets, base, 3 + k, ROWS) for k in range(3)]
    for k in range(3):
        centre = jnp.broadcast_to(jnp.mean(pos[k], axis=1, keepdims=True), (GROUP, BLOCK))
        store_component(centres, base, k, ROWS, centre)
        pos[k] = pos[k] - centre
    for k in range(3, ROWS):
        store_component(centres, base, k, ROWS, jnp.zeros_like(pos[0]))
    norm = pos[0] * pos[0] + pos[1] * pos[1] + pos[2] * pos[2]
    own = pos[0] * strength[0] + pos[1] * strength[1] + pos[2] * strength[2]
    near = pos + [norm, jnp.ones_like(norm)]
    tilt = [0.5 * s for s in strength] + [own]
    for rows, values in ((near_rows, near), (tilt_rows, tilt)):
        for k, value in enumerate(values):
            store_component(rows, 0, k, ROWS, value)


def source_features(gathered, weight, left, charge):
    pos = [component(gathered, 0, k, ROWS) for k in range(3)]
    strength = [component(gathered, 0, 3 + k, ROWS) for k in range(3)]
    inv_core = 1.0 / component(gathered, 0, 6, ROWS)
    inv_square = inv_core * inv_core
    norm = pos[0] * pos[0] + pos[1] * pos[1] + pos[2] * pos[2]
    twice = -2.0 * inv_square
    shape = [p * twice for p in pos] + [inv_square, norm * inv_square + 1.0]
    for k, value in enumerate(shape):
        store_component(left, 0, k, ROWS, value)
    scale = inv_square * inv_core * weight
    for k, value in enumerate(strength + cross(pos, strength)):
        store_component(charge, 0, k, ROWS, value * scale)


NT = (((1,), (1,)), ((), ()))
TN = (((0,), (0,)), ((), ()))


def put_tiles(window, first, tiles):
    window[pl.ds(pl.multiple_of(first * ROWS, ROWS), tiles.shape[0]), :] = tiles[...]


def prepare_targets(state, near_rows, tilt_rows):
    targets, features, centres, total = state
    near_rows[...] = jnp.zeros_like(near_rows)
    tilt_rows[...] = jnp.zeros_like(tilt_rows)
    total[...] = jnp.zeros_like(total)

    def prepare(step, carry):
        target_features(targets, step, centres, near_rows, tilt_rows)
        for u in range(GROUP):
            rows = slice(u * ROWS, (u + 1) * ROWS)
            features[step * GROUP + u, :, :BLOCK] = six_slots(near_rows[rows, :], (0, 1, 2, 0, 1, 0))
            features[step * GROUP + u, :, BLOCK:] = six_slots(tilt_rows[rows, :], (0, 1, 2, 0, 1, 0))
        return carry

    lax.fori_loop(0, features.shape[0] // GROUP, prepare, 0)


def run_class(kind, lists, window, state, scratch):
    _, features, centres, total = state
    gathered, left, charge_next, charge, first_half, second_half = scratch
    listed = lists[2 * ROWS + kind, 0]

    def entry_at(step, u):
        entry = jnp.minimum(step * GROUP + u, listed - 1)
        return entry // BLOCK * (3 * ROWS) + kind, lax.rem(entry, BLOCK)

    def target_of(step, u):
        row, column = entry_at(step, u)
        return lists[row, column]

    def prepare_sources(step):
        for u in range(GROUP):
            row, column = entry_at(step, u)
            gathered[u * ROWS : (u + 1) * ROWS, :] = (
                window[tile_rows(lists[row + ROWS, column], ROWS), :]
                - centres[tile_rows(lists[row, column], ROWS), :]
            )
        order = lax.broadcasted_iota(jnp.int32, (GROUP, BLOCK), 0) + step * GROUP
        weight = jnp.where(order < listed, 1.0, 0.0).astype(jnp.float32)
        source_features(gathered, weight, left, charge_next)

    def products(step, u, held):
        shape = six_slots(left[u * ROWS : (u + 1) * ROWS, :], (0, 0, 0, 1, 1, 2))
        held[u % HALF] = lax.dot_general(
            shape, features[target_of(step, u)], TN, preferred_element_type=jnp.float32
        )

    def weights(u, held):
        near = held[u % HALF, :, :BLOCK]
        tilt = held[u % HALF, :, BLOCK:]
        q = lax.rsqrt(near)
        q2 = q * q
        q3 = q2 * q
        f = q3 * (q2 + (2.0 / 3.0))
        h = (q3 * q2) * (q2 + 0.4) * tilt
        fh = f.astype(jnp.bfloat16)
        fl = (f - fh.astype(jnp.float32)).astype(jnp.bfloat16)
        hh = h.astype(jnp.bfloat16)
        hl = (h - hh.astype(jnp.float32)).astype(jnp.bfloat16)
        return jnp.concatenate(
            [jnp.concatenate([fh, fl], axis=1), jnp.concatenate([hh, hl], axis=1)], axis=0
        )

    def add_up(step, u, stacked):
        pair = charge[u * ROWS : (u + 1) * ROWS, :]
        high = rounded(pair)
        pair = jnp.concatenate([high, pair - high], axis=0).astype(jnp.bfloat16)
        blank = jnp.zeros_like(pair)
        pair = jnp.concatenate(
            [jnp.concatenate([pair, blank], axis=1), jnp.concatenate([blank, pair], axis=1)], axis=0
        )
        sums = jnp.dot(pair, stacked, preferred_element_type=jnp.float32)
        fsum = sums[0:8, :BLOCK] + sums[8:16, :BLOCK] + sums[0:8, BLOCK:]
        hsum = sums[16:24, :BLOCK] + sums[24:32, :BLOCK] + sums[16:24, BLOCK:]
        total[tile_rows(target_of(step, u), 2 * ROWS), :] += jnp.concatenate([fsum, hsum], axis=0)

    def turn(step, carry):
        stacked = {}
        for u in range(HALF):
            stacked[u] = weights(u, first_half)
            products(step, HALF + u, second_half)
            add_up(step, u, stacked[u])
        prepare_sources(step + 1)
        for u in range(HALF, GROUP):
            stacked[u] = weights(u, second_half)
            products(step + 1, u - HALF, first_half)
            add_up(step, u, stacked[u])
        charge[...] = charge_next[...]
        return carry

    @pl.when(listed > 0)
    def _():
        left[...] = jnp.zeros_like(left)
        charge_next[...] = jnp.zeros_like(charge_next)
        prepare_sources(0)
        for u in range(HALF):
            products(0, u, first_half)
        charge[...] = charge_next[...]
        lax.fori_loop(0, (listed + GROUP - 1) // GROUP, turn, 0)


def finish(targets, centres, totals, out_ref):
    blocks = out_ref.shape[1] // 6

    def one(step, carry):
        base = pl.multiple_of(step * GROUP * ROWS, GROUP * ROWS)
        wide = pl.multiple_of(step * GROUP * 2 * ROWS, GROUP * 2 * ROWS)
        pos = [
            component(targets, base, k, ROWS) - component(centres, base, k, ROWS) for k in range(3)
        ]
        strength = [component(targets, base, 3 + k, ROWS) for k in range(3)]
        fa, fb, ha, hb = [
            [
                sum(component(total, wide, start + k, 2 * ROWS) for total in totals)
                for k in range(3)
            ]
            for start in (0, 3, 8, 11)
        ]
        swirl = cross(pos, fa)
        lean = cross(strength, fa)
        bend = cross(pos, ha)
        member = step * GROUP // blocks
        inside = lax.rem(step * GROUP, blocks)
        for k in range(3):
            velocity = (-1.5 * biot_factor) * (swirl[k] - fb[k])
            stretch = (-1.5 * biot_factor) * lean[k] + (7.5 * biot_factor) * (bend[k] - hb[k])
            out_ref[member, pl.ds(pl.multiple_of(k * blocks + inside, GROUP), GROUP), :] = velocity
            out_ref[member, pl.ds(pl.multiple_of((3 + k) * blocks + inside, GROUP), GROUP), :] = stretch
        return carry

    lax.fori_loop(0, targets.shape[0] // ROWS // GROUP, one, 0)


def sort_list(coded, sorted_list, blocks, members):
    length = coded.shape[1]
    t = coded[...] // SLOTS
    s = coded[...] % SLOTS
    t = t - lax.axis_index("across") * blocks
    t = jnp.where(t < 0, t + members * blocks, t)
    partner = jnp.where(lax.axis_index("blk") % 2 == 0, REACH + 1, REACH - 1)
    run = s // blocks
    mine = t < blocks
    t = jnp.where(mine, t, t - blocks)
    home = run == REACH
    near = home | (run == partner)
    kind = jnp.where(
        near, jnp.where(mine, jnp.where(home, 0, 1), 2), jnp.where(mine, 4, 3)
    )
    kind = jnp.where(coded[...] < 0, CLASSES - 1, kind)
    member = jnp.where(lax.broadcasted_iota(jnp.int32, (CLASSES, length), 0) == kind, 1.0, 0.0)
    row = lax.broadcasted_iota(jnp.int32, (length, length), 0)
    column = lax.broadcasted_iota(jnp.int32, (length, length), 1)
    before = jnp.where(row < column, 1.0, 0.0).astype(jnp.bfloat16)
    earlier = jnp.dot(member.astype(jnp.bfloat16), before, preferred_element_type=jnp.float32)
    rank = jnp.sum(member * earlier, axis=0, keepdims=True).astype(jnp.int32)
    place = jnp.where(row == rank, 1.0, 0.0).astype(jnp.bfloat16)
    values = [t // BLOCK, t % BLOCK, s // BLOCK, s % BLOCK]
    values = [member * value.astype(jnp.float32) for value in values]
    values = jnp.concatenate(values, axis=0).astype(jnp.bfloat16)
    found = lax.dot_general(values, place, NT, preferred_element_type=jnp.float32)
    number = jnp.broadcast_to(jnp.sum(member, axis=1, keepdims=True), (CLASSES, BLOCK))
    for j in range(length // BLOCK):
        part = found[:, j * BLOCK : (j + 1) * BLOCK]
        high, low = part[0:8], part[8:16]
        slot_high, slot_low = part[16:24], part[24:32]
        rows = [high * BLOCK + low, slot_high * BLOCK + slot_low, number]
        sorted_list[j * 24 : (j + 1) * 24, :] = jnp.concatenate(rows, axis=0).astype(jnp.int32)


class shifted_window:
    def __init__(self, ref, start):
        self.ref, self.start = ref, start * ROWS

    def __getitem__(self, index):
        rows, lanes = index
        return self.ref[pl.ds(pl.multiple_of(rows.start - self.start, ROWS), rows.size), lanes]


def home_kernel(coded, own, *refs, members):
    sorted_list, features, centres, total = refs[:4]
    near_rows, tilt_rows, lists, sems = refs[4:8]
    scratch = refs[8:]
    state = (own, features, centres, total)
    blocks = own.shape[0] // ROWS
    sort_list(coded, sorted_list, blocks, members)
    to_scalars = pltpu.make_async_copy(sorted_list, lists, sems.at[0])
    to_scalars.start()
    prepare_targets(state, near_rows, tilt_rows)
    to_scalars.wait()
    run_class(0, lists, shifted_window(own, REACH * blocks), state, scratch)


def side_of_partner():
    return jnp.where(lax.axis_index("blk") % 2 == 0, REACH + 1, REACH - 1)


def near_kernel(sorted_list, own, partner, *refs, members):
    others, refs = refs[: members - 1], refs[members - 1 :]
    targets, features, centres, total = state = refs[:4]
    window, near_rows, tilt_rows, lists, sems = refs[4:9]
    scratch = refs[9:]
    to_scalars = pltpu.make_async_copy(sorted_list, lists, sems.at[0])
    to_scalars.start()
    blocks = own.shape[0] // ROWS
    put_tiles(window, REACH * blocks, own)
    put_tiles(window, side_of_partner() * blocks, partner)
    for r, other in enumerate(others):
        put_tiles(targets, r * blocks, other)
    prepare_targets(state, near_rows, tilt_rows)
    to_scalars.wait()
    run_class(2, lists, window, state, scratch)


def partner_kernel(sorted_list, partner, own, features, centres, total, lists, sems, *scratch):
    to_scalars = pltpu.make_async_copy(sorted_list, lists, sems.at[0])
    to_scalars.start()
    total[...] = jnp.zeros_like(total)
    to_scalars.wait()
    window = shifted_window(partner, side_of_partner() * (partner.shape[0] // ROWS))
    run_class(1, lists, window, (own, features, centres, total), scratch)


def far_kernel(sorted_list, paired, passed, crossed, *refs):
    targets, features, centres, near_total = refs[:4]
    window, out_ref, total, lists, sems = refs[4:9]
    scratch = refs[9:]
    state = (targets, features, centres, total)
    to_scalars = pltpu.make_async_copy(sorted_list, lists, sems.at[0])
    to_scalars.start()
    blocks = paired.shape[0] // ROWS
    shard = lax.axis_index("blk")
    even = shard // 2 % 2 == 0
    put_tiles(window, jnp.where(even, 2 * REACH, 0) * blocks, paired)
    put_tiles(window, jnp.where(even, 0, 2 * REACH) * blocks, passed)
    put_tiles(window, jnp.where(shard % 2 == 0, REACH - 1, REACH + 1) * blocks, crossed)
    total[...] = jnp.zeros_like(total)
    to_scalars.wait()
    run_class(3, lists, window, state, scratch)
    finish(targets, centres, (near_total, total), out_ref)


def last_kernel(sorted_list, window, own, features, centres, *refs):
    home_total, partner_total, out_ref, total, lists, sems = refs[:6]
    to_scalars = pltpu.make_async_copy(sorted_list, lists, sems.at[0])
    to_scalars.start()
    total[...] = jnp.zeros_like(total)
    to_scalars.wait()
    run_class(4, lists, window, (own, features, centres, total), refs[6:])
    finish(own, centres, (home_total, partner_total, total), out_ref)


def section_kernel(own, sums, *refs):
    returned, (velocity, stretching, section_positions, section_strengths) = refs[:-4], refs[-4:]
    blocks = own.shape[0] // ROWS
    for b in range(blocks):
        lanes = slice(b * BLOCK, (b + 1) * BLOCK)
        for start, result, stepped in ((0, velocity, section_positions), (3, stretching, section_strengths)):
            chosen = pl.ds(start * blocks + b, 3, stride=blocks)
            value = sums[chosen, :]
            for other in returned:
                value = value + other[chosen, :]
            result[:, lanes] = value
            first = b * ROWS + start
            stepped[:, lanes] = own[first : first + 3, :] + section_step * value


def call(kernel, name, inputs, outputs, scratch, flops=0):
    vmem = pl.BlockSpec(memory_space=pltpu.VMEM)
    held = sum(value.size * value.dtype.itemsize for value in (*inputs, *outputs))
    return pl.pallas_call(
        kernel,
        out_shape=outputs,
        in_specs=[vmem for value in inputs],
        out_specs=[vmem for value in outputs],
        scratch_shapes=scratch,
        compiler_params=pltpu.CompilerParams(vmem_limit_bytes=10 * 1024 * 1024 + 2 * held),
        cost_estimate=pl.CostEstimate(flops=flops, bytes_accessed=0, transcendentals=0),
        name=name,
    )(*inputs)


def shards(positions, strengths, radius, block_count, pair_target, pair_slot, pair_count):
    blocks = block_count.shape[0]
    lanes = blocks * BLOCK
    length = pair_target.shape[1]
    members = lax.axis_size("across")
    shard = lax.axis_index("blk")
    count = lax.axis_size("blk")

    def f32(*shape):
        return jax.ShapeDtypeStruct(shape, jnp.float32)

    row = lax.broadcasted_iota(jnp.int32, (blocks, ROWS, BLOCK), 1)
    lane = lax.broadcasted_iota(jnp.int32, (blocks, ROWS, BLOCK), 2)
    cores = radius.reshape(blocks, 1, BLOCK)
    parts = [value.reshape(3, blocks, BLOCK).transpose(1, 0, 2) for value in (positions, strengths)]
    dead = (row >= 3) & (row < 6) & (lane >= block_count[:, None, None])
    own = jnp.where(dead, 0.0, jnp.concatenate(parts + [cores, cores], axis=1))
    own = own.reshape(blocks * ROWS, BLOCK)
    entry = lax.broadcasted_iota(jnp.int32, (1, length), 1)
    coded = jnp.where(entry < pair_count[0], pair_target * SLOTS + pair_slot, -1)
    paired = moved(own, "blk", to_paired_chip)
    others = [
        moved(own, "across", lambda source: (source - away) % members) for away in range(1, members)
    ]
    partner = moved(own, "blk", to_other_core)

    def state_shapes(number):
        return [
            f32(number * blocks * ROWS, BLOCK),
            jax.ShapeDtypeStruct((number * blocks, FEATURES, 2 * BLOCK), jnp.bfloat16),
            f32(number * blocks * ROWS, BLOCK),
            f32(number * blocks * 2 * ROWS, BLOCK),
        ]

    own_shapes, other_shapes = state_shapes(1), state_shapes(members - 1)
    window_shape = f32((2 * REACH + 1) * blocks * ROWS, BLOCK)
    list_shape = jax.ShapeDtypeStruct((3 * ROWS * length // BLOCK, BLOCK), jnp.int32)
    feature_rows = [pltpu.VMEM((GROUP * ROWS, BLOCK), jnp.float32)] * 2
    list_scratch = [pltpu.SMEM(list_shape.shape, jnp.int32), pltpu.SemaphoreType.DMA((4,))]
    scratch = [pltpu.VMEM((GROUP * ROWS, BLOCK), jnp.float32)] * 4 + [
        pltpu.VMEM((HALF, BLOCK, 2 * BLOCK), jnp.float32),
        pltpu.VMEM((HALF, BLOCK, 2 * BLOCK), jnp.float32),
    ]
    window_scratch = pltpu.VMEM(window_shape.shape, jnp.float32)

    lists, *own_state = call(
        lambda *refs: home_kernel(*refs, members=members),
        "home_pairs",
        (coded, own),
        [list_shape] + own_shapes[1:],
        feature_rows + list_scratch + scratch,
        flops=HOME_FLOPS,
    )
    paired, lists = lax.optimization_barrier((paired, lists))
    passed = moved(paired, "blk", along_chips(count))
    other_state = list(call(
        lambda *refs: near_kernel(*refs, members=members),
        "near_pairs",
        (lists, own, partner, *others),
        other_shapes,
        [window_scratch] + feature_rows + list_scratch + scratch,
        flops=NEAR_FLOPS,
    ))
    passed, other_state[3] = lax.optimization_barrier((passed, other_state[3]))
    core = shard % 2
    chip = shard // 2 % 2
    crossed = moved(jnp.where(core == chip, paired, passed), "blk", to_other_core)
    (partner_total,) = call(
        partner_kernel,
        "partner_pairs",
        (lists, partner, own, *own_state[:2]),
        [own_shapes[3]],
        list_scratch + scratch,
        flops=HOME_FLOPS,
    )
    crossed, partner_total = lax.optimization_barrier((crossed, partner_total))
    window, away_sums = call(
        far_kernel,
        "far_pairs",
        (lists, paired, passed, crossed, *other_state),
        [window_shape, f32(members - 1, 6 * blocks, BLOCK)],
        [pltpu.VMEM(other_shapes[3].shape, jnp.float32)] + list_scratch + scratch,
        flops=FAR_FLOPS,
    )
    returned = [
        moved(away_sums[away - 1], "across", lambda source: (source + away) % members)
        for away in range(1, members)
    ]
    (sums,) = call(
        last_kernel,
        "last_pairs",
        (lists, window, own, *own_state, partner_total),
        [f32(1, 6 * blocks, BLOCK)],
        [pltpu.VMEM(own_shapes[3].shape, jnp.float32)] + list_scratch + scratch,
        flops=FAR_FLOPS,
    )
    wide = f32(3, lanes)
    return tuple(
        call(section_kernel, "section", (own, sums[0], *returned), [wide] * 4, [])
    )


def solution(mesh):
    whole = P(None, ("blk", "across"))
    line = P(("blk", "across"))
    return jax.shard_map(
        shards,
        mesh=mesh,
        in_specs=(whole, whole, line, line, P(("blk", "across"), None), P(("blk", "across"), None), line),
        out_specs=(whole, whole, whole, whole),
        check_vma=False,
    )
```

```python
import jax
import jax.numpy as jnp
from jax import lax
from jax.experimental import pallas as pl
from jax.experimental.pallas import tpu as pltpu
from jax.sharding import PartitionSpec as P

BLOCK = 128
ROWS = 8
REACH = 2
GROUP = 8
HALF = 4
SLOTS = 1024
FEATURES = 48
CLASSES = 8

biot_factor = 0.07957747154594767
section_step = 0.05


def moved(value, axis, target_of):
    pairs = [(source, target_of(source)) for source in range(lax.axis_size(axis))]
    return lax.ppermute(value, axis, pairs)


def to_other_core(source):
    return source ^ 1


def shifted(steps, count):
    return lambda source: (source + steps) % count


HOME_FLOPS = 10**10
NEAR_FLOPS = 10**10
FAR_FLOPS = 10**10


def rounded(value):
    return value.astype(jnp.bfloat16).astype(jnp.float32)


def split_three(value):
    first = rounded(value)
    rest = value - first
    second = rounded(rest)
    return first, second, rest - second


def six_slots(tile, order):
    parts = split_three(tile)
    return jnp.concatenate([parts[part] for part in order], axis=0).astype(jnp.bfloat16)


def cross(left, right):
    return [
        left[1] * right[2] - left[2] * right[1],
        left[2] * right[0] - left[0] * right[2],
        left[0] * right[1] - left[1] * right[0],
    ]


def tile_rows(index, rows):
    return pl.ds(pl.multiple_of(index * rows, rows), rows)


def component(ref, base, number, stride):
    return ref[pl.ds(base + number, GROUP, stride=stride), :]


def store_component(ref, base, number, stride, value):
    ref[pl.ds(base + number, GROUP, stride=stride), :] = value


def target_features(targets, step, centres, near_rows, tilt_rows):
    base = pl.multiple_of(step * (GROUP * ROWS), GROUP * ROWS)
    pos = [component(targets, base, k, ROWS) for k in range(3)]
    strength = [component(targets, base, 3 + k, ROWS) for k in range(3)]
    for k in range(3):
        centre = jnp.broadcast_to(jnp.mean(pos[k], axis=1, keepdims=True), (GROUP, BLOCK))
        store_component(centres, base, k, ROWS, centre)
        pos[k] = pos[k] - centre
    for k in range(3, ROWS):
        store_component(centres, base, k, ROWS, jnp.zeros_like(pos[0]))
    norm = pos[0] * pos[0] + pos[1] * pos[1] + pos[2] * pos[2]
    own = pos[0] * strength[0] + pos[1] * strength[1] + pos[2] * strength[2]
    near = pos + [norm, jnp.ones_like(norm)]
    tilt = [0.5 * s for s in strength] + [own]
    for rows, values in ((near_rows, near), (tilt_rows, tilt)):
        for k, value in enumerate(values):
            store_component(rows, 0, k, ROWS, value)


def source_features(gathered, weight, left, charge):
    pos = [component(gathered, 0, k, ROWS) for k in range(3)]
    strength = [component(gathered, 0, 3 + k, ROWS) for k in range(3)]
    inv_core = 1.0 / component(gathered, 0, 6, ROWS)
    inv_square = inv_core * inv_core
    norm = pos[0] * pos[0] + pos[1] * pos[1] + pos[2] * pos[2]
    twice = -2.0 * inv_square
    shape = [p * twice for p in pos] + [inv_square, norm * inv_square + 1.0]
    for k, value in enumerate(shape):
        store_component(left, 0, k, ROWS, value)
    scale = inv_square * inv_core * weight
    for k, value in enumerate(strength + cross(pos, strength)):
        store_component(charge, 0, k, ROWS, value * scale)


NT = (((1,), (1,)), ((), ()))
TN = (((0,), (0,)), ((), ()))


def put_tiles(window, first, tiles):
    window[pl.ds(pl.multiple_of(first * ROWS, ROWS), tiles.shape[0]), :] = tiles[...]


def prepare_targets(state, near_rows, tilt_rows):
    targets, features, centres, total = state
    near_rows[...] = jnp.zeros_like(near_rows)
    tilt_rows[...] = jnp.zeros_like(tilt_rows)
    total[...] = jnp.zeros_like(total)

    def prepare(step, carry):
        target_features(targets, step, centres, near_rows, tilt_rows)
        for u in range(GROUP):
            rows = slice(u * ROWS, (u + 1) * ROWS)
            features[step * GROUP + u, :, :BLOCK] = six_slots(near_rows[rows, :], (0, 1, 2, 0, 1, 0))
            features[step * GROUP + u, :, BLOCK:] = six_slots(tilt_rows[rows, :], (0, 1, 2, 0, 1, 0))
        return carry

    lax.fori_loop(0, features.shape[0] // GROUP, prepare, 0)


def run_class(kind, lists, window, state, scratch):
    _, features, centres, total = state
    gathered, left, charge_next, charge, first_half, second_half = scratch
    listed = lists[2 * ROWS + kind, 0]

    def entry_at(step, u):
        entry = jnp.minimum(step * GROUP + u, listed - 1)
        return entry // BLOCK * (3 * ROWS) + kind, lax.rem(entry, BLOCK)

    def target_of(step, u):
        row, column = entry_at(step, u)
        return lists[row, column]

    def prepare_sources(step):
        for u in range(GROUP):
            row, column = entry_at(step, u)
            gathered[u * ROWS : (u + 1) * ROWS, :] = (
                window[tile_rows(lists[row + ROWS, column], ROWS), :]
                - centres[tile_rows(lists[row, column], ROWS), :]
            )
        order = lax.broadcasted_iota(jnp.int32, (GROUP, BLOCK), 0) + step * GROUP
        weight = jnp.where(order < listed, 1.0, 0.0).astype(jnp.float32)
        source_features(gathered, weight, left, charge_next)

    def products(step, u, held):
        shape = six_slots(left[u * ROWS : (u + 1) * ROWS, :], (0, 0, 0, 1, 1, 2))
        held[u % HALF] = lax.dot_general(
            shape, features[target_of(step, u)], TN, preferred_element_type=jnp.float32
        )

    def weights(u, held):
        near = held[u % HALF, :, :BLOCK]
        tilt = held[u % HALF, :, BLOCK:]
        q = lax.rsqrt(near)
        q2 = q * q
        q3 = q2 * q
        f = q3 * (q2 + (2.0 / 3.0))
        h = (q3 * q2) * (q2 + 0.4) * tilt
        fh = f.astype(jnp.bfloat16)
        fl = (f - fh.astype(jnp.float32)).astype(jnp.bfloat16)
        hh = h.astype(jnp.bfloat16)
        hl = (h - hh.astype(jnp.float32)).astype(jnp.bfloat16)
        return jnp.concatenate(
            [jnp.concatenate([fh, fl], axis=1), jnp.concatenate([hh, hl], axis=1)], axis=0
        )

    def add_up(step, u, stacked):
        pair = charge[u * ROWS : (u + 1) * ROWS, :]
        high = rounded(pair)
        pair = jnp.concatenate([high, pair - high], axis=0).astype(jnp.bfloat16)
        blank = jnp.zeros_like(pair)
        pair = jnp.concatenate(
            [jnp.concatenate([pair, blank], axis=1), jnp.concatenate([blank, pair], axis=1)], axis=0
        )
        sums = jnp.dot(pair, stacked, preferred_element_type=jnp.float32)
        fsum = sums[0:8, :BLOCK] + sums[8:16, :BLOCK] + sums[0:8, BLOCK:]
        hsum = sums[16:24, :BLOCK] + sums[24:32, :BLOCK] + sums[16:24, BLOCK:]
        total[tile_rows(target_of(step, u), 2 * ROWS), :] += jnp.concatenate([fsum, hsum], axis=0)

    def turn(step, carry):
        stacked = {}
        for u in range(HALF):
            stacked[u] = weights(u, first_half)
            products(step, HALF + u, second_half)
            add_up(step, u, stacked[u])
        prepare_sources(step + 1)
        for u in range(HALF, GROUP):
            stacked[u] = weights(u, second_half)
            products(step + 1, u - HALF, first_half)
            add_up(step, u, stacked[u])
        charge[...] = charge_next[...]
        return carry

    @pl.when(listed > 0)
    def _():
        left[...] = jnp.zeros_like(left)
        charge_next[...] = jnp.zeros_like(charge_next)
        prepare_sources(0)
        for u in range(HALF):
            products(0, u, first_half)
        charge[...] = charge_next[...]
        lax.fori_loop(0, (listed + GROUP - 1) // GROUP, turn, 0)


def finish(targets, centres, totals, out_ref):
    blocks = out_ref.shape[1] // 6

    def one(step, carry):
        base = pl.multiple_of(step * GROUP * ROWS, GROUP * ROWS)
        wide = pl.multiple_of(step * GROUP * 2 * ROWS, GROUP * 2 * ROWS)
        pos = [
            component(targets, base, k, ROWS) - component(centres, base, k, ROWS) for k in range(3)
        ]
        strength = [component(targets, base, 3 + k, ROWS) for k in range(3)]
        fa, fb, ha, hb = [
            [
                sum(component(total, wide, start + k, 2 * ROWS) for total in totals)
                for k in range(3)
            ]
            for start in (0, 3, 8, 11)
        ]
        swirl = cross(pos, fa)
        lean = cross(strength, fa)
        bend = cross(pos, ha)
        member = step * GROUP // blocks
        inside = lax.rem(step * GROUP, blocks)
        for k in range(3):
            velocity = (-1.5 * biot_factor) * (swirl[k] - fb[k])
            stretch = (-1.5 * biot_factor) * lean[k] + (7.5 * biot_factor) * (bend[k] - hb[k])
            out_ref[member, pl.ds(pl.multiple_of(k * blocks + inside, GROUP), GROUP), :] = velocity
            out_ref[member, pl.ds(pl.multiple_of((3 + k) * blocks + inside, GROUP), GROUP), :] = stretch
        return carry

    lax.fori_loop(0, targets.shape[0] // ROWS // GROUP, one, 0)


def sort_list(coded, sorted_list, blocks, members):
    length = coded.shape[1]
    t = coded[...] // SLOTS
    s = coded[...] % SLOTS
    t = t - lax.axis_index("across") * blocks
    t = jnp.where(t < 0, t + members * blocks, t)
    run = s // blocks
    mine = t < blocks
    t = jnp.where(mine, t, t - blocks)
    near = (run == REACH) | (run == side_of_partner())
    kind = jnp.where(
        mine,
        jnp.where(near, 0, jnp.where(run == 2 * REACH, 2, 4)),
        jnp.where(near, 1, 3),
    )
    kind = jnp.where(coded[...] < 0, CLASSES - 1, kind)
    member = jnp.where(lax.broadcasted_iota(jnp.int32, (CLASSES, length), 0) == kind, 1.0, 0.0)
    row = lax.broadcasted_iota(jnp.int32, (length, length), 0)
    column = lax.broadcasted_iota(jnp.int32, (length, length), 1)
    before = jnp.where(row < column, 1.0, 0.0).astype(jnp.bfloat16)
    earlier = jnp.dot(member.astype(jnp.bfloat16), before, preferred_element_type=jnp.float32)
    rank = jnp.sum(member * earlier, axis=0, keepdims=True).astype(jnp.int32)
    place = jnp.where(row == rank, 1.0, 0.0).astype(jnp.bfloat16)
    values = [t // BLOCK, t % BLOCK, s // BLOCK, s % BLOCK]
    values = [member * value.astype(jnp.float32) for value in values]
    values = jnp.concatenate(values, axis=0).astype(jnp.bfloat16)
    found = lax.dot_general(values, place, NT, preferred_element_type=jnp.float32)
    number = jnp.broadcast_to(jnp.sum(member, axis=1, keepdims=True), (CLASSES, BLOCK))
    for j in range(length // BLOCK):
        part = found[:, j * BLOCK : (j + 1) * BLOCK]
        high, low = part[0:8], part[8:16]
        slot_high, slot_low = part[16:24], part[24:32]
        rows = [high * BLOCK + low, slot_high * BLOCK + slot_low, number]
        sorted_list[j * 24 : (j + 1) * 24, :] = jnp.concatenate(rows, axis=0).astype(jnp.int32)


class shifted_window:
    def __init__(self, ref, start):
        self.ref, self.start = ref, start * ROWS

    def __getitem__(self, index):
        rows, lanes = index
        return self.ref[pl.ds(pl.multiple_of(rows.start - self.start, ROWS), rows.size), lanes]


def side_of_partner():
    return jnp.where(lax.axis_index("blk") % 2 == 0, REACH + 1, REACH - 1)


def home_kernel(coded, own, partner, *refs, members):
    sorted_list, features, centres, total = refs[:4]
    window, near_rows, tilt_rows, lists, sems = refs[4:9]
    scratch = refs[9:]
    state = (own, features, centres, total)
    blocks = own.shape[0] // ROWS
    sort_list(coded, sorted_list, blocks, members)
    to_scalars = pltpu.make_async_copy(sorted_list, lists, sems.at[0])
    to_scalars.start()
    put_tiles(window, REACH * blocks, own)
    put_tiles(window, side_of_partner() * blocks, partner)
    prepare_targets(state, near_rows, tilt_rows)
    to_scalars.wait()
    run_class(0, lists, window, state, scratch)


def near_kernel(sorted_list, own, partner, *refs, members):
    others, refs = refs[: members - 1], refs[members - 1 :]
    targets, features, centres, total = state = refs[:4]
    window, near_rows, tilt_rows, lists, sems = refs[4:9]
    scratch = refs[9:]
    to_scalars = pltpu.make_async_copy(sorted_list, lists, sems.at[0])
    to_scalars.start()
    blocks = own.shape[0] // ROWS
    put_tiles(window, REACH * blocks, own)
    put_tiles(window, side_of_partner() * blocks, partner)
    for r, other in enumerate(others):
        put_tiles(targets, r * blocks, other)
    prepare_targets(state, near_rows, tilt_rows)
    to_scalars.wait()
    run_class(1, lists, window, state, scratch)


def middle_kernel(sorted_list, above, own, features, centres, total, lists, sems, *scratch):
    to_scalars = pltpu.make_async_copy(sorted_list, lists, sems.at[0])
    to_scalars.start()
    total[...] = jnp.zeros_like(total)
    to_scalars.wait()
    window = shifted_window(above, 2 * REACH * (above.shape[0] // ROWS))
    run_class(2, lists, window, (own, features, centres, total), scratch)


def far_kernel(sorted_list, below, above, crossed, *refs):
    targets, features, centres, near_total = refs[:4]
    window, out_ref, total, lists, sems = refs[4:9]
    scratch = refs[9:]
    state = (targets, features, centres, total)
    to_scalars = pltpu.make_async_copy(sorted_list, lists, sems.at[0])
    to_scalars.start()
    blocks = below.shape[0] // ROWS
    put_tiles(window, 0, below)
    put_tiles(window, 2 * REACH * blocks, above)
    put_tiles(window, (2 * REACH - side_of_partner()) * blocks, crossed)
    total[...] = jnp.zeros_like(total)
    to_scalars.wait()
    run_class(3, lists, window, state, scratch)
    finish(targets, centres, (near_total, total), out_ref)


def last_kernel(sorted_list, window, own, features, centres, *refs):
    home_total, middle_total, out_ref, total, lists, sems = refs[:6]
    to_scalars = pltpu.make_async_copy(sorted_list, lists, sems.at[0])
    to_scalars.start()
    total[...] = jnp.zeros_like(total)
    to_scalars.wait()
    run_class(4, lists, window, (own, features, centres, total), refs[6:])
    finish(own, centres, (home_total, middle_total, total), out_ref)


def section_kernel(own, sums, *refs):
    returned, (velocity, stretching, section_positions, section_strengths) = refs[:-4], refs[-4:]
    blocks = own.shape[0] // ROWS
    for b in range(blocks):
        lanes = slice(b * BLOCK, (b + 1) * BLOCK)
        for start, result, stepped in ((0, velocity, section_positions), (3, stretching, section_strengths)):
            chosen = pl.ds(start * blocks + b, 3, stride=blocks)
            value = sums[chosen, :]
            for other in returned:
                value = value + other[chosen, :]
            result[:, lanes] = value
            first = b * ROWS + start
            stepped[:, lanes] = own[first : first + 3, :] + section_step * value


def call(kernel, name, inputs, outputs, scratch, flops=0):
    vmem = pl.BlockSpec(memory_space=pltpu.VMEM)
    held = sum(value.size * value.dtype.itemsize for value in (*inputs, *outputs))
    return pl.pallas_call(
        kernel,
        out_shape=outputs,
        in_specs=[vmem for value in inputs],
        out_specs=[vmem for value in outputs],
        scratch_shapes=scratch,
        compiler_params=pltpu.CompilerParams(vmem_limit_bytes=10 * 1024 * 1024 + 2 * held),
        cost_estimate=pl.CostEstimate(flops=flops, bytes_accessed=0, transcendentals=0),
        name=name,
    )(*inputs)


def shards(positions, strengths, radius, block_count, pair_target, pair_slot, pair_count):
    blocks = block_count.shape[0]
    lanes = blocks * BLOCK
    length = pair_target.shape[1]
    members = lax.axis_size("across")
    shard = lax.axis_index("blk")
    count = lax.axis_size("blk")

    def f32(*shape):
        return jax.ShapeDtypeStruct(shape, jnp.float32)

    row = lax.broadcasted_iota(jnp.int32, (blocks, ROWS, BLOCK), 1)
    lane = lax.broadcasted_iota(jnp.int32, (blocks, ROWS, BLOCK), 2)
    cores = radius.reshape(blocks, 1, BLOCK)
    parts = [value.reshape(3, blocks, BLOCK).transpose(1, 0, 2) for value in (positions, strengths)]
    dead = (row >= 3) & (row < 6) & (lane >= block_count[:, None, None])
    own = jnp.where(dead, 0.0, jnp.concatenate(parts + [cores, cores], axis=1))
    own = own.reshape(blocks * ROWS, BLOCK)
    entry = lax.broadcasted_iota(jnp.int32, (1, length), 1)
    coded = jnp.where(entry < pair_count[0], pair_target * SLOTS + pair_slot, -1)
    others = [
        moved(own, "across", lambda source: (source - away) % members) for away in range(1, members)
    ]
    partner = moved(own, "blk", to_other_core)
    below = moved(own, "blk", shifted(REACH, count))
    above = moved(own, "blk", shifted(-REACH, count))

    def state_shapes(number):
        return [
            f32(number * blocks * ROWS, BLOCK),
            jax.ShapeDtypeStruct((number * blocks, FEATURES, 2 * BLOCK), jnp.bfloat16),
            f32(number * blocks * ROWS, BLOCK),
            f32(number * blocks * 2 * ROWS, BLOCK),
        ]

    own_shapes, other_shapes = state_shapes(1), state_shapes(members - 1)
    window_shape = f32((2 * REACH + 1) * blocks * ROWS, BLOCK)
    list_shape = jax.ShapeDtypeStruct((3 * ROWS * length // BLOCK, BLOCK), jnp.int32)
    feature_rows = [pltpu.VMEM((GROUP * ROWS, BLOCK), jnp.float32)] * 2
    list_scratch = [pltpu.SMEM(list_shape.shape, jnp.int32), pltpu.SemaphoreType.DMA((4,))]
    scratch = [pltpu.VMEM((GROUP * ROWS, BLOCK), jnp.float32)] * 4 + [
        pltpu.VMEM((HALF, BLOCK, 2 * BLOCK), jnp.float32),
        pltpu.VMEM((HALF, BLOCK, 2 * BLOCK), jnp.float32),
    ]
    window_scratch = pltpu.VMEM(window_shape.shape, jnp.float32)

    lists, *own_state = call(
        lambda *refs: home_kernel(*refs, members=members),
        "home_pairs",
        (coded, own, partner),
        [list_shape] + own_shapes[1:],
        [window_scratch] + feature_rows + list_scratch + scratch,
        flops=HOME_FLOPS,
    )
    other_state = list(call(
        lambda *refs: near_kernel(*refs, members=members),
        "near_pairs",
        (lists, own, partner, *others),
        other_shapes,
        [window_scratch] + feature_rows + list_scratch + scratch,
        flops=NEAR_FLOPS,
    ))
    below, above, other_state[3] = lax.optimization_barrier((below, above, other_state[3]))
    crossed = moved(jnp.where(shard % 2 == 0, above, below), "blk", to_other_core)
    (middle_total,) = call(
        middle_kernel,
        "middle_pairs",
        (lists, above, own, *own_state[:2]),
        [own_shapes[3]],
        list_scratch + scratch,
        flops=HOME_FLOPS,
    )
    crossed, middle_total = lax.optimization_barrier((crossed, middle_total))
    window, away_sums = call(
        far_kernel,
        "far_pairs",
        (lists, below, above, crossed, *other_state),
        [window_shape, f32(members - 1, 6 * blocks, BLOCK)],
        [pltpu.VMEM(other_shapes[3].shape, jnp.float32)] + list_scratch + scratch,
        flops=FAR_FLOPS,
    )
    returned = [
        moved(away_sums[away - 1], "across", lambda source: (source + away) % members)
        for away in range(1, members)
    ]
    (sums,) = call(
        last_kernel,
        "last_pairs",
        (lists, window, own, *own_state, middle_total),
        [f32(1, 6 * blocks, BLOCK)],
        [pltpu.VMEM(own_shapes[3].shape, jnp.float32)] + list_scratch + scratch,
        flops=FAR_FLOPS,
    )
    wide = f32(3, lanes)
    return tuple(
        call(section_kernel, "section", (own, sums[0], *returned), [wide] * 4, [])
    )


def solution(mesh):
    whole = P(None, ("blk", "across"))
    line = P(("blk", "across"))
    return jax.shard_map(
        shards,
        mesh=mesh,
        in_specs=(whole, whole, line, line, P(("blk", "across"), None), P(("blk", "across"), None), line),
        out_specs=(whole, whole, whole, whole),
        check_vma=False,
    )
```

```python
import jax
import jax.numpy as jnp
from jax import lax
from jax.experimental import pallas as pl
from jax.experimental.pallas import tpu as pltpu
from jax.sharding import PartitionSpec as P

BLOCK = 128
ROWS = 8
REACH = 2
GROUP = 8
HALF = 4
SLOTS = 1024
FEATURES = 48
CLASSES = 8

F_SCALE = (2.0 / 3.0) ** 1.5
H_SCALE = 5.0 * (2.0 / 3.0) ** 2.5
biot_factor = 0.07957747154594767
section_step = 0.05


def moved(value, axis, target_of):
    pairs = [(source, target_of(source)) for source in range(lax.axis_size(axis))]
    return lax.ppermute(value, axis, pairs)


def to_other_core(source):
    return source ^ 1


def shifted(steps, count):
    return lambda source: (source + steps) % count


HOME_FLOPS = 10**10
NEAR_FLOPS = 10**10
FAR_FLOPS = 10**10


def rounded(value):
    return value.astype(jnp.bfloat16).astype(jnp.float32)


def split_three(value):
    first = rounded(value)
    rest = value - first
    second = rounded(rest)
    return first, second, rest - second


def six_slots(tile, order):
    parts = split_three(tile)
    return jnp.concatenate([parts[part] for part in order], axis=0).astype(jnp.bfloat16)


def cross(left, right):
    return [
        left[1] * right[2] - left[2] * right[1],
        left[2] * right[0] - left[0] * right[2],
        left[0] * right[1] - left[1] * right[0],
    ]


def tile_rows(index, rows):
    return pl.ds(pl.multiple_of(index * rows, rows), rows)


def component(ref, base, number, stride):
    return ref[pl.ds(base + number, GROUP, stride=stride), :]


def store_component(ref, base, number, stride, value):
    ref[pl.ds(base + number, GROUP, stride=stride), :] = value


def target_features(targets, step, centres, near_rows, tilt_rows):
    base = pl.multiple_of(step * (GROUP * ROWS), GROUP * ROWS)
    pos = [component(targets, base, k, ROWS) for k in range(3)]
    strength = [component(targets, base, 3 + k, ROWS) for k in range(3)]
    for k in range(3):
        centre = jnp.broadcast_to(jnp.mean(pos[k], axis=1, keepdims=True), (GROUP, BLOCK))
        store_component(centres, base, k, ROWS, centre)
        pos[k] = pos[k] - centre
    for k in range(3, ROWS):
        store_component(centres, base, k, ROWS, jnp.zeros_like(pos[0]))
    norm = pos[0] * pos[0] + pos[1] * pos[1] + pos[2] * pos[2]
    own = pos[0] * strength[0] + pos[1] * strength[1] + pos[2] * strength[2]
    near = [(2.0 / 3.0) * value for value in pos + [norm, jnp.ones_like(norm)]]
    tilt = [0.5 * s for s in strength] + [own]
    for rows, values in ((near_rows, near), (tilt_rows, tilt)):
        for k, value in enumerate(values):
            store_component(rows, 0, k, ROWS, value)


def source_features(gathered, weight, left, charge):
    pos = [component(gathered, 0, k, ROWS) for k in range(3)]
    strength = [component(gathered, 0, 3 + k, ROWS) for k in range(3)]
    inv_core = 1.0 / component(gathered, 0, 6, ROWS)
    inv_square = inv_core * inv_core
    norm = pos[0] * pos[0] + pos[1] * pos[1] + pos[2] * pos[2]
    twice = -2.0 * inv_square
    shape = [p * twice for p in pos] + [inv_square, norm * inv_square + 1.0]
    for k, value in enumerate(shape):
        store_component(left, 0, k, ROWS, value)
    scale = inv_square * inv_core * weight
    for k, value in enumerate(strength + cross(pos, strength)):
        store_component(charge, 0, k, ROWS, value * scale)


NT = (((1,), (1,)), ((), ()))
TN = (((0,), (0,)), ((), ()))


def put_tiles(window, first, tiles):
    window[pl.ds(pl.multiple_of(first * ROWS, ROWS), tiles.shape[0]), :] = tiles[...]


def prepare_targets(state, near_rows, tilt_rows):
    targets, features, centres, total = state
    near_rows[...] = jnp.zeros_like(near_rows)
    tilt_rows[...] = jnp.zeros_like(tilt_rows)
    total[...] = jnp.zeros_like(total)

    def prepare(step, carry):
        target_features(targets, step, centres, near_rows, tilt_rows)
        for u in range(GROUP):
            rows = slice(u * ROWS, (u + 1) * ROWS)
            features[step * GROUP + u, :, :BLOCK] = six_slots(near_rows[rows, :], (0, 1, 2, 0, 1, 0))
            features[step * GROUP + u, :, BLOCK:] = six_slots(tilt_rows[rows, :], (0, 1, 2, 0, 1, 0))
        return carry

    lax.fori_loop(0, features.shape[0] // GROUP, prepare, 0)


def run_class(lists, window, state, scratch):
    _, features, centres, total = state
    gathered, left, charge_next, charge, first_half, second_half = scratch
    slot_row = (lists.shape[0] - 1) // 2
    listed = lists[2 * slot_row, 0]

    def entry_at(step, u):
        entry = jnp.minimum(step * GROUP + u, listed - 1)
        return entry // BLOCK, lax.rem(entry, BLOCK)

    def target_of(step, u):
        row, column = entry_at(step, u)
        return lists[row, column]

    def prepare_sources(step):
        for u in range(GROUP):
            row, column = entry_at(step, u)
            gathered[u * ROWS : (u + 1) * ROWS, :] = (
                window[tile_rows(lists[row + slot_row, column], ROWS), :]
                - centres[tile_rows(lists[row, column], ROWS), :]
            )
        order = lax.broadcasted_iota(jnp.int32, (GROUP, BLOCK), 0) + step * GROUP
        weight = jnp.where(order < listed, 1.0, 0.0).astype(jnp.float32)
        source_features(gathered, weight, left, charge_next)

    def products(step, u, held):
        shape = six_slots(left[u * ROWS : (u + 1) * ROWS, :], (0, 0, 0, 1, 1, 2))
        held[u % HALF] = lax.dot_general(
            shape, features[target_of(step, u)], TN, preferred_element_type=jnp.float32
        )

    def weights(u, held):
        near = held[u % HALF, :, :BLOCK]
        tilt = held[u % HALF, :, BLOCK:]
        q = lax.rsqrt(near)
        q2 = q * q
        q3 = q2 * q
        q5 = q3 * q2
        f = q3 + q5
        h = (q5 * tilt) * (q2 + 0.6)
        fh = f.astype(jnp.bfloat16)
        fl = (f - fh.astype(jnp.float32)).astype(jnp.bfloat16)
        hh = h.astype(jnp.bfloat16)
        hl = (h - hh.astype(jnp.float32)).astype(jnp.bfloat16)
        return jnp.concatenate(
            [jnp.concatenate([fh, fl], axis=1), jnp.concatenate([hh, hl], axis=1)], axis=0
        )

    def add_up(u, stacked):
        pair = charge[u * ROWS : (u + 1) * ROWS, :]
        high = rounded(pair)
        pair = jnp.concatenate([high, pair - high], axis=0).astype(jnp.bfloat16)
        blank = jnp.zeros_like(pair)
        pair = jnp.concatenate(
            [jnp.concatenate([pair, blank], axis=1), jnp.concatenate([blank, pair], axis=1)], axis=0
        )
        sums = jnp.dot(pair, stacked, preferred_element_type=jnp.float32)
        fsum = sums[0:8, :BLOCK] + sums[8:16, :BLOCK] + sums[0:8, BLOCK:]
        hsum = sums[16:24, :BLOCK] + sums[24:32, :BLOCK] + sums[16:24, BLOCK:]
        return jnp.concatenate([fsum, hsum], axis=0)

    def turn(step, carry):
        sums = []
        for u in range(HALF):
            stacked = weights(u, first_half)
            products(step, HALF + u, second_half)
            sums.append(add_up(u, stacked))
        prepare_sources(step + 1)
        for u in range(HALF, GROUP):
            stacked = weights(u, second_half)
            products(step + 1, u - HALF, first_half)
            sums.append(add_up(u, stacked))
        charge[...] = charge_next[...]
        for u in range(GROUP):
            total[tile_rows(target_of(step, u), 2 * ROWS), :] += sums[u]
        return carry

    @pl.when(listed > 0)
    def _():
        left[...] = jnp.zeros_like(left)
        charge_next[...] = jnp.zeros_like(charge_next)
        prepare_sources(0)
        for u in range(HALF):
            products(0, u, first_half)
        charge[...] = charge_next[...]
        lax.fori_loop(0, (listed + GROUP - 1) // GROUP, turn, 0)


def finish(targets, centres, totals, out_ref):
    blocks = out_ref.shape[1] // 6

    def one(step, carry):
        base = pl.multiple_of(step * GROUP * ROWS, GROUP * ROWS)
        wide = pl.multiple_of(step * GROUP * 2 * ROWS, GROUP * 2 * ROWS)
        pos = [
            component(targets, base, k, ROWS) - component(centres, base, k, ROWS) for k in range(3)
        ]
        strength = [component(targets, base, 3 + k, ROWS) for k in range(3)]
        fa, fb, ha, hb = [
            [
                sum(component(total, wide, start + k, 2 * ROWS) for total in totals)
                for k in range(3)
            ]
            for start in (0, 3, 8, 11)
        ]
        swirl = cross(pos, fa)
        lean = cross(strength, fa)
        bend = cross(pos, ha)
        member = step * GROUP // blocks
        inside = lax.rem(step * GROUP, blocks)
        for k in range(3):
            velocity = (-F_SCALE * biot_factor) * (swirl[k] - fb[k])
            stretch = (-F_SCALE * biot_factor) * lean[k] + (H_SCALE * biot_factor) * (bend[k] - hb[k])
            out_ref[member, pl.ds(pl.multiple_of(k * blocks + inside, GROUP), GROUP), :] = velocity
            out_ref[member, pl.ds(pl.multiple_of((3 + k) * blocks + inside, GROUP), GROUP), :] = stretch
        return carry

    lax.fori_loop(0, targets.shape[0] // ROWS // GROUP, one, 0, unroll=2)


def sort_list(coded, sorted_list, blocks, members):
    length = coded.shape[1]
    t = coded[...] // SLOTS
    s = coded[...] % SLOTS
    t = t - lax.axis_index("across") * blocks
    t = jnp.where(t < 0, t + members * blocks, t)
    run = s // blocks
    mine = t < blocks
    t = jnp.where(mine, t, t - blocks)
    near = (run == REACH) | (run == side_of_partner())
    kind = jnp.where(
        mine,
        jnp.where(near, 0, jnp.where(run == 2 * REACH, 2, 4)),
        jnp.where(near, 1, 3),
    )
    kind = jnp.where(coded[...] < 0, CLASSES - 1, kind)
    member = jnp.where(lax.broadcasted_iota(jnp.int32, (CLASSES, length), 0) == kind, 1.0, 0.0)
    row = lax.broadcasted_iota(jnp.int32, (length, length), 0)
    column = lax.broadcasted_iota(jnp.int32, (length, length), 1)
    before = jnp.where(row < column, 1.0, 0.0).astype(jnp.bfloat16)
    earlier = jnp.dot(member.astype(jnp.bfloat16), before, preferred_element_type=jnp.float32)
    rank = jnp.sum(member * earlier, axis=0, keepdims=True).astype(jnp.int32)
    place = jnp.where(row == rank, 1.0, 0.0).astype(jnp.bfloat16)
    values = [t // BLOCK, t % BLOCK, s // BLOCK, s % BLOCK]
    values = [member * value.astype(jnp.float32) for value in values]
    values = jnp.concatenate(values, axis=0).astype(jnp.bfloat16)
    found = lax.dot_general(values, place, NT, preferred_element_type=jnp.float32)
    number = jnp.broadcast_to(jnp.sum(member, axis=1, keepdims=True), (CLASSES, BLOCK))
    targets = found[0:8] * BLOCK + found[8:16]
    slots = found[16:24] * BLOCK + found[24:32]
    columns = [slice(j * BLOCK, (j + 1) * BLOCK) for j in range(length // BLOCK)]
    rows = sorted_list.shape[1]
    for kind in range(CLASSES - 1):
        one = slice(kind, kind + 1)
        parts = [targets[one, c] for c in columns] + [slots[one, c] for c in columns] + [number[one]]
        padding = rows - len(parts)
        if padding:
            parts.append(jnp.zeros((padding, BLOCK), jnp.float32))
        sorted_list[kind] = jnp.concatenate(parts, axis=0).astype(jnp.int32)


def list_rows(length):
    return 2 * (length // BLOCK) + 1


def read_list(kind, sorted_list, lists, sems):
    copy = pltpu.make_async_copy(sorted_list.at[kind, pl.ds(0, lists.shape[0])], lists, sems.at[0])
    copy.start()
    return copy


class shifted_window:
    def __init__(self, ref, start):
        self.ref, self.start = ref, start * ROWS

    def __getitem__(self, index):
        rows, lanes = index
        return self.ref[pl.ds(pl.multiple_of(rows.start - self.start, ROWS), rows.size), lanes]


def side_of_partner():
    return jnp.where(lax.axis_index("blk") % 2 == 0, REACH + 1, REACH - 1)


def home_kernel(coded, own, partner, *refs, members):
    sorted_list, features, centres, total = refs[:4]
    window, near_rows, tilt_rows, lists, sems = refs[4:9]
    scratch = refs[9:]
    state = (own, features, centres, total)
    blocks = own.shape[0] // ROWS
    sort_list(coded, sorted_list, blocks, members)
    to_scalars = read_list(0, sorted_list, lists, sems)
    put_tiles(window, REACH * blocks, own)
    put_tiles(window, side_of_partner() * blocks, partner)
    prepare_targets(state, near_rows, tilt_rows)
    to_scalars.wait()
    run_class(lists, window, state, scratch)


def near_kernel(sorted_list, own, partner, *refs, members):
    others, refs = refs[: members - 1], refs[members - 1 :]
    targets, features, centres, total = state = refs[:4]
    window, near_rows, tilt_rows, lists, sems = refs[4:9]
    scratch = refs[9:]
    to_scalars = read_list(1, sorted_list, lists, sems)
    blocks = own.shape[0] // ROWS
    put_tiles(window, REACH * blocks, own)
    put_tiles(window, side_of_partner() * blocks, partner)
    for r, other in enumerate(others):
        put_tiles(targets, r * blocks, other)
    prepare_targets(state, near_rows, tilt_rows)
    to_scalars.wait()
    run_class(lists, window, state, scratch)


def middle_kernel(sorted_list, above, own, features, centres, total, lists, sems, *scratch):
    to_scalars = read_list(2, sorted_list, lists, sems)
    total[...] = jnp.zeros_like(total)
    to_scalars.wait()
    window = shifted_window(above, 2 * REACH * (above.shape[0] // ROWS))
    run_class(lists, window, (own, features, centres, total), scratch)


def far_kernel(sorted_list, below, above, crossed, *refs):
    targets, features, centres, near_total = refs[:4]
    window, out_ref, total, lists, sems = refs[4:9]
    scratch = refs[9:]
    state = (targets, features, centres, total)
    to_scalars = read_list(3, sorted_list, lists, sems)
    blocks = below.shape[0] // ROWS
    put_tiles(window, 0, below)
    put_tiles(window, 2 * REACH * blocks, above)
    put_tiles(window, (2 * REACH - side_of_partner()) * blocks, crossed)
    total[...] = jnp.zeros_like(total)
    to_scalars.wait()
    run_class(lists, window, state, scratch)
    finish(targets, centres, (near_total, total), out_ref)


def last_kernel(sorted_list, window, own, features, centres, *refs):
    home_total, middle_total, out_ref, total, lists, sems = refs[:6]
    to_scalars = read_list(4, sorted_list, lists, sems)
    total[...] = jnp.zeros_like(total)
    to_scalars.wait()
    run_class(lists, window, (own, features, centres, total), refs[6:])
    finish(own, centres, (home_total, middle_total, total), out_ref)


def section_kernel(own, sums, *refs):
    returned, (velocity, stretching, section_positions, section_strengths) = refs[:-4], refs[-4:]
    blocks = own.shape[0] // ROWS
    for b in range(blocks):
        lanes = slice(b * BLOCK, (b + 1) * BLOCK)
        for start, result, stepped in ((0, velocity, section_positions), (3, stretching, section_strengths)):
            chosen = pl.ds(start * blocks + b, 3, stride=blocks)
            value = sums[chosen, :]
            for other in returned:
                value = value + other[chosen, :]
            result[:, lanes] = value
            first = b * ROWS + start
            stepped[:, lanes] = own[first : first + 3, :] + section_step * value


def call(kernel, name, inputs, outputs, scratch, flops=0):
    vmem = pl.BlockSpec(memory_space=pltpu.VMEM)
    held = sum(value.size * value.dtype.itemsize for value in (*inputs, *outputs))
    return pl.pallas_call(
        kernel,
        out_shape=outputs,
        in_specs=[vmem for value in inputs],
        out_specs=[vmem for value in outputs],
        scratch_shapes=scratch,
        compiler_params=pltpu.CompilerParams(vmem_limit_bytes=10 * 1024 * 1024 + 2 * held),
        cost_estimate=pl.CostEstimate(flops=flops, bytes_accessed=0, transcendentals=0),
        name=name,
    )(*inputs)


def shards(positions, strengths, radius, block_count, pair_target, pair_slot, pair_count):
    blocks = block_count.shape[0]
    lanes = blocks * BLOCK
    length = pair_target.shape[1]
    members = lax.axis_size("across")
    shard = lax.axis_index("blk")
    count = lax.axis_size("blk")

    def f32(*shape):
        return jax.ShapeDtypeStruct(shape, jnp.float32)

    row = lax.broadcasted_iota(jnp.int32, (blocks, ROWS, BLOCK), 1)
    lane = lax.broadcasted_iota(jnp.int32, (blocks, ROWS, BLOCK), 2)
    cores = radius.reshape(blocks, 1, BLOCK)
    parts = [value.reshape(3, blocks, BLOCK).transpose(1, 0, 2) for value in (positions, strengths)]
    dead = (row >= 3) & (row < 6) & (lane >= block_count[:, None, None])
    own = jnp.where(dead, 0.0, jnp.concatenate(parts + [cores, cores], axis=1))
    own = own.reshape(blocks * ROWS, BLOCK)
    entry = lax.broadcasted_iota(jnp.int32, (1, length), 1)
    coded = jnp.where(entry < pair_count[0], pair_target * SLOTS + pair_slot, -1)
    others = [
        moved(own, "across", lambda source: (source - away) % members) for away in range(1, members)
    ]
    partner = moved(own, "blk", to_other_core)
    below = moved(own, "blk", shifted(REACH, count))
    above = moved(own, "blk", shifted(-REACH, count))

    def state_shapes(number):
        return [
            f32(number * blocks * ROWS, BLOCK),
            jax.ShapeDtypeStruct((number * blocks, FEATURES, 2 * BLOCK), jnp.bfloat16),
            f32(number * blocks * ROWS, BLOCK),
            f32(number * blocks * 2 * ROWS, BLOCK),
        ]

    own_shapes, other_shapes = state_shapes(1), state_shapes(members - 1)
    window_shape = f32((2 * REACH + 1) * blocks * ROWS, BLOCK)
    rows = list_rows(length)
    list_shape = jax.ShapeDtypeStruct((CLASSES - 1, -(-rows // ROWS) * ROWS, BLOCK), jnp.int32)
    feature_rows = [pltpu.VMEM((GROUP * ROWS, BLOCK), jnp.float32)] * 2
    list_scratch = [pltpu.SMEM((rows, BLOCK), jnp.int32), pltpu.SemaphoreType.DMA((1,))]
    scratch = [pltpu.VMEM((GROUP * ROWS, BLOCK), jnp.float32)] * 4 + [
        pltpu.VMEM((HALF, BLOCK, 2 * BLOCK), jnp.float32),
        pltpu.VMEM((HALF, BLOCK, 2 * BLOCK), jnp.float32),
    ]
    window_scratch = pltpu.VMEM(window_shape.shape, jnp.float32)

    lists, *own_state = call(
        lambda *refs: home_kernel(*refs, members=members),
        "home_pairs",
        (coded, own, partner),
        [list_shape] + own_shapes[1:],
        [window_scratch] + feature_rows + list_scratch + scratch,
        flops=HOME_FLOPS,
    )
    other_state = list(call(
        lambda *refs: near_kernel(*refs, members=members),
        "near_pairs",
        (lists, own, partner, *others),
        other_shapes,
        [window_scratch] + feature_rows + list_scratch + scratch,
        flops=NEAR_FLOPS,
    ))
    below, above, other_state[3] = lax.optimization_barrier((below, above, other_state[3]))
    crossed = moved(jnp.where(shard % 2 == 0, above, below), "blk", to_other_core)
    (middle_total,) = call(
        middle_kernel,
        "middle_pairs",
        (lists, above, own, *own_state[:2]),
        [own_shapes[3]],
        list_scratch + scratch,
        flops=HOME_FLOPS,
    )
    crossed, middle_total = lax.optimization_barrier((crossed, middle_total))
    window, away_sums = call(
        far_kernel,
        "far_pairs",
        (lists, below, above, crossed, *other_state),
        [window_shape, f32(members - 1, 6 * blocks, BLOCK)],
        [pltpu.VMEM(other_shapes[3].shape, jnp.float32)] + list_scratch + scratch,
        flops=FAR_FLOPS,
    )
    returned = [
        moved(away_sums[away - 1], "across", lambda source: (source + away) % members)
        for away in range(1, members)
    ]
    (sums,) = call(
        last_kernel,
        "last_pairs",
        (lists, window, own, *own_state, middle_total),
        [f32(1, 6 * blocks, BLOCK)],
        [pltpu.VMEM(own_shapes[3].shape, jnp.float32)] + list_scratch + scratch,
        flops=FAR_FLOPS,
    )
    wide = f32(3, lanes)
    return tuple(
        call(section_kernel, "section", (own, sums[0], *returned), [wide] * 4, [])
    )


def solution(mesh):
    whole = P(None, ("blk", "across"))
    line = P(("blk", "across"))
    return jax.shard_map(
        shards,
        mesh=mesh,
        in_specs=(whole, whole, line, line, P(("blk", "across"), None), P(("blk", "across"), None), line),
        out_specs=(whole, whole, whole, whole),
        check_vma=False,
    )
```

```python
import jax
import jax.numpy as jnp
from jax import lax
from jax.experimental import pallas as pl
from jax.experimental.pallas import tpu as pltpu
from jax.sharding import PartitionSpec as P

BLOCK = 128
ROWS = 8
REACH = 2
GROUP = 8
HALF = 4
SLOTS = 1024
FEATURES = 48
CLASSES = 8

F_SCALE = (2.0 / 3.0) ** 1.5
H_SCALE = 5.0 * (2.0 / 3.0) ** 2.5
biot_factor = 0.07957747154594767
section_step = 0.05


def moved(value, axis, target_of):
    pairs = [(source, target_of(source)) for source in range(lax.axis_size(axis))]
    return lax.ppermute(value, axis, pairs)


def to_other_core(source):
    return source ^ 1


def shifted(steps, count):
    return lambda source: (source + steps) % count


HOME_FLOPS = 10**10
NEAR_FLOPS = 10**10
FAR_FLOPS = 10**10


def rounded(value):
    return value.astype(jnp.bfloat16).astype(jnp.float32)


def split_three(value):
    first = rounded(value)
    rest = value - first
    second = rounded(rest)
    return first, second, rest - second


def six_slots(tile, order):
    parts = split_three(tile)
    return jnp.concatenate([parts[part] for part in order], axis=0).astype(jnp.bfloat16)


def cross(left, right):
    return [
        left[1] * right[2] - left[2] * right[1],
        left[2] * right[0] - left[0] * right[2],
        left[0] * right[1] - left[1] * right[0],
    ]


def tile_rows(index, rows):
    return pl.ds(pl.multiple_of(index * rows, rows), rows)


def component(ref, base, number, stride):
    return ref[pl.ds(base + number, GROUP, stride=stride), :]


def store_component(ref, base, number, stride, value):
    ref[pl.ds(base + number, GROUP, stride=stride), :] = value


def target_features(targets, step, centres, near_rows, tilt_rows):
    base = pl.multiple_of(step * (GROUP * ROWS), GROUP * ROWS)
    pos = [component(targets, base, k, ROWS) for k in range(3)]
    strength = [component(targets, base, 3 + k, ROWS) for k in range(3)]
    for k in range(3):
        centre = jnp.broadcast_to(jnp.mean(pos[k], axis=1, keepdims=True), (GROUP, BLOCK))
        store_component(centres, base, k, ROWS, centre)
        pos[k] = pos[k] - centre
    for k in range(3, ROWS):
        store_component(centres, base, k, ROWS, jnp.zeros_like(pos[0]))
    norm = pos[0] * pos[0] + pos[1] * pos[1] + pos[2] * pos[2]
    own = pos[0] * strength[0] + pos[1] * strength[1] + pos[2] * strength[2]
    near = [(2.0 / 3.0) * value for value in pos + [norm, jnp.ones_like(norm)]]
    tilt = [0.5 * s for s in strength] + [own]
    for rows, values in ((near_rows, near), (tilt_rows, tilt)):
        for k, value in enumerate(values):
            store_component(rows, 0, k, ROWS, value)


def source_features(gathered, weight, left, charge):
    pos = [component(gathered, 0, k, ROWS) for k in range(3)]
    strength = [component(gathered, 0, 3 + k, ROWS) for k in range(3)]
    inv_core = 1.0 / component(gathered, 0, 6, ROWS)
    inv_square = inv_core * inv_core
    norm = pos[0] * pos[0] + pos[1] * pos[1] + pos[2] * pos[2]
    twice = -2.0 * inv_square
    shape = [p * twice for p in pos] + [inv_square, norm * inv_square + 1.0]
    for k, value in enumerate(shape):
        store_component(left, 0, k, ROWS, value)
    scale = inv_square * inv_core * weight
    for k, value in enumerate(strength + cross(pos, strength)):
        store_component(charge, 0, k, ROWS, value * scale)


NT = (((1,), (1,)), ((), ()))
TN = (((0,), (0,)), ((), ()))


def put_tiles(window, first, tiles):
    window[pl.ds(pl.multiple_of(first * ROWS, ROWS), tiles.shape[0]), :] = tiles[...]


def prepare_targets(state, near_rows, tilt_rows):
    targets, features, centres, total = state
    near_rows[...] = jnp.zeros_like(near_rows)
    tilt_rows[...] = jnp.zeros_like(tilt_rows)
    total[...] = jnp.zeros_like(total)

    def prepare(step, carry):
        target_features(targets, step, centres, near_rows, tilt_rows)
        for u in range(GROUP):
            rows = slice(u * ROWS, (u + 1) * ROWS)
            features[step * GROUP + u, :, :BLOCK] = six_slots(near_rows[rows, :], (0, 1, 2, 0, 1, 0))
            features[step * GROUP + u, :, BLOCK:] = six_slots(tilt_rows[rows, :], (0, 1, 2, 0, 1, 0))
        return carry

    lax.fori_loop(0, features.shape[0] // GROUP, prepare, 0)


def run_class(lists, window, state, scratch):
    _, features, centres, total = state
    gathered, left, left_next, left_after, charge, charge_next, charge_after = scratch[:7]
    first_half, second_half = scratch[7:]
    slot_row = (lists.shape[0] - 1) // 2
    listed = lists[2 * slot_row, 0]

    def entry_at(step, u):
        entry = jnp.minimum(step * GROUP + u, listed - 1)
        return entry // BLOCK, lax.rem(entry, BLOCK)

    def target_of(step, u):
        row, column = entry_at(step, u)
        return lists[row, column]

    def prepare_sources(step):
        for u in range(GROUP):
            row, column = entry_at(step, u)
            gathered[u * ROWS : (u + 1) * ROWS, :] = (
                window[tile_rows(lists[row + slot_row, column], ROWS), :]
                - centres[tile_rows(lists[row, column], ROWS), :]
            )
        order = lax.broadcasted_iota(jnp.int32, (GROUP, BLOCK), 0) + step * GROUP
        weight = jnp.where(order < listed, 1.0, 0.0).astype(jnp.float32)
        source_features(gathered, weight, left_after, charge_after)

    def move_up():
        left[...] = left_next[...]
        left_next[...] = left_after[...]
        charge[...] = charge_next[...]
        charge_next[...] = charge_after[...]

    def products(step, u, held, source):
        shape = six_slots(source[u * ROWS : (u + 1) * ROWS, :], (0, 0, 0, 1, 1, 2))
        held[u % HALF] = lax.dot_general(
            shape, features[target_of(step, u)], TN, preferred_element_type=jnp.float32
        )

    def weights(u, held):
        near = held[u % HALF, :, :BLOCK]
        tilt = held[u % HALF, :, BLOCK:]
        q = lax.rsqrt(near)
        q2 = q * q
        q3 = q2 * q
        q5 = q3 * q2
        f = q3 + q5
        h = (q5 * tilt) * (q2 + 0.6)
        fh = f.astype(jnp.bfloat16)
        fl = (f - fh.astype(jnp.float32)).astype(jnp.bfloat16)
        hh = h.astype(jnp.bfloat16)
        hl = (h - hh.astype(jnp.float32)).astype(jnp.bfloat16)
        return jnp.concatenate(
            [jnp.concatenate([fh, fl], axis=1), jnp.concatenate([hh, hl], axis=1)], axis=0
        )

    def add_up(u, stacked):
        pair = charge[u * ROWS : (u + 1) * ROWS, :]
        high = rounded(pair)
        pair = jnp.concatenate([high, pair - high], axis=0).astype(jnp.bfloat16)
        blank = jnp.zeros_like(pair)
        pair = jnp.concatenate(
            [jnp.concatenate([pair, blank], axis=1), jnp.concatenate([blank, pair], axis=1)], axis=0
        )
        sums = jnp.dot(pair, stacked, preferred_element_type=jnp.float32)
        fsum = sums[0:8, :BLOCK] + sums[8:16, :BLOCK] + sums[0:8, BLOCK:]
        hsum = sums[16:24, :BLOCK] + sums[24:32, :BLOCK] + sums[16:24, BLOCK:]
        return jnp.concatenate([fsum, hsum], axis=0)

    def turn(step, carry):
        sums = []
        for u in range(HALF):
            stacked = weights(u, first_half)
            products(step, HALF + u, second_half, left)
            sums.append(add_up(u, stacked))
        prepare_sources(step + 2)
        for u in range(HALF, GROUP):
            stacked = weights(u, second_half)
            products(step + 1, u - HALF, first_half, left_next)
            sums.append(add_up(u, stacked))
        for u in range(GROUP):
            total[tile_rows(target_of(step, u), 2 * ROWS), :] += sums[u]
        move_up()
        return carry

    @pl.when(listed > 0)
    def _():
        left_after[...] = jnp.zeros_like(left_after)
        charge_after[...] = jnp.zeros_like(charge_after)
        prepare_sources(0)
        move_up()
        prepare_sources(1)
        move_up()
        for u in range(HALF):
            products(0, u, first_half, left)
        lax.fori_loop(0, (listed + GROUP - 1) // GROUP, turn, 0)


def finish(targets, centres, totals, out_ref):
    blocks = out_ref.shape[1] // 6

    def one(step, carry):
        base = pl.multiple_of(step * GROUP * ROWS, GROUP * ROWS)
        wide = pl.multiple_of(step * GROUP * 2 * ROWS, GROUP * 2 * ROWS)
        pos = [
            component(targets, base, k, ROWS) - component(centres, base, k, ROWS) for k in range(3)
        ]
        strength = [component(targets, base, 3 + k, ROWS) for k in range(3)]
        fa, fb, ha, hb = [
            [
                sum(component(total, wide, start + k, 2 * ROWS) for total in totals)
                for k in range(3)
            ]
            for start in (0, 3, 8, 11)
        ]
        swirl = cross(pos, fa)
        lean = cross(strength, fa)
        bend = cross(pos, ha)
        member = step * GROUP // blocks
        inside = lax.rem(step * GROUP, blocks)
        for k in range(3):
            velocity = (-F_SCALE * biot_factor) * (swirl[k] - fb[k])
            stretch = (-F_SCALE * biot_factor) * lean[k] + (H_SCALE * biot_factor) * (bend[k] - hb[k])
            out_ref[member, pl.ds(pl.multiple_of(k * blocks + inside, GROUP), GROUP), :] = velocity
            out_ref[member, pl.ds(pl.multiple_of((3 + k) * blocks + inside, GROUP), GROUP), :] = stretch
        return carry

    lax.fori_loop(0, targets.shape[0] // ROWS // GROUP, one, 0, unroll=2)


def sort_list(coded, sorted_list, blocks, members):
    length = coded.shape[1]
    t = coded[...] // SLOTS
    s = coded[...] % SLOTS
    t = t - lax.axis_index("across") * blocks
    t = jnp.where(t < 0, t + members * blocks, t)
    run = s // blocks
    mine = t < blocks
    t = jnp.where(mine, t, t - blocks)
    near = (run == REACH) | (run == side_of_partner())
    kind = jnp.where(
        mine,
        jnp.where(near, 0, jnp.where(run == 2 * REACH, 2, 4)),
        jnp.where(near, 1, 3),
    )
    kind = jnp.where(coded[...] < 0, CLASSES - 1, kind)
    member = jnp.where(lax.broadcasted_iota(jnp.int32, (CLASSES, length), 0) == kind, 1.0, 0.0)
    row = lax.broadcasted_iota(jnp.int32, (length, length), 0)
    column = lax.broadcasted_iota(jnp.int32, (length, length), 1)
    before = jnp.where(row < column, 1.0, 0.0).astype(jnp.bfloat16)
    earlier = jnp.dot(member.astype(jnp.bfloat16), before, preferred_element_type=jnp.float32)
    rank = jnp.sum(member * earlier, axis=0, keepdims=True).astype(jnp.int32)
    place = jnp.where(row == rank, 1.0, 0.0).astype(jnp.bfloat16)
    values = [t // BLOCK, t % BLOCK, s // BLOCK, s % BLOCK]
    values = [member * value.astype(jnp.float32) for value in values]
    values = jnp.concatenate(values, axis=0).astype(jnp.bfloat16)
    found = lax.dot_general(values, place, NT, preferred_element_type=jnp.float32)
    number = jnp.broadcast_to(jnp.sum(member, axis=1, keepdims=True), (CLASSES, BLOCK))
    targets = found[0:8] * BLOCK + found[8:16]
    slots = found[16:24] * BLOCK + found[24:32]
    columns = [slice(j * BLOCK, (j + 1) * BLOCK) for j in range(length // BLOCK)]
    rows = sorted_list.shape[1]
    for kind in range(CLASSES - 1):
        one = slice(kind, kind + 1)
        parts = [targets[one, c] for c in columns] + [slots[one, c] for c in columns] + [number[one]]
        padding = rows - len(parts)
        if padding:
            parts.append(jnp.zeros((padding, BLOCK), jnp.float32))
        sorted_list[kind] = jnp.concatenate(parts, axis=0).astype(jnp.int32)


def list_rows(length):
    return 2 * (length // BLOCK) + 1


def read_list(kind, sorted_list, lists, sems):
    copy = pltpu.make_async_copy(sorted_list.at[kind, pl.ds(0, lists.shape[0])], lists, sems.at[0])
    copy.start()
    return copy


class shifted_window:
    def __init__(self, ref, start):
        self.ref, self.start = ref, start * ROWS

    def __getitem__(self, index):
        rows, lanes = index
        return self.ref[pl.ds(pl.multiple_of(rows.start - self.start, ROWS), rows.size), lanes]


def side_of_partner():
    return jnp.where(lax.axis_index("blk") % 2 == 0, REACH + 1, REACH - 1)


def home_kernel(coded, own, partner, *refs, members):
    sorted_list, features, centres, total = refs[:4]
    window, near_rows, tilt_rows, lists, sems = refs[4:9]
    scratch = refs[9:]
    state = (own, features, centres, total)
    blocks = own.shape[0] // ROWS
    sort_list(coded, sorted_list, blocks, members)
    to_scalars = read_list(0, sorted_list, lists, sems)
    put_tiles(window, REACH * blocks, own)
    put_tiles(window, side_of_partner() * blocks, partner)
    prepare_targets(state, near_rows, tilt_rows)
    to_scalars.wait()
    run_class(lists, window, state, scratch)


def near_kernel(sorted_list, own, partner, *refs, members):
    others, refs = refs[: members - 1], refs[members - 1 :]
    targets, features, centres, total = state = refs[:4]
    window, near_rows, tilt_rows, lists, sems = refs[4:9]
    scratch = refs[9:]
    to_scalars = read_list(1, sorted_list, lists, sems)
    blocks = own.shape[0] // ROWS
    put_tiles(window, REACH * blocks, own)
    put_tiles(window, side_of_partner() * blocks, partner)
    for r, other in enumerate(others):
        put_tiles(targets, r * blocks, other)
    prepare_targets(state, near_rows, tilt_rows)
    to_scalars.wait()
    run_class(lists, window, state, scratch)


def middle_kernel(sorted_list, above, own, features, centres, total, lists, sems, *scratch):
    to_scalars = read_list(2, sorted_list, lists, sems)
    total[...] = jnp.zeros_like(total)
    to_scalars.wait()
    window = shifted_window(above, 2 * REACH * (above.shape[0] // ROWS))
    run_class(lists, window, (own, features, centres, total), scratch)


def far_kernel(sorted_list, below, above, crossed, *refs):
    targets, features, centres, near_total = refs[:4]
    window, out_ref, total, lists, sems = refs[4:9]
    scratch = refs[9:]
    state = (targets, features, centres, total)
    to_scalars = read_list(3, sorted_list, lists, sems)
    blocks = below.shape[0] // ROWS
    put_tiles(window, 0, below)
    put_tiles(window, 2 * REACH * blocks, above)
    put_tiles(window, (2 * REACH - side_of_partner()) * blocks, crossed)
    total[...] = jnp.zeros_like(total)
    to_scalars.wait()
    run_class(lists, window, state, scratch)
    finish(targets, centres, (near_total, total), out_ref)


def last_kernel(sorted_list, window, own, features, centres, *refs):
    home_total, middle_total, out_ref, total, lists, sems = refs[:6]
    to_scalars = read_list(4, sorted_list, lists, sems)
    total[...] = jnp.zeros_like(total)
    to_scalars.wait()
    run_class(lists, window, (own, features, centres, total), refs[6:])
    finish(own, centres, (home_total, middle_total, total), out_ref)


def section_kernel(own, sums, *refs):
    returned, (velocity, stretching, section_positions, section_strengths) = refs[:-4], refs[-4:]
    blocks = own.shape[0] // ROWS
    for b in range(blocks):
        lanes = slice(b * BLOCK, (b + 1) * BLOCK)
        for start, result, stepped in ((0, velocity, section_positions), (3, stretching, section_strengths)):
            chosen = pl.ds(start * blocks + b, 3, stride=blocks)
            value = sums[chosen, :]
            for other in returned:
                value = value + other[chosen, :]
            result[:, lanes] = value
            first = b * ROWS + start
            stepped[:, lanes] = own[first : first + 3, :] + section_step * value


def call(kernel, name, inputs, outputs, scratch, flops=0):
    vmem = pl.BlockSpec(memory_space=pltpu.VMEM)
    held = sum(value.size * value.dtype.itemsize for value in (*inputs, *outputs))
    return pl.pallas_call(
        kernel,
        out_shape=outputs,
        in_specs=[vmem for value in inputs],
        out_specs=[vmem for value in outputs],
        scratch_shapes=scratch,
        compiler_params=pltpu.CompilerParams(vmem_limit_bytes=10 * 1024 * 1024 + 2 * held),
        cost_estimate=pl.CostEstimate(flops=flops, bytes_accessed=0, transcendentals=0),
        name=name,
    )(*inputs)


def shards(positions, strengths, radius, block_count, pair_target, pair_slot, pair_count):
    blocks = block_count.shape[0]
    lanes = blocks * BLOCK
    length = pair_target.shape[1]
    members = lax.axis_size("across")
    shard = lax.axis_index("blk")
    count = lax.axis_size("blk")

    def f32(*shape):
        return jax.ShapeDtypeStruct(shape, jnp.float32)

    row = lax.broadcasted_iota(jnp.int32, (blocks, ROWS, BLOCK), 1)
    lane = lax.broadcasted_iota(jnp.int32, (blocks, ROWS, BLOCK), 2)
    cores = radius.reshape(blocks, 1, BLOCK)
    parts = [value.reshape(3, blocks, BLOCK).transpose(1, 0, 2) for value in (positions, strengths)]
    dead = (row >= 3) & (row < 6) & (lane >= block_count[:, None, None])
    own = jnp.where(dead, 0.0, jnp.concatenate(parts + [cores, cores], axis=1))
    own = own.reshape(blocks * ROWS, BLOCK)
    entry = lax.broadcasted_iota(jnp.int32, (1, length), 1)
    coded = jnp.where(entry < pair_count[0], pair_target * SLOTS + pair_slot, -1)
    others = [
        moved(own, "across", lambda source: (source - away) % members) for away in range(1, members)
    ]
    partner = moved(own, "blk", to_other_core)
    above = moved(own, "blk", shifted(-REACH, count))
    below = moved(own, "blk", shifted(REACH, count))

    def state_shapes(number):
        return [
            f32(number * blocks * ROWS, BLOCK),
            jax.ShapeDtypeStruct((number * blocks, FEATURES, 2 * BLOCK), jnp.bfloat16),
            f32(number * blocks * ROWS, BLOCK),
            f32(number * blocks * 2 * ROWS, BLOCK),
        ]

    own_shapes, other_shapes = state_shapes(1), state_shapes(members - 1)
    window_shape = f32((2 * REACH + 1) * blocks * ROWS, BLOCK)
    rows = list_rows(length)
    list_shape = jax.ShapeDtypeStruct((CLASSES - 1, -(-rows // ROWS) * ROWS, BLOCK), jnp.int32)
    feature_rows = [pltpu.VMEM((GROUP * ROWS, BLOCK), jnp.float32)] * 2
    list_scratch = [pltpu.SMEM((rows, BLOCK), jnp.int32), pltpu.SemaphoreType.DMA((1,))]
    scratch = [pltpu.VMEM((GROUP * ROWS, BLOCK), jnp.float32)] * 7 + [
        pltpu.VMEM((HALF, BLOCK, 2 * BLOCK), jnp.float32),
        pltpu.VMEM((HALF, BLOCK, 2 * BLOCK), jnp.float32),
    ]
    window_scratch = pltpu.VMEM(window_shape.shape, jnp.float32)

    lists, *own_state = call(
        lambda *refs: home_kernel(*refs, members=members),
        "home_pairs",
        (coded, own, partner),
        [list_shape] + own_shapes[1:],
        [window_scratch] + feature_rows + list_scratch + scratch,
        flops=HOME_FLOPS,
    )
    other_state = list(call(
        lambda *refs: near_kernel(*refs, members=members),
        "near_pairs",
        (lists, own, partner, *others),
        other_shapes,
        [window_scratch] + feature_rows + list_scratch + scratch,
        flops=NEAR_FLOPS,
    ))
    above, below, other_state[3] = lax.optimization_barrier((above, below, other_state[3]))
    crossed = moved(jnp.where(shard % 2 == 0, above, below), "blk", to_other_core)
    (middle_total,) = call(
        middle_kernel,
        "middle_pairs",
        (lists, above, own, *own_state[:2]),
        [own_shapes[3]],
        list_scratch + scratch,
        flops=HOME_FLOPS,
    )
    crossed, middle_total = lax.optimization_barrier((crossed, middle_total))
    window, away_sums = call(
        far_kernel,
        "far_pairs",
        (lists, below, above, crossed, *other_state),
        [window_shape, f32(members - 1, 6 * blocks, BLOCK)],
        [pltpu.VMEM(other_shapes[3].shape, jnp.float32)] + list_scratch + scratch,
        flops=FAR_FLOPS,
    )
    returned = [
        moved(away_sums[away - 1], "across", lambda source: (source + away) % members)
        for away in range(1, members)
    ]
    (sums,) = call(
        last_kernel,
        "last_pairs",
        (lists, window, own, *own_state, middle_total),
        [f32(1, 6 * blocks, BLOCK)],
        [pltpu.VMEM(own_shapes[3].shape, jnp.float32)] + list_scratch + scratch,
        flops=FAR_FLOPS,
    )
    wide = f32(3, lanes)
    return tuple(
        call(section_kernel, "section", (own, sums[0], *returned), [wide] * 4, [])
    )


def solution(mesh):
    whole = P(None, ("blk", "across"))
    line = P(("blk", "across"))
    return jax.shard_map(
        shards,
        mesh=mesh,
        in_specs=(whole, whole, line, line, P(("blk", "across"), None), P(("blk", "across"), None), line),
        out_specs=(whole, whole, whole, whole),
        check_vma=False,
    )
```

```python
import jax
import jax.numpy as jnp
from jax import lax
from jax.experimental import pallas as pl
from jax.experimental.pallas import tpu as pltpu
from jax.sharding import PartitionSpec as P

BLOCK = 128
ROWS = 8
REACH = 2
GROUP = 8
HALF = 4
FEATURES = 48
CLASSES = 8

F_SCALE = (2.0 / 3.0) ** 1.5
H_SCALE = 5.0 * (2.0 / 3.0) ** 2.5
biot_factor = 0.07957747154594767
section_step = 0.05


def moved(value, axis, target_of):
    pairs = [(source, target_of(source)) for source in range(lax.axis_size(axis))]
    return lax.ppermute(value, axis, pairs)


def to_other_core(source):
    return source ^ 1


def shifted(steps, count):
    return lambda source: (source + steps) % count


HOME_FLOPS = 10**10
NEAR_FLOPS = 10**10
FAR_FLOPS = 10**10


def rounded(value):
    return value.astype(jnp.bfloat16).astype(jnp.float32)


def split_three(value):
    first = rounded(value)
    rest = value - first
    second = rounded(rest)
    return first, second, rest - second


def six_slots(tile, order):
    parts = split_three(tile)
    return jnp.concatenate([parts[part] for part in order], axis=0).astype(jnp.bfloat16)


def cross(left, right):
    return [
        left[1] * right[2] - left[2] * right[1],
        left[2] * right[0] - left[0] * right[2],
        left[0] * right[1] - left[1] * right[0],
    ]


def tile_rows(index, rows):
    return pl.ds(pl.multiple_of(index * rows, rows), rows)


def component(ref, base, number, stride):
    return ref[pl.ds(base + number, GROUP, stride=stride), :]


def store_component(ref, base, number, stride, value):
    ref[pl.ds(base + number, GROUP, stride=stride), :] = value


def target_features(targets, step, centres, near_rows, tilt_rows):
    base = pl.multiple_of(step * (GROUP * ROWS), GROUP * ROWS)
    pos = [component(targets, base, k, ROWS) for k in range(3)]
    strength = [component(targets, base, 3 + k, ROWS) for k in range(3)]
    for k in range(3):
        centre = jnp.broadcast_to(jnp.mean(pos[k], axis=1, keepdims=True), (GROUP, BLOCK))
        store_component(centres, base, k, ROWS, centre)
        pos[k] = pos[k] - centre
    for k in range(3, ROWS):
        store_component(centres, base, k, ROWS, jnp.zeros_like(pos[0]))
    norm = pos[0] * pos[0] + pos[1] * pos[1] + pos[2] * pos[2]
    own = pos[0] * strength[0] + pos[1] * strength[1] + pos[2] * strength[2]
    near = [(2.0 / 3.0) * value for value in pos + [norm, jnp.ones_like(norm)]]
    tilt = [0.5 * s for s in strength] + [own]
    for rows, values in ((near_rows, near), (tilt_rows, tilt)):
        for k, value in enumerate(values):
            store_component(rows, 0, k, ROWS, value)


def source_features(gathered, weight, left, charge):
    pos = [component(gathered, 0, k, ROWS) for k in range(3)]
    strength = [component(gathered, 0, 3 + k, ROWS) for k in range(3)]
    inv_core = 1.0 / component(gathered, 0, 6, ROWS)
    inv_square = inv_core * inv_core
    norm = pos[0] * pos[0] + pos[1] * pos[1] + pos[2] * pos[2]
    twice = -2.0 * inv_square
    shape = [p * twice for p in pos] + [inv_square, norm * inv_square + 1.0]
    for k, value in enumerate(shape):
        store_component(left, 0, k, ROWS, value)
    scale = inv_square * inv_core * weight
    for k, value in enumerate(strength + cross(pos, strength)):
        store_component(charge, 0, k, ROWS, value * scale)


NT = (((1,), (1,)), ((), ()))
TN = (((0,), (0,)), ((), ()))


def put_tiles(window, first, tiles, length):
    base = pl.multiple_of(first * ROWS, ROWS)
    blocks = tiles.shape[0] // ROWS
    window[pl.ds(base, blocks * ROWS), :] = tiles[...]
    number = 2 * length // BLOCK + 1
    counts = tiles[(number + 1) * ROWS - 1 : (number + 1) * ROWS, :]
    row = lax.broadcasted_iota(jnp.int32, (blocks, BLOCK), 0)
    lane = lax.broadcasted_iota(jnp.int32, (blocks, BLOCK), 1)
    counts = jnp.sum(jnp.where(row == lane, counts, 0.0), axis=1, keepdims=True)
    alive = jnp.where(lane.astype(jnp.float32) < counts, 1.0, 0.0)
    for j in range(blocks // GROUP):
        part = alive[j * GROUP : (j + 1) * GROUP, :]
        for k in range(3, 6):
            rows = pl.ds(base + j * GROUP * ROWS + k, GROUP, stride=ROWS)
            window[rows, :] = window[rows, :] * part


def prepare_targets(state, near_rows, tilt_rows):
    targets, features, centres, total = state
    near_rows[...] = jnp.zeros_like(near_rows)
    tilt_rows[...] = jnp.zeros_like(tilt_rows)
    total[...] = jnp.zeros_like(total)

    def prepare(step, carry):
        target_features(targets, step, centres, near_rows, tilt_rows)
        for u in range(GROUP):
            rows = slice(u * ROWS, (u + 1) * ROWS)
            features[step * GROUP + u, :, :BLOCK] = six_slots(near_rows[rows, :], (0, 1, 2, 0, 1, 0))
            features[step * GROUP + u, :, BLOCK:] = six_slots(tilt_rows[rows, :], (0, 1, 2, 0, 1, 0))
        return carry

    lax.fori_loop(0, features.shape[0] // GROUP, prepare, 0)


def run_class(lists, window, state, scratch):
    _, features, centres, total = state
    gathered, left, left_next, left_after, charge, charge_next, charge_after = scratch[:7]
    first_half, second_half = scratch[7:]
    slot_row = (lists.shape[0] - 1) // 2
    listed = lists[2 * slot_row, 0]

    def entry_at(step, u):
        entry = jnp.minimum(step * GROUP + u, listed - 1)
        return entry // BLOCK, lax.rem(entry, BLOCK)

    def target_of(step, u):
        row, column = entry_at(step, u)
        return lists[row, column]

    def prepare_sources(step):
        for u in range(GROUP):
            row, column = entry_at(step, u)
            gathered[u * ROWS : (u + 1) * ROWS, :] = (
                window[tile_rows(lists[row + slot_row, column], ROWS), :]
                - centres[tile_rows(lists[row, column], ROWS), :]
            )
        order = lax.broadcasted_iota(jnp.int32, (GROUP, BLOCK), 0) + step * GROUP
        weight = jnp.where(order < listed, 1.0, 0.0).astype(jnp.float32)
        source_features(gathered, weight, left_after, charge_after)

    def move_up():
        left[...] = left_next[...]
        left_next[...] = left_after[...]
        charge[...] = charge_next[...]
        charge_next[...] = charge_after[...]

    def products(step, u, held, source):
        shape = six_slots(source[u * ROWS : (u + 1) * ROWS, :], (0, 0, 0, 1, 1, 2))
        held[u % HALF] = lax.dot_general(
            shape, features[target_of(step, u)], TN, preferred_element_type=jnp.float32
        )

    def weights(u, held):
        near = held[u % HALF, :, :BLOCK]
        tilt = held[u % HALF, :, BLOCK:]
        q = lax.rsqrt(near)
        q2 = q * q
        q3 = q2 * q
        q5 = q3 * q2
        f = q3 + q5
        h = (q5 * tilt) * (q2 + 0.6)
        fh = f.astype(jnp.bfloat16)
        fl = (f - fh.astype(jnp.float32)).astype(jnp.bfloat16)
        hh = h.astype(jnp.bfloat16)
        hl = (h - hh.astype(jnp.float32)).astype(jnp.bfloat16)
        return jnp.concatenate(
            [jnp.concatenate([fh, fl], axis=1), jnp.concatenate([hh, hl], axis=1)], axis=0
        )

    def add_up(u, stacked):
        pair = charge[u * ROWS : (u + 1) * ROWS, :]
        high = rounded(pair)
        pair = jnp.concatenate([high, pair - high], axis=0).astype(jnp.bfloat16)
        blank = jnp.zeros_like(pair)
        pair = jnp.concatenate(
            [jnp.concatenate([pair, blank], axis=1), jnp.concatenate([blank, pair], axis=1)], axis=0
        )
        sums = jnp.dot(pair, stacked, preferred_element_type=jnp.float32)
        fsum = sums[0:8, :BLOCK] + sums[8:16, :BLOCK] + sums[0:8, BLOCK:]
        hsum = sums[16:24, :BLOCK] + sums[24:32, :BLOCK] + sums[16:24, BLOCK:]
        return jnp.concatenate([fsum, hsum], axis=0)

    def turn(step, carry):
        sums = []
        for u in range(HALF):
            stacked = weights(u, first_half)
            products(step, HALF + u, second_half, left)
            sums.append(add_up(u, stacked))
        prepare_sources(step + 2)
        for u in range(HALF, GROUP):
            stacked = weights(u, second_half)
            products(step + 1, u - HALF, first_half, left_next)
            sums.append(add_up(u, stacked))
        for u in range(GROUP):
            total[tile_rows(target_of(step, u), 2 * ROWS), :] += sums[u]
        move_up()
        return carry

    @pl.when(listed > 0)
    def _():
        left_after[...] = jnp.zeros_like(left_after)
        charge_after[...] = jnp.zeros_like(charge_after)
        prepare_sources(0)
        move_up()
        prepare_sources(1)
        move_up()
        for u in range(HALF):
            products(0, u, first_half, left)
        lax.fori_loop(0, (listed + GROUP - 1) // GROUP, turn, 0)


def finish(targets, centres, totals, out_ref):
    blocks = out_ref.shape[1] // 6

    def one(step, carry):
        base = pl.multiple_of(step * GROUP * ROWS, GROUP * ROWS)
        wide = pl.multiple_of(step * GROUP * 2 * ROWS, GROUP * 2 * ROWS)
        pos = [
            component(targets, base, k, ROWS) - component(centres, base, k, ROWS) for k in range(3)
        ]
        strength = [component(targets, base, 3 + k, ROWS) for k in range(3)]
        fa, fb, ha, hb = [
            [
                sum(component(total, wide, start + k, 2 * ROWS) for total in totals)
                for k in range(3)
            ]
            for start in (0, 3, 8, 11)
        ]
        swirl = cross(pos, fa)
        lean = cross(strength, fa)
        bend = cross(pos, ha)
        member = step * GROUP // blocks
        inside = lax.rem(step * GROUP, blocks)
        for k in range(3):
            velocity = (-F_SCALE * biot_factor) * (swirl[k] - fb[k])
            stretch = (-F_SCALE * biot_factor) * lean[k] + (H_SCALE * biot_factor) * (bend[k] - hb[k])
            out_ref[member, pl.ds(pl.multiple_of(k * blocks + inside, GROUP), GROUP), :] = velocity
            out_ref[member, pl.ds(pl.multiple_of((3 + k) * blocks + inside, GROUP), GROUP), :] = stretch
        return carry

    lax.fori_loop(0, targets.shape[0] // ROWS // GROUP, one, 0, unroll=2)


def sort_list(own, length, sorted_list, blocks, members):
    rows = [own[b * ROWS + ROWS - 1 : (b + 1) * ROWS, :] for b in range(2 * length // BLOCK + 1)]
    half = length // BLOCK
    t = jnp.concatenate(rows[:half], axis=1).astype(jnp.int32)
    s = jnp.concatenate(rows[half : 2 * half], axis=1).astype(jnp.int32)
    number = jnp.concatenate([rows[2 * half]] * half, axis=1).astype(jnp.int32)
    entry = lax.broadcasted_iota(jnp.int32, (1, length), 1)
    t = t - lax.axis_index("across") * blocks
    t = jnp.where(t < 0, t + members * blocks, t)
    run = s // blocks
    mine = t < blocks
    t = jnp.where(mine, t, t - blocks)
    near = (run == REACH) | (run == side_of_partner())
    kind = jnp.where(
        mine,
        jnp.where(near, 0, jnp.where(run == 2 * REACH, 2, 4)),
        jnp.where(near, 1, 3),
    )
    kind = jnp.where(entry < number, kind, CLASSES - 1)
    member = jnp.where(lax.broadcasted_iota(jnp.int32, (CLASSES, length), 0) == kind, 1.0, 0.0)
    row = lax.broadcasted_iota(jnp.int32, (length, length), 0)
    column = lax.broadcasted_iota(jnp.int32, (length, length), 1)
    before = jnp.where(row < column, 1.0, 0.0).astype(jnp.bfloat16)
    earlier = jnp.dot(member.astype(jnp.bfloat16), before, preferred_element_type=jnp.float32)
    rank = jnp.sum(member * earlier, axis=0, keepdims=True).astype(jnp.int32)
    place = jnp.where(row == rank, 1.0, 0.0).astype(jnp.bfloat16)
    values = [t // BLOCK, t % BLOCK, s // BLOCK, s % BLOCK]
    values = [member * value.astype(jnp.float32) for value in values]
    values = jnp.concatenate(values, axis=0).astype(jnp.bfloat16)
    found = lax.dot_general(values, place, NT, preferred_element_type=jnp.float32)
    number = jnp.broadcast_to(jnp.sum(member, axis=1, keepdims=True), (CLASSES, BLOCK))
    targets = found[0:8] * BLOCK + found[8:16]
    slots = found[16:24] * BLOCK + found[24:32]
    columns = [slice(j * BLOCK, (j + 1) * BLOCK) for j in range(length // BLOCK)]
    rows = sorted_list.shape[1]
    for kind in range(CLASSES - 1):
        one = slice(kind, kind + 1)
        parts = [targets[one, c] for c in columns] + [slots[one, c] for c in columns] + [number[one]]
        padding = rows - len(parts)
        if padding:
            parts.append(jnp.zeros((padding, BLOCK), jnp.float32))
        sorted_list[kind] = jnp.concatenate(parts, axis=0).astype(jnp.int32)


def list_rows(length):
    return 2 * (length // BLOCK) + 1


def read_list(kind, sorted_list, lists, sems):
    copy = pltpu.make_async_copy(sorted_list.at[kind, pl.ds(0, lists.shape[0])], lists, sems.at[0])
    copy.start()
    return copy


class shifted_window:
    def __init__(self, ref, start):
        self.ref, self.start = ref, start * ROWS

    def __getitem__(self, index):
        rows, lanes = index
        return self.ref[pl.ds(pl.multiple_of(rows.start - self.start, ROWS), rows.size), lanes]


def side_of_partner():
    return jnp.where(lax.axis_index("blk") % 2 == 0, REACH + 1, REACH - 1)


def home_kernel(own, partner, *refs, members, length):
    sorted_list, live, features, centres, total = refs[:5]
    window, near_rows, tilt_rows, lists, sems = refs[5:10]
    scratch = refs[10:]
    state = (live, features, centres, total)
    blocks = own.shape[0] // ROWS
    sort_list(own, length, sorted_list, blocks, members)
    to_scalars = read_list(0, sorted_list, lists, sems)
    put_tiles(live, 0, own, length)
    window[pl.ds(REACH * blocks * ROWS, blocks * ROWS), :] = live[...]
    put_tiles(window, side_of_partner() * blocks, partner, length)
    prepare_targets(state, near_rows, tilt_rows)
    to_scalars.wait()
    run_class(lists, window, state, scratch)


def near_kernel(sorted_list, live, partner, *refs, members, length):
    others, refs = refs[: members - 1], refs[members - 1 :]
    targets, features, centres, total = state = refs[:4]
    window, near_rows, tilt_rows, lists, sems = refs[4:9]
    scratch = refs[9:]
    to_scalars = read_list(1, sorted_list, lists, sems)
    blocks = live.shape[0] // ROWS
    window[pl.ds(REACH * blocks * ROWS, blocks * ROWS), :] = live[...]
    put_tiles(window, side_of_partner() * blocks, partner, length)
    for r, other in enumerate(others):
        put_tiles(targets, r * blocks, other, length)
    prepare_targets(state, near_rows, tilt_rows)
    to_scalars.wait()
    run_class(lists, window, state, scratch)


def middle_kernel(sorted_list, above, live, features, centres, *refs, length):
    total, window, lists, sems = refs[:4]
    to_scalars = read_list(2, sorted_list, lists, sems)
    total[...] = jnp.zeros_like(total)
    put_tiles(window, 0, above, length)
    to_scalars.wait()
    window = shifted_window(window, 2 * REACH * (above.shape[0] // ROWS))
    run_class(lists, window, (live, features, centres, total), refs[4:])


def far_kernel(sorted_list, below, above, crossed, *refs, length):
    targets, features, centres, near_total = refs[:4]
    window, out_ref, total, lists, sems = refs[4:9]
    scratch = refs[9:]
    state = (targets, features, centres, total)
    to_scalars = read_list(3, sorted_list, lists, sems)
    blocks = below.shape[0] // ROWS
    put_tiles(window, 0, below, length)
    put_tiles(window, 2 * REACH * blocks, above, length)
    put_tiles(window, (2 * REACH - side_of_partner()) * blocks, crossed, length)
    total[...] = jnp.zeros_like(total)
    to_scalars.wait()
    run_class(lists, window, state, scratch)
    finish(targets, centres, (near_total, total), out_ref)


def last_kernel(sorted_list, window, own, features, centres, *refs):
    home_total, middle_total, out_ref, total, lists, sems = refs[:6]
    to_scalars = read_list(4, sorted_list, lists, sems)
    total[...] = jnp.zeros_like(total)
    to_scalars.wait()
    run_class(lists, window, (own, features, centres, total), refs[6:])
    finish(own, centres, (home_total, middle_total, total), out_ref)


def section_kernel(own, sums, *refs):
    returned, (velocity, stretching, section_positions, section_strengths) = refs[:-4], refs[-4:]
    blocks = own.shape[0] // ROWS
    for b in range(blocks):
        lanes = slice(b * BLOCK, (b + 1) * BLOCK)
        for start, result, stepped in ((0, velocity, section_positions), (3, stretching, section_strengths)):
            chosen = pl.ds(start * blocks + b, 3, stride=blocks)
            value = sums[chosen, :]
            for other in returned:
                value = value + other[chosen, :]
            result[:, lanes] = value
            first = b * ROWS + start
            stepped[:, lanes] = own[first : first + 3, :] + section_step * value


def call(kernel, name, inputs, outputs, scratch, flops=0):
    vmem = pl.BlockSpec(memory_space=pltpu.VMEM)
    held = sum(value.size * value.dtype.itemsize for value in (*inputs, *outputs))
    return pl.pallas_call(
        kernel,
        out_shape=outputs,
        in_specs=[vmem for value in inputs],
        out_specs=[vmem for value in outputs],
        scratch_shapes=scratch,
        compiler_params=pltpu.CompilerParams(vmem_limit_bytes=10 * 1024 * 1024 + 2 * held),
        cost_estimate=pl.CostEstimate(flops=flops, bytes_accessed=0, transcendentals=0),
        name=name,
    )(*inputs)


def shards(positions, strengths, radius, block_count, pair_target, pair_slot, pair_count):
    blocks = block_count.shape[0]
    lanes = blocks * BLOCK
    length = pair_target.shape[1]
    members = lax.axis_size("across")
    shard = lax.axis_index("blk")
    count = lax.axis_size("blk")

    def f32(*shape):
        return jax.ShapeDtypeStruct(shape, jnp.float32)

    parts = [value.reshape(3, blocks, BLOCK).transpose(1, 0, 2) for value in (positions, strengths)]
    listed = jnp.concatenate(
        [
            pair_target[0],
            pair_slot[0],
            jnp.broadcast_to(pair_count, (BLOCK,)),
            block_count,
            jnp.zeros((lanes - 2 * length - BLOCK - blocks,), jnp.int32),
        ]
    )
    listed = listed.astype(jnp.float32).reshape(blocks, 1, BLOCK)
    own = jnp.concatenate(parts + [radius.reshape(blocks, 1, BLOCK), listed], axis=1)
    own = own.reshape(blocks * ROWS, BLOCK)
    others = [
        moved(own, "across", lambda source: (source - away) % members) for away in range(1, members)
    ]
    partner = moved(own, "blk", to_other_core)
    above = moved(own, "blk", shifted(-REACH, count))
    below = moved(own, "blk", shifted(REACH, count))

    def state_shapes(number):
        return [
            f32(number * blocks * ROWS, BLOCK),
            jax.ShapeDtypeStruct((number * blocks, FEATURES, 2 * BLOCK), jnp.bfloat16),
            f32(number * blocks * ROWS, BLOCK),
            f32(number * blocks * 2 * ROWS, BLOCK),
        ]

    own_shapes, other_shapes = state_shapes(1), state_shapes(members - 1)
    window_shape = f32((2 * REACH + 1) * blocks * ROWS, BLOCK)
    rows = list_rows(length)
    list_shape = jax.ShapeDtypeStruct((CLASSES - 1, -(-rows // ROWS) * ROWS, BLOCK), jnp.int32)
    feature_rows = [pltpu.VMEM((GROUP * ROWS, BLOCK), jnp.float32)] * 2
    list_scratch = [pltpu.SMEM((rows, BLOCK), jnp.int32), pltpu.SemaphoreType.DMA((1,))]
    scratch = [pltpu.VMEM((GROUP * ROWS, BLOCK), jnp.float32)] * 7 + [
        pltpu.VMEM((HALF, BLOCK, 2 * BLOCK), jnp.float32),
        pltpu.VMEM((HALF, BLOCK, 2 * BLOCK), jnp.float32),
    ]
    window_scratch = pltpu.VMEM(window_shape.shape, jnp.float32)

    lists, live, *own_state = call(
        lambda *refs: home_kernel(*refs, members=members, length=length),
        "home_pairs",
        (own, partner),
        [list_shape] + own_shapes,
        [window_scratch] + feature_rows + list_scratch + scratch,
        flops=HOME_FLOPS,
    )
    other_state = list(call(
        lambda *refs: near_kernel(*refs, members=members, length=length),
        "near_pairs",
        (lists, live, partner, *others),
        other_shapes,
        [window_scratch] + feature_rows + list_scratch + scratch,
        flops=NEAR_FLOPS,
    ))
    above, below, other_state[3] = lax.optimization_barrier((above, below, other_state[3]))
    crossed = moved(jnp.where(shard % 2 == 0, above, below), "blk", to_other_core)
    (middle_total,) = call(
        lambda *refs: middle_kernel(*refs, length=length),
        "middle_pairs",
        (lists, above, live, *own_state[:2]),
        [own_shapes[3]],
        [pltpu.VMEM(own.shape, jnp.float32)] + list_scratch + scratch,
        flops=HOME_FLOPS,
    )
    crossed, middle_total = lax.optimization_barrier((crossed, middle_total))
    window, away_sums = call(
        lambda *refs: far_kernel(*refs, length=length),
        "far_pairs",
        (lists, below, above, crossed, *other_state),
        [window_shape, f32(members - 1, 6 * blocks, BLOCK)],
        [pltpu.VMEM(other_shapes[3].shape, jnp.float32)] + list_scratch + scratch,
        flops=FAR_FLOPS,
    )
    returned = [
        moved(away_sums[away - 1], "across", lambda source: (source + away) % members)
        for away in range(1, members)
    ]
    (sums,) = call(
        last_kernel,
        "last_pairs",
        (lists, window, live, *own_state, middle_total),
        [f32(1, 6 * blocks, BLOCK)],
        [pltpu.VMEM(own_shapes[3].shape, jnp.float32)] + list_scratch + scratch,
        flops=FAR_FLOPS,
    )
    wide = f32(3, lanes)
    return tuple(
        call(section_kernel, "section", (live, sums[0], *returned), [wide] * 4, [])
    )


def solution(mesh):
    whole = P(None, ("blk", "across"))
    line = P(("blk", "across"))
    return jax.shard_map(
        shards,
        mesh=mesh,
        in_specs=(whole, whole, line, line, P(("blk", "across"), None), P(("blk", "across"), None), line),
        out_specs=(whole, whole, whole, whole),
        check_vma=False,
    )
```

```python
import jax
import jax.numpy as jnp
from jax import lax
from jax.experimental import pallas as pl
from jax.experimental.pallas import tpu as pltpu
from jax.sharding import PartitionSpec as P

BLOCK = 128
ROWS = 8
REACH = 2
GROUP = 8
HALF = 4
FEATURES = 48
CLASSES = 8

F_SCALE = (2.0 / 3.0) ** 1.5
H_SCALE = 5.0 * (2.0 / 3.0) ** 2.5
biot_factor = 0.07957747154594767
section_step = 0.05


def moved(value, axis, target_of):
    pairs = [(source, target_of(source)) for source in range(lax.axis_size(axis))]
    return lax.ppermute(value, axis, pairs)


def to_other_core(source):
    return source ^ 1


def shifted(steps, count):
    return lambda source: (source + steps) % count


HOME_FLOPS = 10**10
NEAR_FLOPS = 10**10
FAR_FLOPS = 10**10


def rounded(value):
    return value.astype(jnp.bfloat16).astype(jnp.float32)


def split_three(value):
    first = rounded(value)
    rest = value - first
    second = rounded(rest)
    return first, second, rest - second


def six_slots(tile, order):
    parts = split_three(tile)
    return jnp.concatenate([parts[part] for part in order], axis=0).astype(jnp.bfloat16)


def cross(left, right):
    return [
        left[1] * right[2] - left[2] * right[1],
        left[2] * right[0] - left[0] * right[2],
        left[0] * right[1] - left[1] * right[0],
    ]


def tile_rows(index, rows):
    return pl.ds(pl.multiple_of(index * rows, rows), rows)


def component(ref, base, number, stride):
    return ref[pl.ds(base + number, GROUP, stride=stride), :]


def store_component(ref, base, number, stride, value):
    ref[pl.ds(base + number, GROUP, stride=stride), :] = value


def target_features(targets, step, centres, near_rows, tilt_rows):
    base = pl.multiple_of(step * (GROUP * ROWS), GROUP * ROWS)
    pos = [component(targets, base, k, ROWS) for k in range(3)]
    strength = [component(targets, base, 3 + k, ROWS) for k in range(3)]
    for k in range(3):
        centre = jnp.broadcast_to(jnp.mean(pos[k], axis=1, keepdims=True), (GROUP, BLOCK))
        store_component(centres, base, k, ROWS, centre)
        pos[k] = pos[k] - centre
    for k in range(3, ROWS):
        store_component(centres, base, k, ROWS, jnp.zeros_like(pos[0]))
    norm = pos[0] * pos[0] + pos[1] * pos[1] + pos[2] * pos[2]
    own = pos[0] * strength[0] + pos[1] * strength[1] + pos[2] * strength[2]
    near = [(2.0 / 3.0) * value for value in pos + [norm, jnp.ones_like(norm)]]
    tilt = [0.5 * s for s in strength] + [own]
    for rows, values in ((near_rows, near), (tilt_rows, tilt)):
        for k, value in enumerate(values):
            store_component(rows, 0, k, ROWS, value)


def source_features(gathered, weight, left, charge):
    pos = [component(gathered, 0, k, ROWS) for k in range(3)]
    strength = [component(gathered, 0, 3 + k, ROWS) for k in range(3)]
    inv_core = 1.0 / component(gathered, 0, 6, ROWS)
    inv_square = inv_core * inv_core
    norm = pos[0] * pos[0] + pos[1] * pos[1] + pos[2] * pos[2]
    twice = -2.0 * inv_square
    shape = [p * twice for p in pos] + [inv_square, norm * inv_square + 1.0]
    for k, value in enumerate(shape):
        store_component(left, 0, k, ROWS, value)
    scale = inv_square * inv_core * weight
    for k, value in enumerate(strength + cross(pos, strength)):
        store_component(charge, 0, k, ROWS, value * scale)


NT = (((1,), (1,)), ((), ()))
TN = (((0,), (0,)), ((), ()))


def put_tiles(window, first, tiles, length):
    base = pl.multiple_of(first * ROWS, ROWS)
    blocks = tiles.shape[0] // ROWS
    window[pl.ds(base, blocks * ROWS), :] = tiles[...]
    number = 2 * length // BLOCK + 1
    counts = tiles[(number + 1) * ROWS - 1 : (number + 1) * ROWS, :]
    row = lax.broadcasted_iota(jnp.int32, (blocks, BLOCK), 0)
    lane = lax.broadcasted_iota(jnp.int32, (blocks, BLOCK), 1)
    counts = jnp.sum(jnp.where(row == lane, counts, 0.0), axis=1, keepdims=True)
    alive = jnp.where(lane.astype(jnp.float32) < counts, 1.0, 0.0)
    for j in range(blocks // GROUP):
        part = alive[j * GROUP : (j + 1) * GROUP, :]
        for k in range(3, 6):
            rows = pl.ds(base + j * GROUP * ROWS + k, GROUP, stride=ROWS)
            window[rows, :] = window[rows, :] * part


def prepare_targets(state, near_rows, tilt_rows):
    targets, features, centres, total = state
    near_rows[...] = jnp.zeros_like(near_rows)
    tilt_rows[...] = jnp.zeros_like(tilt_rows)
    total[...] = jnp.zeros_like(total)

    def prepare(step, carry):
        target_features(targets, step, centres, near_rows, tilt_rows)
        for u in range(GROUP):
            rows = slice(u * ROWS, (u + 1) * ROWS)
            features[step * GROUP + u, :, :BLOCK] = six_slots(near_rows[rows, :], (0, 1, 2, 0, 1, 0))
            features[step * GROUP + u, :, BLOCK:] = six_slots(tilt_rows[rows, :], (0, 1, 2, 0, 1, 0))
        return carry

    lax.fori_loop(0, features.shape[0] // GROUP, prepare, 0)


def run_class(lists, window, state, scratch):
    _, features, centres, total = state
    gathered, left, left_next, left_after, charge, charge_next, charge_after = scratch[:7]
    first_half, second_half = scratch[7:]
    slot_row = (lists.shape[0] - 1) // 2
    listed = lists[2 * slot_row, 0]

    def entry_at(step, u):
        entry = jnp.minimum(step * GROUP + u, listed - 1)
        return entry // BLOCK, lax.rem(entry, BLOCK)

    def target_of(step, u):
        row, column = entry_at(step, u)
        return lists[row, column]

    def prepare_sources(step):
        for u in range(GROUP):
            row, column = entry_at(step, u)
            gathered[u * ROWS : (u + 1) * ROWS, :] = (
                window[tile_rows(lists[row + slot_row, column], ROWS), :]
                - centres[tile_rows(lists[row, column], ROWS), :]
            )
        order = lax.broadcasted_iota(jnp.int32, (GROUP, BLOCK), 0) + step * GROUP
        weight = jnp.where(order < listed, 1.0, 0.0).astype(jnp.float32)
        source_features(gathered, weight, left_after, charge_after)

    def move_up():
        left[...] = left_next[...]
        left_next[...] = left_after[...]
        charge[...] = charge_next[...]
        charge_next[...] = charge_after[...]

    def products(step, u, held, source):
        shape = six_slots(source[u * ROWS : (u + 1) * ROWS, :], (0, 0, 0, 1, 1, 2))
        held[u % HALF] = lax.dot_general(
            shape, features[target_of(step, u)], TN, preferred_element_type=jnp.float32
        )

    def weights(u, held):
        near = held[u % HALF, :, :BLOCK]
        tilt = held[u % HALF, :, BLOCK:]
        q = lax.rsqrt(near)
        q2 = q * q
        q3 = q2 * q
        q5 = q3 * q2
        f = q3 + q5
        h = (q5 * tilt) * (q2 + 0.6)
        fh = f.astype(jnp.bfloat16)
        fl = (f - fh.astype(jnp.float32)).astype(jnp.bfloat16)
        hh = h.astype(jnp.bfloat16)
        hl = (h - hh.astype(jnp.float32)).astype(jnp.bfloat16)
        return jnp.concatenate(
            [jnp.concatenate([fh, fl], axis=1), jnp.concatenate([hh, hl], axis=1)], axis=0
        )

    def add_up(u, stacked):
        pair = charge[u * ROWS : (u + 1) * ROWS, :]
        high = rounded(pair)
        pair = jnp.concatenate([high, pair - high], axis=0).astype(jnp.bfloat16)
        blank = jnp.zeros_like(pair)
        pair = jnp.concatenate(
            [jnp.concatenate([pair, blank], axis=1), jnp.concatenate([blank, pair], axis=1)], axis=0
        )
        sums = jnp.dot(pair, stacked, preferred_element_type=jnp.float32)
        fsum = sums[0:8, :BLOCK] + sums[8:16, :BLOCK] + sums[0:8, BLOCK:]
        hsum = sums[16:24, :BLOCK] + sums[24:32, :BLOCK] + sums[16:24, BLOCK:]
        return jnp.concatenate([fsum, hsum], axis=0)

    def turn(step, carry):
        sums = []
        for u in range(HALF):
            stacked = weights(u, first_half)
            products(step, HALF + u, second_half, left)
            sums.append(add_up(u, stacked))
        prepare_sources(step + 2)
        for u in range(HALF, GROUP):
            stacked = weights(u, second_half)
            products(step + 1, u - HALF, first_half, left_next)
            sums.append(add_up(u, stacked))
        for u in range(GROUP):
            total[tile_rows(target_of(step, u), 2 * ROWS), :] += sums[u]
        move_up()
        return carry

    @pl.when(listed > 0)
    def _():
        left_after[...] = jnp.zeros_like(left_after)
        charge_after[...] = jnp.zeros_like(charge_after)
        prepare_sources(0)
        move_up()
        prepare_sources(1)
        move_up()
        for u in range(HALF):
            products(0, u, first_half, left)
        lax.fori_loop(0, (listed + GROUP - 1) // GROUP, turn, 0)


def finish(targets, centres, totals, out_ref):
    blocks = out_ref.shape[1] // 6

    def one(step, carry):
        base = pl.multiple_of(step * GROUP * ROWS, GROUP * ROWS)
        wide = pl.multiple_of(step * GROUP * 2 * ROWS, GROUP * 2 * ROWS)
        pos = [
            component(targets, base, k, ROWS) - component(centres, base, k, ROWS) for k in range(3)
        ]
        strength = [component(targets, base, 3 + k, ROWS) for k in range(3)]
        fa, fb, ha, hb = [
            [
                sum(component(total, wide, start + k, 2 * ROWS) for total in totals)
                for k in range(3)
            ]
            for start in (0, 3, 8, 11)
        ]
        swirl = cross(pos, fa)
        lean = cross(strength, fa)
        bend = cross(pos, ha)
        member = step * GROUP // blocks
        inside = lax.rem(step * GROUP, blocks)
        for k in range(3):
            velocity = (-F_SCALE * biot_factor) * (swirl[k] - fb[k])
            stretch = (-F_SCALE * biot_factor) * lean[k] + (H_SCALE * biot_factor) * (bend[k] - hb[k])
            out_ref[member, pl.ds(pl.multiple_of(k * blocks + inside, GROUP), GROUP), :] = velocity
            out_ref[member, pl.ds(pl.multiple_of((3 + k) * blocks + inside, GROUP), GROUP), :] = stretch
        return carry

    lax.fori_loop(0, targets.shape[0] // ROWS // GROUP, one, 0, unroll=2)


def sort_list(own, length, sorted_list, blocks, members):
    rows = [own[b * ROWS + ROWS - 1 : (b + 1) * ROWS, :] for b in range(2 * length // BLOCK + 1)]
    half = length // BLOCK
    t = jnp.concatenate(rows[:half], axis=1).astype(jnp.int32)
    s = jnp.concatenate(rows[half : 2 * half], axis=1).astype(jnp.int32)
    number = rows[2 * half][:, 0:1].astype(jnp.int32)
    entry = lax.broadcasted_iota(jnp.int32, (1, length), 1)
    t = t - lax.axis_index("across") * blocks
    t = jnp.where(t < 0, t + members * blocks, t)
    run = s // blocks
    mine = t < blocks
    t = jnp.where(mine, t, t - blocks)
    near = (run == REACH) | (run == side_of_partner())
    kind = jnp.where(
        mine,
        jnp.where(near, 0, jnp.where(run == 2 * REACH, 2, 4)),
        jnp.where(near, 1, jnp.where(run == 0, 5, 3)),
    )
    kind = jnp.where(entry < number, kind, CLASSES - 1)
    member = jnp.where(lax.broadcasted_iota(jnp.int32, (CLASSES, length), 0) == kind, 1.0, 0.0)
    row = lax.broadcasted_iota(jnp.int32, (length, length), 0)
    column = lax.broadcasted_iota(jnp.int32, (length, length), 1)
    before = jnp.where(row < column, 1.0, 0.0).astype(jnp.bfloat16)
    earlier = jnp.dot(member.astype(jnp.bfloat16), before, preferred_element_type=jnp.float32)
    rank = jnp.sum(member * earlier, axis=0, keepdims=True).astype(jnp.int32)
    place = jnp.where(row == rank, 1.0, 0.0).astype(jnp.bfloat16)
    values = [t // BLOCK, t % BLOCK, s // BLOCK, s % BLOCK]
    values = [member * value.astype(jnp.float32) for value in values]
    values = jnp.concatenate(values, axis=0).astype(jnp.bfloat16)
    found = lax.dot_general(values, place, NT, preferred_element_type=jnp.float32)
    number = jnp.broadcast_to(jnp.sum(member, axis=1, keepdims=True), (CLASSES, BLOCK))
    targets = found[0:8] * BLOCK + found[8:16]
    slots = found[16:24] * BLOCK + found[24:32]
    columns = [slice(j * BLOCK, (j + 1) * BLOCK) for j in range(length // BLOCK)]
    rows = sorted_list.shape[1]
    for kind in range(CLASSES - 1):
        one = slice(kind, kind + 1)
        parts = [targets[one, c] for c in columns] + [slots[one, c] for c in columns] + [number[one]]
        padding = rows - len(parts)
        if padding:
            parts.append(jnp.zeros((padding, BLOCK), jnp.float32))
        sorted_list[kind] = jnp.concatenate(parts, axis=0).astype(jnp.int32)


def list_rows(length):
    return 2 * (length // BLOCK) + 1


def read_list(kind, sorted_list, lists, sems):
    copy = pltpu.make_async_copy(sorted_list.at[kind, pl.ds(0, lists.shape[0])], lists, sems.at[0])
    copy.start()
    return copy


class shifted_window:
    def __init__(self, ref, start):
        self.ref, self.start = ref, start * ROWS

    def __getitem__(self, index):
        rows, lanes = index
        return self.ref[pl.ds(pl.multiple_of(rows.start - self.start, ROWS), rows.size), lanes]


def side_of_partner():
    return jnp.where(lax.axis_index("blk") % 2 == 0, REACH + 1, REACH - 1)


def home_kernel(own, partner, *refs, members, length):
    sorted_list, live, features, centres, total = refs[:5]
    window, near_rows, tilt_rows, lists, sems = refs[5:10]
    scratch = refs[10:]
    state = (live, features, centres, total)
    blocks = own.shape[0] // ROWS
    sort_list(own, length, sorted_list, blocks, members)
    to_scalars = read_list(0, sorted_list, lists, sems)
    put_tiles(live, 0, own, length)
    window[pl.ds(REACH * blocks * ROWS, blocks * ROWS), :] = live[...]
    put_tiles(window, side_of_partner() * blocks, partner, length)
    prepare_targets(state, near_rows, tilt_rows)
    to_scalars.wait()
    run_class(lists, window, state, scratch)


def near_kernel(sorted_list, live, partner, *refs, members, length):
    others, refs = refs[: members - 1], refs[members - 1 :]
    targets, features, centres, total = state = refs[:4]
    window, near_rows, tilt_rows, lists, sems = refs[4:9]
    scratch = refs[9:]
    to_scalars = read_list(1, sorted_list, lists, sems)
    blocks = live.shape[0] // ROWS
    window[pl.ds(REACH * blocks * ROWS, blocks * ROWS), :] = live[...]
    put_tiles(window, side_of_partner() * blocks, partner, length)
    for r, other in enumerate(others):
        put_tiles(targets, r * blocks, other, length)
    prepare_targets(state, near_rows, tilt_rows)
    to_scalars.wait()
    run_class(lists, window, state, scratch)


def single_kernel(sorted_list, tiles, targets, features, centres, *refs, kind, run, length):
    total, window, lists, sems = refs[:4]
    to_scalars = read_list(kind, sorted_list, lists, sems)
    total[...] = jnp.zeros_like(total)
    put_tiles(window, 0, tiles, length)
    to_scalars.wait()
    window = shifted_window(window, run * (tiles.shape[0] // ROWS))
    run_class(lists, window, (targets, features, centres, total), refs[4:])


def far_kernel(sorted_list, below, above, crossed, *refs, length):
    targets, features, centres, near_total, below_total = refs[:5]
    window, out_ref, total, lists, sems = refs[5:10]
    scratch = refs[10:]
    state = (targets, features, centres, total)
    to_scalars = read_list(3, sorted_list, lists, sems)
    blocks = below.shape[0] // ROWS
    put_tiles(window, 0, below, length)
    put_tiles(window, 2 * REACH * blocks, above, length)
    put_tiles(window, (2 * REACH - side_of_partner()) * blocks, crossed, length)
    total[...] = jnp.zeros_like(total)
    to_scalars.wait()
    run_class(lists, window, state, scratch)
    finish(targets, centres, (near_total, below_total, total), out_ref)


def last_kernel(sorted_list, window, own, features, centres, *refs):
    home_total, middle_total, out_ref, total, lists, sems = refs[:6]
    to_scalars = read_list(4, sorted_list, lists, sems)
    total[...] = jnp.zeros_like(total)
    to_scalars.wait()
    run_class(lists, window, (own, features, centres, total), refs[6:])
    finish(own, centres, (home_total, middle_total, total), out_ref)


def section_kernel(own, sums, *refs):
    returned, (velocity, stretching, section_positions, section_strengths) = refs[:-4], refs[-4:]
    blocks = own.shape[0] // ROWS
    for b in range(blocks):
        lanes = slice(b * BLOCK, (b + 1) * BLOCK)
        for start, result, stepped in ((0, velocity, section_positions), (3, stretching, section_strengths)):
            chosen = pl.ds(start * blocks + b, 3, stride=blocks)
            value = sums[chosen, :]
            for other in returned:
                value = value + other[chosen, :]
            result[:, lanes] = value
            first = b * ROWS + start
            stepped[:, lanes] = own[first : first + 3, :] + section_step * value


def call(kernel, name, inputs, outputs, scratch, flops=0):
    vmem = pl.BlockSpec(memory_space=pltpu.VMEM)
    held = sum(value.size * value.dtype.itemsize for value in (*inputs, *outputs))
    return pl.pallas_call(
        kernel,
        out_shape=outputs,
        in_specs=[vmem for value in inputs],
        out_specs=[vmem for value in outputs],
        scratch_shapes=scratch,
        compiler_params=pltpu.CompilerParams(vmem_limit_bytes=10 * 1024 * 1024 + 2 * held),
        cost_estimate=pl.CostEstimate(flops=flops, bytes_accessed=0, transcendentals=0),
        name=name,
    )(*inputs)


def shards(positions, strengths, radius, block_count, pair_target, pair_slot, pair_count):
    blocks = block_count.shape[0]
    lanes = blocks * BLOCK
    length = pair_target.shape[1]
    members = lax.axis_size("across")
    shard = lax.axis_index("blk")
    count = lax.axis_size("blk")

    def f32(*shape):
        return jax.ShapeDtypeStruct(shape, jnp.float32)

    parts = [value.reshape(3, blocks, BLOCK).transpose(1, 0, 2) for value in (positions, strengths)]
    listed = jnp.concatenate(
        [
            pair_target[0],
            pair_slot[0],
            pair_count,
            jnp.zeros((BLOCK - 1,), jnp.int32),
            block_count,
            jnp.zeros((lanes - 2 * length - BLOCK - blocks,), jnp.int32),
        ]
    )
    listed = listed.astype(jnp.float32).reshape(blocks, 1, BLOCK)
    own = jnp.concatenate(parts + [radius.reshape(blocks, 1, BLOCK), listed], axis=1)
    own = own.reshape(blocks * ROWS, BLOCK)
    others = [
        moved(own, "across", lambda source: (source - away) % members) for away in range(1, members)
    ]
    partner = moved(own, "blk", to_other_core)
    below = moved(own, "blk", shifted(REACH, count))

    def state_shapes(number):
        return [
            f32(number * blocks * ROWS, BLOCK),
            jax.ShapeDtypeStruct((number * blocks, FEATURES, 2 * BLOCK), jnp.bfloat16),
            f32(number * blocks * ROWS, BLOCK),
            f32(number * blocks * 2 * ROWS, BLOCK),
        ]

    own_shapes, other_shapes = state_shapes(1), state_shapes(members - 1)
    window_shape = f32((2 * REACH + 1) * blocks * ROWS, BLOCK)
    rows = list_rows(length)
    list_shape = jax.ShapeDtypeStruct((CLASSES - 1, -(-rows // ROWS) * ROWS, BLOCK), jnp.int32)
    feature_rows = [pltpu.VMEM((GROUP * ROWS, BLOCK), jnp.float32)] * 2
    list_scratch = [pltpu.SMEM((rows, BLOCK), jnp.int32), pltpu.SemaphoreType.DMA((1,))]
    scratch = [pltpu.VMEM((GROUP * ROWS, BLOCK), jnp.float32)] * 7 + [
        pltpu.VMEM((HALF, BLOCK, 2 * BLOCK), jnp.float32),
        pltpu.VMEM((HALF, BLOCK, 2 * BLOCK), jnp.float32),
    ]
    window_scratch = pltpu.VMEM(window_shape.shape, jnp.float32)

    lists, live, *own_state = call(
        lambda *refs: home_kernel(*refs, members=members, length=length),
        "home_pairs",
        (own, partner),
        [list_shape] + own_shapes,
        [window_scratch] + feature_rows + list_scratch + scratch,
        flops=HOME_FLOPS,
    )
    late, lists = lax.optimization_barrier((own, lists))
    above = moved(late, "blk", shifted(-REACH, count))
    other_state = list(call(
        lambda *refs: near_kernel(*refs, members=members, length=length),
        "near_pairs",
        (lists, live, partner, *others),
        other_shapes,
        [window_scratch] + feature_rows + list_scratch + scratch,
        flops=NEAR_FLOPS,
    ))
    (below_total,) = call(
        lambda *refs: single_kernel(*refs, kind=5, run=0, length=length),
        "below_pairs",
        (lists, below, *other_state[:3]),
        [other_shapes[3]],
        [pltpu.VMEM(own.shape, jnp.float32)] + list_scratch + scratch,
        flops=HOME_FLOPS,
    )
    above, below_total = lax.optimization_barrier((above, below_total))
    crossed = moved(jnp.where(shard % 2 == 0, above, below), "blk", to_other_core)
    (middle_total,) = call(
        lambda *refs: single_kernel(*refs, kind=2, run=2 * REACH, length=length),
        "middle_pairs",
        (lists, above, live, *own_state[:2]),
        [own_shapes[3]],
        [pltpu.VMEM(own.shape, jnp.float32)] + list_scratch + scratch,
        flops=HOME_FLOPS,
    )
    crossed, middle_total = lax.optimization_barrier((crossed, middle_total))
    window, away_sums = call(
        lambda *refs: far_kernel(*refs, length=length),
        "far_pairs",
        (lists, below, above, crossed, *other_state, below_total),
        [window_shape, f32(members - 1, 6 * blocks, BLOCK)],
        [pltpu.VMEM(other_shapes[3].shape, jnp.float32)] + list_scratch + scratch,
        flops=FAR_FLOPS,
    )
    returned = [
        moved(away_sums[away - 1], "across", lambda source: (source + away) % members)
        for away in range(1, members)
    ]
    (sums,) = call(
        last_kernel,
        "last_pairs",
        (lists, window, live, *own_state, middle_total),
        [f32(1, 6 * blocks, BLOCK)],
        [pltpu.VMEM(own_shapes[3].shape, jnp.float32)] + list_scratch + scratch,
        flops=FAR_FLOPS,
    )
    wide = f32(3, lanes)
    return tuple(
        call(section_kernel, "section", (live, sums[0], *returned), [wide] * 4, [])
    )


def solution(mesh):
    whole = P(None, ("blk", "across"))
    line = P(("blk", "across"))
    return jax.shard_map(
        shards,
        mesh=mesh,
        in_specs=(whole, whole, line, line, P(("blk", "across"), None), P(("blk", "across"), None), line),
        out_specs=(whole, whole, whole, whole),
        check_vma=False,
    )
```

```python
import jax
import jax.numpy as jnp
from jax import lax
from jax.experimental import pallas as pl
from jax.experimental.pallas import tpu as pltpu
from jax.sharding import PartitionSpec as P

BLOCK = 128
ROWS = 8
REACH = 2
GROUP = 8
HALF = 4
FEATURES = 48
CLASSES = 8

F_SCALE = (2.0 / 3.0) ** 1.5
H_SCALE = 5.0 * (2.0 / 3.0) ** 2.5
biot_factor = 0.07957747154594767
section_step = 0.05


def moved(value, axis, target_of):
    pairs = [(source, target_of(source)) for source in range(lax.axis_size(axis))]
    return lax.ppermute(value, axis, pairs)


def to_other_core(source):
    return source ^ 1


def shifted(steps, count):
    return lambda source: (source + steps) % count


HOME_FLOPS = 10**10
NEAR_FLOPS = 10**10
FAR_FLOPS = 10**10


def rounded(value):
    return value.astype(jnp.bfloat16).astype(jnp.float32)


def split_three(value):
    first = rounded(value)
    rest = value - first
    second = rounded(rest)
    return first, second, rest - second


def six_slots(tile, order):
    parts = split_three(tile)
    return jnp.concatenate([parts[part] for part in order], axis=0).astype(jnp.bfloat16)


def cross(left, right):
    return [
        left[1] * right[2] - left[2] * right[1],
        left[2] * right[0] - left[0] * right[2],
        left[0] * right[1] - left[1] * right[0],
    ]


def tile_rows(index, rows):
    return pl.ds(pl.multiple_of(index * rows, rows), rows)


def component(ref, base, number, stride):
    return ref[pl.ds(base + number, GROUP, stride=stride), :]


def store_component(ref, base, number, stride, value):
    ref[pl.ds(base + number, GROUP, stride=stride), :] = value


def target_features(targets, step, centres, near_rows, tilt_rows):
    base = pl.multiple_of(step * (GROUP * ROWS), GROUP * ROWS)
    pos = [component(targets, base, k, ROWS) for k in range(3)]
    strength = [component(targets, base, 3 + k, ROWS) for k in range(3)]
    for k in range(3):
        centre = jnp.broadcast_to(jnp.mean(pos[k], axis=1, keepdims=True), (GROUP, BLOCK))
        store_component(centres, base, k, ROWS, centre)
        pos[k] = pos[k] - centre
    for k in range(3, ROWS):
        store_component(centres, base, k, ROWS, jnp.zeros_like(pos[0]))
    norm = pos[0] * pos[0] + pos[1] * pos[1] + pos[2] * pos[2]
    own = pos[0] * strength[0] + pos[1] * strength[1] + pos[2] * strength[2]
    near = [(2.0 / 3.0) * value for value in pos + [norm, jnp.ones_like(norm)]]
    tilt = [0.5 * s for s in strength] + [own]
    for rows, values in ((near_rows, near), (tilt_rows, tilt)):
        for k, value in enumerate(values):
            store_component(rows, 0, k, ROWS, value)


def source_features(gathered, weight, left, charge):
    pos = [component(gathered, 0, k, ROWS) for k in range(3)]
    strength = [component(gathered, 0, 3 + k, ROWS) for k in range(3)]
    inv_core = 1.0 / component(gathered, 0, 6, ROWS)
    inv_square = inv_core * inv_core
    norm = pos[0] * pos[0] + pos[1] * pos[1] + pos[2] * pos[2]
    twice = -2.0 * inv_square
    shape = [p * twice for p in pos] + [inv_square, norm * inv_square + 1.0]
    for k, value in enumerate(shape):
        store_component(left, 0, k, ROWS, value)
    scale = inv_square * inv_core * weight
    for k, value in enumerate(strength + cross(pos, strength)):
        store_component(charge, 0, k, ROWS, value * scale)


NT = (((1,), (1,)), ((), ()))
TN = (((0,), (0,)), ((), ()))


def put_tiles(window, first, tiles, length):
    base = pl.multiple_of(first * ROWS, ROWS)
    blocks = tiles.shape[0] // ROWS
    window[pl.ds(base, blocks * ROWS), :] = tiles[...]
    row = (2 * length // BLOCK + 1) * ROWS - 1
    counts = tiles[row : row + 1, :]
    row = lax.broadcasted_iota(jnp.int32, (blocks, BLOCK), 0)
    lane = lax.broadcasted_iota(jnp.int32, (blocks, BLOCK), 1)
    counts = jnp.sum(jnp.where(row == lane, counts, 0.0), axis=1, keepdims=True)
    alive = jnp.where(lane.astype(jnp.float32) < counts, 1.0, 0.0)
    for j in range(blocks // GROUP):
        part = alive[j * GROUP : (j + 1) * GROUP, :]
        for k in range(3, 6):
            rows = pl.ds(base + j * GROUP * ROWS + k, GROUP, stride=ROWS)
            window[rows, :] = window[rows, :] * part


def prepare_targets(state, near_rows, tilt_rows):
    targets, features, centres, total = state
    near_rows[...] = jnp.zeros_like(near_rows)
    tilt_rows[...] = jnp.zeros_like(tilt_rows)
    total[...] = jnp.zeros_like(total)

    def prepare(step, carry):
        target_features(targets, step, centres, near_rows, tilt_rows)
        for u in range(GROUP):
            rows = slice(u * ROWS, (u + 1) * ROWS)
            features[step * GROUP + u, :, :BLOCK] = six_slots(near_rows[rows, :], (0, 1, 2, 0, 1, 0))
            features[step * GROUP + u, :, BLOCK:] = six_slots(tilt_rows[rows, :], (0, 1, 2, 0, 1, 0))
        return carry

    lax.fori_loop(0, features.shape[0] // GROUP, prepare, 0)


def run_class(lists, window, state, scratch):
    _, features, centres, total = state
    gathered, left, charge_next, charge, first_half, second_half = scratch
    slot_row = (lists.shape[0] - 1) // 2
    listed = lists[2 * slot_row, 0]

    def entry_at(step, u):
        entry = jnp.minimum(step * GROUP + u, listed - 1)
        return entry // BLOCK, lax.rem(entry, BLOCK)

    def target_of(step, u):
        row, column = entry_at(step, u)
        return lists[row, column]

    def prepare_sources(step):
        for u in range(GROUP):
            row, column = entry_at(step, u)
            gathered[u * ROWS : (u + 1) * ROWS, :] = (
                window[tile_rows(lists[row + slot_row, column], ROWS), :]
                - centres[tile_rows(lists[row, column], ROWS), :]
            )
        order = lax.broadcasted_iota(jnp.int32, (GROUP, BLOCK), 0) + step * GROUP
        weight = jnp.where(order < listed, 1.0, 0.0).astype(jnp.float32)
        source_features(gathered, weight, left, charge_next)

    def products(step, u, held):
        shape = six_slots(left[u * ROWS : (u + 1) * ROWS, :], (0, 0, 0, 1, 1, 2))
        held[u % HALF] = lax.dot_general(
            shape, features[target_of(step, u)], TN, preferred_element_type=jnp.float32
        )

    def weights(u, held):
        near = held[u % HALF, :, :BLOCK]
        tilt = held[u % HALF, :, BLOCK:]
        q = lax.rsqrt(near)
        q2 = q * q
        q3 = q2 * q
        q5 = q3 * q2
        f = q3 + q5
        h = (q5 * tilt) * (q2 + 0.6)
        fh = f.astype(jnp.bfloat16)
        fl = (f - fh.astype(jnp.float32)).astype(jnp.bfloat16)
        hh = h.astype(jnp.bfloat16)
        hl = (h - hh.astype(jnp.float32)).astype(jnp.bfloat16)
        return jnp.concatenate(
            [jnp.concatenate([fh, fl], axis=1), jnp.concatenate([hh, hl], axis=1)], axis=0
        )

    def add_up(u, stacked):
        pair = charge[u * ROWS : (u + 1) * ROWS, :]
        high = rounded(pair)
        pair = jnp.concatenate([high, pair - high], axis=0).astype(jnp.bfloat16)
        blank = jnp.zeros_like(pair)
        pair = jnp.concatenate(
            [jnp.concatenate([pair, blank], axis=1), jnp.concatenate([blank, pair], axis=1)], axis=0
        )
        sums = jnp.dot(pair, stacked, preferred_element_type=jnp.float32)
        fsum = sums[0:8, :BLOCK] + sums[8:16, :BLOCK] + sums[0:8, BLOCK:]
        hsum = sums[16:24, :BLOCK] + sums[24:32, :BLOCK] + sums[16:24, BLOCK:]
        return jnp.concatenate([fsum, hsum], axis=0)

    def turn(step, carry):
        sums = []
        for u in range(HALF):
            stacked = weights(u, first_half)
            products(step, HALF + u, second_half)
            sums.append(add_up(u, stacked))
        prepare_sources(step + 1)
        for u in range(HALF, GROUP):
            stacked = weights(u, second_half)
            products(step + 1, u - HALF, first_half)
            sums.append(add_up(u, stacked))
        charge[...] = charge_next[...]
        for u in range(GROUP):
            total[tile_rows(target_of(step, u), 2 * ROWS), :] += sums[u]
        return carry

    @pl.when(listed > 0)
    def _():
        left[...] = jnp.zeros_like(left)
        charge_next[...] = jnp.zeros_like(charge_next)
        prepare_sources(0)
        for u in range(HALF):
            products(0, u, first_half)
        charge[...] = charge_next[...]
        lax.fori_loop(0, (listed + GROUP - 1) // GROUP, turn, 0)


def finish(targets, centres, totals, out_ref):
    blocks = out_ref.shape[1] // 6

    def one(step, carry):
        base = pl.multiple_of(step * GROUP * ROWS, GROUP * ROWS)
        wide = pl.multiple_of(step * GROUP * 2 * ROWS, GROUP * 2 * ROWS)
        pos = [
            component(targets, base, k, ROWS) - component(centres, base, k, ROWS) for k in range(3)
        ]
        strength = [component(targets, base, 3 + k, ROWS) for k in range(3)]
        fa, fb, ha, hb = [
            [
                sum(component(total, wide, start + k, 2 * ROWS) for total in totals)
                for k in range(3)
            ]
            for start in (0, 3, 8, 11)
        ]
        swirl = cross(pos, fa)
        lean = cross(strength, fa)
        bend = cross(pos, ha)
        member = step * GROUP // blocks
        inside = lax.rem(step * GROUP, blocks)
        for k in range(3):
            velocity = (-F_SCALE * biot_factor) * (swirl[k] - fb[k])
            stretch = (-F_SCALE * biot_factor) * lean[k] + (H_SCALE * biot_factor) * (bend[k] - hb[k])
            out_ref[member, pl.ds(pl.multiple_of(k * blocks + inside, GROUP), GROUP), :] = velocity
            out_ref[member, pl.ds(pl.multiple_of((3 + k) * blocks + inside, GROUP), GROUP), :] = stretch
        return carry

    lax.fori_loop(0, targets.shape[0] // ROWS // GROUP, one, 0, unroll=2)


def sort_list(number, own, length, sorted_list, blocks, members):
    rows = [own[b * ROWS + ROWS - 1 : (b + 1) * ROWS, :] for b in range(2 * length // BLOCK)]
    half = length // BLOCK
    t = jnp.concatenate(rows[:half], axis=1).astype(jnp.int32)
    s = jnp.concatenate(rows[half : 2 * half], axis=1).astype(jnp.int32)
    entry = lax.broadcasted_iota(jnp.int32, (1, length), 1)
    t = t - lax.axis_index("across") * blocks
    t = jnp.where(t < 0, t + members * blocks, t)
    run = s // blocks
    mine = t < blocks
    t = jnp.where(mine, t, t - blocks)
    near = (run == REACH) | (run == side_of_partner())
    kind = jnp.where(
        mine,
        jnp.where(near, 0, 4),
        jnp.where(near | (run == 0), 1, jnp.where(run == 2 * REACH, 2, 3)),
    )
    kind = jnp.where(entry < number, kind, CLASSES - 1)
    member = jnp.where(lax.broadcasted_iota(jnp.int32, (CLASSES, length), 0) == kind, 1.0, 0.0)
    row = lax.broadcasted_iota(jnp.int32, (length, length), 0)
    column = lax.broadcasted_iota(jnp.int32, (length, length), 1)
    before = jnp.where(row < column, 1.0, 0.0).astype(jnp.bfloat16)
    earlier = jnp.dot(member.astype(jnp.bfloat16), before, preferred_element_type=jnp.float32)
    rank = jnp.sum(member * earlier, axis=0, keepdims=True).astype(jnp.int32)
    place = jnp.where(row == rank, 1.0, 0.0).astype(jnp.bfloat16)
    values = [t // BLOCK, t % BLOCK, s // BLOCK, s % BLOCK]
    values = [member * value.astype(jnp.float32) for value in values]
    values = jnp.concatenate(values, axis=0).astype(jnp.bfloat16)
    found = lax.dot_general(values, place, NT, preferred_element_type=jnp.float32)
    number = jnp.broadcast_to(jnp.sum(member, axis=1, keepdims=True), (CLASSES, BLOCK))
    targets = found[0:8] * BLOCK + found[8:16]
    slots = found[16:24] * BLOCK + found[24:32]
    columns = [slice(j * BLOCK, (j + 1) * BLOCK) for j in range(length // BLOCK)]
    rows = sorted_list.shape[1]
    for kind in range(CLASSES - 1):
        one = slice(kind, kind + 1)
        parts = [targets[one, c] for c in columns] + [slots[one, c] for c in columns] + [number[one]]
        padding = rows - len(parts)
        if padding:
            parts.append(jnp.zeros((padding, BLOCK), jnp.float32))
        sorted_list[kind] = jnp.concatenate(parts, axis=0).astype(jnp.int32)


def list_rows(length):
    return 2 * (length // BLOCK) + 1


def read_list(kind, sorted_list, lists, sems):
    copy = pltpu.make_async_copy(sorted_list.at[kind, pl.ds(0, lists.shape[0])], lists, sems.at[0])
    copy.start()
    return copy


class shifted_window:
    def __init__(self, ref, start):
        self.ref, self.start = ref, start * ROWS

    def __getitem__(self, index):
        rows, lanes = index
        return self.ref[pl.ds(pl.multiple_of(rows.start - self.start, ROWS), rows.size), lanes]


def side_of_partner():
    return jnp.where(lax.axis_index("blk") % 2 == 0, REACH + 1, REACH - 1)


def home_kernel(number, own, partner, *refs, members, length):
    sorted_list, live, features, centres, total = refs[:5]
    window, near_rows, tilt_rows, lists, sems = refs[5:10]
    scratch = refs[10:]
    state = (live, features, centres, total)
    blocks = own.shape[0] // ROWS
    sort_list(number[0], own, length, sorted_list, blocks, members)
    to_scalars = read_list(0, sorted_list, lists, sems)
    put_tiles(live, 0, own, length)
    window[pl.ds(REACH * blocks * ROWS, blocks * ROWS), :] = live[...]
    put_tiles(window, side_of_partner() * blocks, partner, length)
    prepare_targets(state, near_rows, tilt_rows)
    to_scalars.wait()
    run_class(lists, window, state, scratch)


def near_kernel(sorted_list, live, partner, below, *refs, members, length):
    others, refs = refs[: members - 1], refs[members - 1 :]
    targets, features, centres, total = state = refs[:4]
    window, near_rows, tilt_rows, lists, sems = refs[4:9]
    scratch = refs[9:]
    to_scalars = read_list(1, sorted_list, lists, sems)
    blocks = live.shape[0] // ROWS
    window[pl.ds(REACH * blocks * ROWS, blocks * ROWS), :] = live[...]
    put_tiles(window, side_of_partner() * blocks, partner, length)
    put_tiles(window, 0, below, length)
    for r, other in enumerate(others):
        put_tiles(targets, r * blocks, other, length)
    prepare_targets(state, near_rows, tilt_rows)
    to_scalars.wait()
    run_class(lists, window, state, scratch)


def single_kernel(sorted_list, tiles, targets, features, centres, *refs, kind, run, length):
    total, window, lists, sems = refs[:4]
    to_scalars = read_list(kind, sorted_list, lists, sems)
    total[...] = jnp.zeros_like(total)
    put_tiles(window, 0, tiles, length)
    to_scalars.wait()
    window = shifted_window(window, run * (tiles.shape[0] // ROWS))
    run_class(lists, window, (targets, features, centres, total), refs[4:])


def far_kernel(sorted_list, below, above, crossed, *refs, length):
    targets, features, centres, near_total, middle_total = refs[:5]
    window, out_ref, total, lists, sems = refs[5:10]
    scratch = refs[10:]
    state = (targets, features, centres, total)
    to_scalars = read_list(3, sorted_list, lists, sems)
    blocks = below.shape[0] // ROWS
    put_tiles(window, 0, below, length)
    put_tiles(window, 2 * REACH * blocks, above, length)
    put_tiles(window, (2 * REACH - side_of_partner()) * blocks, crossed, length)
    total[...] = jnp.zeros_like(total)
    to_scalars.wait()
    run_class(lists, window, state, scratch)
    finish(targets, centres, (near_total, middle_total, total), out_ref)


def last_kernel(sorted_list, window, own, features, centres, *refs):
    home_total, out_ref, total, lists, sems = refs[:5]
    to_scalars = read_list(4, sorted_list, lists, sems)
    total[...] = jnp.zeros_like(total)
    to_scalars.wait()
    run_class(lists, window, (own, features, centres, total), refs[5:])
    finish(own, centres, (home_total, total), out_ref)


def section_kernel(own, sums, *refs):
    returned, (velocity, stretching, section_positions, section_strengths) = refs[:-4], refs[-4:]
    blocks = own.shape[0] // ROWS
    for b in range(blocks):
        lanes = slice(b * BLOCK, (b + 1) * BLOCK)
        for start, result, stepped in ((0, velocity, section_positions), (3, stretching, section_strengths)):
            chosen = pl.ds(start * blocks + b, 3, stride=blocks)
            value = sums[chosen, :]
            for other in returned:
                value = value + other[chosen, :]
            result[:, lanes] = value
            first = b * ROWS + start
            stepped[:, lanes] = own[first : first + 3, :] + section_step * value


def call(kernel, name, inputs, outputs, scratch, flops=0):
    vmem = pl.BlockSpec(memory_space=pltpu.VMEM)
    smem = pl.BlockSpec(memory_space=pltpu.SMEM)
    held = sum(value.size * value.dtype.itemsize for value in (*inputs, *outputs))
    return pl.pallas_call(
        kernel,
        out_shape=outputs,
        in_specs=[smem if value.dtype == jnp.int32 and value.ndim == 1 else vmem for value in inputs],
        out_specs=[vmem for value in outputs],
        scratch_shapes=scratch,
        compiler_params=pltpu.CompilerParams(vmem_limit_bytes=10 * 1024 * 1024 + 2 * held),
        cost_estimate=pl.CostEstimate(flops=flops, bytes_accessed=0, transcendentals=0),
        name=name,
    )(*inputs)


def shards(positions, strengths, radius, block_count, pair_target, pair_slot, pair_count):
    blocks = block_count.shape[0]
    lanes = blocks * BLOCK
    length = pair_target.shape[1]
    members = lax.axis_size("across")
    shard = lax.axis_index("blk")
    count = lax.axis_size("blk")

    def f32(*shape):
        return jax.ShapeDtypeStruct(shape, jnp.float32)

    parts = [value.reshape(3, blocks, BLOCK).transpose(1, 0, 2) for value in (positions, strengths)]
    rows, start = [], 0
    for value in (pair_target[0], pair_slot[0], block_count):
        rows.append(jnp.pad(value, (start, lanes - start - value.shape[0])))
        start += -(-value.shape[0] // BLOCK) * BLOCK
    listed = sum(rows).astype(jnp.float32).reshape(blocks, 1, BLOCK)
    own = jnp.concatenate(parts + [radius.reshape(blocks, 1, BLOCK), listed], axis=1)
    own = own.reshape(blocks * ROWS, BLOCK)
    others = [
        moved(own, "across", lambda source: (source - away) % members) for away in range(1, members)
    ]
    partner = moved(own, "blk", to_other_core)
    below = moved(own, "blk", shifted(REACH, count))

    def state_shapes(number):
        return [
            f32(number * blocks * ROWS, BLOCK),
            jax.ShapeDtypeStruct((number * blocks, FEATURES, 2 * BLOCK), jnp.bfloat16),
            f32(number * blocks * ROWS, BLOCK),
            f32(number * blocks * 2 * ROWS, BLOCK),
        ]

    own_shapes, other_shapes = state_shapes(1), state_shapes(members - 1)
    window_shape = f32((2 * REACH + 1) * blocks * ROWS, BLOCK)
    rows = list_rows(length)
    list_shape = jax.ShapeDtypeStruct((CLASSES - 1, -(-rows // ROWS) * ROWS, BLOCK), jnp.int32)
    feature_rows = [pltpu.VMEM((GROUP * ROWS, BLOCK), jnp.float32)] * 2
    list_scratch = [pltpu.SMEM((rows, BLOCK), jnp.int32), pltpu.SemaphoreType.DMA((1,))]
    scratch = [pltpu.VMEM((GROUP * ROWS, BLOCK), jnp.float32)] * 4 + [
        pltpu.VMEM((HALF, BLOCK, 2 * BLOCK), jnp.float32),
        pltpu.VMEM((HALF, BLOCK, 2 * BLOCK), jnp.float32),
    ]
    window_scratch = pltpu.VMEM(window_shape.shape, jnp.float32)

    lists, live, *own_state = call(
        lambda *refs: home_kernel(*refs, members=members, length=length),
        "home_pairs",
        (pair_count, own, partner),
        [list_shape] + own_shapes,
        [window_scratch] + feature_rows + list_scratch + scratch,
        flops=HOME_FLOPS,
    )
    late, lists = lax.optimization_barrier((own, lists))
    above = moved(late, "blk", shifted(-REACH, count))
    other_state = list(call(
        lambda *refs: near_kernel(*refs, members=members, length=length),
        "near_pairs",
        (lists, live, partner, below, *others),
        other_shapes,
        [window_scratch] + feature_rows + list_scratch + scratch,
        flops=NEAR_FLOPS,
    ))
    above, other_state[3] = lax.optimization_barrier((above, other_state[3]))
    crossed = moved(jnp.where(shard % 2 == 0, above, below), "blk", to_other_core)
    (middle_total,) = call(
        lambda *refs: single_kernel(*refs, kind=2, run=2 * REACH, length=length),
        "middle_pairs",
        (lists, above, *other_state[:3]),
        [other_shapes[3]],
        [pltpu.VMEM(own.shape, jnp.float32)] + list_scratch + scratch,
        flops=HOME_FLOPS,
    )
    crossed, middle_total = lax.optimization_barrier((crossed, middle_total))
    window, away_sums = call(
        lambda *refs: far_kernel(*refs, length=length),
        "far_pairs",
        (lists, below, above, crossed, *other_state, middle_total),
        [window_shape, f32(members - 1, 6 * blocks, BLOCK)],
        [pltpu.VMEM(other_shapes[3].shape, jnp.float32)] + list_scratch + scratch,
        flops=FAR_FLOPS,
    )
    returned = [
        moved(away_sums[away - 1], "across", lambda source: (source + away) % members)
        for away in range(1, members)
    ]
    (sums,) = call(
        last_kernel,
        "last_pairs",
        (lists, window, live, *own_state),
        [f32(1, 6 * blocks, BLOCK)],
        [pltpu.VMEM(own_shapes[3].shape, jnp.float32)] + list_scratch + scratch,
        flops=FAR_FLOPS,
    )
    wide = f32(3, lanes)
    return tuple(
        call(section_kernel, "section", (live, sums[0], *returned), [wide] * 4, [])
    )


def solution(mesh):
    whole = P(None, ("blk", "across"))
    line = P(("blk", "across"))
    return jax.shard_map(
        shards,
        mesh=mesh,
        in_specs=(whole, whole, line, line, P(("blk", "across"), None), P(("blk", "across"), None), line),
        out_specs=(whole, whole, whole, whole),
        check_vma=False,
    )
```

```python
import jax
import jax.numpy as jnp
from jax import lax
from jax.experimental import pallas as pl
from jax.experimental.pallas import tpu as pltpu
from jax.sharding import PartitionSpec as P

BLOCK = 128
ROWS = 8
REACH = 2
GROUP = 8
HALF = 4
FEATURES = 48
CLASSES = 8

F_SCALE = (2.0 / 3.0) ** 1.5
H_SCALE = 5.0 * (2.0 / 3.0) ** 2.5
biot_factor = 0.07957747154594767
section_step = 0.05


def moved(value, axis, target_of):
    pairs = [(source, target_of(source)) for source in range(lax.axis_size(axis))]
    return lax.ppermute(value, axis, pairs)


def to_other_core(source):
    return source ^ 1


def shifted(steps, count):
    return lambda source: (source + steps) % count


HOME_FLOPS = 10**10
NEAR_FLOPS = 10**10
FAR_FLOPS = 10**10


def rounded(value):
    return value.astype(jnp.bfloat16).astype(jnp.float32)


def split_three(value):
    first = rounded(value)
    rest = value - first
    second = rounded(rest)
    return first, second, rest - second


def six_slots(tile, order):
    parts = split_three(tile)
    return jnp.concatenate([parts[part] for part in order], axis=0).astype(jnp.bfloat16)


def cross(left, right):
    return [
        left[1] * right[2] - left[2] * right[1],
        left[2] * right[0] - left[0] * right[2],
        left[0] * right[1] - left[1] * right[0],
    ]


def tile_rows(index, rows):
    return pl.ds(pl.multiple_of(index * rows, rows), rows)


def component(ref, base, number, stride):
    return ref[pl.ds(base + number, GROUP, stride=stride), :]


def store_component(ref, base, number, stride, value):
    ref[pl.ds(base + number, GROUP, stride=stride), :] = value


def target_features(targets, step, centres, near_rows, tilt_rows):
    base = pl.multiple_of(step * (GROUP * ROWS), GROUP * ROWS)
    pos = [component(targets, base, k, ROWS) for k in range(3)]
    strength = [component(targets, base, 3 + k, ROWS) for k in range(3)]
    for k in range(3):
        centre = jnp.broadcast_to(jnp.mean(pos[k], axis=1, keepdims=True), (GROUP, BLOCK))
        store_component(centres, base, k, ROWS, centre)
        pos[k] = pos[k] - centre
    for k in range(3, ROWS):
        store_component(centres, base, k, ROWS, jnp.zeros_like(pos[0]))
    norm = pos[0] * pos[0] + pos[1] * pos[1] + pos[2] * pos[2]
    own = pos[0] * strength[0] + pos[1] * strength[1] + pos[2] * strength[2]
    near = [(2.0 / 3.0) * value for value in pos + [norm, jnp.ones_like(norm)]]
    tilt = [0.5 * s for s in strength] + [own]
    for rows, values in ((near_rows, near), (tilt_rows, tilt)):
        for k, value in enumerate(values):
            store_component(rows, 0, k, ROWS, value)


def source_features(gathered, weight, left, charge):
    pos = [component(gathered, 0, k, ROWS) for k in range(3)]
    strength = [component(gathered, 0, 3 + k, ROWS) for k in range(3)]
    inv_core = 1.0 / component(gathered, 0, 6, ROWS)
    inv_square = inv_core * inv_core
    norm = pos[0] * pos[0] + pos[1] * pos[1] + pos[2] * pos[2]
    twice = -2.0 * inv_square
    shape = [p * twice for p in pos] + [inv_square, norm * inv_square + 1.0]
    for k, value in enumerate(shape):
        store_component(left, 0, k, ROWS, value)
    scale = inv_square * inv_core * weight
    for k, value in enumerate(strength + cross(pos, strength)):
        store_component(charge, 0, k, ROWS, value * scale)


NT = (((1,), (1,)), ((), ()))
TN = (((0,), (0,)), ((), ()))


def put_tiles(window, first, tiles, length):
    base = pl.multiple_of(first * ROWS, ROWS)
    blocks = tiles.shape[0] // ROWS
    window[pl.ds(base, blocks * ROWS), :] = tiles[...]
    row = (2 * length // BLOCK + 1) * ROWS - 1
    counts = tiles[row : row + 1, :]
    row = lax.broadcasted_iota(jnp.int32, (blocks, BLOCK), 0)
    lane = lax.broadcasted_iota(jnp.int32, (blocks, BLOCK), 1)
    counts = jnp.sum(jnp.where(row == lane, counts, 0.0), axis=1, keepdims=True)
    alive = jnp.where(lane.astype(jnp.float32) < counts, 1.0, 0.0)
    for j in range(blocks // GROUP):
        part = alive[j * GROUP : (j + 1) * GROUP, :]
        for k in range(3, 6):
            rows = pl.ds(base + j * GROUP * ROWS + k, GROUP, stride=ROWS)
            window[rows, :] = window[rows, :] * part


def prepare_targets(state, near_rows, tilt_rows):
    targets, features, centres, total = state
    near_rows[...] = jnp.zeros_like(near_rows)
    tilt_rows[...] = jnp.zeros_like(tilt_rows)
    total[...] = jnp.zeros_like(total)

    def prepare(step, carry):
        target_features(targets, step, centres, near_rows, tilt_rows)
        for u in range(GROUP):
            rows = slice(u * ROWS, (u + 1) * ROWS)
            features[step * GROUP + u, :, :BLOCK] = six_slots(near_rows[rows, :], (0, 1, 2, 0, 1, 0))
            features[step * GROUP + u, :, BLOCK:] = six_slots(tilt_rows[rows, :], (0, 1, 2, 0, 1, 0))
        return carry

    lax.fori_loop(0, features.shape[0] // GROUP, prepare, 0)


def run_class(lists, window, state, scratch):
    _, features, centres, total = state
    gathered, left, charge_next, charge, first_half, second_half = scratch
    slot_row = (lists.shape[0] - 1) // 2
    listed = lists[2 * slot_row, 0]

    def entry_at(step, u):
        entry = jnp.minimum(step * GROUP + u, listed - 1)
        return entry // BLOCK, lax.rem(entry, BLOCK)

    def target_of(step, u):
        row, column = entry_at(step, u)
        return lists[row, column]

    def prepare_sources(step):
        for u in range(GROUP):
            row, column = entry_at(step, u)
            gathered[u * ROWS : (u + 1) * ROWS, :] = (
                window[tile_rows(lists[row + slot_row, column], ROWS), :]
                - centres[tile_rows(lists[row, column], ROWS), :]
            )
        order = lax.broadcasted_iota(jnp.int32, (GROUP, BLOCK), 0) + step * GROUP
        weight = jnp.where(order < listed, 1.0, 0.0).astype(jnp.float32)
        source_features(gathered, weight, left, charge_next)

    def products(step, u, held):
        shape = six_slots(left[u * ROWS : (u + 1) * ROWS, :], (0, 0, 0, 1, 1, 2))
        held[u % HALF] = lax.dot_general(
            shape, features[target_of(step, u)], TN, preferred_element_type=jnp.float32
        )

    def weights(u, held):
        near = held[u % HALF, :, :BLOCK]
        tilt = held[u % HALF, :, BLOCK:]
        q = lax.rsqrt(near)
        q2 = q * q
        q3 = q2 * q
        q5 = q3 * q2
        f = q3 + q5
        h = (q5 * tilt) * (q2 + 0.6)
        fh = f.astype(jnp.bfloat16)
        fl = (f - fh.astype(jnp.float32)).astype(jnp.bfloat16)
        hh = h.astype(jnp.bfloat16)
        hl = (h - hh.astype(jnp.float32)).astype(jnp.bfloat16)
        return jnp.concatenate(
            [jnp.concatenate([fh, fl], axis=1), jnp.concatenate([hh, hl], axis=1)], axis=0
        )

    def add_up(u, stacked):
        pair = charge[u * ROWS : (u + 1) * ROWS, :]
        high = rounded(pair)
        pair = jnp.concatenate([high, pair - high], axis=0).astype(jnp.bfloat16)
        blank = jnp.zeros_like(pair)
        pair = jnp.concatenate(
            [jnp.concatenate([pair, blank], axis=1), jnp.concatenate([blank, pair], axis=1)], axis=0
        )
        sums = jnp.dot(pair, stacked, preferred_element_type=jnp.float32)
        fsum = sums[0:8, :BLOCK] + sums[8:16, :BLOCK] + sums[0:8, BLOCK:]
        hsum = sums[16:24, :BLOCK] + sums[24:32, :BLOCK] + sums[16:24, BLOCK:]
        return jnp.concatenate([fsum, hsum], axis=0)

    def turn(step, carry):
        sums = []
        for u in range(HALF):
            stacked = weights(u, first_half)
            products(step, HALF + u, second_half)
            sums.append(add_up(u, stacked))
        prepare_sources(step + 1)
        for u in range(HALF, GROUP):
            stacked = weights(u, second_half)
            products(step + 1, u - HALF, first_half)
            sums.append(add_up(u, stacked))
        charge[...] = charge_next[...]
        for u in range(GROUP):
            total[tile_rows(target_of(step, u), 2 * ROWS), :] += sums[u]
        return carry

    @pl.when(listed > 0)
    def _():
        left[...] = jnp.zeros_like(left)
        charge_next[...] = jnp.zeros_like(charge_next)
        prepare_sources(0)
        for u in range(HALF):
            products(0, u, first_half)
        charge[...] = charge_next[...]
        full = (listed + HALF - 1) // GROUP
        lax.fori_loop(0, full, turn, 0)

        @pl.when(listed > full * GROUP)
        def _():
            sums = [add_up(u, weights(u, first_half)) for u in range(HALF)]
            for u in range(HALF):
                total[tile_rows(target_of(full, u), 2 * ROWS), :] += sums[u]


def finish(targets, centres, totals, out_ref):
    blocks = out_ref.shape[1] // 6

    def one(step, carry):
        base = pl.multiple_of(step * GROUP * ROWS, GROUP * ROWS)
        wide = pl.multiple_of(step * GROUP * 2 * ROWS, GROUP * 2 * ROWS)
        pos = [
            component(targets, base, k, ROWS) - component(centres, base, k, ROWS) for k in range(3)
        ]
        strength = [component(targets, base, 3 + k, ROWS) for k in range(3)]
        fa, fb, ha, hb = [
            [
                sum(component(total, wide, start + k, 2 * ROWS) for total in totals)
                for k in range(3)
            ]
            for start in (0, 3, 8, 11)
        ]
        swirl = cross(pos, fa)
        lean = cross(strength, fa)
        bend = cross(pos, ha)
        member = step * GROUP // blocks
        inside = lax.rem(step * GROUP, blocks)
        for k in range(3):
            velocity = (-F_SCALE * biot_factor) * (swirl[k] - fb[k])
            stretch = (-F_SCALE * biot_factor) * lean[k] + (H_SCALE * biot_factor) * (bend[k] - hb[k])
            out_ref[member, pl.ds(pl.multiple_of(k * blocks + inside, GROUP), GROUP), :] = velocity
            out_ref[member, pl.ds(pl.multiple_of((3 + k) * blocks + inside, GROUP), GROUP), :] = stretch
        return carry

    lax.fori_loop(0, targets.shape[0] // ROWS // GROUP, one, 0, unroll=2)


def sort_list(number, own, length, sorted_list, blocks, members):
    rows = [own[b * ROWS + ROWS - 1 : (b + 1) * ROWS, :] for b in range(2 * length // BLOCK)]
    half = length // BLOCK
    t = jnp.concatenate(rows[:half], axis=1).astype(jnp.int32)
    s = jnp.concatenate(rows[half : 2 * half], axis=1).astype(jnp.int32)
    entry = lax.broadcasted_iota(jnp.int32, (1, length), 1)
    t = t - lax.axis_index("across") * blocks
    t = jnp.where(t < 0, t + members * blocks, t)
    run = s // blocks
    mine = t < blocks
    t = jnp.where(mine, t, t - blocks)
    near = (run == REACH) | (run == side_of_partner())
    kind = jnp.where(
        mine,
        jnp.where(near, 0, jnp.where(run == 0, 5, 4)),
        jnp.where(near | (run == 0), 1, jnp.where(run == 2 * REACH, 2, 3)),
    )
    kind = jnp.where(entry < number, kind, CLASSES - 1)
    member = jnp.where(lax.broadcasted_iota(jnp.int32, (CLASSES, length), 0) == kind, 1.0, 0.0)
    row = lax.broadcasted_iota(jnp.int32, (length, length), 0)
    column = lax.broadcasted_iota(jnp.int32, (length, length), 1)
    before = jnp.where(row < column, 1.0, 0.0).astype(jnp.bfloat16)
    earlier = jnp.dot(member.astype(jnp.bfloat16), before, preferred_element_type=jnp.float32)
    rank = jnp.sum(member * earlier, axis=0, keepdims=True).astype(jnp.int32)
    place = jnp.where(row == rank, 1.0, 0.0).astype(jnp.bfloat16)
    values = [t // BLOCK, t % BLOCK, s // BLOCK, s % BLOCK]
    values = [member * value.astype(jnp.float32) for value in values]
    values = jnp.concatenate(values, axis=0).astype(jnp.bfloat16)
    found = lax.dot_general(values, place, NT, preferred_element_type=jnp.float32)
    number = jnp.broadcast_to(jnp.sum(member, axis=1, keepdims=True), (CLASSES, BLOCK))
    targets = found[0:8] * BLOCK + found[8:16]
    slots = found[16:24] * BLOCK + found[24:32]
    columns = [slice(j * BLOCK, (j + 1) * BLOCK) for j in range(length // BLOCK)]
    rows = sorted_list.shape[1]
    for kind in range(CLASSES - 1):
        one = slice(kind, kind + 1)
        parts = [targets[one, c] for c in columns] + [slots[one, c] for c in columns] + [number[one]]
        padding = rows - len(parts)
        if padding:
            parts.append(jnp.zeros((padding, BLOCK), jnp.float32))
        sorted_list[kind] = jnp.concatenate(parts, axis=0).astype(jnp.int32)


def list_rows(length):
    return 2 * (length // BLOCK) + 1


def read_list(kind, sorted_list, lists, sems):
    copy = pltpu.make_async_copy(sorted_list.at[kind, pl.ds(0, lists.shape[0])], lists, sems.at[0])
    copy.start()
    return copy


class shifted_window:
    def __init__(self, ref, start):
        self.ref, self.start = ref, start * ROWS

    def __getitem__(self, index):
        rows, lanes = index
        return self.ref[pl.ds(pl.multiple_of(rows.start - self.start, ROWS), rows.size), lanes]


def side_of_partner():
    return jnp.where(lax.axis_index("blk") % 2 == 0, REACH + 1, REACH - 1)


def home_kernel(number, own, partner, *refs, members, length):
    sorted_list, live, features, centres, total = refs[:5]
    window, near_rows, tilt_rows, lists, sems = refs[5:10]
    scratch = refs[10:]
    state = (live, features, centres, total)
    blocks = own.shape[0] // ROWS
    sort_list(number[0], own, length, sorted_list, blocks, members)
    to_scalars = read_list(0, sorted_list, lists, sems)
    put_tiles(live, 0, own, length)
    window[pl.ds(REACH * blocks * ROWS, blocks * ROWS), :] = live[...]
    put_tiles(window, side_of_partner() * blocks, partner, length)
    prepare_targets(state, near_rows, tilt_rows)
    to_scalars.wait()
    run_class(lists, window, state, scratch)


def near_kernel(sorted_list, live, partner, below, *refs, members, length):
    others, refs = refs[: members - 1], refs[members - 1 :]
    own_features, own_centres = refs[:2]
    targets, features, centres, total = state = refs[2:6]
    own_total, window, near_rows, tilt_rows, own_lists, own_sems, lists, sems = refs[6:14]
    scratch = refs[14:]
    to_scalars = read_list(1, sorted_list, lists, sems)
    own_to_scalars = read_list(5, sorted_list, own_lists, own_sems)
    blocks = live.shape[0] // ROWS
    own_total[...] = jnp.zeros_like(own_total)
    window[pl.ds(REACH * blocks * ROWS, blocks * ROWS), :] = live[...]
    put_tiles(window, side_of_partner() * blocks, partner, length)
    put_tiles(window, 0, below, length)
    for r, other in enumerate(others):
        put_tiles(targets, r * blocks, other, length)
    prepare_targets(state, near_rows, tilt_rows)
    to_scalars.wait()
    run_class(lists, window, state, scratch)
    own_to_scalars.wait()
    run_class(own_lists, window, (live, own_features, own_centres, own_total), scratch)


def single_kernel(sorted_list, tiles, targets, features, centres, *refs, kind, run, length):
    total, window, lists, sems = refs[:4]
    to_scalars = read_list(kind, sorted_list, lists, sems)
    total[...] = jnp.zeros_like(total)
    put_tiles(window, 0, tiles, length)
    to_scalars.wait()
    window = shifted_window(window, run * (tiles.shape[0] // ROWS))
    run_class(lists, window, (targets, features, centres, total), refs[4:])


def far_kernel(sorted_list, below, above, crossed, *refs, length):
    targets, features, centres, near_total, middle_total = refs[:5]
    window, out_ref, total, lists, sems = refs[5:10]
    scratch = refs[10:]
    state = (targets, features, centres, total)
    to_scalars = read_list(3, sorted_list, lists, sems)
    blocks = below.shape[0] // ROWS
    put_tiles(window, 0, below, length)
    put_tiles(window, 2 * REACH * blocks, above, length)
    put_tiles(window, (2 * REACH - side_of_partner()) * blocks, crossed, length)
    total[...] = jnp.zeros_like(total)
    to_scalars.wait()
    run_class(lists, window, state, scratch)
    finish(targets, centres, (near_total, middle_total, total), out_ref)


def last_kernel(sorted_list, window, own, features, centres, *refs):
    home_total, near_total, out_ref, total, lists, sems = refs[:6]
    to_scalars = read_list(4, sorted_list, lists, sems)
    total[...] = jnp.zeros_like(total)
    to_scalars.wait()
    run_class(lists, window, (own, features, centres, total), refs[6:])
    finish(own, centres, (home_total, near_total, total), out_ref)


def section_kernel(own, sums, *refs):
    returned, (velocity, stretching, section_positions, section_strengths) = refs[:-4], refs[-4:]
    blocks = own.shape[0] // ROWS
    for b in range(blocks):
        lanes = slice(b * BLOCK, (b + 1) * BLOCK)
        for start, result, stepped in ((0, velocity, section_positions), (3, stretching, section_strengths)):
            chosen = pl.ds(start * blocks + b, 3, stride=blocks)
            value = sums[chosen, :]
            for other in returned:
                value = value + other[chosen, :]
            result[:, lanes] = value
            first = b * ROWS + start
            stepped[:, lanes] = own[first : first + 3, :] + section_step * value


def call(kernel, name, inputs, outputs, scratch, flops=0):
    vmem = pl.BlockSpec(memory_space=pltpu.VMEM)
    smem = pl.BlockSpec(memory_space=pltpu.SMEM)
    held = sum(value.size * value.dtype.itemsize for value in (*inputs, *outputs))
    return pl.pallas_call(
        kernel,
        out_shape=outputs,
        in_specs=[smem if value.dtype == jnp.int32 and value.ndim == 1 else vmem for value in inputs],
        out_specs=[vmem for value in outputs],
        scratch_shapes=scratch,
        compiler_params=pltpu.CompilerParams(vmem_limit_bytes=10 * 1024 * 1024 + 2 * held),
        cost_estimate=pl.CostEstimate(flops=flops, bytes_accessed=0, transcendentals=0),
        name=name,
    )(*inputs)


def shards(positions, strengths, radius, block_count, pair_target, pair_slot, pair_count):
    blocks = block_count.shape[0]
    lanes = blocks * BLOCK
    length = pair_target.shape[1]
    members = lax.axis_size("across")
    shard = lax.axis_index("blk")
    count = lax.axis_size("blk")

    def f32(*shape):
        return jax.ShapeDtypeStruct(shape, jnp.float32)

    parts = [value.reshape(3, blocks, BLOCK).transpose(1, 0, 2) for value in (positions, strengths)]
    rows, start = [], 0
    for value in (pair_target[0], pair_slot[0], block_count):
        rows.append(jnp.pad(value, (start, lanes - start - value.shape[0])))
        start += -(-value.shape[0] // BLOCK) * BLOCK
    listed = sum(rows).astype(jnp.float32).reshape(blocks, 1, BLOCK)
    own = jnp.concatenate(parts + [radius.reshape(blocks, 1, BLOCK), listed], axis=1)
    own = own.reshape(blocks * ROWS, BLOCK)
    others = [
        moved(own, "across", lambda source: (source - away) % members) for away in range(1, members)
    ]
    partner = moved(own, "blk", to_other_core)
    below = moved(own, "blk", shifted(REACH, count))

    def state_shapes(number):
        return [
            f32(number * blocks * ROWS, BLOCK),
            jax.ShapeDtypeStruct((number * blocks, FEATURES, 2 * BLOCK), jnp.bfloat16),
            f32(number * blocks * ROWS, BLOCK),
            f32(number * blocks * 2 * ROWS, BLOCK),
        ]

    own_shapes, other_shapes = state_shapes(1), state_shapes(members - 1)
    window_shape = f32((2 * REACH + 1) * blocks * ROWS, BLOCK)
    rows = list_rows(length)
    list_shape = jax.ShapeDtypeStruct((CLASSES - 1, -(-rows // ROWS) * ROWS, BLOCK), jnp.int32)
    feature_rows = [pltpu.VMEM((GROUP * ROWS, BLOCK), jnp.float32)] * 2
    list_scratch = [pltpu.SMEM((rows, BLOCK), jnp.int32), pltpu.SemaphoreType.DMA((1,))]
    scratch = [pltpu.VMEM((GROUP * ROWS, BLOCK), jnp.float32)] * 4 + [
        pltpu.VMEM((HALF, BLOCK, 2 * BLOCK), jnp.float32),
        pltpu.VMEM((HALF, BLOCK, 2 * BLOCK), jnp.float32),
    ]
    window_scratch = pltpu.VMEM(window_shape.shape, jnp.float32)

    lists, live, *own_state = call(
        lambda *refs: home_kernel(*refs, members=members, length=length),
        "home_pairs",
        (pair_count, own, partner),
        [list_shape] + own_shapes,
        [window_scratch] + feature_rows + list_scratch + scratch,
        flops=HOME_FLOPS,
    )
    late, lists = lax.optimization_barrier((own, lists))
    above = moved(late, "blk", shifted(-REACH, count))
    *other_state, near_own_total = list(call(
        lambda *refs: near_kernel(*refs, members=members, length=length),
        "near_pairs",
        (lists, live, partner, below, *others, *own_state[:2]),
        other_shapes + [own_shapes[3]],
        [window_scratch] + feature_rows + 2 * list_scratch + scratch,
        flops=NEAR_FLOPS,
    ))
    above, other_state[3] = lax.optimization_barrier((above, other_state[3]))
    crossed = moved(jnp.where(shard % 2 == 0, above, below), "blk", to_other_core)
    (middle_total,) = call(
        lambda *refs: single_kernel(*refs, kind=2, run=2 * REACH, length=length),
        "middle_pairs",
        (lists, above, *other_state[:3]),
        [other_shapes[3]],
        [pltpu.VMEM(own.shape, jnp.float32)] + list_scratch + scratch,
        flops=HOME_FLOPS,
    )
    crossed, middle_total = lax.optimization_barrier((crossed, middle_total))
    window, away_sums = call(
        lambda *refs: far_kernel(*refs, length=length),
        "far_pairs",
        (lists, below, above, crossed, *other_state, middle_total),
        [window_shape, f32(members - 1, 6 * blocks, BLOCK)],
        [pltpu.VMEM(other_shapes[3].shape, jnp.float32)] + list_scratch + scratch,
        flops=FAR_FLOPS,
    )
    returned = [
        moved(away_sums[away - 1], "across", lambda source: (source + away) % members)
        for away in range(1, members)
    ]
    (sums,) = call(
        last_kernel,
        "last_pairs",
        (lists, window, live, *own_state, near_own_total),
        [f32(1, 6 * blocks, BLOCK)],
        [pltpu.VMEM(own_shapes[3].shape, jnp.float32)] + list_scratch + scratch,
        flops=FAR_FLOPS,
    )
    wide = f32(3, lanes)
    return tuple(
        call(section_kernel, "section", (live, sums[0], *returned), [wide] * 4, [])
    )


def solution(mesh):
    whole = P(None, ("blk", "across"))
    line = P(("blk", "across"))
    return jax.shard_map(
        shards,
        mesh=mesh,
        in_specs=(whole, whole, line, line, P(("blk", "across"), None), P(("blk", "across"), None), line),
        out_specs=(whole, whole, whole, whole),
        check_vma=False,
    )
```

```python
import jax
import jax.numpy as jnp
from jax import lax
from jax.experimental import pallas as pl
from jax.experimental.pallas import tpu as pltpu
from jax.sharding import PartitionSpec as P

BLOCK = 128
ROWS = 8
REACH = 2
GROUP = 8
HALF = 4
FEATURES = 48
CLASSES = 8

F_SCALE = (2.0 / 3.0) ** 1.5
H_SCALE = 5.0 * (2.0 / 3.0) ** 2.5
biot_factor = 0.07957747154594767
section_step = 0.05


def moved(value, axis, target_of):
    pairs = [(source, target_of(source)) for source in range(lax.axis_size(axis))]
    return lax.ppermute(value, axis, pairs)


def to_other_core(source):
    return source ^ 1


def shifted(steps, count):
    return lambda source: (source + steps) % count


HOME_FLOPS = 10**10
NEAR_FLOPS = 10**10
FAR_FLOPS = 10**10


def rounded(value):
    return value.astype(jnp.bfloat16).astype(jnp.float32)


def split_three(value):
    first = rounded(value)
    rest = value - first
    second = rounded(rest)
    return first, second, rest - second


def six_slots(tile, order):
    parts = split_three(tile)
    return jnp.concatenate([parts[part] for part in order], axis=0).astype(jnp.bfloat16)


def cross(left, right):
    return [
        left[1] * right[2] - left[2] * right[1],
        left[2] * right[0] - left[0] * right[2],
        left[0] * right[1] - left[1] * right[0],
    ]


def tile_rows(index, rows):
    return pl.ds(pl.multiple_of(index * rows, rows), rows)


def component(ref, base, number, stride):
    return ref[pl.ds(base + number, GROUP, stride=stride), :]


def store_component(ref, base, number, stride, value):
    ref[pl.ds(base + number, GROUP, stride=stride), :] = value


def target_features(targets, step, centres, near_rows, tilt_rows):
    base = pl.multiple_of(step * (GROUP * ROWS), GROUP * ROWS)
    pos = [component(targets, base, k, ROWS) for k in range(3)]
    strength = [component(targets, base, 3 + k, ROWS) for k in range(3)]
    for k in range(3):
        centre = jnp.broadcast_to(jnp.mean(pos[k], axis=1, keepdims=True), (GROUP, BLOCK))
        store_component(centres, base, k, ROWS, centre)
        pos[k] = pos[k] - centre
    for k in range(3, ROWS):
        store_component(centres, base, k, ROWS, jnp.zeros_like(pos[0]))
    norm = pos[0] * pos[0] + pos[1] * pos[1] + pos[2] * pos[2]
    own = pos[0] * strength[0] + pos[1] * strength[1] + pos[2] * strength[2]
    near = [(2.0 / 3.0) * value for value in pos + [norm, jnp.ones_like(norm)]]
    tilt = [0.5 * s for s in strength] + [own]
    for rows, values in ((near_rows, near), (tilt_rows, tilt)):
        for k, value in enumerate(values):
            store_component(rows, 0, k, ROWS, value)


def source_features(gathered, weight, left, charge):
    pos = [component(gathered, 0, k, ROWS) for k in range(3)]
    strength = [component(gathered, 0, 3 + k, ROWS) for k in range(3)]
    inv_core = 1.0 / component(gathered, 0, 6, ROWS)
    inv_square = inv_core * inv_core
    norm = pos[0] * pos[0] + pos[1] * pos[1] + pos[2] * pos[2]
    twice = -2.0 * inv_square
    shape = [p * twice for p in pos] + [inv_square, norm * inv_square + 1.0]
    for k, value in enumerate(shape):
        store_component(left, 0, k, ROWS, value)
    scale = inv_square * inv_core * weight
    for k, value in enumerate(strength + cross(pos, strength)):
        store_component(charge, 0, k, ROWS, value * scale)


NT = (((1,), (1,)), ((), ()))
TN = (((0,), (0,)), ((), ()))


def put_tiles(window, first, tiles, length):
    base = pl.multiple_of(first * ROWS, ROWS)
    blocks = tiles.shape[0] // ROWS
    window[pl.ds(base, blocks * ROWS), :] = tiles[...]
    row = (2 * length // BLOCK + 1) * ROWS - 1
    counts = tiles[row : row + 1, :]
    row = lax.broadcasted_iota(jnp.int32, (blocks, BLOCK), 0)
    lane = lax.broadcasted_iota(jnp.int32, (blocks, BLOCK), 1)
    counts = jnp.sum(jnp.where(row == lane, counts, 0.0), axis=1, keepdims=True)
    alive = jnp.where(lane.astype(jnp.float32) < counts, 1.0, 0.0)
    for j in range(blocks // GROUP):
        part = alive[j * GROUP : (j + 1) * GROUP, :]
        for k in range(3, 6):
            rows = pl.ds(base + j * GROUP * ROWS + k, GROUP, stride=ROWS)
            window[rows, :] = window[rows, :] * part


def prepare_targets(state, near_rows, tilt_rows):
    targets, features, centres, total = state
    near_rows[...] = jnp.zeros_like(near_rows)
    tilt_rows[...] = jnp.zeros_like(tilt_rows)
    total[...] = jnp.zeros_like(total)

    def prepare(step, carry):
        target_features(targets, step, centres, near_rows, tilt_rows)
        for u in range(GROUP):
            rows = slice(u * ROWS, (u + 1) * ROWS)
            features[step * GROUP + u, :, :BLOCK] = six_slots(near_rows[rows, :], (0, 1, 2, 0, 1, 0))
            features[step * GROUP + u, :, BLOCK:] = six_slots(tilt_rows[rows, :], (0, 1, 2, 0, 1, 0))
        return carry

    lax.fori_loop(0, features.shape[0] // GROUP, prepare, 0)


def run_class(lists, window, state, scratch):
    _, features, centres, total = state
    gathered, left, charge_next, charge, first_half, second_half = scratch
    slot_row = (lists.shape[0] - 1) // 2
    listed = lists[2 * slot_row, 0]

    def entry_at(step, u):
        entry = jnp.minimum(step * GROUP + u, listed - 1)
        return entry // BLOCK, lax.rem(entry, BLOCK)

    def target_of(step, u):
        row, column = entry_at(step, u)
        return lists[row, column]

    def prepare_sources(step):
        for u in range(GROUP):
            row, column = entry_at(step, u)
            gathered[u * ROWS : (u + 1) * ROWS, :] = (
                window[tile_rows(lists[row + slot_row, column], ROWS), :]
                - centres[tile_rows(lists[row, column], ROWS), :]
            )
        order = lax.broadcasted_iota(jnp.int32, (GROUP, BLOCK), 0) + step * GROUP
        weight = jnp.where(order < listed, 1.0, 0.0).astype(jnp.float32)
        source_features(gathered, weight, left, charge_next)

    def products(step, u, held):
        shape = six_slots(left[u * ROWS : (u + 1) * ROWS, :], (0, 0, 0, 1, 1, 2))
        held[u % HALF] = lax.dot_general(
            shape, features[target_of(step, u)], TN, preferred_element_type=jnp.float32
        )

    def weights(u, held):
        near = held[u % HALF, :, :BLOCK]
        tilt = held[u % HALF, :, BLOCK:]
        q = lax.rsqrt(near)
        q2 = q * q
        q3 = q2 * q
        q5 = q3 * q2
        f = q3 + q5
        h = (q5 * tilt) * (q2 + 0.6)
        fh = f.astype(jnp.bfloat16)
        fl = (f - fh.astype(jnp.float32)).astype(jnp.bfloat16)
        hh = h.astype(jnp.bfloat16)
        hl = (h - hh.astype(jnp.float32)).astype(jnp.bfloat16)
        return jnp.concatenate(
            [jnp.concatenate([fh, fl], axis=1), jnp.concatenate([hh, hl], axis=1)], axis=0
        )

    def add_up(u, stacked):
        pair = charge[u * ROWS : (u + 1) * ROWS, :]
        high = rounded(pair)
        pair = jnp.concatenate([high, pair - high], axis=0).astype(jnp.bfloat16)
        blank = jnp.zeros_like(pair)
        pair = jnp.concatenate(
            [jnp.concatenate([pair, blank], axis=1), jnp.concatenate([blank, pair], axis=1)], axis=0
        )
        sums = jnp.dot(pair, stacked, preferred_element_type=jnp.float32)
        fsum = sums[0:8, :BLOCK] + sums[8:16, :BLOCK] + sums[0:8, BLOCK:]
        hsum = sums[16:24, :BLOCK] + sums[24:32, :BLOCK] + sums[16:24, BLOCK:]
        return jnp.concatenate([fsum, hsum], axis=0)

    def turn(step, carry):
        sums = []
        for u in range(HALF):
            stacked = weights(u, first_half)
            products(step, HALF + u, second_half)
            sums.append(add_up(u, stacked))
        prepare_sources(step + 1)
        for u in range(HALF, GROUP):
            stacked = weights(u, second_half)
            products(step + 1, u - HALF, first_half)
            sums.append(add_up(u, stacked))
        charge[...] = charge_next[...]
        for u in range(GROUP):
            total[tile_rows(target_of(step, u), 2 * ROWS), :] += sums[u]
        return carry

    @pl.when(listed > 0)
    def _():
        left[...] = jnp.zeros_like(left)
        charge_next[...] = jnp.zeros_like(charge_next)
        prepare_sources(0)
        for u in range(HALF):
            products(0, u, first_half)
        charge[...] = charge_next[...]
        full = (listed + HALF - 1) // GROUP
        lax.fori_loop(0, full, turn, 0)

        @pl.when(listed > full * GROUP)
        def _():
            sums = [add_up(u, weights(u, first_half)) for u in range(HALF)]
            for u in range(HALF):
                total[tile_rows(target_of(full, u), 2 * ROWS), :] += sums[u]


def finish(targets, centres, totals, out_ref):
    blocks = out_ref.shape[1] // 6

    def one(step, carry):
        base = pl.multiple_of(step * GROUP * ROWS, GROUP * ROWS)
        wide = pl.multiple_of(step * GROUP * 2 * ROWS, GROUP * 2 * ROWS)
        pos = [
            component(targets, base, k, ROWS) - component(centres, base, k, ROWS) for k in range(3)
        ]
        strength = [component(targets, base, 3 + k, ROWS) for k in range(3)]
        fa, fb, ha, hb = [
            [
                sum(component(total, wide, start + k, 2 * ROWS) for total in totals)
                for k in range(3)
            ]
            for start in (0, 3, 8, 11)
        ]
        swirl = cross(pos, fa)
        lean = cross(strength, fa)
        bend = cross(pos, ha)
        member = step * GROUP // blocks
        inside = lax.rem(step * GROUP, blocks)
        for k in range(3):
            velocity = (-F_SCALE * biot_factor) * (swirl[k] - fb[k])
            stretch = (-F_SCALE * biot_factor) * lean[k] + (H_SCALE * biot_factor) * (bend[k] - hb[k])
            out_ref[member, pl.ds(pl.multiple_of(k * blocks + inside, GROUP), GROUP), :] = velocity
            out_ref[member, pl.ds(pl.multiple_of((3 + k) * blocks + inside, GROUP), GROUP), :] = stretch
        return carry

    lax.fori_loop(0, targets.shape[0] // ROWS // GROUP, one, 0, unroll=2)


def sort_list(number, own, length, sorted_list, blocks, members):
    rows = [own[b * ROWS + ROWS - 1 : (b + 1) * ROWS, :] for b in range(2 * length // BLOCK)]
    half = length // BLOCK
    t = jnp.concatenate(rows[:half], axis=1).astype(jnp.int32)
    s = jnp.concatenate(rows[half : 2 * half], axis=1).astype(jnp.int32)
    entry = lax.broadcasted_iota(jnp.int32, (1, length), 1)
    t = t - lax.axis_index("across") * blocks
    t = jnp.where(t < 0, t + members * blocks, t)
    run = s // blocks
    mine = t < blocks
    t = jnp.where(mine, t, t - blocks)
    near = (run == REACH) | (run == side_of_partner())
    kind = jnp.where(
        mine,
        jnp.where(near, 0, jnp.where(run == 0, 5, 4)),
        jnp.where(near, 1, jnp.where(run == 0, 6, jnp.where(run == 2 * REACH, 2, 3))),
    )
    kind = jnp.where(entry < number, kind, CLASSES - 1)
    member = jnp.where(lax.broadcasted_iota(jnp.int32, (CLASSES, length), 0) == kind, 1.0, 0.0)
    row = lax.broadcasted_iota(jnp.int32, (length, length), 0)
    column = lax.broadcasted_iota(jnp.int32, (length, length), 1)
    before = jnp.where(row < column, 1.0, 0.0).astype(jnp.bfloat16)
    earlier = jnp.dot(member.astype(jnp.bfloat16), before, preferred_element_type=jnp.float32)
    rank = jnp.sum(member * earlier, axis=0, keepdims=True).astype(jnp.int32)
    place = jnp.where(row == rank, 1.0, 0.0).astype(jnp.bfloat16)
    values = [t // BLOCK, t % BLOCK, s // BLOCK, s % BLOCK]
    values = [member * value.astype(jnp.float32) for value in values]
    values = jnp.concatenate(values, axis=0).astype(jnp.bfloat16)
    found = lax.dot_general(values, place, NT, preferred_element_type=jnp.float32)
    number = jnp.broadcast_to(jnp.sum(member, axis=1, keepdims=True), (CLASSES, BLOCK))
    targets = found[0:8] * BLOCK + found[8:16]
    slots = found[16:24] * BLOCK + found[24:32]
    columns = [slice(j * BLOCK, (j + 1) * BLOCK) for j in range(length // BLOCK)]
    rows = sorted_list.shape[1]
    for kind in range(CLASSES - 1):
        one = slice(kind, kind + 1)
        parts = [targets[one, c] for c in columns] + [slots[one, c] for c in columns] + [number[one]]
        padding = rows - len(parts)
        if padding:
            parts.append(jnp.zeros((padding, BLOCK), jnp.float32))
        sorted_list[kind] = jnp.concatenate(parts, axis=0).astype(jnp.int32)


def list_rows(length):
    return 2 * (length // BLOCK) + 1


def read_list(kind, sorted_list, lists, sems):
    copy = pltpu.make_async_copy(sorted_list.at[kind, pl.ds(0, lists.shape[0])], lists, sems.at[0])
    copy.start()
    return copy


class shifted_window:
    def __init__(self, ref, start):
        self.ref, self.start = ref, start * ROWS

    def __getitem__(self, index):
        rows, lanes = index
        return self.ref[pl.ds(pl.multiple_of(rows.start - self.start, ROWS), rows.size), lanes]


def side_of_partner():
    return jnp.where(lax.axis_index("blk") % 2 == 0, REACH + 1, REACH - 1)


def home_kernel(number, own, partner, *refs, members, length):
    sorted_list, live, features, centres, total = refs[:5]
    window, near_rows, tilt_rows, lists, sems = refs[5:10]
    scratch = refs[10:]
    state = (live, features, centres, total)
    blocks = own.shape[0] // ROWS
    sort_list(number[0], own, length, sorted_list, blocks, members)
    to_scalars = read_list(0, sorted_list, lists, sems)
    put_tiles(live, 0, own, length)
    window[pl.ds(REACH * blocks * ROWS, blocks * ROWS), :] = live[...]
    put_tiles(window, side_of_partner() * blocks, partner, length)
    prepare_targets(state, near_rows, tilt_rows)
    to_scalars.wait()
    run_class(lists, window, state, scratch)


def near_kernel(sorted_list, live, partner, *refs, members, length):
    others, refs = refs[: members - 1], refs[members - 1 :]
    targets, features, centres, total = state = refs[:4]
    window, near_rows, tilt_rows, lists, sems = refs[4:9]
    scratch = refs[9:]
    to_scalars = read_list(1, sorted_list, lists, sems)
    blocks = live.shape[0] // ROWS
    window[pl.ds(REACH * blocks * ROWS, blocks * ROWS), :] = live[...]
    put_tiles(window, side_of_partner() * blocks, partner, length)
    for r, other in enumerate(others):
        put_tiles(targets, r * blocks, other, length)
    prepare_targets(state, near_rows, tilt_rows)
    to_scalars.wait()
    run_class(lists, window, state, scratch)


def below_kernel(sorted_list, below, live, own_features, own_centres, *refs, length):
    targets, features, centres, total, own_total = refs[:5]
    window, lists, sems, own_lists, own_sems = refs[5:10]
    scratch = refs[10:]
    to_scalars = read_list(6, sorted_list, lists, sems)
    own_to_scalars = read_list(5, sorted_list, own_lists, own_sems)
    total[...] = jnp.zeros_like(total)
    own_total[...] = jnp.zeros_like(own_total)
    put_tiles(window, 0, below, length)
    to_scalars.wait()
    run_class(lists, window, (targets, features, centres, total), scratch)
    own_to_scalars.wait()
    run_class(own_lists, window, (live, own_features, own_centres, own_total), scratch)


def single_kernel(sorted_list, tiles, targets, features, centres, *refs, kind, run, length):
    total, window, lists, sems = refs[:4]
    to_scalars = read_list(kind, sorted_list, lists, sems)
    total[...] = jnp.zeros_like(total)
    put_tiles(window, 0, tiles, length)
    to_scalars.wait()
    window = shifted_window(window, run * (tiles.shape[0] // ROWS))
    run_class(lists, window, (targets, features, centres, total), refs[4:])


def far_kernel(sorted_list, below, above, crossed, *refs, length):
    targets, features, centres, near_total, below_total, middle_total = refs[:6]
    window, out_ref, total, lists, sems = refs[6:11]
    scratch = refs[11:]
    state = (targets, features, centres, total)
    to_scalars = read_list(3, sorted_list, lists, sems)
    blocks = below.shape[0] // ROWS
    put_tiles(window, 0, below, length)
    put_tiles(window, 2 * REACH * blocks, above, length)
    put_tiles(window, (2 * REACH - side_of_partner()) * blocks, crossed, length)
    total[...] = jnp.zeros_like(total)
    to_scalars.wait()
    run_class(lists, window, state, scratch)
    finish(targets, centres, (near_total, below_total, middle_total, total), out_ref)


def last_kernel(sorted_list, window, own, features, centres, *refs):
    home_total, below_total, out_ref, total, lists, sems = refs[:6]
    to_scalars = read_list(4, sorted_list, lists, sems)
    total[...] = jnp.zeros_like(total)
    to_scalars.wait()
    run_class(lists, window, (own, features, centres, total), refs[6:])
    finish(own, centres, (home_total, below_total, total), out_ref)


def section_kernel(own, sums, *refs):
    returned, (velocity, stretching, section_positions, section_strengths) = refs[:-4], refs[-4:]
    blocks = own.shape[0] // ROWS
    for b in range(blocks):
        lanes = slice(b * BLOCK, (b + 1) * BLOCK)
        for start, result, stepped in ((0, velocity, section_positions), (3, stretching, section_strengths)):
            chosen = pl.ds(start * blocks + b, 3, stride=blocks)
            value = sums[chosen, :]
            for other in returned:
                value = value + other[chosen, :]
            result[:, lanes] = value
            first = b * ROWS + start
            stepped[:, lanes] = own[first : first + 3, :] + section_step * value


def call(kernel, name, inputs, outputs, scratch, flops=0):
    vmem = pl.BlockSpec(memory_space=pltpu.VMEM)
    smem = pl.BlockSpec(memory_space=pltpu.SMEM)
    held = sum(value.size * value.dtype.itemsize for value in (*inputs, *outputs))
    return pl.pallas_call(
        kernel,
        out_shape=outputs,
        in_specs=[smem if value.dtype == jnp.int32 and value.ndim == 1 else vmem for value in inputs],
        out_specs=[vmem for value in outputs],
        scratch_shapes=scratch,
        compiler_params=pltpu.CompilerParams(vmem_limit_bytes=10 * 1024 * 1024 + 2 * held),
        cost_estimate=pl.CostEstimate(flops=flops, bytes_accessed=0, transcendentals=0),
        name=name,
    )(*inputs)


def shards(positions, strengths, radius, block_count, pair_target, pair_slot, pair_count):
    blocks = block_count.shape[0]
    lanes = blocks * BLOCK
    length = pair_target.shape[1]
    members = lax.axis_size("across")
    shard = lax.axis_index("blk")
    count = lax.axis_size("blk")

    def f32(*shape):
        return jax.ShapeDtypeStruct(shape, jnp.float32)

    parts = [value.reshape(3, blocks, BLOCK).transpose(1, 0, 2) for value in (positions, strengths)]
    rows, start = [], 0
    for value in (pair_target[0], pair_slot[0], block_count):
        rows.append(jnp.pad(value, (start, lanes - start - value.shape[0])))
        start += -(-value.shape[0] // BLOCK) * BLOCK
    listed = sum(rows).astype(jnp.float32).reshape(blocks, 1, BLOCK)
    own = jnp.concatenate(parts + [radius.reshape(blocks, 1, BLOCK), listed], axis=1)
    own = own.reshape(blocks * ROWS, BLOCK)
    others = [
        moved(own, "across", lambda source: (source - away) % members) for away in range(1, members)
    ]
    partner = moved(own, "blk", to_other_core)
    below = moved(own, "blk", shifted(REACH, count))

    def state_shapes(number):
        return [
            f32(number * blocks * ROWS, BLOCK),
            jax.ShapeDtypeStruct((number * blocks, FEATURES, 2 * BLOCK), jnp.bfloat16),
            f32(number * blocks * ROWS, BLOCK),
            f32(number * blocks * 2 * ROWS, BLOCK),
        ]

    own_shapes, other_shapes = state_shapes(1), state_shapes(members - 1)
    window_shape = f32((2 * REACH + 1) * blocks * ROWS, BLOCK)
    rows = list_rows(length)
    list_shape = jax.ShapeDtypeStruct((CLASSES - 1, -(-rows // ROWS) * ROWS, BLOCK), jnp.int32)
    feature_rows = [pltpu.VMEM((GROUP * ROWS, BLOCK), jnp.float32)] * 2
    list_scratch = [pltpu.SMEM((rows, BLOCK), jnp.int32), pltpu.SemaphoreType.DMA((1,))]
    scratch = [pltpu.VMEM((GROUP * ROWS, BLOCK), jnp.float32)] * 4 + [
        pltpu.VMEM((HALF, BLOCK, 2 * BLOCK), jnp.float32),
        pltpu.VMEM((HALF, BLOCK, 2 * BLOCK), jnp.float32),
    ]
    window_scratch = pltpu.VMEM(window_shape.shape, jnp.float32)

    lists, live, *own_state = call(
        lambda *refs: home_kernel(*refs, members=members, length=length),
        "home_pairs",
        (pair_count, own, partner),
        [list_shape] + own_shapes,
        [window_scratch] + feature_rows + list_scratch + scratch,
        flops=HOME_FLOPS,
    )
    late, lists = lax.optimization_barrier((own, lists))
    above = moved(late, "blk", shifted(-REACH, count))
    other_state = list(call(
        lambda *refs: near_kernel(*refs, members=members, length=length),
        "near_pairs",
        (lists, live, partner, *others),
        other_shapes,
        [window_scratch] + feature_rows + list_scratch + scratch,
        flops=NEAR_FLOPS,
    ))
    below_total, below_own_total = call(
        lambda *refs: below_kernel(*refs, length=length),
        "below_pairs",
        (lists, below, live, *own_state[:2], *other_state[:3]),
        [other_shapes[3], own_shapes[3]],
        [pltpu.VMEM(own.shape, jnp.float32)] + 2 * list_scratch + scratch,
        flops=HOME_FLOPS,
    )
    above, below_total = lax.optimization_barrier((above, below_total))
    crossed = moved(jnp.where(shard % 2 == 0, above, below), "blk", to_other_core)
    (middle_total,) = call(
        lambda *refs: single_kernel(*refs, kind=2, run=2 * REACH, length=length),
        "middle_pairs",
        (lists, above, *other_state[:3]),
        [other_shapes[3]],
        [pltpu.VMEM(own.shape, jnp.float32)] + list_scratch + scratch,
        flops=HOME_FLOPS,
    )
    crossed, middle_total = lax.optimization_barrier((crossed, middle_total))
    window, away_sums = call(
        lambda *refs: far_kernel(*refs, length=length),
        "far_pairs",
        (lists, below, above, crossed, *other_state, below_total, middle_total),
        [window_shape, f32(members - 1, 6 * blocks, BLOCK)],
        [pltpu.VMEM(other_shapes[3].shape, jnp.float32)] + list_scratch + scratch,
        flops=FAR_FLOPS,
    )
    returned = [
        moved(away_sums[away - 1], "across", lambda source: (source + away) % members)
        for away in range(1, members)
    ]
    (sums,) = call(
        last_kernel,
        "last_pairs",
        (lists, window, live, *own_state, below_own_total),
        [f32(1, 6 * blocks, BLOCK)],
        [pltpu.VMEM(own_shapes[3].shape, jnp.float32)] + list_scratch + scratch,
        flops=FAR_FLOPS,
    )
    wide = f32(3, lanes)
    return tuple(
        call(section_kernel, "section", (live, sums[0], *returned), [wide] * 4, [])
    )


def solution(mesh):
    whole = P(None, ("blk", "across"))
    line = P(("blk", "across"))
    return jax.shard_map(
        shards,
        mesh=mesh,
        in_specs=(whole, whole, line, line, P(("blk", "across"), None), P(("blk", "across"), None), line),
        out_specs=(whole, whole, whole, whole),
        check_vma=False,
    )
```

```python
import jax
import jax.numpy as jnp
from jax import lax
from jax.experimental import pallas as pl
from jax.experimental.pallas import tpu as pltpu
from jax.sharding import PartitionSpec as P

BLOCK = 128
ROWS = 8
REACH = 2
GROUP = 8
HALF = 4
FEATURES = 48
CLASSES = 8

F_SCALE = (2.0 / 3.0) ** 1.5
H_SCALE = 5.0 * (2.0 / 3.0) ** 2.5
biot_factor = 0.07957747154594767
section_step = 0.05


def moved(value, axis, target_of):
    pairs = [(source, target_of(source)) for source in range(lax.axis_size(axis))]
    return lax.ppermute(value, axis, pairs)


def to_other_core(source):
    return source ^ 1


def shifted(steps, count):
    return lambda source: (source + steps) % count


HOME_FLOPS = 10**10
NEAR_FLOPS = 10**10
FAR_FLOPS = 10**10


def rounded(value):
    return value.astype(jnp.bfloat16).astype(jnp.float32)


def split_three(value):
    first = rounded(value)
    rest = value - first
    second = rounded(rest)
    return first, second, rest - second


def six_slots(tile, order):
    parts = split_three(tile)
    return jnp.concatenate([parts[part] for part in order], axis=0).astype(jnp.bfloat16)


def cross(left, right):
    return [
        left[1] * right[2] - left[2] * right[1],
        left[2] * right[0] - left[0] * right[2],
        left[0] * right[1] - left[1] * right[0],
    ]


def tile_rows(index, rows):
    return pl.ds(pl.multiple_of(index * rows, rows), rows)


def component(ref, base, number, stride):
    return ref[pl.ds(base + number, GROUP, stride=stride), :]


def store_component(ref, base, number, stride, value):
    ref[pl.ds(base + number, GROUP, stride=stride), :] = value


def target_features(targets, step, centres, near_rows, tilt_rows):
    base = pl.multiple_of(step * (GROUP * ROWS), GROUP * ROWS)
    pos = [component(targets, base, k, ROWS) for k in range(3)]
    strength = [component(targets, base, 3 + k, ROWS) for k in range(3)]
    for k in range(3):
        centre = jnp.broadcast_to(jnp.mean(pos[k], axis=1, keepdims=True), (GROUP, BLOCK))
        store_component(centres, base, k, ROWS, centre)
        pos[k] = pos[k] - centre
    for k in range(3, ROWS):
        store_component(centres, base, k, ROWS, jnp.zeros_like(pos[0]))
    norm = pos[0] * pos[0] + pos[1] * pos[1] + pos[2] * pos[2]
    own = pos[0] * strength[0] + pos[1] * strength[1] + pos[2] * strength[2]
    near = [(2.0 / 3.0) * value for value in pos + [norm, jnp.ones_like(norm)]]
    tilt = [0.5 * s for s in strength] + [own]
    for rows, values in ((near_rows, near), (tilt_rows, tilt)):
        for k, value in enumerate(values):
            store_component(rows, 0, k, ROWS, value)


def source_features(gathered, weight, left, charge):
    pos = [component(gathered, 0, k, ROWS) for k in range(3)]
    strength = [component(gathered, 0, 3 + k, ROWS) for k in range(3)]
    inv_core = 1.0 / component(gathered, 0, 6, ROWS)
    inv_square = inv_core * inv_core
    norm = pos[0] * pos[0] + pos[1] * pos[1] + pos[2] * pos[2]
    twice = -2.0 * inv_square
    shape = [p * twice for p in pos] + [inv_square, norm * inv_square + 1.0]
    for k, value in enumerate(shape):
        store_component(left, 0, k, ROWS, value)
    scale = inv_square * inv_core * weight
    for k, value in enumerate(strength + cross(pos, strength)):
        store_component(charge, 0, k, ROWS, value * scale)


NT = (((1,), (1,)), ((), ()))
TN = (((0,), (0,)), ((), ()))


def put_tiles(window, first, tiles, length):
    base = pl.multiple_of(first * ROWS, ROWS)
    blocks = tiles.shape[0] // ROWS
    window[pl.ds(base, blocks * ROWS), :] = tiles[...]
    row = (2 * length // BLOCK + 1) * ROWS - 1
    counts = tiles[row : row + 1, :]
    row = lax.broadcasted_iota(jnp.int32, (blocks, BLOCK), 0)
    lane = lax.broadcasted_iota(jnp.int32, (blocks, BLOCK), 1)
    counts = jnp.sum(jnp.where(row == lane, counts, 0.0), axis=1, keepdims=True)
    alive = jnp.where(lane.astype(jnp.float32) < counts, 1.0, 0.0)
    for j in range(blocks // GROUP):
        part = alive[j * GROUP : (j + 1) * GROUP, :]
        for k in range(3, 6):
            rows = pl.ds(base + j * GROUP * ROWS + k, GROUP, stride=ROWS)
            window[rows, :] = window[rows, :] * part


def prepare_targets(state, near_rows, tilt_rows):
    targets, features, centres, total = state
    near_rows[...] = jnp.zeros_like(near_rows)
    tilt_rows[...] = jnp.zeros_like(tilt_rows)
    total[...] = jnp.zeros_like(total)

    def prepare(step, carry):
        target_features(targets, step, centres, near_rows, tilt_rows)
        for u in range(GROUP):
            rows = slice(u * ROWS, (u + 1) * ROWS)
            features[step * GROUP + u, :, :BLOCK] = six_slots(near_rows[rows, :], (0, 1, 2, 0, 1, 0))
            features[step * GROUP + u, :, BLOCK:] = six_slots(tilt_rows[rows, :], (0, 1, 2, 0, 1, 0))
        return carry

    lax.fori_loop(0, features.shape[0] // GROUP, prepare, 0)


def run_class(lists, window, state, scratch):
    _, features, centres, total = state
    gathered, left, charge_next, charge, first_half, second_half = scratch
    slot_row = (lists.shape[0] - 1) // 2
    listed = lists[2 * slot_row, 0]

    def entry_at(step, u):
        entry = jnp.minimum(step * GROUP + u, listed - 1)
        return entry // BLOCK, lax.rem(entry, BLOCK)

    def target_of(step, u):
        row, column = entry_at(step, u)
        return lists[row, column]

    def prepare_sources(step):
        for u in range(GROUP):
            row, column = entry_at(step, u)
            gathered[u * ROWS : (u + 1) * ROWS, :] = (
                window[tile_rows(lists[row + slot_row, column], ROWS), :]
                - centres[tile_rows(lists[row, column], ROWS), :]
            )
        order = lax.broadcasted_iota(jnp.int32, (GROUP, BLOCK), 0) + step * GROUP
        weight = jnp.where(order < listed, 1.0, 0.0).astype(jnp.float32)
        source_features(gathered, weight, left, charge_next)

    def products(step, u, held):
        shape = six_slots(left[u * ROWS : (u + 1) * ROWS, :], (0, 0, 0, 1, 1, 2))
        held[u % HALF] = lax.dot_general(
            shape, features[target_of(step, u)], TN, preferred_element_type=jnp.float32
        )

    def weights(u, held):
        near = held[u % HALF, :, :BLOCK]
        tilt = held[u % HALF, :, BLOCK:]
        q = lax.rsqrt(near)
        q2 = q * q
        q3 = q2 * q
        q5 = q3 * q2
        f = q3 + q5
        h = (q5 * tilt) * (q2 + 0.6)
        fh = f.astype(jnp.bfloat16)
        fl = (f - fh.astype(jnp.float32)).astype(jnp.bfloat16)
        hh = h.astype(jnp.bfloat16)
        hl = (h - hh.astype(jnp.float32)).astype(jnp.bfloat16)
        return jnp.concatenate(
            [jnp.concatenate([fh, fl], axis=1), jnp.concatenate([hh, hl], axis=1)], axis=0
        )

    def add_up(u, stacked):
        pair = charge[u * ROWS : (u + 1) * ROWS, :]
        high = rounded(pair)
        pair = jnp.concatenate([high, pair - high], axis=0).astype(jnp.bfloat16)
        blank = jnp.zeros_like(pair)
        pair = jnp.concatenate(
            [jnp.concatenate([pair, blank], axis=1), jnp.concatenate([blank, pair], axis=1)], axis=0
        )
        sums = jnp.dot(pair, stacked, preferred_element_type=jnp.float32)
        fsum = sums[0:8, :BLOCK] + sums[8:16, :BLOCK] + sums[0:8, BLOCK:]
        hsum = sums[16:24, :BLOCK] + sums[24:32, :BLOCK] + sums[16:24, BLOCK:]
        return jnp.concatenate([fsum, hsum], axis=0)

    def turn(step, carry):
        sums = []
        for u in range(HALF):
            stacked = weights(u, first_half)
            products(step, HALF + u, second_half)
            sums.append(add_up(u, stacked))
        prepare_sources(step + 1)
        for u in range(HALF, GROUP):
            stacked = weights(u, second_half)
            products(step + 1, u - HALF, first_half)
            sums.append(add_up(u, stacked))
        charge[...] = charge_next[...]
        for u in range(GROUP):
            total[tile_rows(target_of(step, u), 2 * ROWS), :] += sums[u]
        return carry

    @pl.when(listed > 0)
    def _():
        left[...] = jnp.zeros_like(left)
        charge_next[...] = jnp.zeros_like(charge_next)
        prepare_sources(0)
        for u in range(HALF):
            products(0, u, first_half)
        charge[...] = charge_next[...]
        full = (listed + HALF - 1) // GROUP
        lax.fori_loop(0, full, turn, 0)

        @pl.when(listed > full * GROUP)
        def _():
            sums = [add_up(u, weights(u, first_half)) for u in range(HALF)]
            for u in range(HALF):
                total[tile_rows(target_of(full, u), 2 * ROWS), :] += sums[u]


def finish(targets, centres, totals, out_ref):
    blocks = out_ref.shape[1] // 6

    def one(step, carry):
        base = pl.multiple_of(step * GROUP * ROWS, GROUP * ROWS)
        wide = pl.multiple_of(step * GROUP * 2 * ROWS, GROUP * 2 * ROWS)
        pos = [
            component(targets, base, k, ROWS) - component(centres, base, k, ROWS) for k in range(3)
        ]
        strength = [component(targets, base, 3 + k, ROWS) for k in range(3)]
        fa, fb, ha, hb = [
            [
                sum(component(total, wide, start + k, 2 * ROWS) for total in totals)
                for k in range(3)
            ]
            for start in (0, 3, 8, 11)
        ]
        swirl = cross(pos, fa)
        lean = cross(strength, fa)
        bend = cross(pos, ha)
        member = step * GROUP // blocks
        inside = lax.rem(step * GROUP, blocks)
        for k in range(3):
            velocity = (-F_SCALE * biot_factor) * (swirl[k] - fb[k])
            stretch = (-F_SCALE * biot_factor) * lean[k] + (H_SCALE * biot_factor) * (bend[k] - hb[k])
            out_ref[member, pl.ds(pl.multiple_of(k * blocks + inside, GROUP), GROUP), :] = velocity
            out_ref[member, pl.ds(pl.multiple_of((3 + k) * blocks + inside, GROUP), GROUP), :] = stretch
        return carry

    lax.fori_loop(0, targets.shape[0] // ROWS // GROUP, one, 0, unroll=2)


def sort_list(number, own, length, sorted_list, blocks, members):
    rows = [own[b * ROWS + ROWS - 1 : (b + 1) * ROWS, :] for b in range(2 * length // BLOCK)]
    half = length // BLOCK
    t = jnp.concatenate(rows[:half], axis=1).astype(jnp.int32)
    s = jnp.concatenate(rows[half : 2 * half], axis=1).astype(jnp.int32)
    entry = lax.broadcasted_iota(jnp.int32, (1, length), 1)
    t = t - lax.axis_index("across") * blocks
    t = jnp.where(t < 0, t + members * blocks, t)
    run = s // blocks
    mine = t < blocks
    t = jnp.where(mine, t, t - blocks)
    near = (run == REACH) | (run == side_of_partner())
    kind = jnp.where(
        mine,
        jnp.where(near, 0, jnp.where(run == 0, 5, 4)),
        jnp.where(near, 1, jnp.where(run == 0, 2, 3)),
    )
    kind = jnp.where(entry < number, kind, CLASSES - 1)
    member = jnp.where(lax.broadcasted_iota(jnp.int32, (CLASSES, length), 0) == kind, 1.0, 0.0)
    row = lax.broadcasted_iota(jnp.int32, (length, length), 0)
    column = lax.broadcasted_iota(jnp.int32, (length, length), 1)
    before = jnp.where(row < column, 1.0, 0.0).astype(jnp.bfloat16)
    earlier = jnp.dot(member.astype(jnp.bfloat16), before, preferred_element_type=jnp.float32)
    rank = jnp.sum(member * earlier, axis=0, keepdims=True).astype(jnp.int32)
    place = jnp.where(row == rank, 1.0, 0.0).astype(jnp.bfloat16)
    values = [t // BLOCK, t % BLOCK, s // BLOCK, s % BLOCK]
    values = [member * value.astype(jnp.float32) for value in values]
    values = jnp.concatenate(values, axis=0).astype(jnp.bfloat16)
    found = lax.dot_general(values, place, NT, preferred_element_type=jnp.float32)
    number = jnp.broadcast_to(jnp.sum(member, axis=1, keepdims=True), (CLASSES, BLOCK))
    targets = found[0:8] * BLOCK + found[8:16]
    slots = found[16:24] * BLOCK + found[24:32]
    columns = [slice(j * BLOCK, (j + 1) * BLOCK) for j in range(length // BLOCK)]
    rows = sorted_list.shape[1]
    for kind in range(CLASSES - 1):
        one = slice(kind, kind + 1)
        parts = [targets[one, c] for c in columns] + [slots[one, c] for c in columns] + [number[one]]
        padding = rows - len(parts)
        if padding:
            parts.append(jnp.zeros((padding, BLOCK), jnp.float32))
        sorted_list[kind] = jnp.concatenate(parts, axis=0).astype(jnp.int32)


def list_rows(length):
    return 2 * (length // BLOCK) + 1


def read_list(kind, sorted_list, lists, sems):
    copy = pltpu.make_async_copy(sorted_list.at[kind, pl.ds(0, lists.shape[0])], lists, sems.at[0])
    copy.start()
    return copy


class shifted_window:
    def __init__(self, ref, start):
        self.ref, self.start = ref, start * ROWS

    def __getitem__(self, index):
        rows, lanes = index
        return self.ref[pl.ds(pl.multiple_of(rows.start - self.start, ROWS), rows.size), lanes]


def side_of_partner():
    return jnp.where(lax.axis_index("blk") % 2 == 0, REACH + 1, REACH - 1)


def home_kernel(number, own, partner, *refs, members, length):
    sorted_list, live, features, centres, total = refs[:5]
    window, near_rows, tilt_rows, lists, sems = refs[5:10]
    scratch = refs[10:]
    state = (live, features, centres, total)
    blocks = own.shape[0] // ROWS
    sort_list(number[0], own, length, sorted_list, blocks, members)
    to_scalars = read_list(0, sorted_list, lists, sems)
    put_tiles(live, 0, own, length)
    window[pl.ds(REACH * blocks * ROWS, blocks * ROWS), :] = live[...]
    put_tiles(window, side_of_partner() * blocks, partner, length)
    prepare_targets(state, near_rows, tilt_rows)
    to_scalars.wait()
    run_class(lists, window, state, scratch)


def near_kernel(sorted_list, live, partner, *refs, members, length):
    others, refs = refs[: members - 1], refs[members - 1 :]
    targets, features, centres, total = state = refs[:4]
    window, near_rows, tilt_rows, lists, sems = refs[4:9]
    scratch = refs[9:]
    to_scalars = read_list(1, sorted_list, lists, sems)
    blocks = live.shape[0] // ROWS
    window[pl.ds(REACH * blocks * ROWS, blocks * ROWS), :] = live[...]
    put_tiles(window, side_of_partner() * blocks, partner, length)
    for r, other in enumerate(others):
        put_tiles(targets, r * blocks, other, length)
    prepare_targets(state, near_rows, tilt_rows)
    to_scalars.wait()
    run_class(lists, window, state, scratch)


def single_kernel(sorted_list, tiles, targets, features, centres, *refs, kind, length):
    total, window, lists, sems = refs[:4]
    to_scalars = read_list(kind, sorted_list, lists, sems)
    total[...] = jnp.zeros_like(total)
    put_tiles(window, 0, tiles, length)
    to_scalars.wait()
    run_class(lists, window, (targets, features, centres, total), refs[4:])


def far_kernel(sorted_list, above, crossed, *refs, length):
    targets, features, centres, near_total, below_total = refs[:5]
    window, out_ref, total, lists, sems = refs[5:10]
    scratch = refs[10:]
    state = (targets, features, centres, total)
    to_scalars = read_list(3, sorted_list, lists, sems)
    blocks = above.shape[0] // ROWS
    put_tiles(window, 2 * REACH * blocks, above, length)
    put_tiles(window, (2 * REACH - side_of_partner()) * blocks, crossed, length)
    total[...] = jnp.zeros_like(total)
    to_scalars.wait()
    run_class(lists, window, state, scratch)
    finish(targets, centres, (near_total, below_total, total), out_ref)


def last_kernel(sorted_list, window, own, features, centres, *refs):
    home_total, below_total, out_ref, total, lists, sems = refs[:6]
    to_scalars = read_list(4, sorted_list, lists, sems)
    total[...] = jnp.zeros_like(total)
    to_scalars.wait()
    run_class(lists, window, (own, features, centres, total), refs[6:])
    finish(own, centres, (home_total, below_total, total), out_ref)


def section_kernel(own, sums, *refs):
    returned, (velocity, stretching, section_positions, section_strengths) = refs[:-4], refs[-4:]
    blocks = own.shape[0] // ROWS
    for b in range(blocks):
        lanes = slice(b * BLOCK, (b + 1) * BLOCK)
        for start, result, stepped in ((0, velocity, section_positions), (3, stretching, section_strengths)):
            chosen = pl.ds(start * blocks + b, 3, stride=blocks)
            value = sums[chosen, :]
            for other in returned:
                value = value + other[chosen, :]
            result[:, lanes] = value
            first = b * ROWS + start
            stepped[:, lanes] = own[first : first + 3, :] + section_step * value


def call(kernel, name, inputs, outputs, scratch, flops=0):
    vmem = pl.BlockSpec(memory_space=pltpu.VMEM)
    smem = pl.BlockSpec(memory_space=pltpu.SMEM)
    held = sum(value.size * value.dtype.itemsize for value in (*inputs, *outputs))
    return pl.pallas_call(
        kernel,
        out_shape=outputs,
        in_specs=[smem if value.dtype == jnp.int32 and value.ndim == 1 else vmem for value in inputs],
        out_specs=[vmem for value in outputs],
        scratch_shapes=scratch,
        compiler_params=pltpu.CompilerParams(vmem_limit_bytes=10 * 1024 * 1024 + 2 * held),
        cost_estimate=pl.CostEstimate(flops=flops, bytes_accessed=0, transcendentals=0),
        name=name,
    )(*inputs)


def shards(positions, strengths, radius, block_count, pair_target, pair_slot, pair_count):
    blocks = block_count.shape[0]
    lanes = blocks * BLOCK
    length = pair_target.shape[1]
    members = lax.axis_size("across")
    shard = lax.axis_index("blk")
    count = lax.axis_size("blk")

    def f32(*shape):
        return jax.ShapeDtypeStruct(shape, jnp.float32)

    parts = [value.reshape(3, blocks, BLOCK).transpose(1, 0, 2) for value in (positions, strengths)]
    rows, start = [], 0
    for value in (pair_target[0], pair_slot[0], block_count):
        rows.append(jnp.pad(value, (start, lanes - start - value.shape[0])))
        start += -(-value.shape[0] // BLOCK) * BLOCK
    listed = sum(rows).astype(jnp.float32).reshape(blocks, 1, BLOCK)
    own = jnp.concatenate(parts + [radius.reshape(blocks, 1, BLOCK), listed], axis=1)
    own = own.reshape(blocks * ROWS, BLOCK)
    others = [
        moved(own, "across", lambda source: (source - away) % members) for away in range(1, members)
    ]
    partner = moved(own, "blk", to_other_core)
    below = moved(own, "blk", shifted(REACH, count))

    def state_shapes(number):
        return [
            f32(number * blocks * ROWS, BLOCK),
            jax.ShapeDtypeStruct((number * blocks, FEATURES, 2 * BLOCK), jnp.bfloat16),
            f32(number * blocks * ROWS, BLOCK),
            f32(number * blocks * 2 * ROWS, BLOCK),
        ]

    own_shapes, other_shapes = state_shapes(1), state_shapes(members - 1)
    window_shape = f32((2 * REACH + 1) * blocks * ROWS, BLOCK)
    rows = list_rows(length)
    list_shape = jax.ShapeDtypeStruct((CLASSES - 1, -(-rows // ROWS) * ROWS, BLOCK), jnp.int32)
    feature_rows = [pltpu.VMEM((GROUP * ROWS, BLOCK), jnp.float32)] * 2
    list_scratch = [pltpu.SMEM((rows, BLOCK), jnp.int32), pltpu.SemaphoreType.DMA((1,))]
    scratch = [pltpu.VMEM((GROUP * ROWS, BLOCK), jnp.float32)] * 4 + [
        pltpu.VMEM((HALF, BLOCK, 2 * BLOCK), jnp.float32),
        pltpu.VMEM((HALF, BLOCK, 2 * BLOCK), jnp.float32),
    ]
    window_scratch = pltpu.VMEM(window_shape.shape, jnp.float32)

    lists, live, *own_state = call(
        lambda *refs: home_kernel(*refs, members=members, length=length),
        "home_pairs",
        (pair_count, own, partner),
        [list_shape] + own_shapes,
        [window_scratch] + feature_rows + list_scratch + scratch,
        flops=HOME_FLOPS,
    )
    late, lists = lax.optimization_barrier((own, lists))
    above = moved(late, "blk", shifted(-REACH, count))
    other_state = list(call(
        lambda *refs: near_kernel(*refs, members=members, length=length),
        "near_pairs",
        (lists, live, partner, *others),
        other_shapes,
        [window_scratch] + feature_rows + list_scratch + scratch,
        flops=NEAR_FLOPS,
    ))
    (below_total,) = call(
        lambda *refs: single_kernel(*refs, kind=2, length=length),
        "below_pairs",
        (lists, below, *other_state[:3]),
        [other_shapes[3]],
        [pltpu.VMEM(own.shape, jnp.float32)] + list_scratch + scratch,
        flops=HOME_FLOPS,
    )
    above, below_total = lax.optimization_barrier((above, below_total))
    crossed = moved(jnp.where(shard % 2 == 0, above, below), "blk", to_other_core)
    (below_own_total,) = call(
        lambda *refs: single_kernel(*refs, kind=5, length=length),
        "below_own_pairs",
        (lists, below, live, *own_state[:2]),
        [own_shapes[3]],
        [pltpu.VMEM(own.shape, jnp.float32)] + list_scratch + scratch,
        flops=HOME_FLOPS,
    )
    crossed, below_own_total = lax.optimization_barrier((crossed, below_own_total))
    window, away_sums = call(
        lambda *refs: far_kernel(*refs, length=length),
        "far_pairs",
        (lists, above, crossed, *other_state, below_total),
        [window_shape, f32(members - 1, 6 * blocks, BLOCK)],
        [pltpu.VMEM(other_shapes[3].shape, jnp.float32)] + list_scratch + scratch,
        flops=FAR_FLOPS,
    )
    returned = [
        moved(away_sums[away - 1], "across", lambda source: (source + away) % members)
        for away in range(1, members)
    ]
    (sums,) = call(
        last_kernel,
        "last_pairs",
        (lists, window, live, *own_state, below_own_total),
        [f32(1, 6 * blocks, BLOCK)],
        [pltpu.VMEM(own_shapes[3].shape, jnp.float32)] + list_scratch + scratch,
        flops=FAR_FLOPS,
    )
    wide = f32(3, lanes)
    return tuple(
        call(section_kernel, "section", (live, sums[0], *returned), [wide] * 4, [])
    )


def solution(mesh):
    whole = P(None, ("blk", "across"))
    line = P(("blk", "across"))
    return jax.shard_map(
        shards,
        mesh=mesh,
        in_specs=(whole, whole, line, line, P(("blk", "across"), None), P(("blk", "across"), None), line),
        out_specs=(whole, whole, whole, whole),
        check_vma=False,
    )
```

```python
import jax
import jax.numpy as jnp
from jax import lax
from jax.experimental import pallas as pl
from jax.experimental.pallas import tpu as pltpu
from jax.sharding import PartitionSpec as P

BLOCK = 128
ROWS = 8
REACH = 2
GROUP = 8
HALF = 4
FEATURES = 48
CLASSES = 8
QUARTERS = 4

F_SCALE = (2.0 / 3.0) ** 1.5
H_SCALE = 5.0 * (2.0 / 3.0) ** 2.5
biot_factor = 0.07957747154594767
section_step = 0.05


def moved(value, axis, target_of):
    pairs = [(source, target_of(source)) for source in range(lax.axis_size(axis))]
    return lax.ppermute(value, axis, pairs)


def to_other_core(source):
    return source ^ 1


def shifted(steps, count):
    return lambda source: (source + steps) % count


HOME_FLOPS = 10**10
NEAR_FLOPS = 10**10
FAR_FLOPS = 10**10


def rounded(value):
    return value.astype(jnp.bfloat16).astype(jnp.float32)


def split_three(value):
    first = rounded(value)
    rest = value - first
    second = rounded(rest)
    return first, second, rest - second


def six_slots(tile, order):
    parts = split_three(tile)
    return jnp.concatenate([parts[part] for part in order], axis=0).astype(jnp.bfloat16)


def cross(left, right):
    return [
        left[1] * right[2] - left[2] * right[1],
        left[2] * right[0] - left[0] * right[2],
        left[0] * right[1] - left[1] * right[0],
    ]


def tile_rows(index, rows):
    return pl.ds(pl.multiple_of(index * rows, rows), rows)


def component(ref, base, number, stride):
    return ref[pl.ds(base + number, GROUP, stride=stride), :]


def store_component(ref, base, number, stride, value):
    ref[pl.ds(base + number, GROUP, stride=stride), :] = value


def target_features(targets, step, centres, near_rows, tilt_rows):
    base = pl.multiple_of(step * (GROUP * ROWS), GROUP * ROWS)
    pos = [component(targets, base, k, ROWS) for k in range(3)]
    strength = [component(targets, base, 3 + k, ROWS) for k in range(3)]
    for k in range(3):
        centre = jnp.broadcast_to(jnp.mean(pos[k], axis=1, keepdims=True), (GROUP, BLOCK))
        store_component(centres, base, k, ROWS, centre)
        pos[k] = pos[k] - centre
    for k in range(3, ROWS):
        store_component(centres, base, k, ROWS, jnp.zeros_like(pos[0]))
    norm = pos[0] * pos[0] + pos[1] * pos[1] + pos[2] * pos[2]
    own = pos[0] * strength[0] + pos[1] * strength[1] + pos[2] * strength[2]
    near = [(2.0 / 3.0) * value for value in pos + [norm, jnp.ones_like(norm)]]
    tilt = [0.5 * s for s in strength] + [own]
    for rows, values in ((near_rows, near), (tilt_rows, tilt)):
        for k, value in enumerate(values):
            store_component(rows, 0, k, ROWS, value)


def source_features(gathered, weight, left, charge):
    pos = [component(gathered, 0, k, ROWS) for k in range(3)]
    strength = [component(gathered, 0, 3 + k, ROWS) for k in range(3)]
    inv_core = 1.0 / component(gathered, 0, 6, ROWS)
    inv_square = inv_core * inv_core
    norm = pos[0] * pos[0] + pos[1] * pos[1] + pos[2] * pos[2]
    twice = -2.0 * inv_square
    shape = [p * twice for p in pos] + [inv_square, norm * inv_square + 1.0]
    for k, value in enumerate(shape):
        store_component(left, 0, k, ROWS, value)
    scale = inv_square * inv_core * weight
    for k, value in enumerate(strength + cross(pos, strength)):
        store_component(charge, 0, k, ROWS, value * scale)


NT = (((1,), (1,)), ((), ()))
TN = (((0,), (0,)), ((), ()))


def put_tiles(window, first, tiles, length):
    base = pl.multiple_of(first * ROWS, ROWS)
    blocks = tiles.shape[0] // ROWS
    window[pl.ds(base, blocks * ROWS), :] = tiles[...]
    row = (2 * length // BLOCK + 1) * ROWS - 1
    counts = tiles[row : row + 1, :]
    row = lax.broadcasted_iota(jnp.int32, (blocks, BLOCK), 0)
    lane = lax.broadcasted_iota(jnp.int32, (blocks, BLOCK), 1)
    counts = jnp.sum(jnp.where(row == lane, counts, 0.0), axis=1, keepdims=True)
    alive = jnp.where(lane.astype(jnp.float32) < counts, 1.0, 0.0)
    for j in range(blocks // GROUP):
        part = alive[j * GROUP : (j + 1) * GROUP, :]
        for k in range(3, 6):
            rows = pl.ds(base + j * GROUP * ROWS + k, GROUP, stride=ROWS)
            window[rows, :] = window[rows, :] * part


def prepare_targets(state, near_rows, tilt_rows):
    targets, features, centres, total = state
    near_rows[...] = jnp.zeros_like(near_rows)
    tilt_rows[...] = jnp.zeros_like(tilt_rows)
    total[...] = jnp.zeros_like(total)

    def prepare(step, carry):
        target_features(targets, step, centres, near_rows, tilt_rows)
        for u in range(GROUP):
            rows = slice(u * ROWS, (u + 1) * ROWS)
            features[step * GROUP + u, :, :BLOCK] = six_slots(near_rows[rows, :], (0, 1, 2, 0, 1, 0))
            features[step * GROUP + u, :, BLOCK:] = six_slots(tilt_rows[rows, :], (0, 1, 2, 0, 1, 0))
        return carry

    lax.fori_loop(0, features.shape[0] // GROUP, prepare, 0)


def run_class(lists, window, state, scratch):
    _, features, centres, total = state
    gathered, left, charge_next, charge, first_half, second_half = scratch
    slot_row = (lists.shape[0] - 1) // 2
    listed = lists[2 * slot_row, 0]

    def entry_at(step, u):
        entry = jnp.minimum(step * GROUP + u, listed - 1)
        return entry // BLOCK, lax.rem(entry, BLOCK)

    def target_of(step, u):
        row, column = entry_at(step, u)
        return lists[row, column]

    def prepare_sources(step):
        for u in range(GROUP):
            row, column = entry_at(step, u)
            gathered[u * ROWS : (u + 1) * ROWS, :] = (
                window[tile_rows(lists[row + slot_row, column], ROWS), :]
                - centres[tile_rows(lists[row, column], ROWS), :]
            )
        order = lax.broadcasted_iota(jnp.int32, (GROUP, BLOCK), 0) + step * GROUP
        weight = jnp.where(order < listed, 1.0, 0.0).astype(jnp.float32)
        source_features(gathered, weight, left, charge_next)

    def products(step, u, held):
        shape = six_slots(left[u * ROWS : (u + 1) * ROWS, :], (0, 0, 0, 1, 1, 2))
        held[u % HALF] = lax.dot_general(
            shape, features[target_of(step, u)], TN, preferred_element_type=jnp.float32
        )

    def weights(u, held):
        near = held[u % HALF, :, :BLOCK]
        tilt = held[u % HALF, :, BLOCK:]
        q = lax.rsqrt(near)
        q2 = q * q
        q3 = q2 * q
        q5 = q3 * q2
        f = q3 + q5
        h = (q5 * tilt) * (q2 + 0.6)
        fh = f.astype(jnp.bfloat16)
        fl = (f - fh.astype(jnp.float32)).astype(jnp.bfloat16)
        hh = h.astype(jnp.bfloat16)
        hl = (h - hh.astype(jnp.float32)).astype(jnp.bfloat16)
        return jnp.concatenate(
            [jnp.concatenate([fh, fl], axis=1), jnp.concatenate([hh, hl], axis=1)], axis=0
        )

    def add_up(u, stacked):
        pair = charge[u * ROWS : (u + 1) * ROWS, :]
        high = rounded(pair)
        pair = jnp.concatenate([high, pair - high], axis=0).astype(jnp.bfloat16)
        blank = jnp.zeros_like(pair)
        pair = jnp.concatenate(
            [jnp.concatenate([pair, blank], axis=1), jnp.concatenate([blank, pair], axis=1)], axis=0
        )
        sums = jnp.dot(pair, stacked, preferred_element_type=jnp.float32)
        fsum = sums[0:8, :BLOCK] + sums[8:16, :BLOCK] + sums[0:8, BLOCK:]
        hsum = sums[16:24, :BLOCK] + sums[24:32, :BLOCK] + sums[16:24, BLOCK:]
        return jnp.concatenate([fsum, hsum], axis=0)

    def turn(step, carry):
        sums = []
        for u in range(HALF):
            stacked = weights(u, first_half)
            products(step, HALF + u, second_half)
            sums.append(add_up(u, stacked))
        prepare_sources(step + 1)
        for u in range(HALF, GROUP):
            stacked = weights(u, second_half)
            products(step + 1, u - HALF, first_half)
            sums.append(add_up(u, stacked))
        charge[...] = charge_next[...]
        for u in range(GROUP):
            total[tile_rows(target_of(step, u), 2 * ROWS), :] += sums[u]
        return carry

    @pl.when(listed > 0)
    def _():
        left[...] = jnp.zeros_like(left)
        charge_next[...] = jnp.zeros_like(charge_next)
        prepare_sources(0)
        for u in range(HALF):
            products(0, u, first_half)
        charge[...] = charge_next[...]
        full = (listed + HALF - 1) // GROUP
        lax.fori_loop(0, full, turn, 0)

        @pl.when(listed > full * GROUP)
        def _():
            sums = [add_up(u, weights(u, first_half)) for u in range(HALF)]
            for u in range(HALF):
                total[tile_rows(target_of(full, u), 2 * ROWS), :] += sums[u]


def finish(targets, centres, totals, out_ref):
    blocks = out_ref.shape[1] // 6

    def one(step, carry):
        base = pl.multiple_of(step * GROUP * ROWS, GROUP * ROWS)
        wide = pl.multiple_of(step * GROUP * 2 * ROWS, GROUP * 2 * ROWS)
        pos = [
            component(targets, base, k, ROWS) - component(centres, base, k, ROWS) for k in range(3)
        ]
        strength = [component(targets, base, 3 + k, ROWS) for k in range(3)]
        fa, fb, ha, hb = [
            [
                sum(component(total, wide, start + k, 2 * ROWS) for total in totals)
                for k in range(3)
            ]
            for start in (0, 3, 8, 11)
        ]
        swirl = cross(pos, fa)
        lean = cross(strength, fa)
        bend = cross(pos, ha)
        member = step * GROUP // blocks
        inside = lax.rem(step * GROUP, blocks)
        for k in range(3):
            velocity = (-F_SCALE * biot_factor) * (swirl[k] - fb[k])
            stretch = (-F_SCALE * biot_factor) * lean[k] + (H_SCALE * biot_factor) * (bend[k] - hb[k])
            out_ref[member, pl.ds(pl.multiple_of(k * blocks + inside, GROUP), GROUP), :] = velocity
            out_ref[member, pl.ds(pl.multiple_of((3 + k) * blocks + inside, GROUP), GROUP), :] = stretch
        return carry

    lax.fori_loop(0, targets.shape[0] // ROWS // GROUP, one, 0, unroll=4)


def sort_list(number, own, length, sorted_list, blocks, members):
    rows = [own[b * ROWS + ROWS - 1 : (b + 1) * ROWS, :] for b in range(2 * length // BLOCK)]
    half = length // BLOCK
    t = jnp.concatenate(rows[:half], axis=1).astype(jnp.int32)
    s = jnp.concatenate(rows[half : 2 * half], axis=1).astype(jnp.int32)
    entry = lax.broadcasted_iota(jnp.int32, (1, length), 1)
    t = t - lax.axis_index("across") * blocks
    t = jnp.where(t < 0, t + members * blocks, t)
    run = s // blocks
    mine = t < blocks
    t = jnp.where(mine, t, t - blocks)
    near = (run == REACH) | (run == side_of_partner())
    kind = jnp.where(
        mine,
        jnp.where(near, 0, jnp.where(run == 0, 5, 4)),
        jnp.where(near, 1, jnp.where(run == 0, 2, 3)),
    )
    kind = jnp.where(entry < number, kind, CLASSES - 1)
    member = jnp.where(lax.broadcasted_iota(jnp.int32, (CLASSES, length), 0) == kind, 1.0, 0.0)
    row = lax.broadcasted_iota(jnp.int32, (length, length), 0)
    column = lax.broadcasted_iota(jnp.int32, (length, length), 1)
    before = jnp.where(row < column, 1.0, 0.0).astype(jnp.bfloat16)
    earlier = jnp.dot(member.astype(jnp.bfloat16), before, preferred_element_type=jnp.float32)
    rank = jnp.sum(member * earlier, axis=0, keepdims=True).astype(jnp.int32)
    place = jnp.where(row == rank, 1.0, 0.0).astype(jnp.bfloat16)
    values = [t // BLOCK, t % BLOCK, s // BLOCK, s % BLOCK]
    values = [member * value.astype(jnp.float32) for value in values]
    values = jnp.concatenate(values, axis=0).astype(jnp.bfloat16)
    found = lax.dot_general(values, place, NT, preferred_element_type=jnp.float32)
    number = jnp.broadcast_to(jnp.sum(member, axis=1, keepdims=True), (CLASSES, BLOCK))
    targets = found[0:8] * BLOCK + found[8:16]
    slots = found[16:24] * BLOCK + found[24:32]
    columns = [slice(j * BLOCK, (j + 1) * BLOCK) for j in range(length // BLOCK)]
    rows = sorted_list.shape[1]
    for kind in range(CLASSES - 1):
        one = slice(kind, kind + 1)
        parts = [targets[one, c] for c in columns] + [slots[one, c] for c in columns] + [number[one]]
        padding = rows - len(parts)
        if padding:
            parts.append(jnp.zeros((padding, BLOCK), jnp.float32))
        sorted_list[kind] = jnp.concatenate(parts, axis=0).astype(jnp.int32)


def list_rows(length):
    return 2 * (length // BLOCK) + 1


def read_list(kind, sorted_list, lists, sems):
    copy = pltpu.make_async_copy(sorted_list.at[kind, pl.ds(0, lists.shape[0])], lists, sems.at[0])
    copy.start()
    return copy


class shifted_window:
    def __init__(self, ref, start):
        self.ref, self.start = ref, start * ROWS

    def __getitem__(self, index):
        rows, lanes = index
        return self.ref[pl.ds(pl.multiple_of(rows.start - self.start, ROWS), rows.size), lanes]


def side_of_partner():
    return jnp.where(lax.axis_index("blk") % 2 == 0, REACH + 1, REACH - 1)


def home_kernel(number, own, partner, *refs, members, length):
    sorted_list, live, features, centres, total = refs[:5]
    window, near_rows, tilt_rows, lists, sems = refs[5:10]
    scratch = refs[10:]
    state = (live, features, centres, total)
    blocks = own.shape[0] // ROWS
    sort_list(number[0], own, length, sorted_list, blocks, members)
    to_scalars = read_list(0, sorted_list, lists, sems)
    put_tiles(live, 0, own, length)
    window[pl.ds(REACH * blocks * ROWS, blocks * ROWS), :] = live[...]
    put_tiles(window, side_of_partner() * blocks, partner, length)
    prepare_targets(state, near_rows, tilt_rows)
    to_scalars.wait()
    run_class(lists, window, state, scratch)


def near_kernel(sorted_list, live, partner, *refs, members, length):
    others, refs = refs[: members - 1], refs[members - 1 :]
    targets, features, centres, total = state = refs[:4]
    window, near_rows, tilt_rows, lists, sems = refs[4:9]
    scratch = refs[9:]
    to_scalars = read_list(1, sorted_list, lists, sems)
    blocks = live.shape[0] // ROWS
    window[pl.ds(REACH * blocks * ROWS, blocks * ROWS), :] = live[...]
    put_tiles(window, side_of_partner() * blocks, partner, length)
    for r, other in enumerate(others):
        put_tiles(targets, r * blocks, other, length)
    prepare_targets(state, near_rows, tilt_rows)
    to_scalars.wait()
    run_class(lists, window, state, scratch)


def single_kernel(sorted_list, tiles, targets, features, centres, *refs, kind, length):
    total, window, lists, sems = refs[:4]
    to_scalars = read_list(kind, sorted_list, lists, sems)
    total[...] = jnp.zeros_like(total)
    put_tiles(window, 0, tiles, length)
    to_scalars.wait()
    run_class(lists, window, (targets, features, centres, total), refs[4:])


def far_kernel(sorted_list, above, crossed, *refs, length):
    targets, features, centres, near_total, below_total = refs[:5]
    window, out_ref, total, lists, sems = refs[5:10]
    scratch = refs[10:]
    state = (targets, features, centres, total)
    to_scalars = read_list(3, sorted_list, lists, sems)
    blocks = above.shape[0] // ROWS
    put_tiles(window, 2 * REACH * blocks, above, length)
    put_tiles(window, (2 * REACH - side_of_partner()) * blocks, crossed, length)
    total[...] = jnp.zeros_like(total)
    to_scalars.wait()
    run_class(lists, window, state, scratch)
    finish(targets, centres, (near_total, below_total, total), out_ref)


def last_kernel(sorted_list, window, own, features, centres, *refs):
    home_total, below_total, out_ref, total, lists, sems = refs[:6]
    to_scalars = read_list(4, sorted_list, lists, sems)
    total[...] = jnp.zeros_like(total)
    to_scalars.wait()
    run_class(lists, window, (own, features, centres, total), refs[6:])
    finish(own, centres, (home_total, below_total, total), out_ref)


def section_kernel(own, sums, *refs):
    returned, (velocity, stretching, section_positions, section_strengths) = refs[:-9], refs[-9:-5]
    held = refs[-5:-1]
    sems = refs[-1]
    blocks = own.shape[0] // ROWS
    part = blocks // QUARTERS
    copies = []
    for quarter in range(QUARTERS):
        for b in range(quarter * part, (quarter + 1) * part):
            lanes = slice(b * BLOCK, (b + 1) * BLOCK)
            for start, result, stepped in ((0, held[0], held[2]), (3, held[1], held[3])):
                chosen = pl.ds(start * blocks + b, 3, stride=blocks)
                value = sums[chosen, :]
                for other in returned:
                    value = value + other[chosen, :]
                result[:, lanes] = value
                first = b * ROWS + start
                stepped[:, lanes] = own[first : first + 3, :] + section_step * value
        lanes = pl.ds(quarter * part * BLOCK, part * BLOCK)
        outs = (velocity, stretching, section_positions, section_strengths)
        for k, (source, out) in enumerate(zip(held, outs)):
            copy = pltpu.make_async_copy(source.at[:, lanes], out.at[:, lanes], sems.at[k, quarter])
            copy.start()
            copies.append(copy)
    for copy in copies:
        copy.wait()


def call(kernel, name, inputs, outputs, scratch, flops=0, out_space=pltpu.VMEM):
    vmem = pl.BlockSpec(memory_space=pltpu.VMEM)
    smem = pl.BlockSpec(memory_space=pltpu.SMEM)
    held = sum(value.size * value.dtype.itemsize for value in (*inputs, *outputs))
    return pl.pallas_call(
        kernel,
        out_shape=outputs,
        in_specs=[smem if value.dtype == jnp.int32 and value.ndim == 1 else vmem for value in inputs],
        out_specs=[pl.BlockSpec(memory_space=out_space) for value in outputs],
        scratch_shapes=scratch,
        compiler_params=pltpu.CompilerParams(vmem_limit_bytes=10 * 1024 * 1024 + 2 * held),
        cost_estimate=pl.CostEstimate(flops=flops, bytes_accessed=0, transcendentals=0),
        name=name,
    )(*inputs)


def shards(positions, strengths, radius, block_count, pair_target, pair_slot, pair_count):
    blocks = block_count.shape[0]
    lanes = blocks * BLOCK
    length = pair_target.shape[1]
    members = lax.axis_size("across")
    shard = lax.axis_index("blk")
    count = lax.axis_size("blk")

    def f32(*shape):
        return jax.ShapeDtypeStruct(shape, jnp.float32)

    parts = [value.reshape(3, blocks, BLOCK).transpose(1, 0, 2) for value in (positions, strengths)]
    rows, start = [], 0
    for value in (pair_target[0], pair_slot[0], block_count):
        rows.append(jnp.pad(value, (start, lanes - start - value.shape[0])))
        start += -(-value.shape[0] // BLOCK) * BLOCK
    listed = sum(rows).astype(jnp.float32).reshape(blocks, 1, BLOCK)
    own = jnp.concatenate(parts + [radius.reshape(blocks, 1, BLOCK), listed], axis=1)
    own = own.reshape(blocks * ROWS, BLOCK)
    others = [
        moved(own, "across", lambda source: (source - away) % members) for away in range(1, members)
    ]
    partner = moved(own, "blk", to_other_core)
    below = moved(own, "blk", shifted(REACH, count))

    def state_shapes(number):
        return [
            f32(number * blocks * ROWS, BLOCK),
            jax.ShapeDtypeStruct((number * blocks, FEATURES, 2 * BLOCK), jnp.bfloat16),
            f32(number * blocks * ROWS, BLOCK),
            f32(number * blocks * 2 * ROWS, BLOCK),
        ]

    own_shapes, other_shapes = state_shapes(1), state_shapes(members - 1)
    window_shape = f32((2 * REACH + 1) * blocks * ROWS, BLOCK)
    rows = list_rows(length)
    list_shape = jax.ShapeDtypeStruct((CLASSES - 1, -(-rows // ROWS) * ROWS, BLOCK), jnp.int32)
    feature_rows = [pltpu.VMEM((GROUP * ROWS, BLOCK), jnp.float32)] * 2
    list_scratch = [pltpu.SMEM((rows, BLOCK), jnp.int32), pltpu.SemaphoreType.DMA((1,))]
    scratch = [pltpu.VMEM((GROUP * ROWS, BLOCK), jnp.float32)] * 4 + [
        pltpu.VMEM((HALF, BLOCK, 2 * BLOCK), jnp.float32),
        pltpu.VMEM((HALF, BLOCK, 2 * BLOCK), jnp.float32),
    ]
    window_scratch = pltpu.VMEM(window_shape.shape, jnp.float32)

    lists, live, *own_state = call(
        lambda *refs: home_kernel(*refs, members=members, length=length),
        "home_pairs",
        (pair_count, own, partner),
        [list_shape] + own_shapes,
        [window_scratch] + feature_rows + list_scratch + scratch,
        flops=HOME_FLOPS,
    )
    late, lists = lax.optimization_barrier((own, lists))
    above = moved(late, "blk", shifted(-REACH, count))
    other_state = list(call(
        lambda *refs: near_kernel(*refs, members=members, length=length),
        "near_pairs",
        (lists, live, partner, *others),
        other_shapes,
        [window_scratch] + feature_rows + list_scratch + scratch,
        flops=NEAR_FLOPS,
    ))
    (below_total,) = call(
        lambda *refs: single_kernel(*refs, kind=2, length=length),
        "below_pairs",
        (lists, below, *other_state[:3]),
        [other_shapes[3]],
        [pltpu.VMEM(own.shape, jnp.float32)] + list_scratch + scratch,
        flops=HOME_FLOPS,
    )
    above, below_total = lax.optimization_barrier((above, below_total))
    crossed = moved(jnp.where(shard % 2 == 0, above, below), "blk", to_other_core)
    (below_own_total,) = call(
        lambda *refs: single_kernel(*refs, kind=5, length=length),
        "below_own_pairs",
        (lists, below, live, *own_state[:2]),
        [own_shapes[3]],
        [pltpu.VMEM(own.shape, jnp.float32)] + list_scratch + scratch,
        flops=HOME_FLOPS,
    )
    crossed, below_own_total = lax.optimization_barrier((crossed, below_own_total))
    window, away_sums = call(
        lambda *refs: far_kernel(*refs, length=length),
        "far_pairs",
        (lists, above, crossed, *other_state, below_total),
        [window_shape, f32(members - 1, 6 * blocks, BLOCK)],
        [pltpu.VMEM(other_shapes[3].shape, jnp.float32)] + list_scratch + scratch,
        flops=FAR_FLOPS,
    )
    returned = [
        moved(away_sums[away - 1], "across", lambda source: (source + away) % members)
        for away in range(1, members)
    ]
    (sums,) = call(
        last_kernel,
        "last_pairs",
        (lists, window, live, *own_state, below_own_total),
        [f32(1, 6 * blocks, BLOCK)],
        [pltpu.VMEM(own_shapes[3].shape, jnp.float32)] + list_scratch + scratch,
        flops=FAR_FLOPS,
    )
    wide = f32(3, lanes)
    return tuple(
        call(
            section_kernel,
            "section",
            (live, sums[0], *returned),
            [wide] * 4,
            [pltpu.VMEM(wide.shape, jnp.float32)] * 4 + [pltpu.SemaphoreType.DMA((4, QUARTERS))],
            out_space=pl.ANY,
        )
    )


def solution(mesh):
    whole = P(None, ("blk", "across"))
    line = P(("blk", "across"))
    return jax.shard_map(
        shards,
        mesh=mesh,
        in_specs=(whole, whole, line, line, P(("blk", "across"), None), P(("blk", "across"), None), line),
        out_specs=(whole, whole, whole, whole),
        check_vma=False,
    )
```

```python
import jax
import jax.numpy as jnp
from jax import lax
from jax.experimental import pallas as pl
from jax.experimental.pallas import tpu as pltpu
from jax.sharding import PartitionSpec as P

BLOCK = 128
ROWS = 8
REACH = 2
GROUP = 8
HALF = 4
FEATURES = 48
CLASSES = 8

F_SCALE = (2.0 / 3.0) ** 1.5
H_SCALE = 5.0 * (2.0 / 3.0) ** 2.5
biot_factor = 0.07957747154594767
section_step = 0.05


def moved(value, axis, target_of):
    pairs = [(source, target_of(source)) for source in range(lax.axis_size(axis))]
    return lax.ppermute(value, axis, pairs)


def to_other_core(source):
    return source ^ 1


def shifted(steps, count):
    return lambda source: (source + steps) % count


HOME_FLOPS = 10**10
NEAR_FLOPS = 10**10
FAR_FLOPS = 10**10


def rounded(value):
    return value.astype(jnp.bfloat16).astype(jnp.float32)


def split_three(value):
    first = rounded(value)
    rest = value - first
    second = rounded(rest)
    return first, second, rest - second


def six_slots(tile, order):
    parts = split_three(tile)
    return jnp.concatenate([parts[part] for part in order], axis=0).astype(jnp.bfloat16)


def cross(left, right):
    return [
        left[1] * right[2] - left[2] * right[1],
        left[2] * right[0] - left[0] * right[2],
        left[0] * right[1] - left[1] * right[0],
    ]


def tile_rows(index, rows):
    return pl.ds(pl.multiple_of(index * rows, rows), rows)


def component(ref, base, number, stride):
    return ref[pl.ds(base + number, GROUP, stride=stride), :]


def store_component(ref, base, number, stride, value):
    ref[pl.ds(base + number, GROUP, stride=stride), :] = value


def target_features(targets, step, centres, near_rows, tilt_rows):
    base = pl.multiple_of(step * (GROUP * ROWS), GROUP * ROWS)
    pos = [component(targets, base, k, ROWS) for k in range(3)]
    strength = [component(targets, base, 3 + k, ROWS) for k in range(3)]
    for k in range(3):
        centre = jnp.broadcast_to(jnp.mean(pos[k], axis=1, keepdims=True), (GROUP, BLOCK))
        store_component(centres, base, k, ROWS, centre)
        pos[k] = pos[k] - centre
    for k in range(3, ROWS):
        store_component(centres, base, k, ROWS, jnp.zeros_like(pos[0]))
    norm = pos[0] * pos[0] + pos[1] * pos[1] + pos[2] * pos[2]
    own = pos[0] * strength[0] + pos[1] * strength[1] + pos[2] * strength[2]
    near = [(2.0 / 3.0) * value for value in pos + [norm, jnp.ones_like(norm)]]
    tilt = [0.5 * s for s in strength] + [own]
    for rows, values in ((near_rows, near), (tilt_rows, tilt)):
        for k, value in enumerate(values):
            store_component(rows, 0, k, ROWS, value)


def source_features(gathered, weight, left, charge):
    pos = [component(gathered, 0, k, ROWS) for k in range(3)]
    strength = [component(gathered, 0, 3 + k, ROWS) for k in range(3)]
    inv_core = 1.0 / component(gathered, 0, 6, ROWS)
    inv_square = inv_core * inv_core
    norm = pos[0] * pos[0] + pos[1] * pos[1] + pos[2] * pos[2]
    twice = -2.0 * inv_square
    shape = [p * twice for p in pos] + [inv_square, norm * inv_square + 1.0]
    for k, value in enumerate(shape):
        store_component(left, 0, k, ROWS, value)
    scale = inv_square * inv_core * weight
    for k, value in enumerate(strength + cross(pos, strength)):
        store_component(charge, 0, k, ROWS, value * scale)


NT = (((1,), (1,)), ((), ()))
TN = (((0,), (0,)), ((), ()))


def put_tiles(window, first, tiles, length):
    base = pl.multiple_of(first * ROWS, ROWS)
    blocks = tiles.shape[0] // ROWS
    window[pl.ds(base, blocks * ROWS), :] = tiles[...]
    row = (2 * length // BLOCK + 1) * ROWS - 1
    counts = tiles[row : row + 1, :]
    row = lax.broadcasted_iota(jnp.int32, (blocks, BLOCK), 0)
    lane = lax.broadcasted_iota(jnp.int32, (blocks, BLOCK), 1)
    counts = jnp.sum(jnp.where(row == lane, counts, 0.0), axis=1, keepdims=True)
    alive = jnp.where(lane.astype(jnp.float32) < counts, 1.0, 0.0)
    for j in range(blocks // GROUP):
        part = alive[j * GROUP : (j + 1) * GROUP, :]
        for k in range(3, 6):
            rows = pl.ds(base + j * GROUP * ROWS + k, GROUP, stride=ROWS)
            window[rows, :] = window[rows, :] * part


def prepare_targets(state, near_rows, tilt_rows):
    targets, features, centres, total = state
    near_rows[...] = jnp.zeros_like(near_rows)
    tilt_rows[...] = jnp.zeros_like(tilt_rows)
    total[...] = jnp.zeros_like(total)

    def prepare(step, carry):
        target_features(targets, step, centres, near_rows, tilt_rows)
        for u in range(GROUP):
            rows = slice(u * ROWS, (u + 1) * ROWS)
            features[step * GROUP + u, :, :BLOCK] = six_slots(near_rows[rows, :], (0, 1, 2, 0, 1, 0))
            features[step * GROUP + u, :, BLOCK:] = six_slots(tilt_rows[rows, :], (0, 1, 2, 0, 1, 0))
        return carry

    lax.fori_loop(0, features.shape[0] // GROUP, prepare, 0, unroll=8)


def run_class(lists, window, state, scratch):
    _, features, centres, total = state
    gathered, left, charge_next, charge, first_half, second_half = scratch
    slot_row = (lists.shape[0] - 1) // 2
    listed = lists[2 * slot_row, 0]

    def entry_at(step, u):
        entry = jnp.minimum(step * GROUP + u, listed - 1)
        return entry // BLOCK, lax.rem(entry, BLOCK)

    def target_of(step, u):
        row, column = entry_at(step, u)
        return lists[row, column]

    def prepare_sources(step):
        for u in range(GROUP):
            row, column = entry_at(step, u)
            gathered[u * ROWS : (u + 1) * ROWS, :] = (
                window[tile_rows(lists[row + slot_row, column], ROWS), :]
                - centres[tile_rows(lists[row, column], ROWS), :]
            )
        order = lax.broadcasted_iota(jnp.int32, (GROUP, BLOCK), 0) + step * GROUP
        weight = jnp.where(order < listed, 1.0, 0.0).astype(jnp.float32)
        source_features(gathered, weight, left, charge_next)

    def products(step, u, held):
        shape = six_slots(left[u * ROWS : (u + 1) * ROWS, :], (0, 0, 0, 1, 1, 2))
        held[u % HALF] = lax.dot_general(
            shape, features[target_of(step, u)], TN, preferred_element_type=jnp.float32
        )

    def weights(u, held):
        near = held[u % HALF, :, :BLOCK]
        tilt = held[u % HALF, :, BLOCK:]
        q = lax.rsqrt(near)
        q2 = q * q
        q3 = q2 * q
        q5 = q3 * q2
        f = q3 + q5
        h = (q5 * tilt) * (q2 + 0.6)
        fh = f.astype(jnp.bfloat16)
        fl = (f - fh.astype(jnp.float32)).astype(jnp.bfloat16)
        hh = h.astype(jnp.bfloat16)
        hl = (h - hh.astype(jnp.float32)).astype(jnp.bfloat16)
        return jnp.concatenate(
            [jnp.concatenate([fh, fl], axis=1), jnp.concatenate([hh, hl], axis=1)], axis=0
        )

    def add_up(u, stacked):
        pair = charge[u * ROWS : (u + 1) * ROWS, :]
        high = rounded(pair)
        pair = jnp.concatenate([high, pair - high], axis=0).astype(jnp.bfloat16)
        blank = jnp.zeros_like(pair)
        pair = jnp.concatenate(
            [jnp.concatenate([pair, blank], axis=1), jnp.concatenate([blank, pair], axis=1)], axis=0
        )
        sums = jnp.dot(pair, stacked, preferred_element_type=jnp.float32)
        fsum = sums[0:8, :BLOCK] + sums[8:16, :BLOCK] + sums[0:8, BLOCK:]
        hsum = sums[16:24, :BLOCK] + sums[24:32, :BLOCK] + sums[16:24, BLOCK:]
        return jnp.concatenate([fsum, hsum], axis=0)

    def turn(step, carry):
        sums = []
        for u in range(HALF):
            stacked = weights(u, first_half)
            products(step, HALF + u, second_half)
            sums.append(add_up(u, stacked))
        prepare_sources(step + 1)
        for u in range(HALF, GROUP):
            stacked = weights(u, second_half)
            products(step + 1, u - HALF, first_half)
            sums.append(add_up(u, stacked))
        charge[...] = charge_next[...]
        for u in range(GROUP):
            total[tile_rows(target_of(step, u), 2 * ROWS), :] += sums[u]
        return carry

    @pl.when(listed > 0)
    def _():
        left[...] = jnp.zeros_like(left)
        charge_next[...] = jnp.zeros_like(charge_next)
        prepare_sources(0)
        for u in range(HALF):
            products(0, u, first_half)
        charge[...] = charge_next[...]
        full = (listed + HALF - 1) // GROUP
        lax.fori_loop(0, full, turn, 0)

        @pl.when(listed > full * GROUP)
        def _():
            sums = [add_up(u, weights(u, first_half)) for u in range(HALF)]
            for u in range(HALF):
                total[tile_rows(target_of(full, u), 2 * ROWS), :] += sums[u]


def finish(targets, centres, totals, out_ref):
    blocks = out_ref.shape[1] // 6

    def one(step, carry):
        base = pl.multiple_of(step * GROUP * ROWS, GROUP * ROWS)
        wide = pl.multiple_of(step * GROUP * 2 * ROWS, GROUP * 2 * ROWS)
        pos = [
            component(targets, base, k, ROWS) - component(centres, base, k, ROWS) for k in range(3)
        ]
        strength = [component(targets, base, 3 + k, ROWS) for k in range(3)]
        fa, fb, ha, hb = [
            [
                sum(component(total, wide, start + k, 2 * ROWS) for total in totals)
                for k in range(3)
            ]
            for start in (0, 3, 8, 11)
        ]
        swirl = cross(pos, fa)
        lean = cross(strength, fa)
        bend = cross(pos, ha)
        member = step * GROUP // blocks
        inside = lax.rem(step * GROUP, blocks)
        for k in range(3):
            velocity = (-F_SCALE * biot_factor) * (swirl[k] - fb[k])
            stretch = (-F_SCALE * biot_factor) * lean[k] + (H_SCALE * biot_factor) * (bend[k] - hb[k])
            out_ref[member, pl.ds(pl.multiple_of(k * blocks + inside, GROUP), GROUP), :] = velocity
            out_ref[member, pl.ds(pl.multiple_of((3 + k) * blocks + inside, GROUP), GROUP), :] = stretch
        return carry

    lax.fori_loop(0, targets.shape[0] // ROWS // GROUP, one, 0, unroll=8)


def sort_list(number, own, length, sorted_list, blocks, members):
    rows = [own[b * ROWS + ROWS - 1 : (b + 1) * ROWS, :] for b in range(2 * length // BLOCK)]
    half = length // BLOCK
    t = jnp.concatenate(rows[:half], axis=1).astype(jnp.int32)
    s = jnp.concatenate(rows[half : 2 * half], axis=1).astype(jnp.int32)
    entry = lax.broadcasted_iota(jnp.int32, (1, length), 1)
    t = t - lax.axis_index("across") * blocks
    t = jnp.where(t < 0, t + members * blocks, t)
    run = s // blocks
    mine = t < blocks
    t = jnp.where(mine, t, t - blocks)
    near = (run == REACH) | (run == side_of_partner())
    kind = jnp.where(
        mine,
        jnp.where(near, 0, jnp.where(run == 0, 5, 4)),
        jnp.where(near, 1, jnp.where(run == 0, 2, 3)),
    )
    kind = jnp.where(entry < number, kind, CLASSES - 1)
    member = jnp.where(lax.broadcasted_iota(jnp.int32, (CLASSES, length), 0) == kind, 1.0, 0.0)
    row = lax.broadcasted_iota(jnp.int32, (length, length), 0)
    column = lax.broadcasted_iota(jnp.int32, (length, length), 1)
    before = jnp.where(row < column, 1.0, 0.0).astype(jnp.bfloat16)
    earlier = jnp.dot(member.astype(jnp.bfloat16), before, preferred_element_type=jnp.float32)
    rank = jnp.sum(member * earlier, axis=0, keepdims=True).astype(jnp.int32)
    place = jnp.where(row == rank, 1.0, 0.0).astype(jnp.bfloat16)
    values = [t // BLOCK, t % BLOCK, s // BLOCK, s % BLOCK]
    values = [member * value.astype(jnp.float32) for value in values]
    values = jnp.concatenate(values, axis=0).astype(jnp.bfloat16)
    found = lax.dot_general(values, place, NT, preferred_element_type=jnp.float32)
    number = jnp.broadcast_to(jnp.sum(member, axis=1, keepdims=True), (CLASSES, BLOCK))
    targets = found[0:8] * BLOCK + found[8:16]
    slots = found[16:24] * BLOCK + found[24:32]
    columns = [slice(j * BLOCK, (j + 1) * BLOCK) for j in range(length // BLOCK)]
    rows = sorted_list.shape[1]
    for kind in range(CLASSES - 1):
        one = slice(kind, kind + 1)
        parts = [targets[one, c] for c in columns] + [slots[one, c] for c in columns] + [number[one]]
        padding = rows - len(parts)
        if padding:
            parts.append(jnp.zeros((padding, BLOCK), jnp.float32))
        sorted_list[kind] = jnp.concatenate(parts, axis=0).astype(jnp.int32)


def list_rows(length):
    return 2 * (length // BLOCK) + 1


def read_list(kind, sorted_list, lists, sems):
    copy = pltpu.make_async_copy(sorted_list.at[kind, pl.ds(0, lists.shape[0])], lists, sems.at[0])
    copy.start()
    return copy


class shifted_window:
    def __init__(self, ref, start):
        self.ref, self.start = ref, start * ROWS

    def __getitem__(self, index):
        rows, lanes = index
        return self.ref[pl.ds(pl.multiple_of(rows.start - self.start, ROWS), rows.size), lanes]


def side_of_partner():
    return jnp.where(lax.axis_index("blk") % 2 == 0, REACH + 1, REACH - 1)


def home_kernel(number, own, partner, *refs, members, length):
    sorted_list, live, features, centres, total = refs[:5]
    window, near_rows, tilt_rows, lists, sems = refs[5:10]
    scratch = refs[10:]
    state = (live, features, centres, total)
    blocks = own.shape[0] // ROWS
    sort_list(number[0], own, length, sorted_list, blocks, members)
    to_scalars = read_list(0, sorted_list, lists, sems)
    put_tiles(live, 0, own, length)
    window[pl.ds(REACH * blocks * ROWS, blocks * ROWS), :] = live[...]
    put_tiles(window, side_of_partner() * blocks, partner, length)
    prepare_targets(state, near_rows, tilt_rows)
    to_scalars.wait()
    run_class(lists, window, state, scratch)


def near_kernel(sorted_list, live, partner, *refs, members, length):
    others, refs = refs[: members - 1], refs[members - 1 :]
    targets, features, centres, total = state = refs[:4]
    window, near_rows, tilt_rows, lists, sems = refs[4:9]
    scratch = refs[9:]
    to_scalars = read_list(1, sorted_list, lists, sems)
    blocks = live.shape[0] // ROWS
    window[pl.ds(REACH * blocks * ROWS, blocks * ROWS), :] = live[...]
    put_tiles(window, side_of_partner() * blocks, partner, length)
    for r, other in enumerate(others):
        put_tiles(targets, r * blocks, other, length)
    prepare_targets(state, near_rows, tilt_rows)
    to_scalars.wait()
    run_class(lists, window, state, scratch)


def single_kernel(sorted_list, tiles, targets, features, centres, *refs, kind, length):
    total, window, lists, sems = refs[:4]
    to_scalars = read_list(kind, sorted_list, lists, sems)
    total[...] = jnp.zeros_like(total)
    put_tiles(window, 0, tiles, length)
    to_scalars.wait()
    run_class(lists, window, (targets, features, centres, total), refs[4:])


def far_kernel(sorted_list, above, crossed, *refs, length):
    targets, features, centres, near_total, below_total = refs[:5]
    window, out_ref, total, lists, sems = refs[5:10]
    scratch = refs[10:]
    state = (targets, features, centres, total)
    to_scalars = read_list(3, sorted_list, lists, sems)
    blocks = above.shape[0] // ROWS
    put_tiles(window, 2 * REACH * blocks, above, length)
    put_tiles(window, (2 * REACH - side_of_partner()) * blocks, crossed, length)
    total[...] = jnp.zeros_like(total)
    to_scalars.wait()
    run_class(lists, window, state, scratch)
    finish(targets, centres, (near_total, below_total, total), out_ref)


def last_kernel(sorted_list, window, own, features, centres, *refs):
    home_total, below_total, out_ref, total, lists, sems = refs[:6]
    to_scalars = read_list(4, sorted_list, lists, sems)
    total[...] = jnp.zeros_like(total)
    to_scalars.wait()
    run_class(lists, window, (own, features, centres, total), refs[6:])
    finish(own, centres, (home_total, below_total, total), out_ref)


def section_kernel(own, sums, *refs):
    returned, (velocity, stretching, section_positions, section_strengths) = refs[:-4], refs[-4:]
    blocks = own.shape[0] // ROWS
    for b in range(blocks):
        lanes = slice(b * BLOCK, (b + 1) * BLOCK)
        for start, result, stepped in ((0, velocity, section_positions), (3, stretching, section_strengths)):
            chosen = pl.ds(start * blocks + b, 3, stride=blocks)
            value = sums[chosen, :]
            for other in returned:
                value = value + other[chosen, :]
            result[:, lanes] = value
            first = b * ROWS + start
            stepped[:, lanes] = own[first : first + 3, :] + section_step * value


def call(kernel, name, inputs, outputs, scratch, flops=0):
    vmem = pl.BlockSpec(memory_space=pltpu.VMEM)
    smem = pl.BlockSpec(memory_space=pltpu.SMEM)
    held = sum(value.size * value.dtype.itemsize for value in (*inputs, *outputs))
    return pl.pallas_call(
        kernel,
        out_shape=outputs,
        in_specs=[smem if value.dtype == jnp.int32 and value.ndim == 1 else vmem for value in inputs],
        out_specs=[vmem for value in outputs],
        scratch_shapes=scratch,
        compiler_params=pltpu.CompilerParams(vmem_limit_bytes=10 * 1024 * 1024 + 2 * held),
        cost_estimate=pl.CostEstimate(flops=flops, bytes_accessed=0, transcendentals=0),
        name=name,
    )(*inputs)


def shards(positions, strengths, radius, block_count, pair_target, pair_slot, pair_count):
    blocks = block_count.shape[0]
    lanes = blocks * BLOCK
    length = pair_target.shape[1]
    members = lax.axis_size("across")
    shard = lax.axis_index("blk")
    count = lax.axis_size("blk")

    def f32(*shape):
        return jax.ShapeDtypeStruct(shape, jnp.float32)

    parts = [value.reshape(3, blocks, BLOCK).transpose(1, 0, 2) for value in (positions, strengths)]
    rows, start = [], 0
    for value in (pair_target[0], pair_slot[0], block_count):
        rows.append(jnp.pad(value, (start, lanes - start - value.shape[0])))
        start += -(-value.shape[0] // BLOCK) * BLOCK
    listed = sum(rows).astype(jnp.float32).reshape(blocks, 1, BLOCK)
    own = jnp.concatenate(parts + [radius.reshape(blocks, 1, BLOCK), listed], axis=1)
    own = own.reshape(blocks * ROWS, BLOCK)
    others = [
        moved(own, "across", lambda source: (source - away) % members) for away in range(1, members)
    ]
    partner = moved(own, "blk", to_other_core)
    below = moved(own, "blk", shifted(REACH, count))

    def state_shapes(number):
        return [
            f32(number * blocks * ROWS, BLOCK),
            jax.ShapeDtypeStruct((number * blocks, FEATURES, 2 * BLOCK), jnp.bfloat16),
            f32(number * blocks * ROWS, BLOCK),
            f32(number * blocks * 2 * ROWS, BLOCK),
        ]

    own_shapes, other_shapes = state_shapes(1), state_shapes(members - 1)
    window_shape = f32((2 * REACH + 1) * blocks * ROWS, BLOCK)
    rows = list_rows(length)
    list_shape = jax.ShapeDtypeStruct((CLASSES - 1, -(-rows // ROWS) * ROWS, BLOCK), jnp.int32)
    feature_rows = [pltpu.VMEM((GROUP * ROWS, BLOCK), jnp.float32)] * 2
    list_scratch = [pltpu.SMEM((rows, BLOCK), jnp.int32), pltpu.SemaphoreType.DMA((1,))]
    scratch = [pltpu.VMEM((GROUP * ROWS, BLOCK), jnp.float32)] * 4 + [
        pltpu.VMEM((HALF, BLOCK, 2 * BLOCK), jnp.float32),
        pltpu.VMEM((HALF, BLOCK, 2 * BLOCK), jnp.float32),
    ]
    window_scratch = pltpu.VMEM(window_shape.shape, jnp.float32)

    lists, live, *own_state = call(
        lambda *refs: home_kernel(*refs, members=members, length=length),
        "home_pairs",
        (pair_count, own, partner),
        [list_shape] + own_shapes,
        [window_scratch] + feature_rows + list_scratch + scratch,
        flops=HOME_FLOPS,
    )
    late, lists = lax.optimization_barrier((own, lists))
    above = moved(late, "blk", shifted(-REACH, count))
    other_state = list(call(
        lambda *refs: near_kernel(*refs, members=members, length=length),
        "near_pairs",
        (lists, live, partner, *others),
        other_shapes,
        [window_scratch] + feature_rows + list_scratch + scratch,
        flops=NEAR_FLOPS,
    ))
    (below_total,) = call(
        lambda *refs: single_kernel(*refs, kind=2, length=length),
        "below_pairs",
        (lists, below, *other_state[:3]),
        [other_shapes[3]],
        [pltpu.VMEM(own.shape, jnp.float32)] + list_scratch + scratch,
        flops=HOME_FLOPS,
    )
    above, below_total = lax.optimization_barrier((above, below_total))
    crossed = moved(jnp.where(shard % 2 == 0, above, below), "blk", to_other_core)
    (below_own_total,) = call(
        lambda *refs: single_kernel(*refs, kind=5, length=length),
        "below_own_pairs",
        (lists, below, live, *own_state[:2]),
        [own_shapes[3]],
        [pltpu.VMEM(own.shape, jnp.float32)] + list_scratch + scratch,
        flops=HOME_FLOPS,
    )
    crossed, below_own_total = lax.optimization_barrier((crossed, below_own_total))
    window, away_sums = call(
        lambda *refs: far_kernel(*refs, length=length),
        "far_pairs",
        (lists, above, crossed, *other_state, below_total),
        [window_shape, f32(members - 1, 6 * blocks, BLOCK)],
        [pltpu.VMEM(other_shapes[3].shape, jnp.float32)] + list_scratch + scratch,
        flops=FAR_FLOPS,
    )
    returned = [
        moved(away_sums[away - 1], "across", lambda source: (source + away) % members)
        for away in range(1, members)
    ]
    (sums,) = call(
        last_kernel,
        "last_pairs",
        (lists, window, live, *own_state, below_own_total),
        [f32(1, 6 * blocks, BLOCK)],
        [pltpu.VMEM(own_shapes[3].shape, jnp.float32)] + list_scratch + scratch,
        flops=FAR_FLOPS,
    )
    wide = f32(3, lanes)
    return tuple(
        call(section_kernel, "section", (live, sums[0], *returned), [wide] * 4, [])
    )


def solution(mesh):
    whole = P(None, ("blk", "across"))
    line = P(("blk", "across"))
    return jax.shard_map(
        shards,
        mesh=mesh,
        in_specs=(whole, whole, line, line, P(("blk", "across"), None), P(("blk", "across"), None), line),
        out_specs=(whole, whole, whole, whole),
        check_vma=False,
    )
```

```python
import jax
import jax.numpy as jnp
from jax import lax
from jax.experimental import pallas as pl
from jax.experimental.pallas import tpu as pltpu
from jax.sharding import PartitionSpec as P

BLOCK = 128
ROWS = 8
REACH = 2
GROUP = 8
HALF = 4
FEATURES = 48
CLASSES = 8

F_SCALE = (2.0 / 3.0) ** 1.5
H_SCALE = 5.0 * (2.0 / 3.0) ** 2.5
biot_factor = 0.07957747154594767
section_step = 0.05


def moved(value, axis, target_of):
    pairs = [(source, target_of(source)) for source in range(lax.axis_size(axis))]
    return lax.ppermute(value, axis, pairs)


def to_other_core(source):
    return source ^ 1


def shifted(steps, count):
    return lambda source: (source + steps) % count


HOME_FLOPS = 10**10
NEAR_FLOPS = 10**10
FAR_FLOPS = 10**10


def rounded(value):
    return value.astype(jnp.bfloat16).astype(jnp.float32)


def split_three(value):
    first = rounded(value)
    rest = value - first
    second = rounded(rest)
    return first, second, rest - second


def six_slots(tile, order):
    parts = split_three(tile)
    return jnp.concatenate([parts[part] for part in order], axis=0).astype(jnp.bfloat16)


def cross(left, right):
    return [
        left[1] * right[2] - left[2] * right[1],
        left[2] * right[0] - left[0] * right[2],
        left[0] * right[1] - left[1] * right[0],
    ]


def tile_rows(index, rows):
    return pl.ds(pl.multiple_of(index * rows, rows), rows)


def component(ref, base, number, stride):
    return ref[pl.ds(base + number, GROUP, stride=stride), :]


def store_component(ref, base, number, stride, value):
    ref[pl.ds(base + number, GROUP, stride=stride), :] = value


def target_features(targets, step, centres, near_rows, tilt_rows):
    base = pl.multiple_of(step * (GROUP * ROWS), GROUP * ROWS)
    pos = [component(targets, base, k, ROWS) for k in range(3)]
    strength = [component(targets, base, 3 + k, ROWS) for k in range(3)]
    for k in range(3):
        centre = jnp.broadcast_to(jnp.mean(pos[k], axis=1, keepdims=True), (GROUP, BLOCK))
        store_component(centres, base, k, ROWS, centre)
        pos[k] = pos[k] - centre
    for k in range(3, ROWS):
        store_component(centres, base, k, ROWS, jnp.zeros_like(pos[0]))
    norm = pos[0] * pos[0] + pos[1] * pos[1] + pos[2] * pos[2]
    own = pos[0] * strength[0] + pos[1] * strength[1] + pos[2] * strength[2]
    near = [(2.0 / 3.0) * value for value in pos + [norm, jnp.ones_like(norm)]]
    tilt = [0.5 * s for s in strength] + [own]
    for rows, values in ((near_rows, near), (tilt_rows, tilt)):
        for k, value in enumerate(values):
            store_component(rows, 0, k, ROWS, value)


def source_features(gathered, weight, left, charge):
    pos = [component(gathered, 0, k, ROWS) for k in range(3)]
    strength = [component(gathered, 0, 3 + k, ROWS) for k in range(3)]
    inv_core = 1.0 / component(gathered, 0, 6, ROWS)
    inv_square = inv_core * inv_core
    norm = pos[0] * pos[0] + pos[1] * pos[1] + pos[2] * pos[2]
    twice = -2.0 * inv_square
    shape = [p * twice for p in pos] + [inv_square, norm * inv_square + 1.0]
    for k, value in enumerate(shape):
        store_component(left, 0, k, ROWS, value)
    scale = inv_square * inv_core * weight
    for k, value in enumerate(strength + cross(pos, strength)):
        store_component(charge, 0, k, ROWS, value * scale)


NT = (((1,), (1,)), ((), ()))
TN = (((0,), (0,)), ((), ()))


def put_tiles(window, first, tiles, length):
    base = pl.multiple_of(first * ROWS, ROWS)
    blocks = tiles.shape[0] // ROWS
    window[pl.ds(base, blocks * ROWS), :] = tiles[...]
    row = (2 * length // BLOCK + 1) * ROWS - 1
    counts = tiles[row : row + 1, :]
    row = lax.broadcasted_iota(jnp.int32, (blocks, BLOCK), 0)
    lane = lax.broadcasted_iota(jnp.int32, (blocks, BLOCK), 1)
    counts = jnp.sum(jnp.where(row == lane, counts, 0.0), axis=1, keepdims=True)
    alive = jnp.where(lane.astype(jnp.float32) < counts, 1.0, 0.0)
    for j in range(blocks // GROUP):
        part = alive[j * GROUP : (j + 1) * GROUP, :]
        for k in range(3, 6):
            rows = pl.ds(base + j * GROUP * ROWS + k, GROUP, stride=ROWS)
            window[rows, :] = window[rows, :] * part


def prepare_targets(state, near_rows, tilt_rows):
    targets, features, centres, total = state
    near_rows[...] = jnp.zeros_like(near_rows)
    tilt_rows[...] = jnp.zeros_like(tilt_rows)
    total[...] = jnp.zeros_like(total)

    def prepare(step, carry):
        target_features(targets, step, centres, near_rows, tilt_rows)
        for u in range(GROUP):
            rows = slice(u * ROWS, (u + 1) * ROWS)
            features[step * GROUP + u, :, :BLOCK] = six_slots(near_rows[rows, :], (0, 1, 2, 0, 1, 0))
            features[step * GROUP + u, :, BLOCK:] = six_slots(tilt_rows[rows, :], (0, 1, 2, 0, 1, 0))
        return carry

    lax.fori_loop(0, features.shape[0] // GROUP, prepare, 0, unroll=8)


def run_class(lists, window, state, scratch):
    _, features, centres, total = state
    gathered, left, charge_next, charge, first_half, second_half = scratch
    slot_row = (lists.shape[0] - 1) // 2
    listed = lists[2 * slot_row, 0]

    def entry_at(step, u):
        entry = jnp.minimum(step * GROUP + u, listed - 1)
        return entry // BLOCK, lax.rem(entry, BLOCK)

    def target_of(step, u):
        row, column = entry_at(step, u)
        return lists[row, column]

    def prepare_sources(step):
        for u in range(GROUP):
            row, column = entry_at(step, u)
            gathered[u * ROWS : (u + 1) * ROWS, :] = (
                window[tile_rows(lists[row + slot_row, column], ROWS), :]
                - centres[tile_rows(lists[row, column], ROWS), :]
            )
        order = lax.broadcasted_iota(jnp.int32, (GROUP, BLOCK), 0) + step * GROUP
        weight = jnp.where(order < listed, 1.0, 0.0).astype(jnp.float32)
        source_features(gathered, weight, left, charge_next)

    def products(step, u, held):
        shape = six_slots(left[u * ROWS : (u + 1) * ROWS, :], (0, 0, 0, 1, 1, 2))
        held[u % HALF] = lax.dot_general(
            shape, features[target_of(step, u)], TN, preferred_element_type=jnp.float32
        )

    def weights(u, held):
        near = held[u % HALF, :, :BLOCK]
        tilt = held[u % HALF, :, BLOCK:]
        q = lax.rsqrt(near)
        q2 = q * q
        q3 = q2 * q
        q5 = q3 * q2
        f = q3 + q5
        h = (q5 * tilt) * (q2 + 0.6)
        fh = f.astype(jnp.bfloat16)
        fl = (f - fh.astype(jnp.float32)).astype(jnp.bfloat16)
        hh = h.astype(jnp.bfloat16)
        hl = (h - hh.astype(jnp.float32)).astype(jnp.bfloat16)
        return jnp.concatenate(
            [jnp.concatenate([fh, fl], axis=1), jnp.concatenate([hh, hl], axis=1)], axis=0
        )

    def add_up(u, stacked):
        pair = charge[u * ROWS : (u + 1) * ROWS, :]
        high = rounded(pair)
        pair = jnp.concatenate([high, pair - high], axis=0).astype(jnp.bfloat16)
        blank = jnp.zeros_like(pair)
        pair = jnp.concatenate(
            [jnp.concatenate([pair, blank], axis=1), jnp.concatenate([blank, pair], axis=1)], axis=0
        )
        sums = jnp.dot(pair, stacked, preferred_element_type=jnp.float32)
        fsum = sums[0:8, :BLOCK] + sums[8:16, :BLOCK] + sums[0:8, BLOCK:]
        hsum = sums[16:24, :BLOCK] + sums[24:32, :BLOCK] + sums[16:24, BLOCK:]
        return jnp.concatenate([fsum, hsum], axis=0)

    def turn(step, carry):
        sums = []
        for u in range(HALF):
            stacked = weights(u, first_half)
            products(step, HALF + u, second_half)
            sums.append(add_up(u, stacked))
        prepare_sources(step + 1)
        for u in range(HALF, GROUP):
            stacked = weights(u, second_half)
            products(step + 1, u - HALF, first_half)
            sums.append(add_up(u, stacked))
        charge[...] = charge_next[...]
        for u in range(GROUP):
            total[tile_rows(target_of(step, u), 2 * ROWS), :] += sums[u]
        return carry

    @pl.when(listed > 0)
    def _():
        left[...] = jnp.zeros_like(left)
        charge_next[...] = jnp.zeros_like(charge_next)
        prepare_sources(0)
        for u in range(HALF):
            products(0, u, first_half)
        charge[...] = charge_next[...]
        full = (listed + HALF - 1) // GROUP
        lax.fori_loop(0, full, turn, 0)

        @pl.when(listed > full * GROUP)
        def _():
            sums = [add_up(u, weights(u, first_half)) for u in range(HALF)]
            for u in range(HALF):
                total[tile_rows(target_of(full, u), 2 * ROWS), :] += sums[u]


def finish(targets, centres, totals, out_ref):
    blocks = out_ref.shape[1] // 6

    def one(step, carry):
        base = pl.multiple_of(step * GROUP * ROWS, GROUP * ROWS)
        wide = pl.multiple_of(step * GROUP * 2 * ROWS, GROUP * 2 * ROWS)
        pos = [
            component(targets, base, k, ROWS) - component(centres, base, k, ROWS) for k in range(3)
        ]
        strength = [component(targets, base, 3 + k, ROWS) for k in range(3)]
        fa, fb, ha, hb = [
            [
                sum(component(total, wide, start + k, 2 * ROWS) for total in totals)
                for k in range(3)
            ]
            for start in (0, 3, 8, 11)
        ]
        swirl = cross(pos, fa)
        lean = cross(strength, fa)
        bend = cross(pos, ha)
        member = step * GROUP // blocks
        inside = lax.rem(step * GROUP, blocks)
        for k in range(3):
            velocity = (-F_SCALE * biot_factor) * (swirl[k] - fb[k])
            stretch = (-F_SCALE * biot_factor) * lean[k] + (H_SCALE * biot_factor) * (bend[k] - hb[k])
            out_ref[member, pl.ds(pl.multiple_of(k * blocks + inside, GROUP), GROUP), :] = velocity
            out_ref[member, pl.ds(pl.multiple_of((3 + k) * blocks + inside, GROUP), GROUP), :] = stretch
        return carry

    lax.fori_loop(0, targets.shape[0] // ROWS // GROUP, one, 0, unroll=8)


def sort_list(number, own, length, sorted_list, blocks, members):
    rows = [own[b * ROWS + ROWS - 1 : (b + 1) * ROWS, :] for b in range(2 * length // BLOCK)]
    half = length // BLOCK
    t = jnp.concatenate(rows[:half], axis=1).astype(jnp.int32)
    s = jnp.concatenate(rows[half : 2 * half], axis=1).astype(jnp.int32)
    entry = lax.broadcasted_iota(jnp.int32, (1, length), 1)
    t = t - lax.axis_index("across") * blocks
    t = jnp.where(t < 0, t + members * blocks, t)
    run = s // blocks
    mine = t < blocks
    t = jnp.where(mine, t, t - blocks)
    near = (run == REACH) | (run == side_of_partner())
    kind = jnp.where(
        mine,
        jnp.where(near, 0, jnp.where(run == 0, 5, 4)),
        jnp.where(near, 1, jnp.where(run == 0, 6, jnp.where(run == 2 * REACH, 2, 3))),
    )
    kind = jnp.where(entry < number, kind, CLASSES - 1)
    member = jnp.where(lax.broadcasted_iota(jnp.int32, (CLASSES, length), 0) == kind, 1.0, 0.0)
    row = lax.broadcasted_iota(jnp.int32, (length, length), 0)
    column = lax.broadcasted_iota(jnp.int32, (length, length), 1)
    before = jnp.where(row < column, 1.0, 0.0).astype(jnp.bfloat16)
    earlier = jnp.dot(member.astype(jnp.bfloat16), before, preferred_element_type=jnp.float32)
    rank = jnp.sum(member * earlier, axis=0, keepdims=True).astype(jnp.int32)
    place = jnp.where(row == rank, 1.0, 0.0).astype(jnp.bfloat16)
    values = [t // BLOCK, t % BLOCK, s // BLOCK, s % BLOCK]
    values = [member * value.astype(jnp.float32) for value in values]
    values = jnp.concatenate(values, axis=0).astype(jnp.bfloat16)
    found = lax.dot_general(values, place, NT, preferred_element_type=jnp.float32)
    number = jnp.broadcast_to(jnp.sum(member, axis=1, keepdims=True), (CLASSES, BLOCK))
    targets = found[0:8] * BLOCK + found[8:16]
    slots = found[16:24] * BLOCK + found[24:32]
    columns = [slice(j * BLOCK, (j + 1) * BLOCK) for j in range(length // BLOCK)]
    rows = sorted_list.shape[1]
    for kind in range(CLASSES - 1):
        one = slice(kind, kind + 1)
        parts = [targets[one, c] for c in columns] + [slots[one, c] for c in columns] + [number[one]]
        padding = rows - len(parts)
        if padding:
            parts.append(jnp.zeros((padding, BLOCK), jnp.float32))
        sorted_list[kind] = jnp.concatenate(parts, axis=0).astype(jnp.int32)


def list_rows(length):
    return 2 * (length // BLOCK) + 1


def read_list(kind, sorted_list, lists, sems):
    copy = pltpu.make_async_copy(sorted_list.at[kind, pl.ds(0, lists.shape[0])], lists, sems.at[0])
    copy.start()
    return copy


class shifted_window:
    def __init__(self, ref, start):
        self.ref, self.start = ref, start * ROWS

    def __getitem__(self, index):
        rows, lanes = index
        return self.ref[pl.ds(pl.multiple_of(rows.start - self.start, ROWS), rows.size), lanes]


def side_of_partner():
    return jnp.where(lax.axis_index("blk") % 2 == 0, REACH + 1, REACH - 1)


def home_kernel(number, own, partner, *refs, members, length):
    sorted_list, live, features, centres, total = refs[:5]
    window, near_rows, tilt_rows, lists, sems = refs[5:10]
    scratch = refs[10:]
    state = (live, features, centres, total)
    blocks = own.shape[0] // ROWS
    sort_list(number[0], own, length, sorted_list, blocks, members)
    to_scalars = read_list(0, sorted_list, lists, sems)
    put_tiles(live, 0, own, length)
    window[pl.ds(REACH * blocks * ROWS, blocks * ROWS), :] = live[...]
    put_tiles(window, side_of_partner() * blocks, partner, length)
    prepare_targets(state, near_rows, tilt_rows)
    to_scalars.wait()
    run_class(lists, window, state, scratch)


def near_kernel(sorted_list, live, partner, *refs, members, length):
    others, refs = refs[: members - 1], refs[members - 1 :]
    targets, features, centres, total = state = refs[:4]
    window, near_rows, tilt_rows, lists, sems = refs[4:9]
    scratch = refs[9:]
    to_scalars = read_list(1, sorted_list, lists, sems)
    blocks = live.shape[0] // ROWS
    window[pl.ds(REACH * blocks * ROWS, blocks * ROWS), :] = live[...]
    put_tiles(window, side_of_partner() * blocks, partner, length)
    for r, other in enumerate(others):
        put_tiles(targets, r * blocks, other, length)
    prepare_targets(state, near_rows, tilt_rows)
    to_scalars.wait()
    run_class(lists, window, state, scratch)


def below_kernel(sorted_list, below, live, own_features, own_centres, *refs, length):
    targets, features, centres, total, own_total = refs[:5]
    window, lists, sems, own_lists, own_sems = refs[5:10]
    scratch = refs[10:]
    to_scalars = read_list(6, sorted_list, lists, sems)
    own_to_scalars = read_list(5, sorted_list, own_lists, own_sems)
    total[...] = jnp.zeros_like(total)
    own_total[...] = jnp.zeros_like(own_total)
    put_tiles(window, 0, below, length)
    to_scalars.wait()
    run_class(lists, window, (targets, features, centres, total), scratch)
    own_to_scalars.wait()
    run_class(own_lists, window, (live, own_features, own_centres, own_total), scratch)


def single_kernel(sorted_list, tiles, targets, features, centres, *refs, kind, run, length):
    total, window, lists, sems = refs[:4]
    to_scalars = read_list(kind, sorted_list, lists, sems)
    total[...] = jnp.zeros_like(total)
    put_tiles(window, 0, tiles, length)
    to_scalars.wait()
    window = shifted_window(window, run * (tiles.shape[0] // ROWS))
    run_class(lists, window, (targets, features, centres, total), refs[4:])


def far_kernel(sorted_list, below, above, crossed, *refs, length):
    targets, features, centres, near_total, below_total, middle_total = refs[:6]
    window, out_ref, total, lists, sems = refs[6:11]
    scratch = refs[11:]
    state = (targets, features, centres, total)
    to_scalars = read_list(3, sorted_list, lists, sems)
    blocks = below.shape[0] // ROWS
    put_tiles(window, 0, below, length)
    put_tiles(window, 2 * REACH * blocks, above, length)
    put_tiles(window, (2 * REACH - side_of_partner()) * blocks, crossed, length)
    total[...] = jnp.zeros_like(total)
    to_scalars.wait()
    run_class(lists, window, state, scratch)
    finish(targets, centres, (near_total, below_total, middle_total, total), out_ref)


def last_kernel(sorted_list, window, own, features, centres, *refs):
    home_total, below_total, out_ref, total, lists, sems = refs[:6]
    to_scalars = read_list(4, sorted_list, lists, sems)
    total[...] = jnp.zeros_like(total)
    to_scalars.wait()
    run_class(lists, window, (own, features, centres, total), refs[6:])
    finish(own, centres, (home_total, below_total, total), out_ref)


def section_kernel(own, sums, *refs):
    returned, (velocity, stretching, section_positions, section_strengths) = refs[:-4], refs[-4:]
    blocks = own.shape[0] // ROWS
    for b in range(blocks):
        lanes = slice(b * BLOCK, (b + 1) * BLOCK)
        for start, result, stepped in ((0, velocity, section_positions), (3, stretching, section_strengths)):
            chosen = pl.ds(start * blocks + b, 3, stride=blocks)
            value = sums[chosen, :]
            for other in returned:
                value = value + other[chosen, :]
            result[:, lanes] = value
            first = b * ROWS + start
            stepped[:, lanes] = own[first : first + 3, :] + section_step * value


def call(kernel, name, inputs, outputs, scratch, flops=0):
    vmem = pl.BlockSpec(memory_space=pltpu.VMEM)
    smem = pl.BlockSpec(memory_space=pltpu.SMEM)
    held = sum(value.size * value.dtype.itemsize for value in (*inputs, *outputs))
    return pl.pallas_call(
        kernel,
        out_shape=outputs,
        in_specs=[smem if value.dtype == jnp.int32 and value.ndim == 1 else vmem for value in inputs],
        out_specs=[vmem for value in outputs],
        scratch_shapes=scratch,
        compiler_params=pltpu.CompilerParams(vmem_limit_bytes=10 * 1024 * 1024 + 2 * held),
        cost_estimate=pl.CostEstimate(flops=flops, bytes_accessed=0, transcendentals=0),
        name=name,
    )(*inputs)


def shards(positions, strengths, radius, block_count, pair_target, pair_slot, pair_count):
    blocks = block_count.shape[0]
    lanes = blocks * BLOCK
    length = pair_target.shape[1]
    members = lax.axis_size("across")
    shard = lax.axis_index("blk")
    count = lax.axis_size("blk")

    def f32(*shape):
        return jax.ShapeDtypeStruct(shape, jnp.float32)

    parts = [value.reshape(3, blocks, BLOCK).transpose(1, 0, 2) for value in (positions, strengths)]
    rows, start = [], 0
    for value in (pair_target[0], pair_slot[0], block_count):
        rows.append(jnp.pad(value, (start, lanes - start - value.shape[0])))
        start += -(-value.shape[0] // BLOCK) * BLOCK
    listed = sum(rows).astype(jnp.float32).reshape(blocks, 1, BLOCK)
    own = jnp.concatenate(parts + [radius.reshape(blocks, 1, BLOCK), listed], axis=1)
    own = own.reshape(blocks * ROWS, BLOCK)
    others = [
        moved(own, "across", lambda source: (source - away) % members) for away in range(1, members)
    ]
    partner = moved(own, "blk", to_other_core)
    below = moved(own, "blk", shifted(REACH, count))

    def state_shapes(number):
        return [
            f32(number * blocks * ROWS, BLOCK),
            jax.ShapeDtypeStruct((number * blocks, FEATURES, 2 * BLOCK), jnp.bfloat16),
            f32(number * blocks * ROWS, BLOCK),
            f32(number * blocks * 2 * ROWS, BLOCK),
        ]

    own_shapes, other_shapes = state_shapes(1), state_shapes(members - 1)
    window_shape = f32((2 * REACH + 1) * blocks * ROWS, BLOCK)
    rows = list_rows(length)
    list_shape = jax.ShapeDtypeStruct((CLASSES - 1, -(-rows // ROWS) * ROWS, BLOCK), jnp.int32)
    feature_rows = [pltpu.VMEM((GROUP * ROWS, BLOCK), jnp.float32)] * 2
    list_scratch = [pltpu.SMEM((rows, BLOCK), jnp.int32), pltpu.SemaphoreType.DMA((1,))]
    scratch = [pltpu.VMEM((GROUP * ROWS, BLOCK), jnp.float32)] * 4 + [
        pltpu.VMEM((HALF, BLOCK, 2 * BLOCK), jnp.float32),
        pltpu.VMEM((HALF, BLOCK, 2 * BLOCK), jnp.float32),
    ]
    window_scratch = pltpu.VMEM(window_shape.shape, jnp.float32)

    lists, live, *own_state = call(
        lambda *refs: home_kernel(*refs, members=members, length=length),
        "home_pairs",
        (pair_count, own, partner),
        [list_shape] + own_shapes,
        [window_scratch] + feature_rows + list_scratch + scratch,
        flops=HOME_FLOPS,
    )
    late, lists = lax.optimization_barrier((own, lists))
    above = moved(late, "blk", shifted(-REACH, count))
    other_state = list(call(
        lambda *refs: near_kernel(*refs, members=members, length=length),
        "near_pairs",
        (lists, live, partner, *others),
        other_shapes,
        [window_scratch] + feature_rows + list_scratch + scratch,
        flops=NEAR_FLOPS,
    ))
    below_total, below_own_total = call(
        lambda *refs: below_kernel(*refs, length=length),
        "below_pairs",
        (lists, below, live, *own_state[:2], *other_state[:3]),
        [other_shapes[3], own_shapes[3]],
        [pltpu.VMEM(own.shape, jnp.float32)] + 2 * list_scratch + scratch,
        flops=HOME_FLOPS,
    )
    above, below_total = lax.optimization_barrier((above, below_total))
    crossed = moved(jnp.where(shard % 2 == 0, above, below), "blk", to_other_core)
    (middle_total,) = call(
        lambda *refs: single_kernel(*refs, kind=2, run=2 * REACH, length=length),
        "middle_pairs",
        (lists, above, *other_state[:3]),
        [other_shapes[3]],
        [pltpu.VMEM(own.shape, jnp.float32)] + list_scratch + scratch,
        flops=HOME_FLOPS,
    )
    crossed, middle_total = lax.optimization_barrier((crossed, middle_total))
    window, away_sums = call(
        lambda *refs: far_kernel(*refs, length=length),
        "far_pairs",
        (lists, below, above, crossed, *other_state, below_total, middle_total),
        [window_shape, f32(members - 1, 6 * blocks, BLOCK)],
        [pltpu.VMEM(other_shapes[3].shape, jnp.float32)] + list_scratch + scratch,
        flops=FAR_FLOPS,
    )
    returned = [
        moved(away_sums[away - 1], "across", lambda source: (source + away) % members)
        for away in range(1, members)
    ]
    (sums,) = call(
        last_kernel,
        "last_pairs",
        (lists, window, live, *own_state, below_own_total),
        [f32(1, 6 * blocks, BLOCK)],
        [pltpu.VMEM(own_shapes[3].shape, jnp.float32)] + list_scratch + scratch,
        flops=FAR_FLOPS,
    )
    wide = f32(3, lanes)
    return tuple(
        call(section_kernel, "section", (live, sums[0], *returned), [wide] * 4, [])
    )


def solution(mesh):
    whole = P(None, ("blk", "across"))
    line = P(("blk", "across"))
    return jax.shard_map(
        shards,
        mesh=mesh,
        in_specs=(whole, whole, line, line, P(("blk", "across"), None), P(("blk", "across"), None), line),
        out_specs=(whole, whole, whole, whole),
        check_vma=False,
    )
```
